32 devices in a mesh: dp: 8 (over z, y), tensor: 4 (over x, core).
Axes of the slice: x: 2, y: 2, z: 4, core: 2. Of those that a mesh axis runs over, the one named last changes fastest.
Arguments:
- tokens_in: bfloat16 [16384, 768], P('dp'), may hold values from -6 to 6
- box_coords: int32 [16384, 4], P('dp'), may hold values from 0 to 999
- rel_x: int32 [32, 512, 512], P('dp'), may hold values from 0 to 31
- rel_y: int32 [32, 512, 512], P('dp'), may hold values from 0 to 31
- mask_tokens: int32 [16384], P('dp'), may hold values from 0 to 1, as said below
- cotangent: bfloat16 [16384, 768], P('dp'), may hold values from -14336 to 14336
- layout_weight: bfloat16 [512, 768], replicated, may hold values from -0.25 to 0.25
- qkv_weight: bfloat16 [3, 768, 768], P(None, None, 'tensor'), may hold values from -0.21875 to 0.21875
- qv_bias: float32 [2, 768], P(None, 'tensor'), may hold values from -4 to 4
- bias_table: bfloat16 [64, 12], P(None, 'tensor'), may hold values from -6 to 6
- out_weight: bfloat16 [768, 768], P('tensor'), may hold values from -1.75 to 1.75
- out_bias: float32 [768], replicated, may hold values from -4 to 4
- ln1_gain: float32 [768], replicated, may hold values from 0.1 to 1.9
- ln1_bias: float32 [768], replicated, may hold values from -4 to 4
- ffn_in_weight: bfloat16 [768, 3072], P(None, 'tensor'), may hold values from -0.21875 to 0.21875
- ffn_in_bias: float32 [3072], P('tensor'), may hold values from -4 to 4
- ffn_out_weight: bfloat16 [3072, 768], P('tensor'), may hold values from -0.109375 to 0.109375
- ffn_out_bias: float32 [768], replicated, may hold values from -4 to 4
- ln2_gain: float32 [768], replicated, may hold values from 0.1 to 1.9
- ln2_bias: float32 [768], replicated, may hold values from -4 to 4
- group_rates: float32 [8], replicated, may hold values from 0.005 to 0.05
Outputs:
- block_out: bfloat16 [16384, 768], P('dp')
- input_grad: float32 [16384, 768], P('dp')
- layout_update: float32 [512, 768], replicated
- qkv_update: float32 [3, 768, 768], P(None, None, 'tensor')
- qv_bias_update: float32 [2, 768], P(None, 'tensor')
- table_update: float32 [64, 12], P(None, 'tensor')
- out_update: float32 [768, 768], P('tensor')
- out_bias_update: float32 [768], replicated
- ln1_gain_update: float32 [768], replicated
- ln1_bias_update: float32 [768], replicated
- ffn_in_update: float32 [768, 3072], P(None, 'tensor')
- ffn_in_bias_update: float32 [3072], P('tensor')
- ffn_out_update: float32 [3072, 768], P('tensor')
- ffn_out_bias_update: float32 [768], replicated
- ln2_gain_update: float32 [768], replicated
- ln2_bias_update: float32 [768], replicated
The draws below stay inside these ranges and needn't reach their ends.
Inputs may be any that keep to these rules, and one draw needn't show every extreme that they name: `mask_tokens`: each window of 512 tokens has at least one masked token.
All inputs are finite; a program needn't handle non-finite values.
Results may differ from the reference program's by a relative error of at most 0.018.
The reference program's roundings to bfloat16 on the way count: a program that leaves them out, or rounds other values in their place, can miss the bound.
Values may be sent and summed in bfloat16 or wider, within the bound.
A program may use at most 192 MiB of HBM per device.

```python
import math
import jax
import jax.numpy as jnp
from jax import lax

D = 768
HEADS = 12
HD = 64
FF = 3072
BUCKETS = 32
LFREQ = 64
GROUPS = 8
WIN = 512
WINDOWS = 32
TOKENS = 16384
LAYOUT_FEATS = 512


def draw_mask_tokens(key, part):
    key = jax.random.fold_in(key, 11)
    first_key, second_key = jax.random.split(key)
    position = jnp.arange(TOKENS, dtype=jnp.int32)
    window = position // WIN
    limit = 80 + 160 * window // max(WINDOWS - 1, 1)
    chance = jax.random.randint(first_key, (TOKENS,), 0, 1000)
    chosen = jax.random.randint(second_key, (WINDOWS,), 0, WIN)
    forced = position % WIN == jnp.repeat(chosen, WIN)
    return jnp.where((chance < limit) | forced, 1, 0).astype(jnp.int32)


def touch_ends(values, own_key, least, largest):
    dims = values.shape
    index_at = [jax.random.randint(jax.random.fold_in(own_key, axis), (), 0, dims[axis]) for axis in range(len(dims))]
    values = values.at[tuple(index_at)].set(least)
    longest = dims.index(max(dims))
    index_at[longest] = (index_at[longest] + 1) % dims[longest]
    return values.at[tuple(index_at)].set(largest)


def level_of(rng, shape, cuts, smallest, high):
    def one(dim, shards_of):
        steps = jax.random.uniform(jax.random.fold_in(jax.random.fold_in(rng, 6), dim), (shards_of,), jnp.float32, smallest / len(cuts), high / len(cuts))
        return jnp.repeat(jnp.exp(steps), shape[dim] // shards_of).reshape((-1,) + (1,) * (len(shape) - dim - 1))

    gain = one(*cuts[0])
    for cut in cuts[1:]:
        gain = gain * one(*cut)
    return gain


def centred(own_key, dims, width, most, shards=(), kind=jnp.bfloat16):
    result = jax.random.normal(own_key, dims, jnp.float32) * width
    if len(shards) > 0:
        result = level_of(own_key, dims, shards, -0.22, 0.18) * result
    return jnp.clip(result, min=-most, max=most).astype(kind)


def setup_inputs(seed: int = 0) -> dict:
    key_of = jax.random.split(jax.random.key(seed), 22)
    return {
        "tokens_in": centred(key_of[0], (TOKENS, D), 1.0, 6.0, ((0, 8),)),
        "box_coords": touch_ends(jax.random.randint(key_of[1], (TOKENS, 4), 0, 1000), jax.random.fold_in(key_of[1], 1), 0, 999).astype(jnp.int32),
        "rel_x": touch_ends(jax.random.randint(key_of[2], (WINDOWS, WIN, WIN), 0, BUCKETS), jax.random.fold_in(key_of[2], 1), 0, BUCKETS - 1).astype(jnp.int32),
        "rel_y": touch_ends(jax.random.randint(key_of[3], (WINDOWS, WIN, WIN), 0, BUCKETS), jax.random.fold_in(key_of[3], 1), 0, BUCKETS - 1).astype(jnp.int32),
        "mask_tokens": draw_mask_tokens(jax.random.fold_in(key_of[21], 71), 0),
        "cotangent": centred(key_of[5], (TOKENS, D), (3 * TOKENS // 20), 14336.0, ((0, 8),)),
        "layout_weight": centred(key_of[6], (LAYOUT_FEATS, D), LAYOUT_FEATS ** -0.5, 0.25),
        "qkv_weight": centred(key_of[7], (3, D, D), D ** -0.5, 0.21875, ((2, 4),)),
        "qv_bias": centred(key_of[8], (2, D), 0.3, 4.0, ((1, 4),), jnp.float32),
        "bias_table": centred(key_of[9], (2 * BUCKETS, HEADS), 0.5, 6.0, ((1, 4),)),
        "out_weight": centred(key_of[10], (D, D), (D // 64) ** -0.5, 1.75, ((0, 4),)),
        "out_bias": centred(key_of[11], (D,), 0.3, 4.0, (), jnp.float32),
        "ln1_gain": jnp.clip(1.0 + 0.18 * jax.random.normal(key_of[12], (D,), jnp.float32), 0.1, 1.9),
        "ln1_bias": centred(key_of[13], (D,), 0.3, 4.0, (), jnp.float32),
        "ffn_in_weight": centred(key_of[14], (D, FF), D ** -0.5, 0.21875, ((1, 4),)),
        "ffn_in_bias": centred(key_of[15], (FF,), 0.3, 4.0, ((0, 4),), jnp.float32),
        "ffn_out_weight": centred(key_of[16], (FF, D), FF ** -0.5, 0.109375, ((0, 4),)),
        "ffn_out_bias": centred(key_of[17], (D,), 0.3, 4.0, (), jnp.float32),
        "ln2_gain": jnp.clip(1.0 + 0.18 * jax.random.normal(key_of[18], (D,), jnp.float32), 0.1, 1.9),
        "ln2_bias": centred(key_of[19], (D,), 0.3, 4.0, (), jnp.float32),
        "group_rates": jnp.clip(jnp.exp(jax.random.uniform(key_of[20], (GROUPS,), jnp.float32, math.log(0.005), math.log(0.05))), 0.005, 0.05),
    }


EPSILON = 1e-05
PRECISION_HIGH = lax.Precision.HIGHEST

@jax.custom_vjp
def low(v):
    return lax.optimization_barrier(v.astype(jnp.bfloat16)).astype(jnp.float32)

@jax.custom_vjp
def low_back(v):
    return v

def low_keep(v):
    return (low(v), None)

def low_pass(kept, grad):
    return (grad,)

def back_keep(v):
    return (v, None)

def back_low(kept, grad):
    return (low(grad),)
low.defvjp(low_keep, low_pass)
low_back.defvjp(back_keep, back_low)

def layout_features(box_coords):
    freq_index = jnp.arange(LFREQ).astype(jnp.float32)
    frequency = jnp.exp(freq_index * (-math.log(1000.0) / LFREQ))
    angles = box_coords.astype(jnp.float32)[:, :, None] * frequency[None, None, :]
    waves = jnp.concatenate([jnp.sin(angles), jnp.cos(angles)], axis=2)
    return waves.reshape(box_coords.shape[0], 8 * LFREQ)

def normalize(values_in, gain_vec, shift_vec):
    row_mean = lax.optimization_barrier(jnp.mean(values_in, axis=-1, keepdims=True))
    centered = values_in - row_mean
    variance = lax.optimization_barrier(jnp.mean(centered * centered, axis=-1, keepdims=True))
    return centered * lax.rsqrt(variance + EPSILON) * gain_vec + shift_vec

def window_attention(queries, key_rows, values, rel_x, rel_y, bias_table):
    pos_bias = bias_table[rel_x] + bias_table[BUCKETS + rel_y]
    scores = jnp.einsum('ihd,jhd->hij', queries, key_rows, precision=PRECISION_HIGH) * HD ** (-0.5)
    scores = low_back(scores + jnp.transpose(pos_bias, (2, 0, 1)))
    attn_probs = jax.nn.softmax(scores, axis=-1)
    attended = jnp.einsum('hij,jhd->ihd', low(attn_probs), values, precision=PRECISION_HIGH)
    return attended.reshape(WIN, HEADS * HD)

def forward(tokens_in, layout_weight, qkv_weight, qv_bias, bias_table, out_weight, out_bias, ln1_gain, ln1_bias, ffn_in_weight, ffn_in_bias, ffn_out_weight, ffn_out_bias, ln2_gain, ln2_bias, features, rel_x, rel_y):
    layer_in = tokens_in + low_back(jnp.dot(features, layout_weight, precision=PRECISION_HIGH))
    layer_low = low(layer_in)
    queries = low(low_back(jnp.dot(layer_low, qkv_weight[0], precision=PRECISION_HIGH) + qv_bias[0]))
    key_rows = low(low_back(jnp.dot(layer_low, qkv_weight[1], precision=PRECISION_HIGH)))
    values = low(low_back(jnp.dot(layer_low, qkv_weight[2], precision=PRECISION_HIGH) + qv_bias[1]))
    block_shape = (WINDOWS, WIN, HEADS, HD)

    def one_window(pieces):
        return jax.checkpoint(window_attention)(pieces[0], pieces[1], pieces[2], pieces[3], pieces[4], bias_table)
    context = lax.map(one_window, (queries.reshape(block_shape), key_rows.reshape(block_shape), values.reshape(block_shape), rel_x, rel_y))
    context = low(low_back(context.reshape(TOKENS, D)))
    residual = layer_in + low_back(jnp.dot(context, out_weight, precision=PRECISION_HIGH)) + out_bias
    normed = normalize(residual, ln1_gain, ln1_bias)
    pre_act = low_back(jnp.dot(low(normed), ffn_in_weight, precision=PRECISION_HIGH) + ffn_in_bias)
    hidden = low(jax.nn.gelu(pre_act))
    residual_two = normed + low_back(jnp.dot(hidden, ffn_out_weight, precision=PRECISION_HIGH)) + ffn_out_bias
    return normalize(residual_two, ln2_gain, ln2_bias)

def reference(tokens_in, box_coords, rel_x, rel_y, mask_tokens, cotangent, layout_weight, qkv_weight, qv_bias, bias_table, out_weight, out_bias, ln1_gain, ln1_bias, ffn_in_weight, ffn_in_bias, ffn_out_weight, ffn_out_bias, ln2_gain, ln2_bias, group_rates):
    features = low(layout_features(box_coords))
    params = tuple((param.astype(jnp.float32) for param in (tokens_in, layout_weight, qkv_weight, qv_bias, bias_table, out_weight, out_bias, ln1_gain, ln1_bias, ffn_in_weight, ffn_in_bias, ffn_out_weight, ffn_out_bias, ln2_gain, ln2_bias)))

    def closed(*inputs):
        return forward(*inputs, features, rel_x, rel_y)
    output, pullback = jax.vjp(closed, *params)
    selected = mask_tokens.astype(jnp.float32)[:, None] * cotangent.astype(jnp.float32)
    gradients = pullback(selected)
    masked_count = jnp.sum(mask_tokens.astype(jnp.float32))
    factor = group_rates / masked_count
    return (output.astype(jnp.bfloat16), gradients[0] / masked_count, gradients[1] * factor[6], gradients[2] * factor[0], gradients[3] * factor[0], gradients[4] * factor[7], gradients[5] * factor[1], gradients[6] * factor[1], gradients[7] * factor[2], gradients[8] * factor[2], gradients[9] * factor[3], gradients[10] * factor[3], gradients[11] * factor[4], gradients[12] * factor[4], gradients[13] * factor[5], gradients[14] * factor[5])
```

```python
import functools
import math

import jax
import jax.numpy as jnp
from jax import lax
from jax.experimental import pallas as pl
from jax.experimental.pallas import tpu as pltpu
from jax.sharding import PartitionSpec as P

HD = 64
LFREQ = 64
BUCKETS = 32
EPSILON = 1e-05
ROWS = 16


def nt(a, b):
    return lax.dot_general(a, b, (((1,), (1,)), ((), ())), preferred_element_type=jnp.float32)


def nn(a, b):
    return jnp.dot(a, b, preferred_element_type=jnp.float32)


def layout_features(box_coords):
    freq_index = jnp.arange(LFREQ).astype(jnp.float32)
    frequency = jnp.exp(freq_index * (-math.log(1000.0) / LFREQ))
    angles = box_coords.astype(jnp.float32)[:, :, None] * frequency[None, None, :]
    waves = jnp.concatenate([jnp.sin(angles), jnp.cos(angles)], axis=2)
    return waves.reshape(box_coords.shape[0], 8 * LFREQ)


def normalize_keep(values_in, gain_vec, shift_vec):
    row_mean = jnp.mean(values_in, axis=-1, keepdims=True)
    centered = values_in - row_mean
    inverse = lax.rsqrt(jnp.mean(centered * centered, axis=-1, keepdims=True) + EPSILON)
    unit_rows = centered * inverse
    return (unit_rows * gain_vec + shift_vec, unit_rows, inverse)


def normalize_back(upstream, unit_rows, inverse, gain_vec):
    scaled = upstream * gain_vec
    mean_one = jnp.mean(scaled, axis=-1, keepdims=True)
    mean_two = jnp.mean(scaled * unit_rows, axis=-1, keepdims=True)
    return (
        (scaled - mean_one - unit_rows * mean_two) * inverse,
        jnp.sum(upstream * unit_rows, axis=0),
        jnp.sum(upstream, axis=0),
    )


def attend_kernel(q_ref, k_ref, v_ref, rx_ref, ry_ref, tab_ref, p_ref, c_ref):
    head = pl.program_id(0)
    win = rx_ref.shape[0]
    q = (q_ref[...].astype(jnp.float32).T * HD ** (-0.5)).astype(jnp.bfloat16)
    s = nn(q, k_ref[...])
    tab = jnp.broadcast_to(tab_ref[pl.ds(head, 1), :], (win, 128))
    parts = []
    for c in range(win // 128):
        sl = slice(128 * c, 128 * c + 128)
        bias_x = jnp.take_along_axis(tab, rx_ref[:, sl], axis=1)
        bias_y = jnp.take_along_axis(tab, ry_ref[:, sl] + BUCKETS, axis=1)
        parts.append(s[:, sl] + (bias_x + bias_y))
    s = jnp.concatenate(parts, axis=1)
    m = jnp.max(s, axis=1, keepdims=True)
    e = jnp.exp(s - m)
    p = e * (1.0 / jnp.sum(e, axis=1, keepdims=True))
    p_ref[0] = p
    c_ref[...] = nt(v_ref[...], p.astype(jnp.bfloat16)).astype(jnp.bfloat16)


def attend(q, k, v, rel_x, rel_y, tab):
    heads, win = tab.shape[0], rel_x.shape[0]
    blk = pl.BlockSpec((HD, win), lambda h: (h, 0))
    full = pl.BlockSpec((win, win), lambda h: (0, 0))
    return pl.pallas_call(
        attend_kernel,
        grid=(heads,),
        in_specs=[blk, blk, blk, full, full, pl.BlockSpec(tab.shape, lambda h: (0, 0))],
        out_specs=[pl.BlockSpec((1, win, win), lambda h: (h, 0, 0)), blk],
        out_shape=[
            jax.ShapeDtypeStruct((heads, win, win), jnp.float32),
            jax.ShapeDtypeStruct((heads * HD, win), jnp.bfloat16),
        ],
        compiler_params=pltpu.CompilerParams(vmem_limit_bytes=48 * 2**20),
        cost_estimate=pl.CostEstimate(
            flops=16 * 10**9, bytes_accessed=20 * 10**6, transcendentals=heads * win * win
        ),
        name="attend",
    )(q, k, v, rel_x, rel_y, tab)


def attend_back_kernel(
    q_ref, k_ref, v_ref, p_ref, dc_ref, rx_ref, ry_ref,
    dq_ref, dk_ref, dv_ref, g_ref, ds_scr, hot_scr, acc,
):
    head = pl.program_id(0)
    heads = pl.num_programs(0)
    win = rx_ref.shape[0]
    dc_t = dc_ref[...]
    dc = dc_t.astype(jnp.float32).T.astype(jnp.bfloat16)
    p = p_ref[0]
    dp = nn(dc, v_ref[...])
    row_dot = jnp.sum(p * dp, axis=1, keepdims=True)
    ds = (p * (dp - row_dot)).astype(jnp.bfloat16)
    dv_ref[...] = nn(dc_t, p.astype(jnp.bfloat16)).astype(jnp.bfloat16)
    dq_ref[...] = (nt(k_ref[...], ds) * HD ** (-0.5)).astype(jnp.bfloat16)
    dk_ref[...] = (nn(q_ref[...], ds) * HD ** (-0.5)).astype(jnp.bfloat16)
    ds_scr[head] = ds

    @pl.when(head == heads - 1)
    def _():
        acc[...] = jnp.zeros_like(acc)
        one, zero = jnp.bfloat16(1), jnp.bfloat16(0)
        half = BUCKETS * ROWS

        def step(g, carry):
            rows = pl.ds(pl.multiple_of(g * ROWS, ROWS), ROWS)
            x = rx_ref[rows, :].astype(jnp.float32).astype(jnp.bfloat16)
            y = ry_ref[rows, :].astype(jnp.float32).astype(jnp.bfloat16)
            for b in range(BUCKETS):
                hot_scr[b * ROWS : (b + 1) * ROWS, :] = jnp.where(x == jnp.bfloat16(b), one, zero)
                hot_scr[half + b * ROWS : half + (b + 1) * ROWS, :] = jnp.where(
                    y == jnp.bfloat16(b), one, zero
                )
            left = ds_scr[:, rows, :].reshape(ds_scr.shape[0] * ROWS, win)
            acc[...] += nt(left, hot_scr[...])
            return carry

        lax.fori_loop(0, win // ROWS, step, 0)
        row = lax.broadcasted_iota(jnp.int32, (ROWS, 2 * half), 0)
        col = lax.broadcasted_iota(jnp.int32, (ROWS, 2 * half), 1) % ROWS
        for h in range(ds_scr.shape[0]):
            part = jnp.where(row == col, acc[h * ROWS : (h + 1) * ROWS, :], 0.0)
            g_ref[h : h + 1, :] = jnp.sum(part, axis=0, keepdims=True)


def attend_back(q, k, v, p, dc, rel_x, rel_y):
    heads, win = p.shape[0], rel_x.shape[0]
    hots = 2 * BUCKETS * ROWS
    blk = pl.BlockSpec((HD, win), lambda h: (h, 0))
    full = pl.BlockSpec((win, win), lambda h: (0, 0))
    dq, dk, dv, g = pl.pallas_call(
        attend_back_kernel,
        grid=(heads,),
        in_specs=[blk, blk, blk, pl.BlockSpec((1, win, win), lambda h: (h, 0, 0)), blk, full, full],
        out_specs=[blk, blk, blk, pl.BlockSpec((heads, hots), lambda h: (0, 0))],
        out_shape=[jax.ShapeDtypeStruct((heads * HD, win), jnp.bfloat16)] * 3
        + [jax.ShapeDtypeStruct((heads, hots), jnp.float32)],
        scratch_shapes=[
            pltpu.VMEM((heads, win, win), jnp.bfloat16),
            pltpu.VMEM((hots, win), jnp.bfloat16),
            pltpu.VMEM((heads * ROWS, hots), jnp.float32),
        ],
        compiler_params=pltpu.CompilerParams(vmem_limit_bytes=56 * 2**20),
        cost_estimate=pl.CostEstimate(
            flops=20 * 10**9, bytes_accessed=20 * 10**6, transcendentals=0
        ),
        name="attend_back",
    )(q, k, v, p, dc, rel_x, rel_y)
    return dq, dk, dv, jnp.sum(g.reshape(heads, 2 * BUCKETS, ROWS), axis=2).T


def bits_of(size):
    return [1 << b for b in range(size.bit_length() - 1)]


def swap(value, axis, size, bit):
    return lax.ppermute(value, axis, [(i, i ^ bit) for i in range(size)])


def gather_pieces(own, axis, size):
    pieces = {0: own}
    for bit in reversed(bits_of(size)):
        for r in list(pieces):
            pieces[r | bit] = swap(pieces[r], axis, size, bit)
    return [pieces[r] for r in range(size)]


def scatter_pieces(pieces, axis, size):
    pieces = dict(enumerate(pieces))
    for bit in bits_of(size):
        for r in [r for r in pieces if r & bit]:
            got = swap(pieces.pop(r).astype(jnp.bfloat16), axis, size, bit)
            pieces[r ^ bit] = pieces[r ^ bit].astype(jnp.float32) + got.astype(jnp.float32)
    return pieces[0]


def reduce_rows(total, axis, size):
    me = lax.axis_index(axis)
    held = total
    for bit in bits_of(size):
        half = held.shape[0] // 2
        side = (me // bit) % 2
        mine = lax.dynamic_slice_in_dim(held, side * half, half)
        other = lax.dynamic_slice_in_dim(held, (1 - side) * half, half)
        got = swap(other.astype(jnp.bfloat16), axis, size, bit)
        held = mine.astype(jnp.float32) + got.astype(jnp.float32)
    held = held.astype(jnp.bfloat16)
    for bit in reversed(bits_of(size)):
        got = swap(held, axis, size, bit)
        side = (me // bit) % 2
        held = jnp.where(
            side == 0, jnp.concatenate([held, got]), jnp.concatenate([got, held])
        )
    return held


def sum_small(value, axis, size):
    for bit in bits_of(size):
        value = value + swap(value, axis, size, bit)
    return value


def place_pieces(pieces, me):
    size, rows = len(pieces), pieces[0].shape[0]
    whole = jnp.zeros((size * rows,) + pieces[0].shape[1:], pieces[0].dtype)
    for r, piece in enumerate(pieces):
        whole = lax.dynamic_update_slice_in_dim(whole, piece, (me ^ r) * rows, 0)
    return whole


def local(
    n_dp, n_t,
    tokens_in, box_coords, rel_x, rel_y, mask_tokens, cotangent, layout_weight, qkv_weight, qv_bias,
    bias_table, out_weight, out_bias, ln1_gain, ln1_bias, ffn_in_weight, ffn_in_bias, ffn_out_weight,
    ffn_out_bias, ln2_gain, ln2_bias, group_rates,
):
    me = lax.axis_index("tensor")
    win = rel_x.shape[1]
    model = tokens_in.shape[1]
    heads_t = bias_table.shape[1]
    cols_t = heads_t * HD
    hid_t = ffn_in_weight.shape[1]
    tok_rows = tokens_in.shape[0] // n_t

    def mine(whole):
        return lax.dynamic_slice_in_dim(whole, me * (whole.shape[0] // n_t), whole.shape[0] // n_t)

    qkv_rows = jnp.transpose(qkv_weight, (0, 2, 1))
    small_own = jnp.concatenate(
        [qv_bias.reshape(-1), ffn_in_bias, bias_table.T.astype(jnp.float32).reshape(-1)]
    )
    small_all = gather_pieces(small_own, "tensor", n_t)
    qkv_all = gather_pieces(qkv_rows, "tensor", n_t)
    rest_all = gather_pieces(
        jnp.concatenate([out_weight, ffn_in_weight.T, ffn_out_weight], axis=0), "tensor", n_t
    )
    wqkv = [jnp.concatenate([piece[n] for piece in qkv_all], axis=0) for n in range(3)]
    wo = jnp.concatenate([piece[:cols_t] for piece in rest_all], axis=0)
    w1 = jnp.concatenate([piece[cols_t : cols_t + hid_t] for piece in rest_all], axis=0)
    w2 = jnp.concatenate([piece[cols_t + hid_t :] for piece in rest_all], axis=0)
    bq = jnp.concatenate([piece[:cols_t] for piece in small_all])
    bv = jnp.concatenate([piece[cols_t : 2 * cols_t] for piece in small_all])
    b1 = jnp.concatenate([piece[2 * cols_t : 2 * cols_t + hid_t] for piece in small_all])
    table = jnp.concatenate(
        [piece[2 * cols_t + hid_t :].reshape(heads_t, 2 * BUCKETS) for piece in small_all]
    )
    table = jnp.pad(table, ((0, 0), (0, 128 - 2 * BUCKETS)))

    count = sum_small(jnp.sum(mask_tokens.astype(jnp.float32)).reshape(1), "dp", n_dp)[0]

    features = layout_features(mine(box_coords)).astype(jnp.bfloat16)
    layer_in = mine(tokens_in).astype(jnp.float32) + nn(features, layout_weight)
    layer_low = layer_in.astype(jnp.bfloat16)
    queries = (nt(wqkv[0], layer_low) + bq[:, None]).astype(jnp.bfloat16)
    key_rows = nt(wqkv[1], layer_low).astype(jnp.bfloat16)
    values = (nt(wqkv[2], layer_low) + bv[:, None]).astype(jnp.bfloat16)
    relx, rely = mine(rel_x)[0], mine(rel_y)[0]
    probs, context_t = attend(queries, key_rows, values, relx, rely, table)
    context = context_t.T
    residual = layer_in + nn(context, wo) + out_bias
    normed, unit_one, inverse_one = normalize_keep(residual, ln1_gain, ln1_bias)
    normed_low = normed.astype(jnp.bfloat16)
    pre_act = nt(normed_low, w1) + b1
    activated, gelu_back = jax.vjp(jax.nn.gelu, pre_act)
    hidden = activated.astype(jnp.bfloat16)
    residual_two = normed + nn(hidden, w2) + ffn_out_bias
    output, unit_two, inverse_two = normalize_keep(residual_two, ln2_gain, ln2_bias)
    block_out = lax.all_gather(output.astype(jnp.bfloat16), "tensor", axis=0, tiled=True)

    selected = mine(mask_tokens).astype(jnp.float32)[:, None] * mine(cotangent).astype(jnp.float32)
    dresid_two, grad_g2, grad_b2 = normalize_back(selected, unit_two, inverse_two, ln2_gain)
    dffn_low = dresid_two.astype(jnp.bfloat16)
    grad_c2 = jnp.sum(dresid_two, axis=0)
    grad_w2 = nn(hidden.T, dffn_low)
    dpre_act = gelu_back(nt(dffn_low, w2))[0].astype(jnp.bfloat16)
    grad_c1 = jnp.sum(dpre_act, axis=0, dtype=jnp.float32)
    grad_w1 = nn(dpre_act.T, normed_low)
    dnormed = dresid_two + nn(dpre_act, w1)
    dresidual, grad_g1, grad_b1 = normalize_back(dnormed, unit_one, inverse_one, ln1_gain)

    def reduced(parts):
        pieces = [
            jnp.concatenate([part[r * rows : (r + 1) * rows] for part, rows in parts], axis=0)
            for r in range(n_t)
        ]
        return reduce_rows(scatter_pieces(pieces, "tensor", n_t), "dp", n_dp)

    w2_sum = reduced([(grad_w2, hid_t)])
    w1_sum = reduced([(grad_w1, hid_t)])

    grad_ob = jnp.sum(dresidual, axis=0)
    dattn_low = dresidual.astype(jnp.bfloat16)
    grad_ow = nn(context_t, dattn_low)
    dcontext = nt(wo, dattn_low).astype(jnp.bfloat16)
    dq, dk, dv, grad_table = attend_back(
        queries, key_rows, values, probs, dcontext, relx, rely
    )
    grad_qkv = [nn(d, layer_low) for d in (dq, dk, dv)]
    grad_bq = jnp.sum(dq, axis=1, dtype=jnp.float32)
    grad_bv = jnp.sum(dv, axis=1, dtype=jnp.float32)
    dlayer = dresidual + sum(nn(d.T, w) for d, w in zip((dq, dk, dv), wqkv))
    grad_lay = nn(features.T, dlayer.astype(jnp.bfloat16))
    lay_rows = grad_lay.shape[0] // n_t
    lay_pieces = [
        lax.dynamic_slice_in_dim(grad_lay, (me ^ r) * lay_rows, lay_rows) for r in range(n_t)
    ]
    rest_sum = reduced(
        [(g, cols_t) for g in grad_qkv]
        + [(grad_ow, cols_t), (jnp.concatenate(lay_pieces, axis=0), lay_rows)]
    )
    din = (dlayer / count).astype(jnp.bfloat16)
    input_grad = place_pieces(gather_pieces(din, "tensor", n_t), me).astype(jnp.float32)
    lay_sum = place_pieces(gather_pieces(rest_sum[4 * cols_t :], "tensor", n_t), me)

    def pieces_of(vec, size):
        return vec.reshape(n_t, size)

    split = jnp.concatenate(
        [
            pieces_of(grad_bq, cols_t),
            pieces_of(grad_bv, cols_t),
            pieces_of(grad_c1, hid_t),
            pieces_of(grad_table.T, heads_t * 2 * BUCKETS),
        ],
        axis=1,
    )
    common = jnp.concatenate([grad_ob, grad_g1, grad_b1, grad_c2, grad_g2, grad_b2])
    whole = jnp.zeros_like(split)
    for r in range(n_t):
        whole = lax.dynamic_update_slice_in_dim(whole, split[r : r + 1], me ^ r, 0)
    flat = jnp.concatenate([whole.reshape(-1), common])
    flat = sum_small(sum_small(flat, "tensor", n_t), "dp", n_dp)
    width = split.shape[1]
    own = lax.dynamic_slice_in_dim(flat, me * width, width)
    common = flat[n_t * width :].reshape(6, model)

    factor = group_rates / count
    f32 = jnp.float32
    qkv_sum = rest_sum[: 3 * cols_t].reshape(3, cols_t, model)
    return (
        block_out,
        input_grad,
        lay_sum.astype(f32) * factor[6],
        jnp.transpose(qkv_sum, (0, 2, 1)).astype(f32) * factor[0],
        own[: 2 * cols_t].reshape(2, cols_t) * factor[0],
        own[2 * cols_t + hid_t :].reshape(heads_t, 2 * BUCKETS).T * factor[7],
        rest_sum[3 * cols_t : 4 * cols_t].astype(f32) * factor[1],
        common[0] * factor[1],
        common[1] * factor[2],
        common[2] * factor[2],
        w1_sum.T.astype(f32) * factor[3],
        own[2 * cols_t : 2 * cols_t + hid_t] * factor[3],
        w2_sum.astype(f32) * factor[4],
        common[3] * factor[4],
        common[4] * factor[5],
        common[5] * factor[5],
    )


def solution(mesh):
    placed = (
        P("dp", None), P("dp", None), P("dp", None, None), P("dp", None, None), P("dp"), P("dp", None),
        P(), P(None, None, "tensor"), P(None, "tensor"), P(None, "tensor"), P("tensor", None),
        P(), P(), P(), P(None, "tensor"), P("tensor"), P("tensor", None), P(), P(), P(), P(),
    )
    return jax.shard_map(
        functools.partial(local, mesh.shape["dp"], mesh.shape["tensor"]),
        mesh=mesh,
        in_specs=placed,
        out_specs=(
            P("dp", None), P("dp", None), P(), P(None, None, "tensor"), P(None, "tensor"),
            P(None, "tensor"), P("tensor", None), P(), P(), P(), P(None, "tensor"), P("tensor"),
            P("tensor", None), P(), P(), P(),
        ),
        check_vma=False,
    )
```

```python
import functools
import math

import jax
import jax.numpy as jnp
from jax import lax
from jax.experimental import pallas as pl
from jax.experimental.pallas import tpu as pltpu
from jax.sharding import PartitionSpec as P

HD = 64
LFREQ = 64
BUCKETS = 32
EPSILON = 1e-05
ROWS = 16
HEADS_T = 3
MESH = pl.DeviceIdType.MESH


def nt(a, b):
    return lax.dot_general(a, b, (((1,), (1,)), ((), ())), preferred_element_type=jnp.float32)


def nn(a, b):
    return jnp.dot(a, b, preferred_element_type=jnp.float32)


def layout_features(box_coords):
    freq_index = jnp.arange(LFREQ).astype(jnp.float32)
    frequency = jnp.exp(freq_index * (-math.log(1000.0) / LFREQ))
    angles = box_coords.astype(jnp.float32)[:, :, None] * frequency[None, None, :]
    waves = jnp.concatenate([jnp.sin(angles), jnp.cos(angles)], axis=2)
    return waves.reshape(box_coords.shape[0], 8 * LFREQ)


def normalize_keep(values_in, gain_vec, shift_vec):
    row_mean = jnp.mean(values_in, axis=-1, keepdims=True)
    centered = values_in - row_mean
    inverse = lax.rsqrt(jnp.mean(centered * centered, axis=-1, keepdims=True) + EPSILON)
    unit_rows = centered * inverse
    return (unit_rows * gain_vec + shift_vec, unit_rows, inverse)


def normalize_back(upstream, unit_rows, inverse, gain_vec):
    scaled = upstream * gain_vec
    mean_one = jnp.mean(scaled, axis=-1, keepdims=True)
    mean_two = jnp.mean(scaled * unit_rows, axis=-1, keepdims=True)
    return (
        (scaled - mean_one - unit_rows * mean_two) * inverse,
        jnp.sum(upstream * unit_rows, axis=0),
        jnp.sum(upstream, axis=0),
    )


def xor_index(index, bit):
    return index + bit - 2 * bit * ((index // bit) % 2)


def signal_peers(peers):
    barrier = pltpu.get_barrier_semaphore()
    for peer in peers:
        pl.semaphore_signal(barrier, inc=1, device_id=peer, device_id_type=MESH)
    pl.semaphore_wait(barrier, len(peers))


def remote(src, dst, send, recv, peer):
    return pltpu.make_async_remote_copy(
        src_ref=src, dst_ref=dst, send_sem=send, recv_sem=recv, device_id=peer, device_id_type=MESH
    )


class Gather:
    def __init__(self, own, place, rows, split, sems, slot, peers):
        self.own, self.place, self.rows, self.split = own, place, rows, split
        self.send, self.recv, self.here = sems
        self.slot = slot
        self.mate, self.across, self.beside, self.side = peers

    def copy(self, name):
        s = self.slot
        half = self.rows // 2 if self.split else self.rows
        mine = pl.ds(pl.multiple_of(self.side * half, half), half) if self.split else pl.ds(0, half)
        yours = pl.ds(pl.multiple_of((1 - self.side) * half, half), half)
        whole = pl.ds(0, self.rows)
        if name == "here":
            return pltpu.make_async_copy(self.own(whole), self.place(0, whole), self.here.at[s])
        src, dst, peer, k = {
            "mate": lambda: (self.own(whole), self.place(1, whole), self.mate, 0),
            "across": lambda: (self.own(mine), self.place(2, mine), self.across, 1),
            "pass": lambda: (self.place(2, mine), self.place(3, mine), self.mate, 2),
            "beside": lambda: (self.place(2, mine), self.place(2, mine), self.beside, 3),
            "pass_two": lambda: (self.place(2, yours), self.place(3, yours), self.mate, 4),
        }[name]()
        return remote(src, dst, self.send.at[s, k], self.recv.at[s, k], peer)

    def start(self):
        self.copy("across").start()
        self.copy("mate").start()
        self.copy("here").start()

    def forward(self):
        self.copy("across").wait_recv()
        if self.split:
            self.copy("beside").start()
        self.copy("pass").start()

    def forward_two(self):
        if self.split:
            self.copy("beside").wait_recv()
            self.copy("pass_two").start()

    def arrive_near(self):
        self.copy("here").wait()
        self.copy("mate").wait_recv()

    def arrive_far(self):
        self.copy("pass").wait_recv()
        if self.split:
            self.copy("pass_two").wait_recv()

    def arrive(self):
        self.arrive_near()
        self.arrive_far()

    def finish(self):
        for name in ("mate", "across", "pass") + (("beside", "pass_two") if self.split else ()):
            self.copy(name).wait_send()


def waves(column, frequency, quarter):
    angle = column * frequency
    turns = jnp.floor(angle * (2.0 / math.pi) + 0.5)
    rest = ((angle - turns * 1.5703125) - turns * 4.837512969970703125e-4) - turns * 7.549789948768648e-8
    quadrant = turns.astype(jnp.int32) + quarter
    z = rest * rest
    sine = ((-1.9515295891e-4 * z + 8.3321608736e-3) * z - 1.6666654611e-1) * z * rest + rest
    cosine = ((2.443315711809948e-5 * z - 1.388731625493765e-3) * z + 4.166664568298827e-2) * z * z - 0.5 * z + 1.0
    value = jnp.where(quadrant % 2 == 1, cosine, sine)
    return jnp.where((quadrant // 2) % 2 == 1, -value, value)


def gelu(v):
    return 0.5 * v * (1.0 + jnp.tanh(math.sqrt(2.0 / math.pi) * (v + 0.044715 * (v * v * v))))


def forward_kernel(
    tok_ref, box_ref, rx_ref, ry_ref, mask_ref, cot_ref, freq_ref, lay_ref, vec_ref,
    cols_own, rows_own, qkv_own, wo_own, w1_own, w2_own,
    probs_out, qkvt_out, ctxt_out, low_out, feat_out, unit_out, inv_out, nlow_out, pre_out, hid_out,
    block_out, dres_out, sums_out, wqkv_out, wo_out, w1_out, w2_out,
    wqkv, wo, w1, w2, cols, rows, tabs, layer_in, qkvt, pbuf, ctxt, ctx, normed, pre, hid, acc,
    send, recv, here, out_sem, p_sem,
):
    t, d = lax.axis_index("tensor"), lax.axis_index("dp")
    mate, across = {"tensor": xor_index(t, 1)}, {"tensor": xor_index(t, 2)}
    beside = {"dp": xor_index(d, 1)}
    peers = (mate, across, beside, d % 2)
    win, model = tok_ref.shape
    heads = 4 * HEADS_T
    cols_t = HEADS_T * HD
    sems = (send, recv, here)
    f32, bf16 = jnp.float32, jnp.bfloat16

    def chunk(slot, own, place, count, split=True):
        return Gather(own, place, count, split, sems, slot, peers)

    g_cols = chunk(0, lambda s: cols_own.at[s], lambda r, s: cols.at[r, s], cols_t, False)
    g_rows = chunk(1, lambda s: rows_own.at[s], lambda r, s: rows.at[r, s], 8, False)

    def piece_rows(r, s, count):
        return pl.ds(pl.multiple_of(r * count + s.start, 16), s.size)

    g_qkv = [
        chunk(
            2 + n,
            lambda s, n=n: qkv_own.at[n, s],
            lambda r, s, n=n: wqkv.at[n, piece_rows(r, s, cols_t)],
            cols_t,
        )
        for n in range(3)
    ]
    g_wo = chunk(5, lambda s: wo_own.at[s], lambda r, s: wo.at[piece_rows(r, s, cols_t)], cols_t)

    def part(slot, own, whole, half):
        count = own.shape[0] // 2

        def moved(s):
            return pl.ds(pl.multiple_of(s.start + half * count, 16), s.size)

        return chunk(slot, lambda s: own.at[moved(s)], lambda r, s: whole.at[r, moved(s)], count)

    g_w1 = [part(6 + h, w1_own, w1, h) for h in range(2)]
    g_w2 = [part(8 + h, w2_own, w2, h) for h in range(2)]
    everything = [g_cols, g_rows] + g_qkv + [g_wo] + g_w1 + g_w2

    signal_peers((mate, across, beside))
    for g in [g_cols, g_rows] + g_qkv:
        g.start()

    lane = lax.broadcasted_iota(jnp.int32, (1, 128), 1)
    quarter = jnp.where(lane >= LFREQ, 1, 0)
    block = 128

    @pl.loop(0, win // block)
    def _(i):
        sl = pl.ds(pl.multiple_of(i * block, block), block)
        box = box_ref[sl, :].astype(f32)
        for m in range(4):
            feat_out[sl, 2 * LFREQ * m : 2 * LFREQ * (m + 1)] = waves(
                box[:, m : m + 1], freq_ref[0:1, :], quarter
            ).astype(bf16)
        value = tok_ref[sl, :].astype(f32) + nn(feat_out[sl, :], lay_ref[...])
        layer_in[sl, :] = value
        low_out[sl, :] = value.astype(bf16)

    for g in [g_cols, g_rows] + g_qkv:
        g.forward()
    g_wo.start()
    g_w1[0].start()
    for g in g_qkv:
        g.forward_two()
    g_cols.arrive()
    g_rows.arrive()
    for r in range(4):
        tabs[HEADS_T * r : HEADS_T * (r + 1), :] = rows[r, 1 : 1 + HEADS_T, 0:128]

    for n in range(3):
        g_qkv[n].arrive()

        @pl.loop(0, 4)
        def _(r, n=n):
            sl = pl.ds(pl.multiple_of(r * cols_t, 16), cols_t)
            value = nt(wqkv[n, sl, :], low_out[...])
            qkvt[n, sl, :] = (value + cols[r, :, n : n + 1]).astype(bf16)

    def table_row(h):
        return (tabs[pl.ds(h, 1), :] * 2048.0 + 32768.5).astype(jnp.int32) - 32768

    def p_copy(i, slot):
        return pltpu.make_async_copy(pbuf.at[slot], probs_out.at[pl.ds(2 * i, 2)], p_sem.at[slot])

    @pl.loop(0, heads // 2)
    def _(i):
        slot = i % 2
        sl = pl.ds(pl.multiple_of(i * 2 * HD, 2 * HD), 2 * HD)
        q = (qkvt[0, sl, :].astype(f32).T * HD ** (-0.5)).astype(bf16)
        tab = jnp.broadcast_to((table_row(2 * i) << 16) + table_row(2 * i + 1), (win, 128))
        bias = ([], [])
        for c in range(win // 128):
            at = slice(128 * c, 128 * c + 128)
            word = jnp.take_along_axis(tab, rx_ref[:, at], axis=1) + jnp.take_along_axis(
                tab, ry_ref[:, at] + BUCKETS, axis=1
            )
            second = word << 16
            bias[0].append((word - (second >> 16)).astype(f32) * 2.0**-27)
            bias[1].append(second.astype(f32) * 2.0**-27)

        @pl.when(i >= 2)
        def _():
            p_copy(i - 2, slot).wait()

        for u in range(2):
            rows_u = pl.ds(pl.multiple_of(i * 2 * HD + u * HD, HD), HD)
            s = nn(q[:, u * HD : (u + 1) * HD], qkvt[1, rows_u, :]) + jnp.concatenate(bias[u], axis=1)
            m = jnp.max(s, axis=1, keepdims=True)
            e = jnp.exp(s - m)
            p = e * (1.0 / jnp.sum(e, axis=1, keepdims=True))
            pbuf[slot, u] = p
            ctxt[rows_u, :] = nt(qkvt[2, rows_u, :], p.astype(bf16)).astype(bf16)
        p_copy(i, slot).start()

        @pl.when(i == 0)
        def _():
            g_wo.forward()
            g_w1[1].start()

        @pl.when(i == 1)
        def _():
            g_w1[0].forward()
            g_wo.forward_two()
            g_w2[0].start()

        @pl.when(i == 2)
        def _():
            g_w2[1].start()

        @pl.when(i == 3)
        def _():
            g_w1[1].forward()
            g_w1[0].forward_two()

        @pl.when(i == 5)
        def _():
            g_w2[0].forward()
            g_w1[1].forward_two()

    last = heads // 2
    outs = [
        (qkvt, qkvt_out), (ctxt, ctxt_out), (wqkv, wqkv_out),
    ]
    done = []

    def leave(src, dst):
        c = pltpu.make_async_copy(src, dst, out_sem.at[len(done)])
        c.start()
        done.append(c)

    for src, dst in outs:
        leave(src, dst)
    g_wo.arrive()
    leave(wo, wo_out)

    ctx[...] = ctxt[...].astype(f32).T.astype(bf16)

    @pl.loop(0, win // block)
    def _(i):
        sl = pl.ds(pl.multiple_of(i * block, block), block)
        value = layer_in[sl, :] + nn(ctx[sl, :], wo[...]) + vec_ref[0:1, :]
        mean = jnp.mean(value, axis=1, keepdims=True)
        centered = value - mean
        inverse = lax.rsqrt(jnp.mean(centered * centered, axis=1, keepdims=True) + EPSILON)
        unit = centered * inverse
        unit_out[sl, :] = unit
        inv_out[sl, :] = inverse
        value = unit * vec_ref[1:2, :] + vec_ref[2:3, :]
        normed[sl, :] = value
        nlow_out[sl, :] = value.astype(bf16)

    g_w2[0].forward_two()
    g_w2[1].forward()
    for r in range(4):
        if r == 0:
            for g in g_w1 + g_w2:
                g.arrive_near()
        if r == 2:
            g_w2[1].forward_two()
            for g in g_w1 + g_w2:
                g.arrive_far()
            leave(w1, w1_out)
            leave(w2, w2_out)

        @pl.loop(0, win // 256)
        def _(i, r=r):
            sl = pl.ds(pl.multiple_of(i * 256, 256), 256)
            value = nn(nlow_out[sl, :], w1[r]) + rows[r, 0:1, :]
            pre[r, sl, :] = value
            low_hid = gelu(value).astype(bf16)
            hid[r, sl, :] = low_hid
            more = nn(low_hid, w2[r])
            acc[sl, :] = more if r == 0 else acc[sl, :] + more

        leave(pre.at[r], pre_out.at[r])
        leave(hid.at[r], hid_out.at[r])

    sums_out[...] = jnp.zeros_like(sums_out)

    @pl.loop(0, win // block)
    def _(i):
        sl = pl.ds(pl.multiple_of(i * block, block), block)
        value = normed[sl, :] + acc[sl, :] + vec_ref[3:4, :]
        mean = jnp.mean(value, axis=1, keepdims=True)
        centered = value - mean
        inverse = lax.rsqrt(jnp.mean(centered * centered, axis=1, keepdims=True) + EPSILON)
        unit = centered * inverse
        block_out[sl, :] = (unit * vec_ref[4:5, :] + vec_ref[5:6, :]).astype(bf16)
        selected = mask_ref[sl, :].astype(f32) * cot_ref[sl, :].astype(f32)
        scaled = selected * vec_ref[4:5, :]
        mean_one = jnp.mean(scaled, axis=1, keepdims=True)
        mean_two = jnp.mean(scaled * unit, axis=1, keepdims=True)
        dres = (scaled - mean_one - unit * mean_two) * inverse
        dres_out[sl, :] = dres
        sums_out[0:1, :] += jnp.sum(selected * unit, axis=0, keepdims=True)
        sums_out[1:2, :] += jnp.sum(selected, axis=0, keepdims=True)
        sums_out[2:3, :] += jnp.sum(dres, axis=0, keepdims=True)

    for i in (last - 2, last - 1):
        p_copy(i, i % 2).wait()
    for c in done:
        c.wait()
    for g in everything:
        g.finish()


def forward_window(n_dp, tok, box, rx, ry, mask, cot, freq, lay, vec, cols_own, rows_own, qkv_own, wo_own, w1_own, w2_own):
    win, model = tok.shape
    cols_t, hid_t = wo_own.shape[0], w1_own.shape[1]
    heads = 4 * HEADS_T
    f32, bf16 = jnp.float32, jnp.bfloat16
    shape = jax.ShapeDtypeStruct
    here = pl.BlockSpec(memory_space=pltpu.VMEM)
    away = pl.BlockSpec(memory_space=pl.ANY)
    outs = [
        (shape((heads, win, win), f32), away),
        (shape((3, model, win), bf16), away),
        (shape((model, win), bf16), away),
        (shape((win, model), bf16), here),
        (shape((win, 8 * LFREQ), bf16), here),
        (shape((win, model), f32), here),
        (shape((win, 1), f32), here),
        (shape((win, model), bf16), here),
        (shape((4, win, hid_t), f32), away),
        (shape((4, win, hid_t), bf16), away),
        (shape((win, model), bf16), here),
        (shape((win, model), f32), here),
        (shape((8, model), f32), here),
        (shape((3, model, model), bf16), away),
        (shape((model, model), bf16), away),
        (shape((4, model, hid_t), bf16), away),
        (shape((4, hid_t, model), bf16), away),
    ]
    return pl.pallas_call(
        forward_kernel,
        in_specs=[here] * 9 + [away] * 6,
        out_specs=[spec for _, spec in outs],
        out_shape=[s for s, _ in outs],
        scratch_shapes=[
            pltpu.VMEM((3, model, model), bf16),
            pltpu.VMEM((model, model), bf16),
            pltpu.VMEM((4, model, hid_t), bf16),
            pltpu.VMEM((4, hid_t, model), bf16),
            pltpu.VMEM((4, cols_t, 128), f32),
            pltpu.VMEM((4, 8, model), f32),
            pltpu.VMEM((heads, 128), f32),
            pltpu.VMEM((win, model), f32),
            pltpu.VMEM((3, model, win), bf16),
            pltpu.VMEM((2, 2, win, win), f32),
            pltpu.VMEM((model, win), bf16),
            pltpu.VMEM((win, model), bf16),
            pltpu.VMEM((win, model), f32),
            pltpu.VMEM((4, win, hid_t), f32),
            pltpu.VMEM((4, win, hid_t), bf16),
            pltpu.VMEM((win, model), f32),
            pltpu.SemaphoreType.DMA((10, 5)),
            pltpu.SemaphoreType.DMA((10, 5)),
            pltpu.SemaphoreType.DMA((10,)),
            pltpu.SemaphoreType.DMA((16,)),
            pltpu.SemaphoreType.DMA((2,)),
        ],
        compiler_params=pltpu.CompilerParams(
            vmem_limit_bytes=60 * 2**20, collective_id=0, has_side_effects=True
        ),
        name="forward_window",
    )(tok, box, rx, ry, mask, cot, freq, lay, vec, cols_own, rows_own, qkv_own, wo_own, w1_own, w2_own)


def attend_back_kernel(
    q_ref, k_ref, v_ref, p_ref, dc_ref, rx_ref, ry_ref,
    dq_ref, dk_ref, dv_ref, g_ref, ds_scr, hot_scr, acc,
):
    head = pl.program_id(0)
    heads = pl.num_programs(0)
    win = rx_ref.shape[0]
    dc_t = dc_ref[...]
    dc = dc_t.astype(jnp.float32).T.astype(jnp.bfloat16)
    p = p_ref[0]
    dp = nn(dc, v_ref[...])
    row_dot = jnp.sum(p * dp, axis=1, keepdims=True)
    ds = (p * (dp - row_dot)).astype(jnp.bfloat16)
    dv_ref[...] = nn(dc_t, p.astype(jnp.bfloat16)).astype(jnp.bfloat16)
    dq_ref[...] = (nt(k_ref[...], ds) * HD ** (-0.5)).astype(jnp.bfloat16)
    dk_ref[...] = (nn(q_ref[...], ds) * HD ** (-0.5)).astype(jnp.bfloat16)
    ds_scr[head] = ds

    @pl.when(head == heads - 1)
    def _():
        acc[...] = jnp.zeros_like(acc)
        one, zero = jnp.bfloat16(1), jnp.bfloat16(0)
        half = BUCKETS * ROWS

        def step(g, carry):
            rows = pl.ds(pl.multiple_of(g * ROWS, ROWS), ROWS)
            x = rx_ref[rows, :].astype(jnp.float32).astype(jnp.bfloat16)
            y = ry_ref[rows, :].astype(jnp.float32).astype(jnp.bfloat16)
            for b in range(BUCKETS):
                hot_scr[b * ROWS : (b + 1) * ROWS, :] = jnp.where(x == jnp.bfloat16(b), one, zero)
                hot_scr[half + b * ROWS : half + (b + 1) * ROWS, :] = jnp.where(
                    y == jnp.bfloat16(b), one, zero
                )
            left = ds_scr[:, rows, :].reshape(ds_scr.shape[0] * ROWS, win)
            acc[...] += nt(left, hot_scr[...])
            return carry

        lax.fori_loop(0, win // ROWS, step, 0)
        row = lax.broadcasted_iota(jnp.int32, (ROWS, 2 * half), 0)
        col = lax.broadcasted_iota(jnp.int32, (ROWS, 2 * half), 1) % ROWS
        for h in range(ds_scr.shape[0]):
            part = jnp.where(row == col, acc[h * ROWS : (h + 1) * ROWS, :], 0.0)
            g_ref[h : h + 1, :] = jnp.sum(part, axis=0, keepdims=True)


def attend_back(q, k, v, p, dc, rel_x, rel_y):
    heads, win = p.shape[0], rel_x.shape[0]
    hots = 2 * BUCKETS * ROWS
    blk = pl.BlockSpec((HD, win), lambda h: (h, 0))
    full = pl.BlockSpec((win, win), lambda h: (0, 0))
    dq, dk, dv, g = pl.pallas_call(
        attend_back_kernel,
        grid=(heads,),
        in_specs=[blk, blk, blk, pl.BlockSpec((1, win, win), lambda h: (h, 0, 0)), blk, full, full],
        out_specs=[blk, blk, blk, pl.BlockSpec((heads, hots), lambda h: (0, 0))],
        out_shape=[jax.ShapeDtypeStruct((heads * HD, win), jnp.bfloat16)] * 3
        + [jax.ShapeDtypeStruct((heads, hots), jnp.float32)],
        scratch_shapes=[
            pltpu.VMEM((heads, win, win), jnp.bfloat16),
            pltpu.VMEM((hots, win), jnp.bfloat16),
            pltpu.VMEM((heads * ROWS, hots), jnp.float32),
        ],
        compiler_params=pltpu.CompilerParams(vmem_limit_bytes=56 * 2**20),
        cost_estimate=pl.CostEstimate(
            flops=20 * 10**9, bytes_accessed=20 * 10**6, transcendentals=0
        ),
        name="attend_back",
    )(q, k, v, p, dc, rel_x, rel_y)
    return dq, dk, dv, jnp.sum(g.reshape(heads, 2 * BUCKETS, ROWS), axis=2).T


def bits_of(size):
    return [1 << b for b in range(size.bit_length() - 1)]


def swap(value, axis, size, bit):
    return lax.ppermute(value, axis, [(i, i ^ bit) for i in range(size)])


def gather_pieces(own, axis, size):
    pieces = {0: own}
    for bit in reversed(bits_of(size)):
        for r in list(pieces):
            pieces[r | bit] = swap(pieces[r], axis, size, bit)
    return [pieces[r] for r in range(size)]


def scatter_pieces(pieces, axis, size):
    pieces = dict(enumerate(pieces))
    for bit in bits_of(size):
        for r in [r for r in pieces if r & bit]:
            got = swap(pieces.pop(r).astype(jnp.bfloat16), axis, size, bit)
            pieces[r ^ bit] = pieces[r ^ bit].astype(jnp.float32) + got.astype(jnp.float32)
    return pieces[0]


def reduce_rows(total, axis, size):
    me = lax.axis_index(axis)
    held = total
    for bit in bits_of(size):
        half = held.shape[0] // 2
        side = (me // bit) % 2
        mine = lax.dynamic_slice_in_dim(held, side * half, half)
        other = lax.dynamic_slice_in_dim(held, (1 - side) * half, half)
        got = swap(other.astype(jnp.bfloat16), axis, size, bit)
        held = mine.astype(jnp.float32) + got.astype(jnp.float32)
    held = held.astype(jnp.bfloat16)
    for bit in reversed(bits_of(size)):
        got = swap(held, axis, size, bit)
        side = (me // bit) % 2
        held = jnp.where(
            side == 0, jnp.concatenate([held, got]), jnp.concatenate([got, held])
        )
    return held


def sum_small(value, axis, size):
    for bit in bits_of(size):
        value = value + swap(value, axis, size, bit)
    return value


def place_pieces(pieces, me):
    size, rows = len(pieces), pieces[0].shape[0]
    whole = jnp.zeros((size * rows,) + pieces[0].shape[1:], pieces[0].dtype)
    for r, piece in enumerate(pieces):
        whole = lax.dynamic_update_slice_in_dim(whole, piece, (me ^ r) * rows, 0)
    return whole


def local(
    n_dp, n_t,
    tokens_in, box_coords, rel_x, rel_y, mask_tokens, cotangent, layout_weight, qkv_weight, qv_bias,
    bias_table, out_weight, out_bias, ln1_gain, ln1_bias, ffn_in_weight, ffn_in_bias, ffn_out_weight,
    ffn_out_bias, ln2_gain, ln2_bias, group_rates,
):
    me = lax.axis_index("tensor")
    win = rel_x.shape[1]
    model = tokens_in.shape[1]
    heads_t = bias_table.shape[1]
    cols_t = heads_t * HD
    hid_t = ffn_in_weight.shape[1]
    tok_rows = tokens_in.shape[0] // n_t

    def mine(whole):
        return lax.dynamic_slice_in_dim(whole, me * (whole.shape[0] // n_t), whole.shape[0] // n_t)

    zeros = jnp.zeros((cols_t,), jnp.float32)
    cols_own = jnp.pad(jnp.stack([qv_bias[0], zeros, qv_bias[1]], axis=1), ((0, 0), (0, 125)))
    rows_own = jnp.concatenate(
        [
            ffn_in_bias[None, :],
            jnp.pad(bias_table.T.astype(jnp.float32), ((0, 0), (0, hid_t - 2 * BUCKETS))),
            jnp.zeros((8 - 1 - heads_t, hid_t), jnp.float32),
        ],
        axis=0,
    )
    freq_index = jnp.arange(LFREQ).astype(jnp.float32)
    freq = jnp.exp(freq_index * (-math.log(1000.0) / LFREQ))
    freq = jnp.broadcast_to(jnp.concatenate([freq, freq])[None, :], (8, 2 * LFREQ))
    zero = jnp.zeros_like(out_bias)
    vec = jnp.stack([out_bias, ln1_gain, ln1_bias, ffn_out_bias, ln2_gain, ln2_bias, zero, zero])
    relx, rely = mine(rel_x)[0], mine(rel_y)[0]
    count = sum_small(jnp.sum(mask_tokens.astype(jnp.float32)).reshape(1), "dp", n_dp)[0]

    (
        probs, qkvt, context_t, layer_low, features, unit_one, inverse_one, normed_low, pre_all, hid_all,
        block_own, dresid_two, sums, wqkv, wo, w1, w2,
    ) = forward_window(
        n_dp, mine(tokens_in), mine(box_coords), relx, rely, mine(mask_tokens)[:, None], mine(cotangent), freq,
        layout_weight, vec, cols_own, rows_own, jnp.transpose(qkv_weight, (0, 2, 1)), out_weight, ffn_in_weight, ffn_out_weight,
    )
    queries, key_rows, values = qkvt[0], qkvt[1], qkvt[2]
    block_out = lax.all_gather(block_own, "tensor", axis=0, tiled=True)
    grad_g2, grad_b2, grad_c2 = sums[0], sums[1], sums[2]
    dffn_low = dresid_two.astype(jnp.bfloat16)
    grad_w2, grad_w1, grad_c1, dnormed = [], [], [], dresid_two
    for r in range(n_t):
        grad_w2.append(nn(hid_all[r].T, dffn_low))
        gelu_back = jax.vjp(jax.nn.gelu, pre_all[r])[1]
        dpre = gelu_back(nt(dffn_low, w2[r]))[0].astype(jnp.bfloat16)
        grad_c1.append(jnp.sum(dpre, axis=0, dtype=jnp.float32))
        grad_w1.append(nn(normed_low.T, dpre))
        dnormed = dnormed + nt(dpre, w1[r])
    grad_w2 = jnp.concatenate(grad_w2, axis=0)
    grad_w1 = jnp.concatenate(grad_w1, axis=0)
    grad_c1 = jnp.concatenate(grad_c1)
    dresidual, grad_g1, grad_b1 = normalize_back(dnormed, unit_one, inverse_one, ln1_gain)

    def reduced(parts):
        pieces = [
            jnp.concatenate([part[r * rows : (r + 1) * rows] for part, rows in parts], axis=0)
            for r in range(n_t)
        ]
        return reduce_rows(scatter_pieces(pieces, "tensor", n_t), "dp", n_dp)

    w2_sum = reduced([(grad_w2, hid_t)])
    w1_sum = reduced([(grad_w1, hid_t)])

    grad_ob = jnp.sum(dresidual, axis=0)
    dattn_low = dresidual.astype(jnp.bfloat16)
    grad_ow = nn(context_t, dattn_low)
    dcontext = nt(wo, dattn_low).astype(jnp.bfloat16)
    dq, dk, dv, grad_table = attend_back(
        queries, key_rows, values, probs, dcontext, relx, rely
    )
    grad_qkv = [nn(d, layer_low) for d in (dq, dk, dv)]
    grad_bq = jnp.sum(dq, axis=1, dtype=jnp.float32)
    grad_bv = jnp.sum(dv, axis=1, dtype=jnp.float32)
    dlayer = dresidual + sum(nn(d.T, w) for d, w in zip((dq, dk, dv), wqkv))
    grad_lay = nn(features.T, dlayer.astype(jnp.bfloat16))
    lay_rows = grad_lay.shape[0] // n_t
    lay_pieces = [
        lax.dynamic_slice_in_dim(grad_lay, (me ^ r) * lay_rows, lay_rows) for r in range(n_t)
    ]
    rest_sum = reduced(
        [(g, cols_t) for g in grad_qkv]
        + [(grad_ow, cols_t), (jnp.concatenate(lay_pieces, axis=0), lay_rows)]
    )
    din = (dlayer / count).astype(jnp.bfloat16)
    input_grad = place_pieces(gather_pieces(din, "tensor", n_t), me).astype(jnp.float32)
    lay_sum = place_pieces(gather_pieces(rest_sum[4 * cols_t :], "tensor", n_t), me)

    def pieces_of(vec, size):
        return vec.reshape(n_t, size)

    split = jnp.concatenate(
        [
            pieces_of(grad_bq, cols_t),
            pieces_of(grad_bv, cols_t),
            pieces_of(grad_c1, hid_t),
            pieces_of(grad_table.T, heads_t * 2 * BUCKETS),
        ],
        axis=1,
    )
    common = jnp.concatenate([grad_ob, grad_g1, grad_b1, grad_c2, grad_g2, grad_b2])
    whole = jnp.zeros_like(split)
    for r in range(n_t):
        whole = lax.dynamic_update_slice_in_dim(whole, split[r : r + 1], me ^ r, 0)
    flat = jnp.concatenate([whole.reshape(-1), common])
    flat = sum_small(sum_small(flat, "tensor", n_t), "dp", n_dp)
    width = split.shape[1]
    own = lax.dynamic_slice_in_dim(flat, me * width, width)
    common = flat[n_t * width :].reshape(6, model)

    factor = group_rates / count
    f32 = jnp.float32
    qkv_sum = rest_sum[: 3 * cols_t].reshape(3, cols_t, model)
    return (
        block_out,
        input_grad,
        lay_sum.astype(f32) * factor[6],
        jnp.transpose(qkv_sum, (0, 2, 1)).astype(f32) * factor[0],
        own[: 2 * cols_t].reshape(2, cols_t) * factor[0],
        own[2 * cols_t + hid_t :].reshape(heads_t, 2 * BUCKETS).T * factor[7],
        rest_sum[3 * cols_t : 4 * cols_t].astype(f32) * factor[1],
        common[0] * factor[1],
        common[1] * factor[2],
        common[2] * factor[2],
        w1_sum.astype(f32) * factor[3],
        own[2 * cols_t : 2 * cols_t + hid_t] * factor[3],
        w2_sum.astype(f32) * factor[4],
        common[3] * factor[4],
        common[4] * factor[5],
        common[5] * factor[5],
    )


def solution(mesh):
    placed = (
        P("dp", None), P("dp", None), P("dp", None, None), P("dp", None, None), P("dp"), P("dp", None),
        P(), P(None, None, "tensor"), P(None, "tensor"), P(None, "tensor"), P("tensor", None),
        P(), P(), P(), P(None, "tensor"), P("tensor"), P("tensor", None), P(), P(), P(), P(),
    )
    return jax.shard_map(
        functools.partial(local, mesh.shape["dp"], mesh.shape["tensor"]),
        mesh=mesh,
        in_specs=placed,
        out_specs=(
            P("dp", None), P("dp", None), P(), P(None, None, "tensor"), P(None, "tensor"),
            P(None, "tensor"), P("tensor", None), P(), P(), P(), P(None, "tensor"), P("tensor"),
            P("tensor", None), P(), P(), P(),
        ),
        check_vma=False,
    )
```

```python
import functools
import math

import jax
import jax.numpy as jnp
from jax import lax
from jax.experimental import pallas as pl
from jax.experimental.pallas import tpu as pltpu
from jax.sharding import PartitionSpec as P

HD = 64
LFREQ = 64
BUCKETS = 32
EPSILON = 1e-05
ROWS = 16
HEADS_T = 3
MESH = pl.DeviceIdType.MESH


def nt(a, b):
    return lax.dot_general(a, b, (((1,), (1,)), ((), ())), preferred_element_type=jnp.float32)


def nn(a, b):
    return jnp.dot(a, b, preferred_element_type=jnp.float32)


def xor_index(index, bit):
    return index + bit - 2 * bit * ((index // bit) % 2)


def signal_peers(peers):
    barrier = pltpu.get_barrier_semaphore()
    for peer in peers:
        pl.semaphore_signal(barrier, inc=1, device_id=peer, device_id_type=MESH)
    pl.semaphore_wait(barrier, len(peers))


def remote(src, dst, send, recv, peer):
    return pltpu.make_async_remote_copy(
        src_ref=src, dst_ref=dst, send_sem=send, recv_sem=recv, device_id=peer, device_id_type=MESH
    )


class Gather:
    def __init__(self, own, place, rows, split, sems, slot, peers):
        self.own, self.place, self.rows, self.split = own, place, rows, split
        self.send, self.recv, self.here = sems
        self.slot = slot
        self.mate, self.across, self.beside, self.side = peers

    def copy(self, name):
        s = self.slot
        half = self.rows // 2 if self.split else self.rows
        mine = pl.ds(pl.multiple_of(self.side * half, half), half) if self.split else pl.ds(0, half)
        yours = pl.ds(pl.multiple_of((1 - self.side) * half, half), half)
        whole = pl.ds(0, self.rows)
        if name == "here":
            return pltpu.make_async_copy(self.own(whole), self.place(0, whole), self.here.at[s])
        src, dst, peer, k = {
            "mate": lambda: (self.own(whole), self.place(1, whole), self.mate, 0),
            "across": lambda: (self.own(mine), self.place(2, mine), self.across, 1),
            "pass": lambda: (self.place(2, mine), self.place(3, mine), self.mate, 2),
            "beside": lambda: (self.place(2, mine), self.place(2, mine), self.beside, 3),
            "pass_two": lambda: (self.place(2, yours), self.place(3, yours), self.mate, 4),
        }[name]()
        return remote(src, dst, self.send.at[s, k], self.recv.at[s, k], peer)

    def start(self):
        self.copy("across").start()
        self.copy("mate").start()
        self.copy("here").start()

    def forward(self):
        self.copy("across").wait_recv()
        if self.split:
            self.copy("beside").start()
        self.copy("pass").start()

    def forward_two(self):
        if self.split:
            self.copy("beside").wait_recv()
            self.copy("pass_two").start()

    def arrive_near(self):
        self.copy("here").wait()
        self.copy("mate").wait_recv()

    def arrive_far(self):
        self.copy("pass").wait_recv()
        if self.split:
            self.copy("pass_two").wait_recv()

    def arrive(self):
        self.arrive_near()
        self.arrive_far()

    def finish(self):
        for name in ("mate", "across", "pass") + (("beside", "pass_two") if self.split else ()):
            self.copy(name).wait_send()


def waves(column, frequency, quarter):
    angle = column * frequency
    turns = jnp.floor(angle * (2.0 / math.pi) + 0.5)
    rest = ((angle - turns * 1.5703125) - turns * 4.837512969970703125e-4) - turns * 7.549789948768648e-8
    quadrant = turns.astype(jnp.int32) + quarter
    z = rest * rest
    sine = ((-1.9515295891e-4 * z + 8.3321608736e-3) * z - 1.6666654611e-1) * z * rest + rest
    cosine = ((2.443315711809948e-5 * z - 1.388731625493765e-3) * z + 4.166664568298827e-2) * z * z - 0.5 * z + 1.0
    value = jnp.where(quadrant % 2 == 1, cosine, sine)
    return jnp.where((quadrant // 2) % 2 == 1, -value, value)


def gelu(v):
    return 0.5 * v * (1.0 + jnp.tanh(math.sqrt(2.0 / math.pi) * (v + 0.044715 * (v * v * v))))


def forward_kernel(
    tok_ref, box_ref, rx_ref, ry_ref, mask_ref, cot_ref, freq_ref, lay_ref, vec_ref,
    cols_own, rows_own, qkv_own, wo_own, w1_own, w2_own,
    probs_out, qkvt_out, ctxt_out, low_out, feat_out, unit_out, inv_out, nlow_out, pre_out, hid_out,
    block_out, dres_out, sums_out, wqkv_out, wo_out, w1_out, w2_out,
    wqkv, wo, w1, w2, cols, rows, tabs, layer_in, qkvt, pbuf, ctxt, ctx, normed, pre, hid, acc,
    send, recv, here, out_sem, p_sem,
):
    t, d = lax.axis_index("tensor"), lax.axis_index("dp")
    mate, across = {"tensor": xor_index(t, 1)}, {"tensor": xor_index(t, 2)}
    beside = {"dp": xor_index(d, 1)}
    peers = (mate, across, beside, d % 2)
    win, model = tok_ref.shape
    heads = 4 * HEADS_T
    cols_t = HEADS_T * HD
    sems = (send, recv, here)
    f32, bf16 = jnp.float32, jnp.bfloat16

    def chunk(slot, own, place, count, split=True):
        return Gather(own, place, count, split, sems, slot, peers)

    g_cols = chunk(0, lambda s: cols_own.at[s], lambda r, s: cols.at[r, s], cols_t, False)
    g_rows = chunk(1, lambda s: rows_own.at[s], lambda r, s: rows.at[r, s], 8, False)

    def piece_rows(r, s, count):
        return pl.ds(pl.multiple_of(r * count + s.start, 16), s.size)

    g_qkv = [
        chunk(
            2 + n,
            lambda s, n=n: qkv_own.at[n, s],
            lambda r, s, n=n: wqkv.at[n, piece_rows(r, s, cols_t)],
            cols_t,
        )
        for n in range(3)
    ]
    g_wo = chunk(5, lambda s: wo_own.at[s], lambda r, s: wo.at[piece_rows(r, s, cols_t)], cols_t)

    def part(slot, own, whole, half):
        count = own.shape[0] // 2

        def moved(s):
            return pl.ds(pl.multiple_of(s.start + half * count, 16), s.size)

        return chunk(slot, lambda s: own.at[moved(s)], lambda r, s: whole.at[r, moved(s)], count)

    g_w1 = [part(6 + h, w1_own, w1, h) for h in range(2)]
    g_w2 = [part(8 + h, w2_own, w2, h) for h in range(2)]
    everything = [g_cols, g_rows] + g_qkv + [g_wo] + g_w1 + g_w2

    signal_peers((mate, across, beside))
    for g in [g_cols, g_rows] + g_qkv:
        g.start()

    lane = lax.broadcasted_iota(jnp.int32, (1, 128), 1)
    quarter = jnp.where(lane >= LFREQ, 1, 0)
    block = 128

    @pl.loop(0, win // block)
    def _(i):
        sl = pl.ds(pl.multiple_of(i * block, block), block)
        box = box_ref[sl, :].astype(f32)
        for m in range(4):
            feat_out[sl, 2 * LFREQ * m : 2 * LFREQ * (m + 1)] = waves(
                box[:, m : m + 1], freq_ref[0:1, :], quarter
            ).astype(bf16)
        value = tok_ref[sl, :].astype(f32) + nn(feat_out[sl, :], lay_ref[...])
        layer_in[sl, :] = value
        low_out[sl, :] = value.astype(bf16)

    for g in [g_cols, g_rows] + g_qkv:
        g.forward()
    g_wo.start()
    g_w1[0].start()
    for g in g_qkv:
        g.forward_two()
    g_cols.arrive()
    g_rows.arrive()
    for r in range(4):
        tabs[HEADS_T * r : HEADS_T * (r + 1), :] = rows[r, 1 : 1 + HEADS_T, 0:128]

    for n in range(3):
        g_qkv[n].arrive()

        @pl.loop(0, 4)
        def _(r, n=n):
            sl = pl.ds(pl.multiple_of(r * cols_t, 16), cols_t)
            value = nt(wqkv[n, sl, :], low_out[...])
            qkvt[n, sl, :] = (value + cols[r, :, n : n + 1]).astype(bf16)

    def table_row(h):
        return (tabs[pl.ds(h, 1), :] * 2048.0 + 32768.5).astype(jnp.int32) - 32768

    def p_copy(i, slot):
        return pltpu.make_async_copy(pbuf.at[slot], probs_out.at[pl.ds(2 * i, 2)], p_sem.at[slot])

    @pl.loop(0, heads // 2)
    def _(i):
        slot = i % 2
        sl = pl.ds(pl.multiple_of(i * 2 * HD, 2 * HD), 2 * HD)
        q = (qkvt[0, sl, :].astype(f32).T * HD ** (-0.5)).astype(bf16)
        tab = jnp.broadcast_to((table_row(2 * i) << 16) + table_row(2 * i + 1), (win, 128))
        bias = ([], [])
        for c in range(win // 128):
            at = slice(128 * c, 128 * c + 128)
            word = jnp.take_along_axis(tab, rx_ref[:, at], axis=1) + jnp.take_along_axis(
                tab, ry_ref[:, at] + BUCKETS, axis=1
            )
            second = word << 16
            bias[0].append((word - (second >> 16)).astype(f32) * 2.0**-27)
            bias[1].append(second.astype(f32) * 2.0**-27)

        @pl.when(i >= 2)
        def _():
            p_copy(i - 2, slot).wait()

        for u in range(2):
            rows_u = pl.ds(pl.multiple_of(i * 2 * HD + u * HD, HD), HD)
            s = nn(q[:, u * HD : (u + 1) * HD], qkvt[1, rows_u, :]) + jnp.concatenate(bias[u], axis=1)
            m = jnp.max(s, axis=1, keepdims=True)
            e = jnp.exp(s - m)
            p = e * (1.0 / jnp.sum(e, axis=1, keepdims=True))
            pbuf[slot, u] = p
            ctxt[rows_u, :] = nt(qkvt[2, rows_u, :], p.astype(bf16)).astype(bf16)
        p_copy(i, slot).start()

        @pl.when(i == 0)
        def _():
            g_wo.forward()
            g_w1[1].start()

        @pl.when(i == 1)
        def _():
            g_w1[0].forward()
            g_wo.forward_two()
            g_w2[0].start()

        @pl.when(i == 2)
        def _():
            g_w2[1].start()

        @pl.when(i == 3)
        def _():
            g_w1[1].forward()
            g_w1[0].forward_two()

        @pl.when(i == 5)
        def _():
            g_w2[0].forward()
            g_w1[1].forward_two()

    last = heads // 2
    outs = [
        (qkvt, qkvt_out), (ctxt, ctxt_out), (wqkv, wqkv_out),
    ]
    done = []

    def leave(src, dst):
        c = pltpu.make_async_copy(src, dst, out_sem.at[len(done)])
        c.start()
        done.append(c)

    for src, dst in outs:
        leave(src, dst)
    g_wo.arrive()
    leave(wo, wo_out)

    ctx[...] = ctxt[...].astype(f32).T.astype(bf16)

    @pl.loop(0, win // block)
    def _(i):
        sl = pl.ds(pl.multiple_of(i * block, block), block)
        value = layer_in[sl, :] + nn(ctx[sl, :], wo[...]) + vec_ref[0:1, :]
        mean = jnp.mean(value, axis=1, keepdims=True)
        centered = value - mean
        inverse = lax.rsqrt(jnp.mean(centered * centered, axis=1, keepdims=True) + EPSILON)
        unit = centered * inverse
        unit_out[sl, :] = unit
        inv_out[sl, :] = inverse
        value = unit * vec_ref[1:2, :] + vec_ref[2:3, :]
        normed[sl, :] = value
        nlow_out[sl, :] = value.astype(bf16)

    g_w2[0].forward_two()
    g_w2[1].forward()
    for r in range(4):
        if r == 0:
            for g in g_w1 + g_w2:
                g.arrive_near()
        if r == 2:
            g_w2[1].forward_two()
            for g in g_w1 + g_w2:
                g.arrive_far()
            leave(w1, w1_out)
            leave(w2, w2_out)

        @pl.loop(0, win // 256)
        def _(i, r=r):
            sl = pl.ds(pl.multiple_of(i * 256, 256), 256)
            value = nn(nlow_out[sl, :], w1[r]) + rows[r, 0:1, :]
            pre[r, sl, :] = value
            low_hid = gelu(value).astype(bf16)
            hid[r, sl, :] = low_hid
            more = nn(low_hid, w2[r])
            acc[sl, :] = more if r == 0 else acc[sl, :] + more

        leave(pre.at[r], pre_out.at[r])
        leave(hid.at[r], hid_out.at[r])

    sums_out[...] = jnp.zeros_like(sums_out)

    @pl.loop(0, win // block)
    def _(i):
        sl = pl.ds(pl.multiple_of(i * block, block), block)
        value = normed[sl, :] + acc[sl, :] + vec_ref[3:4, :]
        mean = jnp.mean(value, axis=1, keepdims=True)
        centered = value - mean
        inverse = lax.rsqrt(jnp.mean(centered * centered, axis=1, keepdims=True) + EPSILON)
        unit = centered * inverse
        block_out[sl, :] = (unit * vec_ref[4:5, :] + vec_ref[5:6, :]).astype(bf16)
        selected = mask_ref[sl, :].astype(f32) * cot_ref[sl, :].astype(f32)
        scaled = selected * vec_ref[4:5, :]
        mean_one = jnp.mean(scaled, axis=1, keepdims=True)
        mean_two = jnp.mean(scaled * unit, axis=1, keepdims=True)
        dres = (scaled - mean_one - unit * mean_two) * inverse
        dres_out[sl, :] = dres
        sums_out[0:1, :] += jnp.sum(selected * unit, axis=0, keepdims=True)
        sums_out[1:2, :] += jnp.sum(selected, axis=0, keepdims=True)
        sums_out[2:3, :] += jnp.sum(dres, axis=0, keepdims=True)
        sums_out[3:4, :] += jnp.sum(mask_ref[sl, :].astype(f32), axis=0, keepdims=True)

    for i in (last - 2, last - 1):
        p_copy(i, i % 2).wait()
    for c in done:
        c.wait()
    for g in everything:
        g.finish()


def forward_window(n_dp, tok, box, rx, ry, mask, cot, freq, lay, vec, cols_own, rows_own, qkv_own, wo_own, w1_own, w2_own):
    win, model = tok.shape
    cols_t, hid_t = wo_own.shape[0], w1_own.shape[1]
    heads = 4 * HEADS_T
    f32, bf16 = jnp.float32, jnp.bfloat16
    shape = jax.ShapeDtypeStruct
    here = pl.BlockSpec(memory_space=pltpu.VMEM)
    away = pl.BlockSpec(memory_space=pl.ANY)
    outs = [
        (shape((heads, win, win), f32), away),
        (shape((3, model, win), bf16), away),
        (shape((model, win), bf16), away),
        (shape((win, model), bf16), here),
        (shape((win, 8 * LFREQ), bf16), here),
        (shape((win, model), f32), here),
        (shape((win, 1), f32), here),
        (shape((win, model), bf16), here),
        (shape((4, win, hid_t), f32), away),
        (shape((4, win, hid_t), bf16), away),
        (shape((win, model), bf16), here),
        (shape((win, model), f32), here),
        (shape((8, model), f32), here),
        (shape((3, model, model), bf16), away),
        (shape((model, model), bf16), away),
        (shape((4, model, hid_t), bf16), away),
        (shape((4, hid_t, model), bf16), away),
    ]
    return pl.pallas_call(
        forward_kernel,
        in_specs=[here] * 9 + [away] * 6,
        out_specs=[spec for _, spec in outs],
        out_shape=[s for s, _ in outs],
        scratch_shapes=[
            pltpu.VMEM((3, model, model), bf16),
            pltpu.VMEM((model, model), bf16),
            pltpu.VMEM((4, model, hid_t), bf16),
            pltpu.VMEM((4, hid_t, model), bf16),
            pltpu.VMEM((4, cols_t, 128), f32),
            pltpu.VMEM((4, 8, model), f32),
            pltpu.VMEM((heads, 128), f32),
            pltpu.VMEM((win, model), f32),
            pltpu.VMEM((3, model, win), bf16),
            pltpu.VMEM((2, 2, win, win), f32),
            pltpu.VMEM((model, win), bf16),
            pltpu.VMEM((win, model), bf16),
            pltpu.VMEM((win, model), f32),
            pltpu.VMEM((4, win, hid_t), f32),
            pltpu.VMEM((4, win, hid_t), bf16),
            pltpu.VMEM((win, model), f32),
            pltpu.SemaphoreType.DMA((10, 5)),
            pltpu.SemaphoreType.DMA((10, 5)),
            pltpu.SemaphoreType.DMA((10,)),
            pltpu.SemaphoreType.DMA((16,)),
            pltpu.SemaphoreType.DMA((2,)),
        ],
        compiler_params=pltpu.CompilerParams(
            vmem_limit_bytes=60 * 2**20, collective_id=0, has_side_effects=True
        ),
        name="forward_window",
    )(tok, box, rx, ry, mask, cot, freq, lay, vec, cols_own, rows_own, qkv_own, wo_own, w1_own, w2_own)


def bits_of(size):
    return [1 << b for b in range(size.bit_length() - 1)]


def tn(a, b):
    return lax.dot_general(a, b, (((0,), (0,)), ((), ())), preferred_element_type=jnp.float32)


def add_into(dst, more):
    rows = dst.shape[0]
    step = 64 if rows % 64 == 0 else 16

    @pl.loop(0, rows // step)
    def _(i):
        sl = pl.ds(pl.multiple_of(i * step, step), step)
        total = dst[sl, :].astype(jnp.float32)
        for ref in more:
            total = total + ref[sl, :].astype(jnp.float32)
        dst[sl, :] = total.astype(jnp.bfloat16)


class Reduce:
    def __init__(self, slot, rows, x_first, part, core, first, second, quarters, final, extra, result, sems, peers):
        self.slot, self.rows, self.x_first, self.part = slot, rows, x_first, part
        self.core, self.first, self.second, self.quarters, self.final = core, first, second, quarters, final
        self.extra, self.result = extra, result
        self.send, self.recv, self.here = sems
        self.mate, self.across, self.beside, self.along, self.further, self.side, self.level = peers

    def move(self, k, src, dst, peer):
        return remote(src, dst, self.send.at[self.slot, k], self.recv.at[self.slot, k], peer)

    def half(self, mine):
        h = self.rows // 2
        side = self.side if mine else 1 - self.side
        return pl.ds(pl.multiple_of(side * h, h), h)

    def quarter(self, level):
        q = self.rows // 8
        return pl.ds(pl.multiple_of(self.side * (self.rows // 2) + level * q, q), q)

    def moves(self, stage):
        if stage == 0:
            return [self.move(k, self.part(2 * k + 1), self.core.at[k], self.mate) for k in range(2)]
        if stage == 1 and self.x_first:
            return [self.move(2, self.core.at[1], self.first, self.across)]
        if stage == 1:
            h = self.rows // 2
            return [
                self.move(2 + k, self.core.at[k, self.half(False)], self.first.at[pl.ds(k * h, h)], self.beside)
                for k in range(2)
            ]
        if stage == 2 and self.x_first:
            return [self.move(4, self.core.at[0, self.half(False)], self.second, self.beside)]
        if stage == 2:
            return [self.move(4, self.core.at[1, self.half(True)], self.second, self.across)]
        if stage == 3:
            return [
                self.move(
                    4 + k, self.core.at[0, self.quarter(xor_level(self.level, k))], self.quarters.at[k - 1], self.along[k]
                )
                for k in range(1, 4)
            ]
        if stage == 4:
            rows = self.quarter(self.level)
            return [self.move(7 + k, self.final, self.result.at[rows], self.along[k]) for k in range(1, 4)]
        rows = self.half(True)
        return [self.move(11, self.result.at[rows], self.result.at[rows], self.beside)]

    def own_copy(self):
        return pltpu.make_async_copy(self.final, self.result.at[self.quarter(self.level)], self.here.at[self.slot])

    def more(self, k):
        return self.move(12 + k, self.final_of(k), self.extra.at[k], self.further[k])

    def final_of(self, k):
        return self.final if k == 0 else self.extra.at[len(self.further) + k]

    def take(self, stage):
        for m in self.moves(stage):
            m.wait_recv()
        h = self.rows // 2
        if stage == 0:
            for k in range(2):
                add_into(self.core.at[k], [self.part(2 * k)])
        if stage == 1 and self.x_first:
            add_into(self.core.at[0], [self.first])
        if stage == 1 and not self.x_first:
            for k in range(2):
                add_into(self.core.at[k, self.half(True)], [self.first.at[pl.ds(k * h, h)]])
        if stage == 2:
            add_into(self.core.at[0, self.half(True)], [self.second])
        if stage == 3:
            self.final[...] = self.core[0, self.quarter(self.level), :]
            add_into(self.final, [self.quarters.at[k] for k in range(3)])
            for k in range(len(self.further)):
                self.more(k).start()
                self.more(k).wait()
                total = self.final_of(k)[...].astype(jnp.float32) + self.extra[k].astype(jnp.float32)
                self.final_of(k + 1)[...] = total.astype(jnp.bfloat16)
            if self.further:
                self.final[...] = self.final_of(len(self.further))[...]
            self.own_copy().start()
        if stage == 4:
            self.own_copy().wait()

    def go(self, stage):
        for m in self.moves(stage):
            m.start()

    def next(self, stage):
        self.take(stage)
        if stage < 5:
            self.go(stage + 1)

    def sent(self, stage):
        for m in self.moves(stage):
            m.wait_send()


def xor_level(level, k):
    for bit in (1, 2):
        if k & bit:
            level = xor_index(level, bit)
    return level


def gelu_slope(v):
    k = math.sqrt(2.0 / math.pi)
    square = v * v
    t = jnp.tanh(k * v * (1.0 + 0.044715 * square))
    return 0.5 * (1.0 + t) + (0.5 * k) * v * (1.0 - t * t) * (1.0 + 3 * 0.044715 * square)


SMALL = 16


def backward_kernel(
    n_dp, inv_ref, vec_ref, sums_ref, dres_in, hid_in, pre_in, unit_in, nlow_in, low_in, feat_in, qkvt_in, ctxt_in,
    probs_in, rx_in, ry_in, w1_in, w2_in, wo_in, wqkv_in, block_in,
    block_all, in_all, red1, red2, red3, lay_all, small_out,
    arena, hidb, preb, dres, unit, nlow, nlow_t, dn, low_rows, qkvb, ctxtb, dctx, lowb, featb, wob, rxb, ryb, hot, acc,
    part1, part2, part3, core1, core2, core3, first1, first2, first3, second1, second2, second3,
    quarters1, quarters2, quarters3, final1, final2, final3, extra1, extra2, extra3, small, small_in, short,
    load_sem, send, recv, here, share_send, share_recv, small_send, small_recv, p_sem,
):
    t, d = lax.axis_index("tensor"), lax.axis_index("dp")
    mate, across = {"tensor": xor_index(t, 1)}, {"tensor": xor_index(t, 2)}
    beside = {"dp": xor_index(d, 1)}
    along = [None] + [{"dp": d + 2 * (xor_level((d // 2) % 4, k) - (d // 2) % 4)} for k in range(1, 4)]
    further = [{"dp": xor_index(d, bit)} for bit in bits_of(n_dp) if bit >= 8]
    peers = (mate, across, beside, along, further, d % 2, (d // 2) % 4)
    sems = (send, recv, here)
    f32, bf16 = jnp.float32, jnp.bfloat16
    win, model = dres.shape
    heads = 4 * HEADS_T
    cols_t = HEADS_T * HD
    hid_t = model
    block = 128

    def load(k, src, dst):
        return pltpu.make_async_copy(src, dst, load_sem.at[k])

    def w_rows(r):
        return pl.ds(r * hid_t, hid_t)

    def h_rows(r):
        return pl.ds(r * win, win)

    order = (1, 3, 2, 0)
    ld_dres = load(0, dres_in, dres)
    ld_hid = {r: load(1 + r, hid_in.at[r], hidb.at[h_rows(r)]) for r in order}
    ld_w2 = {r: load(5 + r, w2_in.at[r], arena.at[w_rows(r)]) for r in order}
    ld_w1 = {r: load(9 + r, w1_in.at[r], arena.at[w_rows(4 + r)]) for r in order}
    ld_pre = {r: load(13 + r, pre_in.at[r], preb.at[i % 2]) for i, r in enumerate(order)}
    ld_rest = [
        load(17 + k, src, dst)
        for k, (src, dst) in enumerate(
            [
                (nlow_in, nlow), (unit_in, unit), (ctxt_in, ctxtb), (wo_in, wob), (qkvt_in, qkvb), (low_in, lowb),
                (feat_in, featb), (rx_in, rxb), (ry_in, ryb),
            ]
        )
    ]
    ld_wqkv = [load(26 + n, wqkv_in.at[n], hidb.at[pl.ds(n * model, model)]) for n in range(3)]
    ld_dres.start()
    for r in order:
        ld_hid[r].start()
    for r in order[:2]:
        ld_pre[r].start()
    for r in order:
        ld_w2[r].start()
    ld_rest[0].start()
    for r in order:
        ld_w1[r].start()
    for c in ld_rest[1:]:
        c.start()

    def reduce_of(slot, rows, at, x_first, part, core, first, second, quarters, final, extra, result):
        h, q = rows // 2, rows // 8
        return Reduce(
            slot, rows, x_first, part, core.at[:, pl.ds(at, rows)], first.at[pl.ds(at, rows)],
            second.at[pl.ds(at // 2, h)], quarters.at[:, pl.ds(at // 8, q)], final.at[pl.ds(at // 8, q)],
            extra.at[:, pl.ds(at // 8, q)], result.at[pl.ds(at, rows)], sems, peers,
        )

    def chunks(slot, sizes, x_first, parts, *buffers):
        out, at = [], 0
        for k, (rows, part) in enumerate(zip(sizes, parts)):
            out.append(reduce_of(slot + k, rows, at, x_first, part, *buffers))
            at += rows
        return out

    third = hid_t // 3
    sizes = [third] * 3

    def thirds(ref):
        return [lambda r, k=k: ref.at[r, pl.ds(k * third, third)] for k in range(3)]

    s2 = chunks(0, sizes, True, thirds(part2), core2, first2, second2, quarters2, final2, extra2, red2)
    s1 = chunks(3, sizes, False, thirds(part1), core1, first1, second1, quarters1, final1, extra1, red1)
    lay_t = lay_all.shape[0] // 4
    s3 = chunks(
        6, [2 * cols_t, 2 * cols_t, lay_t], True,
        [
            lambda r: part2.at[r, pl.ds(0, 2 * cols_t)],
            lambda r: part2.at[r, pl.ds(2 * cols_t, 2 * cols_t)],
            lambda r: part3.at[r],
        ],
        core3, first3, second3, quarters3, final3, extra3, red3,
    )

    def share(k, src, whole, rows):
        def at(index):
            return whole.at[pl.ds(pl.multiple_of(index * rows, rows), rows)]

        def moved(j, from_ref, index, peer):
            return remote(from_ref, at(index), share_send.at[k, j], share_recv.at[k, j], peer)

        far = xor_index(t, 2)
        return {
            "here": pltpu.make_async_copy(src, at(t), share_send.at[k, 3]),
            "across": moved(0, src, t, across),
            "mate": moved(1, src, t, mate),
            "pass": moved(2, at(far), far, mate),
        }

    def share_start(c):
        for name in ("across", "mate", "here"):
            c[name].start()

    def share_pass(c):
        c["across"].wait_recv()
        c["pass"].start()

    def share_end(c):
        c["here"].wait()
        c["mate"].wait_recv()
        c["pass"].wait_recv()
        for name in ("across", "mate", "pass"):
            c[name].wait_send()

    sh_block = share(0, block_in, block_all, win)
    sh_in = share(1, low_rows, in_all, win)
    sh_lay = share(2, red3.at[pl.ds(4 * cols_t, lay_t)], lay_all, lay_t)

    signal_peers([mate, across, beside] + along[1:] + further)
    share_start(sh_block)

    small[0] = jnp.zeros_like(small[0])
    small[0, 3:4, :] = sums_ref[2:3, :]
    small[0, 4:6, :] = sums_ref[0:2, :]
    small[0, 6:7, :] = sums_ref[3:4, :]

    def own_row(base, r):
        index = t
        for bit in (1, 2):
            if r & bit:
                index = xor_index(index, bit)
        return pl.ds(base + index, 1)

    ld_dres.wait()

    @pl.loop(0, win // block)
    def _(i):
        sl = pl.ds(pl.multiple_of(i * block, block), block)
        low_rows[sl, :] = dres[sl, :].astype(bf16)

    for j, r in enumerate(order):
        ld_hid[r].wait()

        @pl.loop(0, 3)
        def _(c, r=r):
            sl = pl.ds(pl.multiple_of(c * third, third), third)
            part2[r, sl, :] = tn(hidb[h_rows(r), sl], low_rows[...]).astype(bf16)

        if j == 1:
            for g in s2:
                g.go(0)

    ld_rest[0].wait()
    nlow_t[...] = nlow[...].astype(f32).T.astype(bf16)
    for j, r in enumerate(order):
        ld_pre[r].wait()
        ld_w2[r].wait()
        ld_w1[r].wait()

        @pl.loop(0, 2)
        def _(i, j=j, r=r):
            count = win // 2
            sl = pl.ds(pl.multiple_of(i * count, count), count)
            hs = pl.ds(pl.multiple_of(r * win + i * count, count), count)
            dhid = nt(low_rows[sl, :], arena[w_rows(r), :])
            dpre = (dhid * gelu_slope(preb[j % 2, sl, :])).astype(bf16)
            hidb[hs, :] = dpre
            row = own_row(8, r)
            small[0, row, :] += jnp.sum(dpre.astype(f32), axis=0, keepdims=True)
            more = nt(dpre, arena[w_rows(4 + r), :])
            dn[sl, :] = more if j == 0 else dn[sl, :] + more

        if j + 2 < 4:
            ld_pre[order[j + 2]].start()

        @pl.loop(0, 3)
        def _(c, r=r):
            sl = pl.ds(pl.multiple_of(c * third, third), third)
            part1[r, sl, :] = nn(nlow_t[sl, :], hidb[h_rows(r), :]).astype(bf16)

        if j == 0:
            for g in s2:
                g.next(0)
        if j == 1:
            for g in s1:
                g.go(0)

    for c in ld_wqkv:
        c.start()

    def p_load(h, slot):
        return pltpu.make_async_copy(probs_in.at[h], preb.at[slot, :, pl.ds(0, win)], p_sem.at[slot])

    for h in range(2):
        p_load(h, h).start()
    for g in s1:
        g.next(0)
    share_pass(sh_block)
    for g in s2:
        g.sent(0)

    ld_rest[1].wait()

    @pl.loop(0, win // block)
    def _(i):
        sl = pl.ds(pl.multiple_of(i * block, block), block)
        up = dres[sl, :] + dn[sl, :]
        units = unit[sl, :]
        scaled = up * vec_ref[1:2, :]
        mean_one = jnp.mean(scaled, axis=1, keepdims=True)
        mean_two = jnp.mean(scaled * units, axis=1, keepdims=True)
        value = (scaled - mean_one - units * mean_two) * inv_ref[sl, :]
        dn[sl, :] = value
        low_rows[sl, :] = value.astype(bf16)
        small[0, 0:1, :] += jnp.sum(value, axis=0, keepdims=True)
        small[0, 1:2, :] += jnp.sum(up * units, axis=0, keepdims=True)
        small[0, 2:3, :] += jnp.sum(up, axis=0, keepdims=True)

    for c in ld_rest[2:]:
        c.wait()

    @pl.loop(0, 4)
    def _(r):
        sl = pl.ds(pl.multiple_of(r * cols_t, cols_t), cols_t)
        part2[r, cols_t : 2 * cols_t, :] = nn(ctxtb[sl, :], low_rows[...]).astype(bf16)
        dctx[sl, :] = nt(wob[sl, :], low_rows[...]).astype(bf16)

    def events(index, table):
        for at, todo in table.items():
            @pl.when(index == at)
            def _(todo=todo):
                for f in todo:
                    f()

    def ev(g, stage):
        return lambda: g.next(stage)

    in_heads = {
        3: [ev(s2[0], 1)],
        6: [ev(s1[0], 1), ev(s2[1], 1)],
        9: [ev(s1[1], 1), ev(s2[0], 2)],
        11: [ev(s2[2], 1), ev(s1[2], 1)],
    }

    @pl.loop(0, heads)
    def _(h):
        slot = h % 2
        sl = pl.ds(pl.multiple_of(h * HD, HD), HD)
        dc_t = dctx[sl, :]
        dc = dc_t.astype(f32).T.astype(bf16)
        p_load(h, slot).wait()
        p = preb[slot, :, 0:win]
        dp = nn(dc, qkvb[2, sl, :])
        row_dot = jnp.sum(p * dp, axis=1, keepdims=True)
        ds = (p * (dp - row_dot)).astype(bf16)
        qkvb[2, sl, :] = nn(dc_t, p.astype(bf16)).astype(bf16)
        dq = nt(qkvb[1, sl, :], ds) * HD ** (-0.5)
        dk = nn(qkvb[0, sl, :], ds) * HD ** (-0.5)
        qkvb[0, sl, :] = dq.astype(bf16)
        qkvb[1, sl, :] = dk.astype(bf16)
        arena[pl.ds(pl.multiple_of(h * win, win), win), 0:win] = ds

        @pl.when(h + 2 < heads)
        def _():
            p_load(h + 2, slot).start()

        events(h, in_heads)

    for c in ld_wqkv:
        c.wait()
    for n, at, g in ((2, 0, s3[0]), (0, 2 * cols_t, None), (1, 3 * cols_t, s3[1])):
        @pl.loop(0, 4)
        def _(r, n=n, at=at):
            sl = pl.ds(pl.multiple_of(r * cols_t, cols_t), cols_t)
            part2[r, at : at + cols_t, :] = nn(qkvb[n, sl, :], lowb[...]).astype(bf16)

        if g is not None:
            g.go(0)

    @pl.loop(0, win // block)
    def _(i):
        sl = pl.ds(pl.multiple_of(i * block, block), block)
        value = dn[sl, :]
        for n in range(3):
            value = value + tn(qkvb[n, :, sl], hidb[pl.ds(n * model, model), :])
        low_rows[sl, :] = value.astype(bf16)

    share_start(sh_in)
    for c in range(4):
        rows = [c ^ r for r in range(4)]
        value = tn(featb[:, c * lay_t : (c + 1) * lay_t], low_rows[...]).astype(bf16)
        part3[xor_level(t, c)] = value
    s3[2].go(0)
    for g in s3:
        g.next(0)

    ones = jnp.ones((8, win), bf16)
    short[...] = jnp.zeros_like(short)
    for n, at in ((0, 0), (2, cols_t)):
        total = nt(ones, qkvb[n])
        for r in range(4):
            short[r : r + 1, at : at + cols_t] = total[0:1, r * cols_t : (r + 1) * cols_t]

    acc[...] = jnp.zeros_like(acc)
    one, zero = bf16(1), bf16(0)
    hots = BUCKETS * ROWS
    in_table = {
        1: [ev(s1[0], 2), ev(s2[1], 2)],
        3: [ev(s2[0], 3), ev(s1[1], 2)],
        5: [ev(s1[0], 3), ev(s2[2], 2)],
        7: [ev(s2[1], 3), ev(s1[2], 2), ev(s2[0], 4)],
        9: [ev(s1[1], 3), ev(s2[2], 3), ev(s1[0], 4)],
        11: [ev(s1[2], 3), ev(s2[1], 4)],
        13: [ev(s1[1], 4), ev(s2[2], 4), ev(s1[2], 4)],
        15: [ev(s3[0], 1)],
    }

    @pl.loop(0, win // ROWS // 2)
    def _(i):
        total = None
        for u in range(2):
            at = pl.multiple_of(i * 2 * ROWS + u * ROWS, ROWS)
            x = rxb[pl.ds(at, ROWS), :].astype(f32).astype(bf16)
            y = ryb[pl.ds(at, ROWS), :].astype(f32).astype(bf16)
            for b in range(BUCKETS):
                hot[u, b * ROWS : (b + 1) * ROWS, :] = jnp.where(x == bf16(b), one, zero)
                hot[u, hots + b * ROWS : hots + (b + 1) * ROWS, :] = jnp.where(y == bf16(b), one, zero)
            left = jnp.concatenate(
                [arena[pl.ds(pl.multiple_of(h * win + at, ROWS), ROWS), 0:win] for h in range(heads)], axis=0
            )
            more = nt(left, hot[u])
            total = more if total is None else total + more
        acc[...] += total
        events(i, in_table)

    row = lax.broadcasted_iota(jnp.int32, (ROWS, 2 * hots), 0)
    col = lax.broadcasted_iota(jnp.int32, (ROWS, 2 * hots), 1) % ROWS
    picked = jnp.concatenate(
        [
            jnp.sum(jnp.where(row == col, acc[h * ROWS : (h + 1) * ROWS, :], 0.0), axis=0, keepdims=True)
            for h in range(heads)
        ]
        + [jnp.zeros((16 - heads, 2 * hots), f32)],
        axis=0,
    )
    fold = (
        lax.broadcasted_iota(jnp.int32, (2 * hots, 128), 0) // ROWS
        == lax.broadcasted_iota(jnp.int32, (2 * hots, 128), 1)
    ).astype(f32)
    table = jnp.dot(picked, fold, preferred_element_type=f32, precision=lax.Precision.HIGHEST)
    for r in range(4):
        for a in range(HEADS_T):
            lane = 2 * cols_t + a * 2 * BUCKETS
            short[r : r + 1, lane : lane + 2 * BUCKETS] = table[
                r * HEADS_T + a : r * HEADS_T + a + 1, 0 : 2 * BUCKETS
            ]
    for r in range(4):
        small[0, own_row(12, r), :] = short[r : r + 1, :]

    bits = [mate, across, beside, along[1], along[2]] + further

    def small_move(k):
        return remote(small.at[k], small_in.at[k], small_send.at[k], small_recv.at[k], bits[k])

    def small_step(k):
        def run():
            small_move(k).wait()
            small[k + 1] = small[k] + small_in[k]
            if k + 1 < len(bits):
                small_move(k + 1).start()

        return run

    small_move(0).start()
    steps = [small_step(k) for k in range(len(bits))]
    tail = [
        ev(s3[1], 1), steps[0], ev(s3[2], 1), ev(s3[0], 2), steps[1], ev(s3[1], 2), ev(s3[2], 2), ev(s3[0], 3),
        steps[2], ev(s3[1], 3), ev(s3[2], 3), ev(s3[2], 4), ev(s3[0], 4), ev(s3[1], 4), steps[3],
        ev(s3[2], 5), lambda: share_start(sh_lay), steps[4], ev(s3[0], 5), ev(s3[1], 5),
        lambda: share_pass(sh_in), lambda: share_pass(sh_lay),
    ] + steps[5:] + [ev(g, 5) for g in s2 + s1]
    for f in tail:
        f()
    small_out[...] = small[len(bits)]
    for c in (sh_block, sh_in, sh_lay):
        share_end(c)
    for g in s1 + s3:
        g.sent(0)
    for g in s2 + s1 + s3:
        for stage in range(1, 6):
            g.sent(stage)


def backward_window(n_dp, lay_rows, inv, vec, sums, dres, hid, pre, unit, nlow, low, feat, qkvt, ctxt, probs, rx, ry, w1, w2, wo, wqkv, block_own):
    win, model = dres.shape
    heads = 4 * HEADS_T
    cols_t = HEADS_T * HD
    lay_t = lay_rows // 4
    rest = 4 * cols_t + lay_t
    more = max(0, len(bits_of(n_dp)) - 3)
    levels = 5 + more
    f32, bf16 = jnp.float32, jnp.bfloat16
    shape = jax.ShapeDtypeStruct
    here = pl.BlockSpec(memory_space=pltpu.VMEM)
    away = pl.BlockSpec(memory_space=pl.ANY)
    outs = [
        (shape((4 * win, model), bf16), away),
        (shape((4 * win, model), bf16), away),
        (shape((model, model), bf16), away),
        (shape((model, model), bf16), away),
        (shape((rest, model), bf16), away),
        (shape((lay_rows, model), bf16), away),
        (shape((SMALL, model), f32), here),
    ]
    V = pltpu.VMEM
    S = pltpu.SemaphoreType.DMA
    return pl.pallas_call(
        functools.partial(backward_kernel, n_dp),
        in_specs=[here] * 3 + [away] * 17,
        out_specs=[spec for _, spec in outs],
        out_shape=[s for s, _ in outs],
        scratch_shapes=[
            V((8 * model, model), bf16), V((3 * model, model), bf16), V((2, win, model), f32), V((win, model), f32),
            V((win, model), f32), V((win, model), bf16), V((model, win), bf16), V((win, model), f32),
            V((win, model), bf16), V((3, model, win), bf16), V((model, win), bf16), V((model, win), bf16),
            V((win, model), bf16), V((win, lay_rows), bf16), V((model, model), bf16), V((win, win), jnp.int32),
            V((win, win), jnp.int32), V((2, 2 * BUCKETS * ROWS, win), bf16), V((heads * ROWS, 2 * BUCKETS * ROWS), f32),
            V((4, model, model), bf16), V((4, model, model), bf16), V((4, lay_t, model), bf16),
            V((2, model, model), bf16), V((2, model, model), bf16), V((2, rest, model), bf16),
            V((model, model), bf16), V((model, model), bf16), V((rest, model), bf16),
            V((model // 2, model), bf16), V((model // 2, model), bf16), V((rest // 2, model), bf16),
            V((3, model // 8, model), bf16), V((3, model // 8, model), bf16), V((3, rest // 8, model), bf16),
            V((model // 8, model), bf16), V((model // 8, model), bf16), V((rest // 8, model), bf16),
            V((2 * more + 1, model // 8, model), bf16), V((2 * more + 1, model // 8, model), bf16),
            V((2 * more + 1, rest // 8, model), bf16),
            V((levels + 1, SMALL, model), f32), V((levels, SMALL, model), f32), V((8, model), f32),
            S((29,)), S((9, 12 + max(1, more))), S((9, 12 + max(1, more))), S((9,)), S((3, 4)), S((3, 3)),
            S((levels,)), S((levels,)), S((2,)),
        ],
        compiler_params=pltpu.CompilerParams(
            vmem_limit_bytes=63 * 2**20, collective_id=1, has_side_effects=True
        ),
        name="backward_window",
    )(inv, vec, sums, dres, hid, pre, unit, nlow, low, feat, qkvt, ctxt, probs, rx, ry, w1, w2, wo, wqkv, block_own)


def local(
    n_dp, n_t,
    tokens_in, box_coords, rel_x, rel_y, mask_tokens, cotangent, layout_weight, qkv_weight, qv_bias,
    bias_table, out_weight, out_bias, ln1_gain, ln1_bias, ffn_in_weight, ffn_in_bias, ffn_out_weight,
    ffn_out_bias, ln2_gain, ln2_bias, group_rates,
):
    me = lax.axis_index("tensor")
    win = rel_x.shape[1]
    model = tokens_in.shape[1]
    heads_t = bias_table.shape[1]
    cols_t = heads_t * HD
    hid_t = ffn_in_weight.shape[1]
    tok_rows = tokens_in.shape[0] // n_t

    def mine(whole):
        return lax.dynamic_slice_in_dim(whole, me * (whole.shape[0] // n_t), whole.shape[0] // n_t)

    zeros = jnp.zeros((cols_t,), jnp.float32)
    cols_own = jnp.pad(jnp.stack([qv_bias[0], zeros, qv_bias[1]], axis=1), ((0, 0), (0, 125)))
    rows_own = jnp.concatenate(
        [
            ffn_in_bias[None, :],
            jnp.pad(bias_table.T.astype(jnp.float32), ((0, 0), (0, hid_t - 2 * BUCKETS))),
            jnp.zeros((8 - 1 - heads_t, hid_t), jnp.float32),
        ],
        axis=0,
    )
    freq_index = jnp.arange(LFREQ).astype(jnp.float32)
    freq = jnp.exp(freq_index * (-math.log(1000.0) / LFREQ))
    freq = jnp.broadcast_to(jnp.concatenate([freq, freq])[None, :], (8, 2 * LFREQ))
    zero = jnp.zeros_like(out_bias)
    vec = jnp.stack([out_bias, ln1_gain, ln1_bias, ffn_out_bias, ln2_gain, ln2_bias, zero, zero])
    relx, rely = mine(rel_x)[0], mine(rel_y)[0]

    (
        probs, qkvt, context_t, layer_low, features, unit_one, inverse_one, normed_low, pre_all, hid_all,
        block_own, dresid_two, sums, wqkv, wo, w1, w2,
    ) = forward_window(
        n_dp, mine(tokens_in), mine(box_coords), relx, rely, mine(mask_tokens)[:, None], mine(cotangent), freq,
        layout_weight, vec, cols_own, rows_own, jnp.transpose(qkv_weight, (0, 2, 1)), out_weight, ffn_in_weight, ffn_out_weight,
    )
    block_out, in_all, sum1, sum2, sum3, lay_all, small = backward_window(
        n_dp, layout_weight.shape[0], inverse_one, vec, sums, dresid_two, hid_all, pre_all, unit_one, normed_low, layer_low,
        features, qkvt, context_t, probs, relx, rely, w1, w2, wo, wqkv, block_own,
    )
    f32 = jnp.float32
    count = small[6, 0]
    factor = group_rates / count
    own = lax.dynamic_slice_in_dim(small, 12 + me, 1)[0]
    qkv_sum = jnp.stack([sum3[2 * cols_t : 3 * cols_t], sum3[3 * cols_t : 4 * cols_t], sum3[:cols_t]])
    return (
        block_out,
        in_all.astype(f32) / count,
        lay_all.astype(f32) * factor[6],
        jnp.transpose(qkv_sum, (0, 2, 1)).astype(f32) * factor[0],
        own[: 2 * cols_t].reshape(2, cols_t) * factor[0],
        own[2 * cols_t : 3 * cols_t].reshape(heads_t, 2 * BUCKETS).T * factor[7],
        sum3[cols_t : 2 * cols_t].astype(f32) * factor[1],
        small[0] * factor[1],
        small[1] * factor[2],
        small[2] * factor[2],
        sum1.astype(f32) * factor[3],
        lax.dynamic_slice_in_dim(small, 8 + me, 1)[0] * factor[3],
        sum2.astype(f32) * factor[4],
        small[3] * factor[4],
        small[4] * factor[5],
        small[5] * factor[5],
    )


def solution(mesh):
    placed = (
        P("dp", None), P("dp", None), P("dp", None, None), P("dp", None, None), P("dp"), P("dp", None),
        P(), P(None, None, "tensor"), P(None, "tensor"), P(None, "tensor"), P("tensor", None),
        P(), P(), P(), P(None, "tensor"), P("tensor"), P("tensor", None), P(), P(), P(), P(),
    )
    return jax.shard_map(
        functools.partial(local, mesh.shape["dp"], mesh.shape["tensor"]),
        mesh=mesh,
        in_specs=placed,
        out_specs=(
            P("dp", None), P("dp", None), P(), P(None, None, "tensor"), P(None, "tensor"),
            P(None, "tensor"), P("tensor", None), P(), P(), P(), P(None, "tensor"), P("tensor"),
            P("tensor", None), P(), P(), P(),
        ),
        check_vma=False,
    )
```

```python
import functools
import math

import jax
import jax.numpy as jnp
from jax import lax
from jax.experimental import pallas as pl
from jax.experimental.pallas import tpu as pltpu
from jax.sharding import PartitionSpec as P

HD = 64
LFREQ = 64
BUCKETS = 32
EPSILON = 1e-05
ROWS = 16
HEADS_T = 3
MESH = pl.DeviceIdType.MESH

ORDERS = {
    "A": (True, False, True),
    "B": (True, False, False),
    "C": (True, False, True),
}
SCHEDULE = {
    "start": ("blk0", "blk1",),
    "ffn0.1": ("blkpass0",),
    "ffn1.0": ("blkpass1",),
    "ffn3.1": ("A1.1", "A0.1",),
    "h0": ("A2.1",),
    "h2": ("A0.2",),
    "h5": ("B1.1", "B0.1", "A0.3",),
    "h6": ("B2.1", "A1.2",),
    "h8": ("A0.4", "A2.2", "B1.2",),
    "h10": ("A1.3", "B0.2", "B2.2",),
    "h11": ("blk2", "blk3",),
    "pq": ("A2.3",),
    "pk": ("B1.3", "blkpass2",),
    "dl0": ("A1.4", "blkpass3",),
    "dl3": ("B0.3",),
    "t0": ("Cb.1", "B2.3", "Ca.1", "A2.4",),
    "t3": ("Cc.1", "B1.4",),
    "t6": ("B0.4", "Ca.2",),
    "t9": ("B2.4",),
    "t11": ("Cc.2",),
    "t14": ("Ca.3",),
    "t15": ("Cc.3", "igpass",),
    "tail": (
        "A0.5", "A1.5", "A2.5", "B1.5", "B0.5", "sm0", "Ca.4", "Cb.2", "B2.5", "sm1", "Cc.4", "Ca.5", "Cb.3", "sm2",
        "Cc.5", "lay", "Cb.4", "laypass", "sm3", "sm4", "Cb.5",
    ),
}


def nt(a, b):
    return lax.dot_general(a, b, (((1,), (1,)), ((), ())), preferred_element_type=jnp.float32)


def nn(a, b):
    return jnp.dot(a, b, preferred_element_type=jnp.float32)


def xor_index(index, bit):
    return index + bit - 2 * bit * ((index // bit) % 2)


def signal_peers(peers):
    barrier = pltpu.get_barrier_semaphore()
    for peer in peers:
        pl.semaphore_signal(barrier, inc=1, device_id=peer, device_id_type=MESH)
    pl.semaphore_wait(barrier, len(peers))


def remote(src, dst, send, recv, peer):
    return pltpu.make_async_remote_copy(
        src_ref=src, dst_ref=dst, send_sem=send, recv_sem=recv, device_id=peer, device_id_type=MESH
    )


class Gather:
    def __init__(self, own, place, rows, split, sems, slot, peers):
        self.own, self.place, self.rows, self.split = own, place, rows, split
        self.send, self.recv, self.here = sems
        self.slot = slot
        self.mate, self.across, self.beside, self.side = peers

    def copy(self, name):
        s = self.slot
        half = self.rows // 2 if self.split else self.rows
        mine = pl.ds(pl.multiple_of(self.side * half, half), half) if self.split else pl.ds(0, half)
        yours = pl.ds(pl.multiple_of((1 - self.side) * half, half), half)
        whole = pl.ds(0, self.rows)
        if name == "here":
            return pltpu.make_async_copy(self.own(whole), self.place(0, whole), self.here.at[s])
        src, dst, peer, k = {
            "mate": lambda: (self.own(whole), self.place(1, whole), self.mate, 0),
            "across": lambda: (self.own(mine), self.place(2, mine), self.across, 1),
            "pass": lambda: (self.place(2, mine), self.place(3, mine), self.mate, 2),
            "beside": lambda: (self.place(2, mine), self.place(2, mine), self.beside, 3),
            "pass_two": lambda: (self.place(2, yours), self.place(3, yours), self.mate, 4),
        }[name]()
        return remote(src, dst, self.send.at[s, k], self.recv.at[s, k], peer)

    def start(self):
        self.copy("across").start()
        self.copy("mate").start()
        self.copy("here").start()

    def forward(self):
        self.copy("across").wait_recv()
        if self.split:
            self.copy("beside").start()
        self.copy("pass").start()

    def forward_two(self):
        if self.split:
            self.copy("beside").wait_recv()
            self.copy("pass_two").start()

    def arrive_near(self):
        self.copy("here").wait()
        self.copy("mate").wait_recv()

    def arrive_far(self):
        self.copy("pass").wait_recv()
        if self.split:
            self.copy("pass_two").wait_recv()

    def arrive(self):
        self.arrive_near()
        self.arrive_far()

    def finish(self):
        for name in ("mate", "across", "pass") + (("beside", "pass_two") if self.split else ()):
            self.copy(name).wait_send()


def waves(column, frequency, quarter):
    angle = column * frequency
    turns = jnp.floor(angle * (2.0 / math.pi) + 0.5)
    rest = ((angle - turns * 1.5703125) - turns * 4.837512969970703125e-4) - turns * 7.549789948768648e-8
    quadrant = turns.astype(jnp.int32) + quarter
    z = rest * rest
    sine = ((-1.9515295891e-4 * z + 8.3321608736e-3) * z - 1.6666654611e-1) * z * rest + rest
    cosine = ((2.443315711809948e-5 * z - 1.388731625493765e-3) * z + 4.166664568298827e-2) * z * z - 0.5 * z + 1.0
    value = jnp.where(quadrant % 2 == 1, cosine, sine)
    return jnp.where((quadrant // 2) % 2 == 1, -value, value)


def gelu(v):
    return 0.5 * v * (1.0 + jnp.tanh(math.sqrt(2.0 / math.pi) * (v + 0.044715 * (v * v * v))))


def forward_kernel(
    tok_ref, box_ref, rx_ref, ry_ref, mask_ref, cot_ref, freq_ref, lay_ref, vec_ref,
    cols_own, rows_own, qkv_own, wo_own, w1_own, w2_own,
    probs_out, qkvt_out, ctxt_out, low_out, feat_out, unit_out, inv_out, nlow_out, pre_out, hid_out,
    block_out, dres_out, sums_out, wqkv_out, wo_out, w1_out, w2_out,
    wqkv, wo, w1, w2, cols, rows, tabs, layer_in, qkvt, pbuf, ctxt, ctx, normed, pre, hid, acc,
    send, recv, here, out_sem, p_sem,
):
    t, d = lax.axis_index("tensor"), lax.axis_index("dp")
    mate, across = {"tensor": xor_index(t, 1)}, {"tensor": xor_index(t, 2)}
    beside = {"dp": xor_index(d, 1)}
    peers = (mate, across, beside, d % 2)
    win, model = tok_ref.shape
    heads = 4 * HEADS_T
    cols_t = HEADS_T * HD
    sems = (send, recv, here)
    f32, bf16 = jnp.float32, jnp.bfloat16

    def chunk(slot, own, place, count, split=True):
        return Gather(own, place, count, split, sems, slot, peers)

    g_cols = chunk(0, lambda s: cols_own.at[s], lambda r, s: cols.at[r, s], cols_t, False)
    g_rows = chunk(1, lambda s: rows_own.at[s], lambda r, s: rows.at[r, s], 8, False)

    def piece_rows(r, s, count):
        return pl.ds(pl.multiple_of(r * count + s.start, 16), s.size)

    g_qkv = [
        chunk(
            2 + n,
            lambda s, n=n: qkv_own.at[n, s],
            lambda r, s, n=n: wqkv.at[n, piece_rows(r, s, cols_t)],
            cols_t,
        )
        for n in range(3)
    ]
    g_wo = chunk(5, lambda s: wo_own.at[s], lambda r, s: wo.at[piece_rows(r, s, cols_t)], cols_t)

    def part(slot, own, whole, half):
        count = own.shape[0] // 2

        def moved(s):
            return pl.ds(pl.multiple_of(s.start + half * count, 16), s.size)

        return chunk(slot, lambda s: own.at[moved(s)], lambda r, s: whole.at[r, moved(s)], count)

    g_w1 = [part(6 + h, w1_own, w1, h) for h in range(2)]
    g_w2 = [part(8 + h, w2_own, w2, h) for h in range(2)]
    everything = [g_cols, g_rows] + g_qkv + [g_wo] + g_w1 + g_w2

    signal_peers((mate, across, beside))
    for g in [g_cols, g_rows] + g_qkv:
        g.start()

    lane = lax.broadcasted_iota(jnp.int32, (1, 128), 1)
    quarter = jnp.where(lane >= LFREQ, 1, 0)
    block = 128

    @pl.loop(0, win // block)
    def _(i):
        sl = pl.ds(pl.multiple_of(i * block, block), block)
        box = box_ref[sl, :].astype(f32)
        for m in range(4):
            feat_out[sl, 2 * LFREQ * m : 2 * LFREQ * (m + 1)] = waves(
                box[:, m : m + 1], freq_ref[0:1, :], quarter
            ).astype(bf16)
        value = tok_ref[sl, :].astype(f32) + nn(feat_out[sl, :], lay_ref[...])
        layer_in[sl, :] = value
        low_out[sl, :] = value.astype(bf16)

    for g in [g_cols, g_rows] + g_qkv:
        g.forward()
    g_wo.start()
    g_w1[0].start()
    for g in g_qkv:
        g.forward_two()
    g_cols.arrive()
    g_rows.arrive()
    for r in range(4):
        tabs[HEADS_T * r : HEADS_T * (r + 1), :] = rows[r, 1 : 1 + HEADS_T, 0:128]

    for n in range(3):
        g_qkv[n].arrive()

        @pl.loop(0, 4)
        def _(r, n=n):
            sl = pl.ds(pl.multiple_of(r * cols_t, 16), cols_t)
            value = nt(wqkv[n, sl, :], low_out[...])
            qkvt[n, sl, :] = (value + cols[r, :, n : n + 1]).astype(bf16)

    def table_row(h):
        return (tabs[pl.ds(h, 1), :] * 2048.0 + 32768.5).astype(jnp.int32) - 32768

    def p_copy(i, slot):
        return pltpu.make_async_copy(pbuf.at[slot], probs_out.at[pl.ds(2 * i, 2)], p_sem.at[slot])

    @pl.loop(0, heads // 2)
    def _(i):
        slot = i % 2
        sl = pl.ds(pl.multiple_of(i * 2 * HD, 2 * HD), 2 * HD)
        q = (qkvt[0, sl, :].astype(f32).T * HD ** (-0.5)).astype(bf16)
        tab = jnp.broadcast_to((table_row(2 * i) << 16) + table_row(2 * i + 1), (win, 128))
        bias = ([], [])
        for c in range(win // 128):
            at = slice(128 * c, 128 * c + 128)
            word = jnp.take_along_axis(tab, rx_ref[:, at], axis=1) + jnp.take_along_axis(
                tab, ry_ref[:, at] + BUCKETS, axis=1
            )
            second = word << 16
            bias[0].append((word - (second >> 16)).astype(f32) * 2.0**-27)
            bias[1].append(second.astype(f32) * 2.0**-27)

        @pl.when(i >= 2)
        def _():
            p_copy(i - 2, slot).wait()

        for u in range(2):
            rows_u = pl.ds(pl.multiple_of(i * 2 * HD + u * HD, HD), HD)
            s = nn(q[:, u * HD : (u + 1) * HD], qkvt[1, rows_u, :]) + jnp.concatenate(bias[u], axis=1)
            m = jnp.max(s, axis=1, keepdims=True)
            e = jnp.exp(s - m)
            p = e * (1.0 / jnp.sum(e, axis=1, keepdims=True))
            pbuf[slot, u] = p
            ctxt[rows_u, :] = nt(qkvt[2, rows_u, :], p.astype(bf16)).astype(bf16)
        p_copy(i, slot).start()

        @pl.when(i == 0)
        def _():
            g_wo.forward()
            g_w1[1].start()

        @pl.when(i == 1)
        def _():
            g_w1[0].forward()
            g_wo.forward_two()
            g_w2[0].start()

        @pl.when(i == 2)
        def _():
            g_w2[1].start()

        @pl.when(i == 3)
        def _():
            g_w1[1].forward()
            g_w1[0].forward_two()

        @pl.when(i == 5)
        def _():
            g_w2[0].forward()
            g_w1[1].forward_two()

    last = heads // 2
    outs = [
        (qkvt, qkvt_out), (ctxt, ctxt_out), (wqkv, wqkv_out),
    ]
    done = []

    def leave(src, dst):
        c = pltpu.make_async_copy(src, dst, out_sem.at[len(done)])
        c.start()
        done.append(c)

    for src, dst in outs:
        leave(src, dst)
    g_wo.arrive()
    leave(wo, wo_out)

    ctx[...] = ctxt[...].astype(f32).T.astype(bf16)

    @pl.loop(0, win // block)
    def _(i):
        sl = pl.ds(pl.multiple_of(i * block, block), block)
        value = layer_in[sl, :] + nn(ctx[sl, :], wo[...]) + vec_ref[0:1, :]
        mean = jnp.mean(value, axis=1, keepdims=True)
        centered = value - mean
        inverse = lax.rsqrt(jnp.mean(centered * centered, axis=1, keepdims=True) + EPSILON)
        unit = centered * inverse
        unit_out[sl, :] = unit
        inv_out[sl, :] = inverse
        value = unit * vec_ref[1:2, :] + vec_ref[2:3, :]
        normed[sl, :] = value
        nlow_out[sl, :] = value.astype(bf16)

    g_w2[0].forward_two()
    g_w2[1].forward()
    for r in range(4):
        if r == 0:
            for g in g_w1 + g_w2:
                g.arrive_near()
        if r == 2:
            g_w2[1].forward_two()
            for g in g_w1 + g_w2:
                g.arrive_far()
            leave(w1, w1_out)
            leave(w2, w2_out)

        @pl.loop(0, win // 256)
        def _(i, r=r):
            sl = pl.ds(pl.multiple_of(i * 256, 256), 256)
            value = nn(nlow_out[sl, :], w1[r]) + rows[r, 0:1, :]
            pre[r, sl, :] = value
            low_hid = gelu(value).astype(bf16)
            hid[r, sl, :] = low_hid
            more = nn(low_hid, w2[r])
            acc[sl, :] = more if r == 0 else acc[sl, :] + more

        leave(pre.at[r], pre_out.at[r])
        leave(hid.at[r], hid_out.at[r])

    sums_out[...] = jnp.zeros_like(sums_out)

    @pl.loop(0, win // block)
    def _(i):
        sl = pl.ds(pl.multiple_of(i * block, block), block)
        value = normed[sl, :] + acc[sl, :] + vec_ref[3:4, :]
        mean = jnp.mean(value, axis=1, keepdims=True)
        centered = value - mean
        inverse = lax.rsqrt(jnp.mean(centered * centered, axis=1, keepdims=True) + EPSILON)
        unit = centered * inverse
        block_out[sl, :] = (unit * vec_ref[4:5, :] + vec_ref[5:6, :]).astype(bf16)
        selected = mask_ref[sl, :].astype(f32) * cot_ref[sl, :].astype(f32)
        scaled = selected * vec_ref[4:5, :]
        mean_one = jnp.mean(scaled, axis=1, keepdims=True)
        mean_two = jnp.mean(scaled * unit, axis=1, keepdims=True)
        dres = (scaled - mean_one - unit * mean_two) * inverse
        dres_out[sl, :] = dres
        sums_out[0:1, :] += jnp.sum(selected * unit, axis=0, keepdims=True)
        sums_out[1:2, :] += jnp.sum(selected, axis=0, keepdims=True)
        sums_out[2:3, :] += jnp.sum(dres, axis=0, keepdims=True)
        sums_out[3:4, :] += jnp.sum(mask_ref[sl, :].astype(f32), axis=0, keepdims=True)

    for i in (last - 2, last - 1):
        p_copy(i, i % 2).wait()
    for c in done:
        c.wait()
    for g in everything:
        g.finish()


def forward_window(n_dp, tok, box, rx, ry, mask, cot, freq, lay, vec, cols_own, rows_own, qkv_own, wo_own, w1_own, w2_own):
    win, model = tok.shape
    cols_t, hid_t = wo_own.shape[0], w1_own.shape[1]
    heads = 4 * HEADS_T
    f32, bf16 = jnp.float32, jnp.bfloat16
    shape = jax.ShapeDtypeStruct
    here = pl.BlockSpec(memory_space=pltpu.VMEM)
    away = pl.BlockSpec(memory_space=pl.ANY)
    outs = [
        (shape((heads, win, win), f32), away),
        (shape((3, model, win), bf16), away),
        (shape((model, win), bf16), away),
        (shape((win, model), bf16), here),
        (shape((win, 8 * LFREQ), bf16), here),
        (shape((win, model), f32), here),
        (shape((win, 1), f32), here),
        (shape((win, model), bf16), here),
        (shape((4, win, hid_t), f32), away),
        (shape((4, win, hid_t), bf16), away),
        (shape((win, model), bf16), here),
        (shape((win, model), f32), here),
        (shape((8, model), f32), here),
        (shape((3, model, model), bf16), away),
        (shape((model, model), bf16), away),
        (shape((4, model, hid_t), bf16), away),
        (shape((4, hid_t, model), bf16), away),
    ]
    return pl.pallas_call(
        forward_kernel,
        in_specs=[here] * 9 + [away] * 6,
        out_specs=[spec for _, spec in outs],
        out_shape=[s for s, _ in outs],
        scratch_shapes=[
            pltpu.VMEM((3, model, model), bf16),
            pltpu.VMEM((model, model), bf16),
            pltpu.VMEM((4, model, hid_t), bf16),
            pltpu.VMEM((4, hid_t, model), bf16),
            pltpu.VMEM((4, cols_t, 128), f32),
            pltpu.VMEM((4, 8, model), f32),
            pltpu.VMEM((heads, 128), f32),
            pltpu.VMEM((win, model), f32),
            pltpu.VMEM((3, model, win), bf16),
            pltpu.VMEM((2, 2, win, win), f32),
            pltpu.VMEM((model, win), bf16),
            pltpu.VMEM((win, model), bf16),
            pltpu.VMEM((win, model), f32),
            pltpu.VMEM((4, win, hid_t), f32),
            pltpu.VMEM((4, win, hid_t), bf16),
            pltpu.VMEM((win, model), f32),
            pltpu.SemaphoreType.DMA((10, 5)),
            pltpu.SemaphoreType.DMA((10, 5)),
            pltpu.SemaphoreType.DMA((10,)),
            pltpu.SemaphoreType.DMA((16,)),
            pltpu.SemaphoreType.DMA((2,)),
        ],
        compiler_params=pltpu.CompilerParams(
            vmem_limit_bytes=60 * 2**20, collective_id=0, has_side_effects=True
        ),
        name="forward_window",
    )(tok, box, rx, ry, mask, cot, freq, lay, vec, cols_own, rows_own, qkv_own, wo_own, w1_own, w2_own)


def bits_of(size):
    return [1 << b for b in range(size.bit_length() - 1)]


def tn(a, b):
    return lax.dot_general(a, b, (((0,), (0,)), ((), ())), preferred_element_type=jnp.float32)


def add_into(dst, more):
    rows = dst.shape[0]
    step = 64 if rows % 64 == 0 else 16

    @pl.loop(0, rows // step)
    def _(i):
        sl = pl.ds(pl.multiple_of(i * step, step), step)
        total = dst[sl, :].astype(jnp.float32)
        for ref in more:
            total = total + ref[sl, :].astype(jnp.float32)
        dst[sl, :] = total.astype(dst.dtype)


class Reduce:
    def __init__(self, slot, rows, x_first, part, core, first, second, quarters, final, extra, result, acc, sems, peers):
        self.slot, self.rows, self.x_first, self.part, self.acc = slot, rows, x_first, part, acc
        self.core, self.first, self.second, self.quarters, self.final = core, first, second, quarters, final
        self.extra, self.result = extra, result
        self.send, self.recv, self.here = sems
        self.mate, self.across, self.beside, self.along, self.further, self.side, self.level = peers
        self.total = core.at[0] if acc is None else acc

    def move(self, k, src, dst, peer):
        return remote(src, dst, self.send.at[self.slot, k], self.recv.at[self.slot, k], peer)

    def half(self, mine):
        h = self.rows // 2
        side = self.side if mine else 1 - self.side
        return pl.ds(pl.multiple_of(side * h, h), h)

    def quarter(self, level):
        q = self.rows // 8
        return pl.ds(pl.multiple_of(self.side * (self.rows // 2) + level * q, q), q)

    def moves(self, stage, piece=None):
        h = self.rows // 2
        if stage == 0:
            return [self.move(p, self.part(p), self.core.at[p], self.mate) for p in range(2) if piece in (None, p)]
        if stage == 1 and self.x_first:
            return [self.move(2, self.core.at[1], self.first, self.across)] if piece != 0 else []
        if stage == 1:
            return [
                self.move(2 + p, self.core.at[p, self.half(False)], self.first.at[pl.ds(p * h, h)], self.beside)
                for p in range(2)
                if piece in (None, p)
            ]
        if stage == 2 and self.x_first:
            return [self.move(4, self.core.at[0, self.half(False)], self.second, self.beside)]
        if stage == 2:
            return [self.move(4, self.core.at[1, self.half(True)], self.second, self.across)]
        if stage == 3:
            return [
                self.move(
                    4 + k, self.core.at[0, self.quarter(xor_level(self.level, k))], self.quarters.at[k - 1], self.along[k]
                )
                for k in range(1, 4)
            ]
        if stage == 4:
            rows = self.quarter(self.level)
            return [self.move(7 + k, self.final, self.result.at[rows], self.along[k]) for k in range(1, 4)]
        rows = self.half(True)
        return [self.move(11, self.result.at[rows], self.result.at[rows], self.beside)]

    def own_copy(self):
        return pltpu.make_async_copy(self.final, self.result.at[self.quarter(self.level)], self.here.at[self.slot])

    def more(self, k):
        return self.move(12 + k, self.final_of(k), self.extra.at[k], self.further[k])

    def final_of(self, k):
        return self.final if k == 0 else self.extra.at[len(self.further) + k]

    def round_off(self, rows):
        if self.acc is not None:
            self.core[0, rows, :] = self.acc[rows, :].astype(jnp.bfloat16)

    def merge(self, piece, rows, value):
        value = value + self.core[piece, rows, :].astype(jnp.float32)
        if piece == 0:
            self.total[rows, :] = value.astype(self.total.dtype)
        else:
            self.core[1, rows, :] = value.astype(jnp.bfloat16)

    def from_mate(self, piece):
        for m in self.moves(0, piece):
            m.wait_recv()

    def take(self, stage):
        for m in self.moves(stage):
            m.wait_recv()
        h = self.rows // 2
        if stage == 1 and self.x_first:
            add_into(self.total, [self.first])
        if stage == 1 and not self.x_first:
            add_into(self.core.at[1, self.half(True)], [self.first.at[pl.ds(h, h)]])
            add_into(self.total.at[self.half(True)], [self.first.at[pl.ds(0, h)]])
        if stage == 2:
            add_into(self.total.at[self.half(True)], [self.second])
        if stage == 3:
            value = self.total[self.quarter(self.level), :].astype(jnp.float32)
            for k in range(3):
                value = value + self.quarters[k].astype(jnp.float32)
            self.final[...] = value.astype(jnp.bfloat16)
            for k in range(len(self.further)):
                self.more(k).start()
                self.more(k).wait()
                total = self.final_of(k)[...].astype(jnp.float32) + self.extra[k].astype(jnp.float32)
                self.final_of(k + 1)[...] = total.astype(jnp.bfloat16)
            if self.further:
                self.final[...] = self.final_of(len(self.further))[...]
            self.own_copy().start()
        if stage == 4:
            self.own_copy().wait()

    def go(self, stage, piece=None):
        if stage == 1 and not self.x_first and piece == 0:
            self.round_off(self.half(False))
        if stage == 2 and self.x_first:
            self.round_off(self.half(False))
        if stage == 3:
            self.round_off(self.half(True))
        for m in self.moves(stage, piece):
            m.start()

    def next(self, stage):
        self.take(stage)
        if stage < 5:
            self.go(stage + 1)

    def sent(self, stage):
        for m in self.moves(stage):
            m.wait_send()


def xor_level(level, k):
    for bit in (1, 2):
        if k & bit:
            level = xor_index(level, bit)
    return level


def gelu_slope(v):
    k = math.sqrt(2.0 / math.pi)
    square = v * v
    t = jnp.tanh(k * v * (1.0 + 0.044715 * square))
    return 0.5 * (1.0 + t) + (0.5 * k) * v * (1.0 - t * t) * (1.0 + 3 * 0.044715 * square)


SMALL = 16


def backward_kernel(
    n_dp, inv_ref, vec_ref, sums_ref, dres_in, hid_in, pre_in, unit_in, nlow_in, low_in, feat_in, qkvt_in, ctxt_in,
    probs_in, rx_in, ry_in, w1_in, w2_in, wo_in, wqkv_in, block_in,
    block_all, in_all, red1, red2, red3, lay_all, small_out,
    arena, hidb, preb, dres, unit, nlow, nlow_t, dn, low_rows, qkvb, ctxtb, dctx, lowb, featb, wob, rxb, ryb, hot, acc,
    part1, part2, part3, core1, core2, core3, first1, first2, first3, second1, second2, second3,
    quarters1, quarters2, quarters3, final1, final2, final3, extra1, extra2, extra3, acc3, small, small_in, short,
    load_sem, send, recv, here, share_send, share_recv, small_send, small_recv, p_sem,
):
    t, d = lax.axis_index("tensor"), lax.axis_index("dp")
    mate, across = {"tensor": xor_index(t, 1)}, {"tensor": xor_index(t, 2)}
    beside = {"dp": xor_index(d, 1)}
    along = [None] + [{"dp": d + 2 * (xor_level((d // 2) % 4, k) - (d // 2) % 4)} for k in range(1, 4)]
    further = [{"dp": xor_index(d, bit)} for bit in bits_of(n_dp) if bit >= 8]
    peers = (mate, across, beside, along, further, d % 2, (d // 2) % 4)
    sems = (send, recv, here)
    f32, bf16 = jnp.float32, jnp.bfloat16
    win, model = dres.shape
    heads = 4 * HEADS_T
    cols_t = HEADS_T * HD
    hid_t = model
    block = 128

    def load(k, src, dst):
        return pltpu.make_async_copy(src, dst, load_sem.at[k])

    def w_rows(r):
        return pl.ds(r * hid_t, hid_t)

    def h_rows(r):
        return pl.ds(r * win, win)

    order = (3, 1, 2, 0)
    ld_dres = load(0, dres_in, dres)
    ld_hid = {r: load(1 + r, hid_in.at[r], hidb.at[h_rows(r)]) for r in order}
    ld_w2 = {r: load(5 + r, w2_in.at[r], arena.at[w_rows(r)]) for r in order}
    ld_w1 = {r: load(9 + r, w1_in.at[r], arena.at[w_rows(4 + r)]) for r in order}
    ld_pre = {r: load(13 + r, pre_in.at[r], preb.at[i % 2]) for i, r in enumerate(order)}
    ld_rest = [
        load(17 + k, src, dst)
        for k, (src, dst) in enumerate(
            [
                (nlow_in, nlow), (unit_in, unit), (ctxt_in, ctxtb), (wo_in, wob), (qkvt_in, qkvb), (low_in, lowb),
                (feat_in, featb), (rx_in, rxb), (ry_in, ryb),
            ]
        )
    ]
    ld_wqkv = [load(26 + n, wqkv_in.at[n], hidb.at[pl.ds(n * model, model)]) for n in range(3)]
    ld_dres.start()
    for r in order:
        ld_hid[r].start()
    for r in order[:2]:
        ld_pre[r].start()
    for r in order:
        ld_w2[r].start()
    ld_rest[0].start()
    for r in order:
        ld_w1[r].start()
    for c in ld_rest[1:]:
        c.start()

    def chunks(slot, sizes, orders, parts, core, first, second, quarters, final, extra, result, acc=None):
        out, at = [], 0
        for k, (rows, x_first, part) in enumerate(zip(sizes, orders, parts)):
            q = pl.ds(at // 8, rows // 8)
            out.append(
                Reduce(
                    slot + k, rows, x_first, part, core.at[:, pl.ds(at, rows)], first.at[pl.ds(at, rows)],
                    second.at[pl.ds(at // 2, rows // 2)], quarters.at[:, q], final.at[q], extra.at[:, q],
                    result.at[pl.ds(at, rows)], None if acc is None else acc.at[pl.ds(at, rows)], sems, peers,
                )
            )
            at += rows
        return out

    third = hid_t // 3
    sizes = [third] * 3

    def thirds(ref):
        return [lambda p, k=k: ref.at[p, pl.ds(k * third, third)] for k in range(3)]

    s2 = chunks(
        0, sizes, ORDERS["A"], thirds(part2), core2, first2, second2, quarters2, final2, extra2, red2
    )
    s1 = chunks(
        3, sizes, ORDERS["B"], thirds(part1), core1, first1, second1, quarters1, final1, extra1, red1
    )
    lay_t = lay_all.shape[0] // 4
    s3 = chunks(
        6, [2 * cols_t, 2 * cols_t, lay_t], ORDERS["C"],
        [
            lambda p: part2.at[p, pl.ds(0, 2 * cols_t)],
            lambda p: part2.at[p, pl.ds(2 * cols_t, 2 * cols_t)],
            lambda p: part3.at[p],
        ],
        core3, first3, second3, quarters3, final3, extra3, red3, acc3,
    )

    def share(k, src, whole, rows, part=0, parts=1):
        def at(index):
            return whole.at[pl.ds(pl.multiple_of((index * parts + part) * rows, rows), rows)]

        def moved(j, from_ref, index, peer):
            return remote(from_ref, at(index), share_send.at[k, j], share_recv.at[k, j], peer)

        far = xor_index(t, 2)
        return {
            "here": pltpu.make_async_copy(src, at(t), share_send.at[k, 3]),
            "across": moved(0, src, t, across),
            "mate": moved(1, src, t, mate),
            "pass": moved(2, at(far), far, mate),
        }

    def share_start(c):
        for name in ("across", "mate", "here"):
            c[name].start()

    def share_pass(c):
        c["across"].wait_recv()
        c["pass"].start()

    def share_end(c):
        c["here"].wait()
        c["mate"].wait_recv()
        c["pass"].wait_recv()
        for name in ("across", "mate", "pass"):
            c[name].wait_send()

    quarter_win = win // 4
    sh_block = [
        share(k, block_in.at[pl.ds(k * quarter_win, quarter_win)], block_all, quarter_win, k, 4) for k in range(4)
    ]
    sh_in = share(4, low_rows, in_all, win)
    sh_lay = share(5, red3.at[pl.ds(4 * cols_t, lay_t)], lay_all, lay_t)
    bits = [mate, across, beside, along[1], along[2]] + further

    def small_move(k):
        return remote(small.at[k], small_in.at[k], small_send.at[k], small_recv.at[k], bits[k])

    def small_step(k):
        small_move(k).wait()
        small[k + 1] = small[k] + small_in[k]
        if k + 1 < len(bits):
            small_move(k + 1).start()

    named = {f"A{k}": g for k, g in enumerate(s2)}
    named.update({f"B{k}": g for k, g in enumerate(s1)})
    named.update({f"C{k}": g for k, g in zip("abc", s3)})

    def run(event):
        if event[:2] in named:
            named[event[:2]].next(int(event[3:]))
        elif event[:7] == "blkpass":
            share_pass(sh_block[int(event[7:])])
        elif event[:3] == "blk":
            share_start(sh_block[int(event[3:])])
        elif event == "igpass":
            share_pass(sh_in)
        elif event == "lay":
            share_start(sh_lay)
        elif event == "laypass":
            share_pass(sh_lay)
        elif event[:2] == "sm":
            small_step(int(event[2:]))

    def at_slot(name, index=None):
        if index is None:
            for event in SCHEDULE.get(name, ()):
                run(event)
            return
        for key, todo in SCHEDULE.items():
            if key.startswith(name) and key[len(name) :].isdigit():
                @pl.when(index == int(key[len(name) :]))
                def _(todo=todo):
                    for event in todo:
                        run(event)

    signal_peers([mate, across, beside] + along[1:] + further)
    at_slot("start")

    small[0] = jnp.zeros_like(small[0])
    small[0, 3:4, :] = sums_ref[2:3, :]
    small[0, 4:6, :] = sums_ref[0:2, :]
    small[0, 6:7, :] = sums_ref[3:4, :]

    def own_row(base, r):
        index = t
        for bit in (1, 2):
            if r & bit:
                index = xor_index(index, bit)
        return pl.ds(base + index, 1)

    ld_dres.wait()

    @pl.loop(0, win // block)
    def _(i):
        sl = pl.ds(pl.multiple_of(i * block, block), block)
        low_rows[sl, :] = dres[sl, :].astype(bf16)

    def grad_w2(r, c):
        sl = pl.ds(pl.multiple_of(c * third, third), third)
        return tn(hidb[h_rows(r), sl], low_rows[...])

    def grad_w1(r, c):
        sl = pl.ds(pl.multiple_of(c * third, third), third)
        return nn(nlow_t[sl, :], hidb[h_rows(r), :])

    def for_mate(group, grad, r, part):
        @pl.loop(0, 3)
        def _(c):
            part[r // 2, pl.ds(pl.multiple_of(c * third, third), third), :] = grad(r, c).astype(bf16)

        for g in group:
            g.go(0, r // 2)

    def for_own(group, grad, r):
        for c, g in enumerate(group):
            g.from_mate(r // 2)
            g.merge(r // 2, pl.ds(0, third), grad(r, c))
            g.go(1, r // 2)

    for r in order[:2]:
        ld_hid[r].wait()
        for_mate(s2, grad_w2, r, part2)

    ld_rest[0].wait()
    nlow_t[...] = nlow[...].astype(f32).T.astype(bf16)
    for j, r in enumerate(order):
        ld_pre[r].wait()
        ld_w2[r].wait()
        ld_w1[r].wait()

        @pl.loop(0, 2)
        def _(i, j=j, r=r):
            count = win // 2
            sl = pl.ds(pl.multiple_of(i * count, count), count)
            hs = pl.ds(pl.multiple_of(r * win + i * count, count), count)
            dhid = nt(low_rows[sl, :], arena[w_rows(r), :])
            dpre = (dhid * gelu_slope(preb[j % 2, sl, :])).astype(bf16)
            hidb[hs, :] = dpre
            row = own_row(8, r)
            small[0, row, :] += jnp.sum(dpre.astype(f32), axis=0, keepdims=True)
            more = nt(dpre, arena[w_rows(4 + r), :])
            dn[sl, :] = more if j == 0 else dn[sl, :] + more
            at_slot(f"ffn{j}.", i)

        if j + 2 < 4:
            ld_pre[order[j + 2]].start()
        if j < 2:
            for_mate(s1, grad_w1, r, part1)
        else:
            for_own(s1, grad_w1, r)
        if j == 0:
            for q in order[2:]:
                ld_hid[q].wait()
                for_own(s2, grad_w2, q)
        at_slot(f"ffn{j}.g")

    for c in ld_wqkv:
        c.start()

    def p_load(h, slot):
        return pltpu.make_async_copy(probs_in.at[h], preb.at[slot, :, pl.ds(0, win)], p_sem.at[slot])

    for h in range(2):
        p_load(h, h).start()
    for g in s2:
        g.sent(0)

    ld_rest[1].wait()

    @pl.loop(0, win // block)
    def _(i):
        sl = pl.ds(pl.multiple_of(i * block, block), block)
        up = dres[sl, :] + dn[sl, :]
        units = unit[sl, :]
        scaled = up * vec_ref[1:2, :]
        mean_one = jnp.mean(scaled, axis=1, keepdims=True)
        mean_two = jnp.mean(scaled * units, axis=1, keepdims=True)
        value = (scaled - mean_one - units * mean_two) * inv_ref[sl, :]
        dn[sl, :] = value
        low_rows[sl, :] = value.astype(bf16)
        small[0, 0:1, :] += jnp.sum(value, axis=0, keepdims=True)
        small[0, 1:2, :] += jnp.sum(up * units, axis=0, keepdims=True)
        small[0, 2:3, :] += jnp.sum(up, axis=0, keepdims=True)

    at_slot("ln")
    for c in ld_rest[2:]:
        c.wait()

    @pl.loop(0, 4)
    def _(r):
        sl = pl.ds(pl.multiple_of(r * cols_t, cols_t), cols_t)
        dctx[sl, :] = nt(wob[sl, :], low_rows[...]).astype(bf16)

    at_slot("ow")

    @pl.loop(0, heads)
    def _(h):
        slot = h % 2
        sl = pl.ds(pl.multiple_of(h * HD, HD), HD)
        dc_t = dctx[sl, :]
        dc = dc_t.astype(f32).T.astype(bf16)
        p_load(h, slot).wait()
        p = preb[slot, :, 0:win]
        dp = nn(dc, qkvb[2, sl, :])
        row_dot = jnp.sum(p * dp, axis=1, keepdims=True)
        ds = (p * (dp - row_dot)).astype(bf16)
        qkvb[2, sl, :] = nn(dc_t, p.astype(bf16)).astype(bf16)
        dq = nt(qkvb[1, sl, :], ds) * HD ** (-0.5)
        dk = nn(qkvb[0, sl, :], ds) * HD ** (-0.5)
        qkvb[0, sl, :] = dq.astype(bf16)
        qkvb[1, sl, :] = dk.astype(bf16)
        arena[pl.ds(pl.multiple_of(h * win, win), win), 0:win] = ds

        @pl.when(h + 2 < heads)
        def _():
            p_load(h + 2, slot).start()

        at_slot("h", h)

    for c in ld_wqkv:
        c.wait()
    def rows_of(r):
        return pl.ds(r * cols_t, cols_t)

    def grad_out(r):
        return nn(ctxtb[rows_of(r), :], low_rows[...])

    def grad_proj(n, r):
        return nn(qkvb[n, rows_of(r), :], lowb[...])

    halves = (
        (s3[0], lambda r: grad_proj(2, r), grad_out),
        (s3[1], lambda r: grad_proj(0, r), lambda r: grad_proj(1, r)),
    )
    for k, (g, upper, lower) in enumerate(halves):
        for r in (3, 1):
            at = 2 * cols_t * k
            part2[r // 2, at : at + cols_t, :] = upper(r).astype(bf16)
            part2[r // 2, at + cols_t : at + 2 * cols_t, :] = lower(r).astype(bf16)
            g.go(0, r // 2)
    at_slot("pq")
    for g, upper, lower in halves:
        for r in (2, 0):
            g.from_mate(r // 2)
            g.merge(r // 2, pl.ds(0, cols_t), upper(r))
            g.merge(r // 2, pl.ds(cols_t, cols_t), lower(r))
            g.go(1, r // 2)
    at_slot("pk")

    @pl.loop(0, win // block)
    def _(i):
        sl = pl.ds(pl.multiple_of(i * block, block), block)
        value = dn[sl, :]
        for n in range(3):
            value = value + tn(qkvb[n, :, sl], hidb[pl.ds(n * model, model), :])
        dn[sl, :] = value
        at_slot("dl", i)

    low_rows[...] = dn[...].astype(bf16)

    def grad_lay(r):
        index = t
        for bit in (1, 2):
            if r & bit:
                index = xor_index(index, bit)
        return tn(featb[:, pl.ds(pl.multiple_of(index * lay_t, lay_t), lay_t)], low_rows[...])

    for r in (3, 1):
        part3[r // 2] = grad_lay(r).astype(bf16)
        s3[2].go(0, r // 2)
    at_slot("la")
    for r in (2, 0):
        s3[2].from_mate(r // 2)
        s3[2].merge(r // 2, pl.ds(0, lay_t), grad_lay(r))
        s3[2].go(1, r // 2)
    share_start(sh_in)

    ones = jnp.ones((8, win), bf16)
    short[...] = jnp.zeros_like(short)
    for n, at in ((0, 0), (2, cols_t)):
        total = nt(ones, qkvb[n])
        for r in range(4):
            short[r : r + 1, at : at + cols_t] = total[0:1, r * cols_t : (r + 1) * cols_t]

    acc[...] = jnp.zeros_like(acc)
    one, zero = bf16(1), bf16(0)
    hots = BUCKETS * ROWS
    @pl.loop(0, win // ROWS // 2)
    def _(i):
        total = None
        for u in range(2):
            at = pl.multiple_of(i * 2 * ROWS + u * ROWS, ROWS)
            x = rxb[pl.ds(at, ROWS), :].astype(f32).astype(bf16)
            y = ryb[pl.ds(at, ROWS), :].astype(f32).astype(bf16)
            for b in range(BUCKETS):
                hot[u, b * ROWS : (b + 1) * ROWS, :] = jnp.where(x == bf16(b), one, zero)
                hot[u, hots + b * ROWS : hots + (b + 1) * ROWS, :] = jnp.where(y == bf16(b), one, zero)
            left = jnp.concatenate(
                [arena[pl.ds(pl.multiple_of(h * win + at, ROWS), ROWS), 0:win] for h in range(heads)], axis=0
            )
            more = nt(left, hot[u])
            total = more if total is None else total + more
        acc[...] += total
        at_slot("t", i)

    row = lax.broadcasted_iota(jnp.int32, (ROWS, 2 * hots), 0)
    col = lax.broadcasted_iota(jnp.int32, (ROWS, 2 * hots), 1) % ROWS
    picked = jnp.concatenate(
        [
            jnp.sum(jnp.where(row == col, acc[h * ROWS : (h + 1) * ROWS, :], 0.0), axis=0, keepdims=True)
            for h in range(heads)
        ]
        + [jnp.zeros((16 - heads, 2 * hots), f32)],
        axis=0,
    )
    fold = (
        lax.broadcasted_iota(jnp.int32, (2 * hots, 128), 0) // ROWS
        == lax.broadcasted_iota(jnp.int32, (2 * hots, 128), 1)
    ).astype(f32)
    table = jnp.dot(picked, fold, preferred_element_type=f32, precision=lax.Precision.HIGHEST)
    for r in range(4):
        for a in range(HEADS_T):
            lane = 2 * cols_t + a * 2 * BUCKETS
            short[r : r + 1, lane : lane + 2 * BUCKETS] = table[
                r * HEADS_T + a : r * HEADS_T + a + 1, 0 : 2 * BUCKETS
            ]
    for r in range(4):
        small[0, own_row(12, r), :] = short[r : r + 1, :]

    small_move(0).start()
    at_slot("tail")
    for k in range(5, len(bits)):
        small_step(k)
    small_out[...] = small[len(bits)]
    for c in sh_block + [sh_in, sh_lay]:
        share_end(c)
    for g in s1 + s3:
        g.sent(0)
    for g in s2 + s1 + s3:
        for stage in range(1, 6):
            g.sent(stage)


def backward_window(n_dp, lay_rows, inv, vec, sums, dres, hid, pre, unit, nlow, low, feat, qkvt, ctxt, probs, rx, ry, w1, w2, wo, wqkv, block_own):
    win, model = dres.shape
    heads = 4 * HEADS_T
    cols_t = HEADS_T * HD
    lay_t = lay_rows // 4
    rest = 4 * cols_t + lay_t
    more = max(0, len(bits_of(n_dp)) - 3)
    levels = 5 + more
    f32, bf16 = jnp.float32, jnp.bfloat16
    shape = jax.ShapeDtypeStruct
    here = pl.BlockSpec(memory_space=pltpu.VMEM)
    away = pl.BlockSpec(memory_space=pl.ANY)
    outs = [
        (shape((4 * win, model), bf16), away),
        (shape((4 * win, model), bf16), away),
        (shape((model, model), bf16), away),
        (shape((model, model), bf16), away),
        (shape((rest, model), bf16), away),
        (shape((lay_rows, model), bf16), away),
        (shape((SMALL, model), f32), here),
    ]
    V = pltpu.VMEM
    S = pltpu.SemaphoreType.DMA
    return pl.pallas_call(
        functools.partial(backward_kernel, n_dp),
        in_specs=[here] * 3 + [away] * 17,
        out_specs=[spec for _, spec in outs],
        out_shape=[s for s, _ in outs],
        scratch_shapes=[
            V((8 * model, model), bf16), V((3 * model, model), bf16), V((2, win, model), f32), V((win, model), f32),
            V((win, model), f32), V((win, model), bf16), V((model, win), bf16), V((win, model), f32),
            V((win, model), bf16), V((3, model, win), bf16), V((model, win), bf16), V((model, win), bf16),
            V((win, model), bf16), V((win, lay_rows), bf16), V((model, model), bf16), V((win, win), jnp.int32),
            V((win, win), jnp.int32), V((2, 2 * BUCKETS * ROWS, win), bf16), V((heads * ROWS, 2 * BUCKETS * ROWS), f32),
            V((2, model, model), bf16), V((2, model, model), bf16), V((2, lay_t, model), bf16),
            V((2, model, model), bf16), V((2, model, model), bf16), V((2, rest, model), bf16),
            V((model, model), bf16), V((model, model), bf16), V((rest, model), bf16),
            V((model // 2, model), bf16), V((model // 2, model), bf16), V((rest // 2, model), bf16),
            V((3, model // 8, model), bf16), V((3, model // 8, model), bf16), V((3, rest // 8, model), bf16),
            V((model // 8, model), bf16), V((model // 8, model), bf16), V((rest // 8, model), bf16),
            V((2 * more + 1, model // 8, model), bf16), V((2 * more + 1, model // 8, model), bf16),
            V((2 * more + 1, rest // 8, model), bf16),
            V((rest, model), f32), V((levels + 1, SMALL, model), f32), V((levels, SMALL, model), f32), V((8, model), f32),
            S((29,)), S((9, 12 + max(1, more))), S((9, 12 + max(1, more))), S((9,)), S((6, 4)), S((6, 3)),
            S((levels,)), S((levels,)), S((2,)),
        ],
        compiler_params=pltpu.CompilerParams(
            vmem_limit_bytes=63 * 2**20, collective_id=1, has_side_effects=True
        ),
        name="backward_window",
    )(inv, vec, sums, dres, hid, pre, unit, nlow, low, feat, qkvt, ctxt, probs, rx, ry, w1, w2, wo, wqkv, block_own)


def local(
    n_dp, n_t,
    tokens_in, box_coords, rel_x, rel_y, mask_tokens, cotangent, layout_weight, qkv_weight, qv_bias,
    bias_table, out_weight, out_bias, ln1_gain, ln1_bias, ffn_in_weight, ffn_in_bias, ffn_out_weight,
    ffn_out_bias, ln2_gain, ln2_bias, group_rates,
):
    me = lax.axis_index("tensor")
    win = rel_x.shape[1]
    model = tokens_in.shape[1]
    heads_t = bias_table.shape[1]
    cols_t = heads_t * HD
    hid_t = ffn_in_weight.shape[1]
    tok_rows = tokens_in.shape[0] // n_t

    def mine(whole):
        return lax.dynamic_slice_in_dim(whole, me * (whole.shape[0] // n_t), whole.shape[0] // n_t)

    zeros = jnp.zeros((cols_t,), jnp.float32)
    cols_own = jnp.pad(jnp.stack([qv_bias[0], zeros, qv_bias[1]], axis=1), ((0, 0), (0, 125)))
    rows_own = jnp.concatenate(
        [
            ffn_in_bias[None, :],
            jnp.pad(bias_table.T.astype(jnp.float32), ((0, 0), (0, hid_t - 2 * BUCKETS))),
            jnp.zeros((8 - 1 - heads_t, hid_t), jnp.float32),
        ],
        axis=0,
    )
    freq_index = jnp.arange(LFREQ).astype(jnp.float32)
    freq = jnp.exp(freq_index * (-math.log(1000.0) / LFREQ))
    freq = jnp.broadcast_to(jnp.concatenate([freq, freq])[None, :], (8, 2 * LFREQ))
    zero = jnp.zeros_like(out_bias)
    vec = jnp.stack([out_bias, ln1_gain, ln1_bias, ffn_out_bias, ln2_gain, ln2_bias, zero, zero])
    relx, rely = mine(rel_x)[0], mine(rel_y)[0]

    (
        probs, qkvt, context_t, layer_low, features, unit_one, inverse_one, normed_low, pre_all, hid_all,
        block_own, dresid_two, sums, wqkv, wo, w1, w2,
    ) = forward_window(
        n_dp, mine(tokens_in), mine(box_coords), relx, rely, mine(mask_tokens)[:, None], mine(cotangent), freq,
        layout_weight, vec, cols_own, rows_own, jnp.transpose(qkv_weight, (0, 2, 1)), out_weight, ffn_in_weight, ffn_out_weight,
    )
    block_out, in_all, sum1, sum2, sum3, lay_all, small = backward_window(
        n_dp, layout_weight.shape[0], inverse_one, vec, sums, dresid_two, hid_all, pre_all, unit_one, normed_low, layer_low,
        features, qkvt, context_t, probs, relx, rely, w1, w2, wo, wqkv, block_own,
    )
    f32 = jnp.float32
    count = small[6, 0]
    factor = group_rates / count
    own = lax.dynamic_slice_in_dim(small, 12 + me, 1)[0]
    qkv_sum = jnp.stack([sum3[2 * cols_t : 3 * cols_t], sum3[3 * cols_t : 4 * cols_t], sum3[:cols_t]])
    return (
        block_out,
        in_all.astype(f32) / count,
        lay_all.astype(f32) * factor[6],
        jnp.transpose(qkv_sum, (0, 2, 1)).astype(f32) * factor[0],
        own[: 2 * cols_t].reshape(2, cols_t) * factor[0],
        own[2 * cols_t : 3 * cols_t].reshape(heads_t, 2 * BUCKETS).T * factor[7],
        sum3[cols_t : 2 * cols_t].astype(f32) * factor[1],
        small[0] * factor[1],
        small[1] * factor[2],
        small[2] * factor[2],
        sum1.astype(f32) * factor[3],
        lax.dynamic_slice_in_dim(small, 8 + me, 1)[0] * factor[3],
        sum2.astype(f32) * factor[4],
        small[3] * factor[4],
        small[4] * factor[5],
        small[5] * factor[5],
    )


def solution(mesh):
    placed = (
        P("dp", None), P("dp", None), P("dp", None, None), P("dp", None, None), P("dp"), P("dp", None),
        P(), P(None, None, "tensor"), P(None, "tensor"), P(None, "tensor"), P("tensor", None),
        P(), P(), P(), P(None, "tensor"), P("tensor"), P("tensor", None), P(), P(), P(), P(),
    )
    return jax.shard_map(
        functools.partial(local, mesh.shape["dp"], mesh.shape["tensor"]),
        mesh=mesh,
        in_specs=placed,
        out_specs=(
            P("dp", None), P("dp", None), P(), P(None, None, "tensor"), P(None, "tensor"),
            P(None, "tensor"), P("tensor", None), P(), P(), P(), P(None, "tensor"), P("tensor"),
            P("tensor", None), P(), P(), P(),
        ),
        check_vma=False,
    )
```

```python
import functools
import math

import jax
import jax.numpy as jnp
from jax import lax
from jax.experimental import pallas as pl
from jax.experimental.pallas import tpu as pltpu
from jax.sharding import PartitionSpec as P

HD = 64
LFREQ = 64
BUCKETS = 32
EPSILON = 1e-05
ROWS = 16
HEADS_T = 3
MESH = pl.DeviceIdType.MESH

F_FEAT, F_NEAR, F_HEAD, F_FAR, F_BOTH, F_OUT, F_CONTEXT, F_NORM, F_UP, F_THIRD, F_DONE = range(11)
AT_R, AT_Q, AT_K, AT_V, AT_O, U0, D0, U1, D1, U2, D2 = range(11)
WAYS = {
    AT_R: (1, 0),
    AT_Q: (2, 1),
    AT_K: (2, 1),
    AT_V: (2, 0),
    AT_O: (2, 1),
    U0: (4, 0),
    D0: (4, 0),
    U1: (4, 0),
    D1: (4, 0),
    U2: (2, 1),
    D2: (1, 0),
}
SEND_ORDER = (AT_Q, AT_K, AT_V, AT_O, AT_R, D1, D0, U0, U1, U2, D2)
FORWARD = {
    (F_NEAR, 0): ((AT_Q, 0),),
    (F_HEAD, 2): ((AT_K, 0), (AT_V, 0), (AT_Q, 1),),
    (F_HEAD, 4): ((AT_O, 0), (AT_K, 1), (AT_R, 0), (AT_V, 1),),
    (F_HEAD, 5): ((D1, 0),),
    (F_BOTH, 0): ((D0, 0),),
    (F_HEAD, 6): ((D1, 1),),
    (F_HEAD, 7): ((U0, 0),),
    (F_HEAD, 8): ((U1, 0), (D0, 1), (D1, 2),),
    (F_HEAD, 9): ((AT_O, 1),),
    (F_HEAD, 10): ((U0, 1),),
    (F_HEAD, 11): ((U1, 1),),
    (F_CONTEXT, 0): ((U2, 0), (D0, 2),),
    (F_NORM, 1): ((U0, 2),),
    (F_NORM, 3): ((U1, 2),),
    (F_UP, 2): ((D2, 0), (U2, 1),),
}

START, FFN, NORM, OUT, HEAD, SENT, MERGED, DLAYER, LAYOUT, TABLE, TAIL = range(11)
A0, A1, A2, B0, B1, B2, CA, CB, CC, BLOCK, BLOCK_ON, INPUT_ON, LAY, LAY_ON, SMALL_STEP = range(15)
X_FIRST = (False, True, True, True, False, True, True, False, True)
SCHEDULE = {
    (START, 0): ((BLOCK, 2),),
    (FFN, 2): ((BLOCK_ON, 2),),
    (FFN, 8): ((A0, 1),),
    (FFN, 9): ((A1, 1),),
    (OUT, 0): ((A1, 2),),
    (HEAD, 1): ((A2, 1),),
    (HEAD, 2): ((B1, 1),),
    (HEAD, 4): ((A1, 3), (B0, 1), (A2, 2),),
    (HEAD, 8): ((A1, 4),),
    (HEAD, 10): ((B0, 2), (A2, 3), (B2, 1),),
    (SENT, 0): ((A0, 2), (B2, 2),),
    (MERGED, 0): ((B1, 2),),
    (DLAYER, 2): ((A0, 3),),
    (TABLE, 2): ((CA, 1), (A2, 4), (B1, 3),),
    (TABLE, 3): ((CB, 1),),
    (TABLE, 4): ((B2, 3), (A0, 4),),
    (TABLE, 5): ((BLOCK, 0), (BLOCK, 1), (BLOCK, 3),),
    (TABLE, 6): ((CA, 2), (CC, 1), (B1, 4),),
    (TABLE, 8): ((B0, 3),),
    (TABLE, 11): ((B2, 4),),
    (TAIL, 0): (
        (A1, 5), (A0, 5), (A2, 5), (CA, 3), (CC, 2), (SMALL_STEP, 0), (INPUT_ON, 0), (B0, 4), (B1, 5), (CB, 2),
        (B2, 5), (CA, 4), (CC, 3), (BLOCK_ON, 0), (B0, 5), (BLOCK_ON, 1), (CB, 3), (CA, 5), (CC, 4), (BLOCK_ON, 3),
        (SMALL_STEP, 1), (CC, 5), (LAY, 0), (SMALL_STEP, 2), (CB, 4), (SMALL_STEP, 3), (LAY_ON, 0), (SMALL_STEP, 4),
        (CB, 5),
    ),
}


def nt(a, b):
    return lax.dot_general(a, b, (((1,), (1,)), ((), ())), preferred_element_type=jnp.float32)


def nn(a, b):
    return jnp.dot(a, b, preferred_element_type=jnp.float32)


def xor_index(index, bit):
    return index + bit - 2 * bit * ((index // bit) % 2)


def signal_peers(peers):
    barrier = pltpu.get_barrier_semaphore()
    for peer in peers:
        pl.semaphore_signal(barrier, inc=1, device_id=peer, device_id_type=MESH)


def wait_peers(peers):
    pl.semaphore_wait(pltpu.get_barrier_semaphore(), len(peers))


def remote(src, dst, send, recv, peer):
    return pltpu.make_async_remote_copy(
        src_ref=src, dst_ref=dst, send_sem=send, recv_sem=recv, device_id=peer, device_id_type=MESH
    )


HERE, MATE, ACROSS, PASS, BESIDE, PASS_BESIDE, ALONG, PASS_ALONG, LAST_BESIDE, LAST_ALONG, PASS_LAST = range(11)


class Gather:
    def __init__(self, own, place, rows, kind, bit, sems, slot, peers):
        self.own, self.place, self.rows, self.kind, self.bit = own, place, rows, kind, bit
        self.send, self.recv, self.here = sems
        self.slot = slot
        self.mate, self.across, self.near, self.sides = peers

    def part(self, flip_zero, flip_one):
        if self.kind == 1:
            return pl.ds(0, self.rows)
        if self.kind == 2:
            side = self.sides[self.bit]
            side = 1 - side if flip_zero else side
            return pl.ds(pl.multiple_of(side * (self.rows // 2), 16), self.rows // 2)
        zero = 1 - self.sides[0] if flip_zero else self.sides[0]
        one = 1 - self.sides[1] if flip_one else self.sides[1]
        return pl.ds(pl.multiple_of((zero + 2 * one) * (self.rows // 4), 16), self.rows // 4)

    def halved(self, part, second):
        h = part.size // 2
        return pl.ds(pl.multiple_of(part.start + (h if second else 0), 16), h)

    def copy(self, name):
        s = self.slot
        whole = pl.ds(0, self.rows)
        mine = self.part(False, False)
        if name == HERE:
            return pltpu.make_async_copy(self.own(whole), self.place(0, whole), self.here.at[s])

        def pass_on(rows, k):
            return self.place(2, rows), self.place(3, rows), self.mate, k

        def relay(rows, to, k):
            return self.place(2, rows), self.place(2, rows), self.near[to], k

        src, dst, peer, k = {
            MATE: lambda: (self.own(whole), self.place(1, whole), self.mate, 0),
            ACROSS: lambda: (self.own(mine), self.place(2, mine), self.across, 1),
            PASS: lambda: pass_on(mine, 2),
            BESIDE: lambda: relay(mine, self.bit, 3),
            PASS_BESIDE: lambda: pass_on(self.part(True, False), 4),
            ALONG: lambda: relay(mine, 1, 5),
            PASS_ALONG: lambda: pass_on(self.part(False, True), 6),
            LAST_BESIDE: lambda: relay(self.halved(self.part(False, True), False), 0, 7),
            LAST_ALONG: lambda: relay(self.halved(self.part(True, False), True), 1, 8),
            PASS_LAST: lambda: pass_on(self.part(True, True), 9),
        }[name]()
        return remote(src, dst, self.send.at[s, k], self.recv.at[s, k], peer)

    def names(self, stage):
        return {
            1: (((PASS,), (ACROSS,)),),
            2: (((BESIDE, PASS), (ACROSS,)), ((PASS_BESIDE,), (BESIDE,))),
            4: (
                ((BESIDE, ALONG, PASS), (ACROSS,)),
                ((LAST_BESIDE, LAST_ALONG, PASS_BESIDE, PASS_ALONG), (BESIDE, ALONG)),
                ((PASS_LAST,), (LAST_BESIDE, LAST_ALONG)),
            ),
        }[self.kind][stage]

    def stages(self):
        return {1: 1, 2: 2, 4: 3}[self.kind]

    def start(self):
        self.copy(ACROSS).start()
        self.copy(MATE).start()
        self.copy(HERE).start()

    def forward(self, stage):
        starts, waits = self.names(stage)
        for name in waits:
            self.copy(name).wait_recv()
        for name in starts:
            self.copy(name).start()

    def arrive_near(self):
        self.copy(HERE).wait()
        self.copy(MATE).wait_recv()

    def arrive_far(self):
        for stage in range(self.stages()):
            for name in self.names(stage)[0]:
                if name in (PASS, PASS_BESIDE, PASS_ALONG, PASS_LAST):
                    self.copy(name).wait_recv()

    def finish(self):
        for name in (MATE, ACROSS) + sum((self.names(stage)[0] for stage in range(self.stages())), ()):
            self.copy(name).wait_send()


def waves(column, frequency, quarter):
    angle = column * frequency
    turns = jnp.floor(angle * (2.0 / math.pi) + 0.5)
    rest = ((angle - turns * 1.5703125) - turns * 4.837512969970703125e-4) - turns * 7.549789948768648e-8
    quadrant = turns.astype(jnp.int32) + quarter
    z = rest * rest
    sine = ((-1.9515295891e-4 * z + 8.3321608736e-3) * z - 1.6666654611e-1) * z * rest + rest
    cosine = ((2.443315711809948e-5 * z - 1.388731625493765e-3) * z + 4.166664568298827e-2) * z * z - 0.5 * z + 1.0
    value = jnp.where(quadrant % 2 == 1, cosine, sine)
    return jnp.where((quadrant // 2) % 2 == 1, -value, value)


def gelu(v):
    return 0.5 * v * (1.0 + jnp.tanh(math.sqrt(2.0 / math.pi) * (v + 0.044715 * (v * v * v))))


def row_of(ref):
    return ref[...].reshape(1, ref.shape[0])


def column_of(row):
    return jnp.broadcast_to(row, (8, 128)).T[:, 0:1]


def forward_kernel(
    box_ref, mask_ref, lay_ref, qvb_ref, b1_ref, table_ref, ob_ref, g1_ref, s1_ref, c2_ref, g2_ref, s2_ref,
    tok_in, cot_in, rx_in, ry_in, qkv_own, wo_own, w1_own, w2_own,
    probs_out, qkvt_out, ctxt_out, low_out, feat_out, unit_out, inv_out, nlow_out, pre_out, hid_out,
    block_out, dres_out, sums_out, wqkv_out, wo_out, w1_out, w2_out,
    tokb, cotb, rxb, ryb, vec, rows_own, wqkv, wo, w1, w2, rows, cols, tabs, layer_in, qkvt, pbuf, ctxt, ctx, normed, pre,
    hid, acc, send, recv, here, out_sem, p_sem, in_sem,
):
    t, d = lax.axis_index("tensor"), lax.axis_index("dp")
    mate, across = {"tensor": xor_index(t, 1)}, {"tensor": xor_index(t, 2)}
    near = [{"dp": xor_index(d, 1)}, {"dp": xor_index(d, 2)}]
    peers = (mate, across, near, (d % 2, (d // 2) % 2))
    win, model = tokb.shape
    heads = 4 * HEADS_T
    cols_t = HEADS_T * HD
    hid_t = w1_own.shape[1]
    sems = (send, recv, here)
    f32, bf16 = jnp.float32, jnp.bfloat16
    block = 128

    everyone = [mate, across] + near
    signal_peers(everyone)
    own_rows = pl.ds(pl.multiple_of(t * win, win), win)
    loads = [
        pltpu.make_async_copy(src, dst, in_sem.at[k])
        for k, (src, dst) in enumerate(
            [(tok_in.at[own_rows], tokb), (rx_in.at[t], rxb), (ry_in.at[t], ryb), (cot_in.at[own_rows], cotb)]
        )
    ]
    for c in loads:
        c.start()
    for k, ref in enumerate((ob_ref, g1_ref, s1_ref, c2_ref, g2_ref, s2_ref)):
        vec[k : k + 1, :] = row_of(ref)
    rows_own[...] = jnp.zeros_like(rows_own)
    rows_own[0:1, :] = row_of(b1_ref)
    rows_own[1 : 1 + HEADS_T, 0 : 2 * BUCKETS] = table_ref[...].astype(f32)
    rows_own[4:6, 0:cols_t] = qvb_ref[...]

    def piece_rows(r, s, count):
        return pl.ds(pl.multiple_of(r * count + s.start, 16), s.size)

    gathers = {}

    def chunk(name, own, place, count):
        gathers[name] = Gather(own, place, count, *WAYS[name], sems, name, peers)

    chunk(AT_R, lambda s: rows_own.at[s], lambda r, s: rows.at[r, s], 8)
    for n, name in enumerate((AT_Q, AT_K, AT_V)):
        chunk(
            name,
            lambda s, n=n: qkv_own.at[n, s],
            lambda r, s, n=n: wqkv.at[n, piece_rows(r, s, cols_t)],
            cols_t,
        )
    chunk(AT_O, lambda s: wo_own.at[s], lambda r, s: wo.at[piece_rows(r, s, cols_t)], cols_t)
    third = hid_t // 3
    for k in range(3):
        units = pl.ds(k * third, third)
        chunk(
            U0 + 2 * k, lambda s, units=units: w1_own.at[s, units], lambda r, s, units=units: w1.at[r, s, units], model
        )

        def moved(s, k=k):
            return pl.ds(pl.multiple_of(s.start + k * third, 16), s.size)

        chunk(
            D0 + 2 * k, lambda s, moved=moved: w2_own.at[moved(s)], lambda r, s, moved=moved: w2.at[r, moved(s)], third
        )

    def at_slot(phase, index=0):
        for name, stage in FORWARD.get((phase, index), ()):
            gathers[name].forward(stage)

    def at_loop(phase, index, count, first=0, step=1):
        for k in range(count):
            if (phase, first + step * k) in FORWARD:
                @pl.when(index == k)
                def _(k=k):
                    at_slot(phase, first + step * k)

    def near_pieces(names):
        for name in names:
            gathers[name].arrive_near()

    def far_pieces(names):
        for name in names:
            gathers[name].arrive_far()

    wait_peers(everyone)
    for name in SEND_ORDER:
        gathers[name].start()

    lane = lax.broadcasted_iota(jnp.int32, (1, 128), 1)
    quarter = jnp.where(lane >= LFREQ, 1, 0)
    frequency = jnp.exp((lane % LFREQ).astype(f32) * (-math.log(1000.0) / LFREQ))
    loads[0].wait()

    @pl.loop(0, win // block)
    def _(i):
        sl = pl.ds(pl.multiple_of(i * block, block), block)
        box = box_ref[:, pl.ds(pl.multiple_of(t * win + i * block, block), block)].astype(f32)
        for m in range(4):
            feat_out[sl, 2 * LFREQ * m : 2 * LFREQ * (m + 1)] = waves(
                column_of(box[m : m + 1, :]), frequency, quarter
            ).astype(bf16)
        value = tokb[sl, :].astype(f32) + nn(feat_out[sl, :], lay_ref[...])
        layer_in[sl, :] = value
        low_out[sl, :] = value.astype(bf16)
        at_loop(F_FEAT, i, 4)

    def bias_columns(pieces):
        for r in pieces:
            for n, row in ((0, 4), (2, 5)):
                for c in range(0, cols_t, 64):
                    part = jnp.broadcast_to(rows[r, row : row + 1, 0:256][:, 0:256], (8, 256)).T
                    cols[n, pl.ds(r * cols_t + c, 64), :] = part[c : c + 64, 0:1]
            tabs[HEADS_T * r : HEADS_T * (r + 1), :] = rows[r, 1 : 1 + HEADS_T, 0:128]

    def project(pieces):
        for n in range(3):
            for r in pieces:
                sl = pl.ds(r * cols_t, cols_t)
                value = nt(wqkv[n, sl, :], low_out[...])
                if n != 1:
                    value = value + cols[n, sl, :]
                qkvt[n, sl, :] = value.astype(bf16)

    near_pieces((AT_R, AT_Q, AT_K, AT_V))
    bias_columns((0, 1))
    project((0, 1))
    at_slot(F_NEAR)
    for c in loads[1:3]:
        c.wait()

    def table_row(h):
        return (tabs[pl.ds(h, 1), :] * 2048.0 + 32768.5).astype(jnp.int32) - 32768

    def p_copy(i, slot):
        return pltpu.make_async_copy(pbuf.at[slot], probs_out.at[pl.ds(2 * i, 2)], p_sem.at[slot])

    def two_heads(i):
        slot = i % 2
        sl = pl.ds(pl.multiple_of(i * 2 * HD, 2 * HD), 2 * HD)
        q = (qkvt[0, sl, :].astype(f32).T * HD ** (-0.5)).astype(bf16)
        tab = jnp.broadcast_to((table_row(2 * i) << 16) + table_row(2 * i + 1), (win, 128))
        bias = ([], [])
        for c in range(win // 128):
            at = slice(128 * c, 128 * c + 128)
            word = jnp.take_along_axis(tab, rxb[:, at], axis=1) + jnp.take_along_axis(
                tab, ryb[:, at] + BUCKETS, axis=1
            )
            second = word << 16
            bias[0].append((word - (second >> 16)).astype(f32) * 2.0**-27)
            bias[1].append(second.astype(f32) * 2.0**-27)

        @pl.when(i >= 2)
        def _():
            p_copy(i - 2, slot).wait()

        for u in range(2):
            rows_u = pl.ds(pl.multiple_of(i * 2 * HD + u * HD, HD), HD)
            s = nn(q[:, u * HD : (u + 1) * HD], qkvt[1, rows_u, :]) + jnp.concatenate(bias[u], axis=1)
            m = jnp.max(s, axis=1, keepdims=True)
            e = jnp.exp(s - m)
            p = e * (1.0 / jnp.sum(e, axis=1, keepdims=True))
            pbuf[slot, u] = p
            ctxt[rows_u, :] = nt(qkvt[2, rows_u, :], p.astype(bf16)).astype(bf16)
            at_loop(F_HEAD, i, heads // 2, u, 2)
        p_copy(i, slot).start()

    pl.loop(0, heads // 4)(two_heads)
    at_slot(F_FAR)
    far_pieces((AT_R, AT_Q, AT_K, AT_V))
    bias_columns((2, 3))
    project((2, 3))
    at_slot(F_BOTH)
    pl.loop(heads // 4, heads // 2)(two_heads)

    last = heads // 2
    outs = [
        (qkvt, qkvt_out), (ctxt, ctxt_out), (wqkv, wqkv_out),
    ]
    done = []

    def leave(src, dst):
        c = pltpu.make_async_copy(src, dst, out_sem.at[len(done)])
        c.start()
        done.append(c)

    for src, dst in outs:
        leave(src, dst)
    at_slot(F_OUT)
    near_pieces((AT_O,))
    far_pieces((AT_O,))
    leave(wo, wo_out)
    ctx[...] = ctxt[...].astype(f32).T.astype(bf16)
    at_slot(F_CONTEXT)

    @pl.loop(0, win // block)
    def _(i):
        sl = pl.ds(pl.multiple_of(i * block, block), block)
        value = layer_in[sl, :] + nn(ctx[sl, :], wo[...]) + vec[0:1, :]
        mean = jnp.mean(value, axis=1, keepdims=True)
        centered = value - mean
        inverse = lax.rsqrt(jnp.mean(centered * centered, axis=1, keepdims=True) + EPSILON)
        unit = centered * inverse
        unit_out[sl, :] = unit
        inv_out[sl, :] = inverse
        value = unit * vec[1:2, :] + vec[2:3, :]
        normed[sl, :] = value
        nlow_out[sl, :] = value.astype(bf16)
        at_loop(F_NORM, i, 4)

    near_pieces(range(U0, D2 + 1))
    for src, dst in ((w1, w1_out), (w2, w2_out)):
        leave(src.at[pl.ds(0, 2)], dst.at[pl.ds(0, 2)])
    for r in range(2):
        @pl.loop(0, win // 256)
        def _(i, r=r):
            sl = pl.ds(pl.multiple_of(i * 256, 256), 256)
            value = nn(nlow_out[sl, :], w1[r]) + rows[r, 0:1, :]
            pre[r, sl, :] = value
            low_hid = gelu(value).astype(bf16)
            hid[r, sl, :] = low_hid
            more = nn(low_hid, w2[r])
            acc[sl, :] = more if r == 0 else acc[sl, :] + more
            at_loop(F_UP, i, 2, 2 * r)

        leave(pre.at[r], pre_out.at[r])
        leave(hid.at[r], hid_out.at[r])

    for k in range(3):
        at_slot(F_THIRD, k)
        far_pieces((U0 + 2 * k, D0 + 2 * k))
        units = pl.ds(k * third, third)

        @pl.loop(2, 4)
        def _(r, units=units):
            value = nn(nlow_out[...], w1[r, :, units]) + rows[r, 0:1, units]
            pre[r, :, units] = value
            low_hid = gelu(value).astype(bf16)
            hid[r, :, units] = low_hid
            acc[...] += nn(low_hid, w2[r, units, :])

        at_slot(F_DONE, k)

        for src, dst in ((pre, pre_out), (hid, hid_out)):
            leave(src.at[pl.ds(2, 2), :, units], dst.at[pl.ds(2, 2), :, units])
        leave(w1.at[pl.ds(2, 2), :, units], w1_out.at[pl.ds(2, 2), :, units])
        leave(w2.at[pl.ds(2, 2), units], w2_out.at[pl.ds(2, 2), units])

    loads[3].wait()

    sums_out[...] = jnp.zeros_like(sums_out)

    @pl.loop(0, win // block)
    def _(i):
        sl = pl.ds(pl.multiple_of(i * block, block), block)
        value = normed[sl, :] + acc[sl, :] + vec[3:4, :]
        mean = jnp.mean(value, axis=1, keepdims=True)
        centered = value - mean
        inverse = lax.rsqrt(jnp.mean(centered * centered, axis=1, keepdims=True) + EPSILON)
        unit = centered * inverse
        block_out[sl, :] = (unit * vec[4:5, :] + vec[5:6, :]).astype(bf16)
        mask = column_of(mask_ref[pl.ds((win // block) * t + i, 1), :].astype(f32))
        selected = mask * cotb[sl, :].astype(f32)
        scaled = selected * vec[4:5, :]
        mean_one = jnp.mean(scaled, axis=1, keepdims=True)
        mean_two = jnp.mean(scaled * unit, axis=1, keepdims=True)
        dres = (scaled - mean_one - unit * mean_two) * inverse
        dres_out[sl, :] = dres
        sums_out[0:1, :] += jnp.sum(selected * unit, axis=0, keepdims=True)
        sums_out[1:2, :] += jnp.sum(selected, axis=0, keepdims=True)
        sums_out[2:3, :] += jnp.sum(dres, axis=0, keepdims=True)
        sums_out[3:4, :] += jnp.sum(mask, axis=0, keepdims=True)

    for i in (last - 2, last - 1):
        p_copy(i, i % 2).wait()
    for c in done:
        c.wait()
    for g in gathers.values():
        g.finish()


def forward_window(small, large):
    wo_own, w1_own = large[5:7]
    win, model = large[2].shape[1], large[0].shape[1]
    cols_t, hid_t = wo_own.shape[0], w1_own.shape[1]
    heads = 4 * HEADS_T
    f32, bf16 = jnp.float32, jnp.bfloat16
    shape = jax.ShapeDtypeStruct
    here = pl.BlockSpec(memory_space=pltpu.VMEM)
    away = pl.BlockSpec(memory_space=pl.ANY)
    outs = [
        (shape((heads, win, win), f32), away),
        (shape((3, model, win), bf16), away),
        (shape((model, win), bf16), away),
        (shape((win, model), bf16), here),
        (shape((win, 8 * LFREQ), bf16), here),
        (shape((win, model), f32), here),
        (shape((win, 1), f32), here),
        (shape((win, model), bf16), here),
        (shape((4, win, hid_t), f32), away),
        (shape((4, win, hid_t), bf16), away),
        (shape((win, model), bf16), here),
        (shape((win, model), f32), here),
        (shape((8, model), f32), here),
        (shape((3, model, model), bf16), away),
        (shape((model, model), bf16), away),
        (shape((4, model, hid_t), bf16), away),
        (shape((4, hid_t, model), bf16), away),
    ]
    return pl.pallas_call(
        forward_kernel,
        in_specs=[here] * len(small) + [away] * len(large),
        out_specs=[spec for _, spec in outs],
        out_shape=[s for s, _ in outs],
        scratch_shapes=[
            pltpu.VMEM((win, model), bf16),
            pltpu.VMEM((win, model), bf16),
            pltpu.VMEM((win, win), jnp.int32),
            pltpu.VMEM((win, win), jnp.int32),
            pltpu.VMEM((8, model), f32),
            pltpu.VMEM((8, model), f32),
            pltpu.VMEM((3, model, model), bf16),
            pltpu.VMEM((model, model), bf16),
            pltpu.VMEM((4, model, hid_t), bf16),
            pltpu.VMEM((4, hid_t, model), bf16),
            pltpu.VMEM((4, 8, model), f32),
            pltpu.VMEM((3, model, 1), f32),
            pltpu.VMEM((heads, 128), f32),
            pltpu.VMEM((win, model), f32),
            pltpu.VMEM((3, model, win), bf16),
            pltpu.VMEM((2, 2, win, win), f32),
            pltpu.VMEM((model, win), bf16),
            pltpu.VMEM((win, model), bf16),
            pltpu.VMEM((win, model), f32),
            pltpu.VMEM((4, win, hid_t), f32),
            pltpu.VMEM((4, win, hid_t), bf16),
            pltpu.VMEM((win, model), f32),
            pltpu.SemaphoreType.DMA((11, 10)),
            pltpu.SemaphoreType.DMA((11, 10)),
            pltpu.SemaphoreType.DMA((11,)),
            pltpu.SemaphoreType.DMA((24,)),
            pltpu.SemaphoreType.DMA((2,)),
            pltpu.SemaphoreType.DMA((4,)),
        ],
        compiler_params=pltpu.CompilerParams(
            vmem_limit_bytes=60 * 2**20, collective_id=0, has_side_effects=True
        ),
        name="forward_window",
    )(*small, *large)


def bits_of(size):
    return [1 << b for b in range(size.bit_length() - 1)]


def tn(a, b):
    return lax.dot_general(a, b, (((0,), (0,)), ((), ())), preferred_element_type=jnp.float32)


def add_into(dst, more):
    rows = dst.shape[0]
    step = 64 if rows % 64 == 0 else 16

    @pl.loop(0, rows // step)
    def _(i):
        sl = pl.ds(pl.multiple_of(i * step, step), step)
        total = dst[sl, :].astype(jnp.float32)
        for ref in more:
            total = total + ref[sl, :].astype(jnp.float32)
        dst[sl, :] = total.astype(dst.dtype)


class Reduce:
    def __init__(self, slot, rows, x_first, part, core, first, second, quarters, final, extra, result, acc, sems, peers):
        self.slot, self.rows, self.x_first, self.part, self.acc = slot, rows, x_first, part, acc
        self.core, self.first, self.second, self.quarters, self.final = core, first, second, quarters, final
        self.extra, self.result = extra, result
        self.send, self.recv, self.here = sems
        self.mate, self.across, self.beside, self.along, self.further, self.side, self.level = peers
        self.total = core.at[0] if acc is None else acc

    def move(self, k, src, dst, peer):
        return remote(src, dst, self.send.at[self.slot, k], self.recv.at[self.slot, k], peer)

    def half(self, mine):
        h = self.rows // 2
        side = self.side if mine else 1 - self.side
        return pl.ds(pl.multiple_of(side * h, h), h)

    def quarter(self, level):
        q = self.rows // 8
        return pl.ds(pl.multiple_of(self.side * (self.rows // 2) + level * q, q), q)

    def moves(self, stage, piece=None):
        h = self.rows // 2
        if stage == 0:
            return [self.move(p, self.part(p), self.core.at[p], self.mate) for p in range(2) if piece in (None, p)]
        if stage == 1 and self.x_first:
            return [self.move(2, self.core.at[1], self.first, self.across)] if piece != 0 else []
        if stage == 1:
            return [
                self.move(2 + p, self.core.at[p, self.half(False)], self.first.at[pl.ds(p * h, h)], self.beside)
                for p in range(2)
                if piece in (None, p)
            ]
        if stage == 2 and self.x_first:
            return [self.move(4, self.core.at[0, self.half(False)], self.second, self.beside)]
        if stage == 2:
            return [self.move(4, self.core.at[1, self.half(True)], self.second, self.across)]
        if stage == 3:
            return [
                self.move(
                    4 + k, self.core.at[0, self.quarter(xor_level(self.level, k))], self.quarters.at[k - 1], self.along[k]
                )
                for k in range(1, 4)
            ]
        if stage == 4:
            rows = self.quarter(self.level)
            return [self.move(7 + k, self.final, self.result.at[rows], self.along[k]) for k in range(1, 4)]
        rows = self.half(True)
        return [self.move(11, self.result.at[rows], self.result.at[rows], self.beside)]

    def own_copy(self):
        return pltpu.make_async_copy(self.final, self.result.at[self.quarter(self.level)], self.here.at[self.slot])

    def more(self, k):
        return self.move(12 + k, self.final_of(k), self.extra.at[k], self.further[k])

    def final_of(self, k):
        return self.final if k == 0 else self.extra.at[len(self.further) + k]

    def round_off(self, rows):
        if self.acc is not None:
            self.core[0, rows, :] = self.acc[rows, :].astype(jnp.bfloat16)

    def merge(self, piece, rows, value):
        value = value + self.core[piece, rows, :].astype(jnp.float32)
        if piece == 0:
            self.total[rows, :] = value.astype(self.total.dtype)
        else:
            self.core[1, rows, :] = value.astype(jnp.bfloat16)

    def from_mate(self, piece):
        for m in self.moves(0, piece):
            m.wait_recv()

    def take(self, stage):
        for m in self.moves(stage):
            m.wait_recv()
        h = self.rows // 2
        if stage == 1 and self.x_first:
            add_into(self.total, [self.first])
        if stage == 1 and not self.x_first:
            add_into(self.core.at[1, self.half(True)], [self.first.at[pl.ds(h, h)]])
            add_into(self.total.at[self.half(True)], [self.first.at[pl.ds(0, h)]])
        if stage == 2:
            add_into(self.total.at[self.half(True)], [self.second])
        if stage == 3:
            value = self.total[self.quarter(self.level), :].astype(jnp.float32)
            for k in range(3):
                value = value + self.quarters[k].astype(jnp.float32)
            self.final[...] = value.astype(jnp.bfloat16)
            for k in range(len(self.further)):
                self.more(k).start()
                self.more(k).wait()
                total = self.final_of(k)[...].astype(jnp.float32) + self.extra[k].astype(jnp.float32)
                self.final_of(k + 1)[...] = total.astype(jnp.bfloat16)
            if self.further:
                self.final[...] = self.final_of(len(self.further))[...]
            self.own_copy().start()
        if stage == 4:
            self.own_copy().wait()

    def go(self, stage, piece=None):
        if stage == 1 and not self.x_first and piece == 0:
            self.round_off(self.half(False))
        if stage == 2 and self.x_first:
            self.round_off(self.half(False))
        if stage == 3:
            self.round_off(self.half(True))
        for m in self.moves(stage, piece):
            m.start()

    def next(self, stage):
        self.take(stage)
        if stage < 5:
            self.go(stage + 1)

    def sent(self, stage):
        for m in self.moves(stage):
            m.wait_send()


def xor_level(level, k):
    for bit in (1, 2):
        if k & bit:
            level = xor_index(level, bit)
    return level


def gelu_slope(v):
    k = math.sqrt(2.0 / math.pi)
    square = v * v
    t = jnp.tanh(k * v * (1.0 + 0.044715 * square))
    return 0.5 * (1.0 + t) + (0.5 * k) * v * (1.0 - t * t) * (1.0 + 3 * 0.044715 * square)


SMALL = 16


def backward_kernel(
    n_dp, inv_ref, gain_ref, sums_ref, dres_in, hid_in, pre_in, unit_in, nlow_in, low_in, feat_in, qkvt_in, ctxt_in,
    probs_in, rx_in, ry_in, w1_in, w2_in, wo_in, wqkv_in, block_in,
    block_all, in_all, red1, red2, red3, lay_all, small_out,
    arena, hidb, preb, dres, unit, nlow, nlow_t, dn, low_rows, qkvb, ctxtb, dctx, lowb, featb, wob, rxb, ryb, hot, acc,
    part1, part2, part3, core1, core2, core3, first1, first2, first3, second1, second2, second3,
    quarters1, quarters2, quarters3, final1, final2, final3, extra1, extra2, extra3, acc3, small, small_in, short,
    load_sem, send, recv, here, share_send, share_recv, small_send, small_recv, p_sem,
):
    t, d = lax.axis_index("tensor"), lax.axis_index("dp")
    mate, across = {"tensor": xor_index(t, 1)}, {"tensor": xor_index(t, 2)}
    beside = {"dp": xor_index(d, 1)}
    along = [None] + [{"dp": d + 2 * (xor_level((d // 2) % 4, k) - (d // 2) % 4)} for k in range(1, 4)]
    further = [{"dp": xor_index(d, bit)} for bit in bits_of(n_dp) if bit >= 8]
    peers = (mate, across, beside, along, further, d % 2, (d // 2) % 4)
    sems = (send, recv, here)
    f32, bf16 = jnp.float32, jnp.bfloat16
    win, model = dres.shape
    heads = 4 * HEADS_T
    cols_t = HEADS_T * HD
    hid_t = model
    block = 128

    everyone = [mate, across, beside] + along[1:] + further
    signal_peers(everyone)

    def load(k, src, dst):
        return pltpu.make_async_copy(src, dst, load_sem.at[k])

    def w_rows(r):
        return pl.ds(r * hid_t, hid_t)

    def h_rows(r):
        return pl.ds(r * win, win)

    order = (3, 1, 2, 0)
    ld_dres = load(0, dres_in, dres)
    ld_hid = {r: load(1 + r, hid_in.at[r], hidb.at[h_rows(r)]) for r in order}
    ld_w2 = {r: load(5 + r, w2_in.at[r], arena.at[w_rows(r)]) for r in order}
    ld_w1 = {r: load(9 + r, w1_in.at[r], arena.at[w_rows(4 + r)]) for r in order}
    ld_pre = {r: load(13 + r, pre_in.at[r], preb.at[i % 2]) for i, r in enumerate(order)}
    ld_rest = [
        load(17 + k, src, dst)
        for k, (src, dst) in enumerate(
            [
                (nlow_in, nlow), (unit_in, unit), (ctxt_in, ctxtb), (wo_in, wob), (qkvt_in, qkvb), (low_in, lowb),
                (feat_in, featb), (rx_in.at[t], rxb), (ry_in.at[t], ryb),
            ]
        )
    ]
    ld_wqkv = [load(26 + n, wqkv_in.at[n], hidb.at[pl.ds(n * model, model)]) for n in range(3)]
    ld_dres.start()
    for r in order:
        ld_hid[r].start()
    for r in order[:2]:
        ld_pre[r].start()
    for r in order:
        ld_w2[r].start()
    ld_rest[0].start()
    for r in order:
        ld_w1[r].start()
    for c in ld_rest[1:]:
        c.start()

    def chunks(slot, sizes, orders, parts, core, first, second, quarters, final, extra, result, acc=None):
        out, at = [], 0
        for k, (rows, x_first, part) in enumerate(zip(sizes, orders, parts)):
            q = pl.ds(at // 8, rows // 8)
            out.append(
                Reduce(
                    slot + k, rows, x_first, part, core.at[:, pl.ds(at, rows)], first.at[pl.ds(at, rows)],
                    second.at[pl.ds(at // 2, rows // 2)], quarters.at[:, q], final.at[q], extra.at[:, q],
                    result.at[pl.ds(at, rows)], None if acc is None else acc.at[pl.ds(at, rows)], sems, peers,
                )
            )
            at += rows
        return out

    third = hid_t // 3
    sizes = [third] * 3

    def thirds(ref):
        return [lambda p, k=k: ref.at[p, pl.ds(k * third, third)] for k in range(3)]

    s2 = chunks(
        0, sizes, X_FIRST[:3], thirds(part2), core2, first2, second2, quarters2, final2, extra2, red2
    )
    s1 = chunks(
        3, sizes, X_FIRST[3:6], thirds(part1), core1, first1, second1, quarters1, final1, extra1, red1
    )
    lay_t = lay_all.shape[0] // 4
    s3 = chunks(
        6, [2 * cols_t, 2 * cols_t, lay_t], X_FIRST[6:],
        [
            lambda p: part2.at[p, pl.ds(0, 2 * cols_t)],
            lambda p: part2.at[p, pl.ds(2 * cols_t, 2 * cols_t)],
            lambda p: part3.at[p],
        ],
        core3, first3, second3, quarters3, final3, extra3, red3, acc3,
    )

    def share(k, src, whole, rows, part=0, parts=1):
        def at(index):
            return whole.at[pl.ds(pl.multiple_of((index * parts + part) * rows, rows), rows)]

        def moved(j, from_ref, index, peer):
            return remote(from_ref, at(index), share_send.at[k, j], share_recv.at[k, j], peer)

        far = xor_index(t, 2)
        return {
            "here": pltpu.make_async_copy(src, at(t), share_send.at[k, 3]),
            "across": moved(0, src, t, across),
            "mate": moved(1, src, t, mate),
            "pass": moved(2, at(far), far, mate),
        }

    def share_start(c):
        for name in ("across", "mate", "here"):
            c[name].start()

    def share_pass(c):
        c["across"].wait_recv()
        c["pass"].start()

    def share_end(c):
        c["here"].wait()
        c["mate"].wait_recv()
        c["pass"].wait_recv()
        for name in ("across", "mate", "pass"):
            c[name].wait_send()

    quarter_win = win // 4
    sh_block = [
        share(k, block_in.at[pl.ds(k * quarter_win, quarter_win)], block_all, quarter_win, k, 4) for k in range(4)
    ]
    sh_in = share(4, low_rows, in_all, win)
    sh_lay = share(5, red3.at[pl.ds(4 * cols_t, lay_t)], lay_all, lay_t)
    bits = [mate, across, beside, along[1], along[2]] + further

    def small_move(k):
        return remote(small.at[k], small_in.at[k], small_send.at[k], small_recv.at[k], bits[k])

    def small_step(k):
        small_move(k).wait()
        small[k + 1] = small[k] + small_in[k]
        if k + 1 < len(bits):
            small_move(k + 1).start()

    named = dict(zip(range(A0, CC + 1), s2 + s1 + s3))

    def run(what, stage):
        if what in named:
            named[what].next(stage)
        elif what == BLOCK:
            share_start(sh_block[stage])
        elif what == BLOCK_ON:
            share_pass(sh_block[stage])
        elif what == INPUT_ON:
            share_pass(sh_in)
        elif what == LAY:
            share_start(sh_lay)
        elif what == LAY_ON:
            share_pass(sh_lay)
        elif what == SMALL_STEP:
            small_step(stage)

    def at_slot(phase, index=0):
        for what, stage in SCHEDULE.get((phase, index), ()):
            run(what, stage)

    def at_loop(phase, index, count, first=0):
        for k in range(count):
            if (phase, first + k) in SCHEDULE:
                @pl.when(index == k)
                def _(k=k):
                    at_slot(phase, first + k)


    small[0] = jnp.zeros_like(small[0])
    small[0, 3:4, :] = sums_ref[2:3, :]
    small[0, 4:6, :] = sums_ref[0:2, :]
    small[0, 6:7, :] = sums_ref[3:4, :]

    def own_row(base, r):
        index = t
        for bit in (1, 2):
            if r & bit:
                index = xor_index(index, bit)
        return pl.ds(base + index, 1)

    ld_dres.wait()

    @pl.loop(0, win // block)
    def _(i):
        sl = pl.ds(pl.multiple_of(i * block, block), block)
        low_rows[sl, :] = dres[sl, :].astype(bf16)

    def grad_w2(r, c):
        sl = pl.ds(pl.multiple_of(c * third, third), third)
        return tn(hidb[h_rows(r), sl], low_rows[...])

    def grad_w1(r, c):
        sl = pl.ds(pl.multiple_of(c * third, third), third)
        return nn(nlow_t[sl, :], hidb[h_rows(r), :])

    def for_mate(group, grad, r, part):
        @pl.loop(0, 3)
        def _(c):
            part[r // 2, pl.ds(pl.multiple_of(c * third, third), third), :] = grad(r, c).astype(bf16)

        for g in group:
            g.go(0, r // 2)

    def for_own(group, grad, r):
        for c, g in enumerate(group):
            g.from_mate(r // 2)
            g.merge(r // 2, pl.ds(0, third), grad(r, c))
            g.go(1, r // 2)

    for r in order[:2]:
        ld_hid[r].wait()
        if r == order[0]:
            for_mate((), grad_w2, r, part2)
            wait_peers(everyone)
            at_slot(START)
            for g in s2:
                g.go(0, r // 2)
        else:
            for_mate(s2, grad_w2, r, part2)

    ld_rest[0].wait()
    nlow_t[...] = nlow[...].astype(f32).T.astype(bf16)
    for j, r in enumerate(order):
        ld_pre[r].wait()
        ld_w2[r].wait()
        ld_w1[r].wait()

        @pl.loop(0, 2)
        def _(i, j=j, r=r):
            count = win // 2
            sl = pl.ds(pl.multiple_of(i * count, count), count)
            hs = pl.ds(pl.multiple_of(r * win + i * count, count), count)
            dhid = nt(low_rows[sl, :], arena[w_rows(r), :])
            dpre = (dhid * gelu_slope(preb[j % 2, sl, :])).astype(bf16)
            hidb[hs, :] = dpre
            row = own_row(8, r)
            small[0, row, :] += jnp.sum(dpre.astype(f32), axis=0, keepdims=True)
            more = nt(dpre, arena[w_rows(4 + r), :])
            dn[sl, :] = more if j == 0 else dn[sl, :] + more
            at_loop(FFN, i, 2, 3 * j)

        if j + 2 < 4:
            ld_pre[order[j + 2]].start()
        if j < 2:
            for_mate(s1, grad_w1, r, part1)
        else:
            for_own(s1, grad_w1, r)
        if j == 0:
            for q in order[2:]:
                ld_hid[q].wait()
                for_own(s2, grad_w2, q)
        at_slot(FFN, 3 * j + 2)

    for c in ld_wqkv:
        c.start()

    def p_load(h, slot):
        return pltpu.make_async_copy(probs_in.at[h], preb.at[slot, :, pl.ds(0, win)], p_sem.at[slot])

    for h in range(2):
        p_load(h, h).start()
    for g in s2:
        g.sent(0)

    ld_rest[1].wait()

    @pl.loop(0, win // block)
    def _(i):
        sl = pl.ds(pl.multiple_of(i * block, block), block)
        up = dres[sl, :] + dn[sl, :]
        units = unit[sl, :]
        scaled = up * row_of(gain_ref)
        mean_one = jnp.mean(scaled, axis=1, keepdims=True)
        mean_two = jnp.mean(scaled * units, axis=1, keepdims=True)
        value = (scaled - mean_one - units * mean_two) * inv_ref[sl, :]
        dn[sl, :] = value
        low_rows[sl, :] = value.astype(bf16)
        small[0, 0:1, :] += jnp.sum(value, axis=0, keepdims=True)
        small[0, 1:2, :] += jnp.sum(up * units, axis=0, keepdims=True)
        small[0, 2:3, :] += jnp.sum(up, axis=0, keepdims=True)

    at_slot(NORM)
    for c in ld_rest[2:]:
        c.wait()

    @pl.loop(0, 4)
    def _(r):
        sl = pl.ds(pl.multiple_of(r * cols_t, cols_t), cols_t)
        dctx[sl, :] = nt(wob[sl, :], low_rows[...]).astype(bf16)

    at_slot(OUT)

    @pl.loop(0, heads)
    def _(h):
        slot = h % 2
        sl = pl.ds(pl.multiple_of(h * HD, HD), HD)
        dc_t = dctx[sl, :]
        dc = dc_t.astype(f32).T.astype(bf16)
        p_load(h, slot).wait()
        p = preb[slot, :, 0:win]
        dp = nn(dc, qkvb[2, sl, :])
        row_dot = jnp.sum(p * dp, axis=1, keepdims=True)
        ds = (p * (dp - row_dot)).astype(bf16)
        qkvb[2, sl, :] = nn(dc_t, p.astype(bf16)).astype(bf16)
        dq = nt(qkvb[1, sl, :], ds) * HD ** (-0.5)
        dk = nn(qkvb[0, sl, :], ds) * HD ** (-0.5)
        qkvb[0, sl, :] = dq.astype(bf16)
        qkvb[1, sl, :] = dk.astype(bf16)
        arena[pl.ds(pl.multiple_of(h * win, win), win), 0:win] = ds

        @pl.when(h + 2 < heads)
        def _():
            p_load(h + 2, slot).start()

        at_loop(HEAD, h, heads)

    for c in ld_wqkv:
        c.wait()
    def rows_of(r):
        return pl.ds(r * cols_t, cols_t)

    def grad_out(r):
        return nn(ctxtb[rows_of(r), :], low_rows[...])

    def grad_proj(n, r):
        return nn(qkvb[n, rows_of(r), :], lowb[...])

    halves = (
        (s3[0], lambda r: grad_proj(2, r), grad_out),
        (s3[1], lambda r: grad_proj(0, r), lambda r: grad_proj(1, r)),
    )
    for k, (g, upper, lower) in enumerate(halves):
        for r in (3, 1):
            at = 2 * cols_t * k
            part2[r // 2, at : at + cols_t, :] = upper(r).astype(bf16)
            part2[r // 2, at + cols_t : at + 2 * cols_t, :] = lower(r).astype(bf16)
            g.go(0, r // 2)
    at_slot(SENT)
    for g, upper, lower in halves:
        for r in (2, 0):
            g.from_mate(r // 2)
            g.merge(r // 2, pl.ds(0, cols_t), upper(r))
            g.merge(r // 2, pl.ds(cols_t, cols_t), lower(r))
            g.go(1, r // 2)
    at_slot(MERGED)

    @pl.loop(0, win // block)
    def _(i):
        sl = pl.ds(pl.multiple_of(i * block, block), block)
        value = dn[sl, :]
        for n in range(3):
            value = value + tn(qkvb[n, :, sl], hidb[pl.ds(n * model, model), :])
        dn[sl, :] = value
        at_loop(DLAYER, i, 4)

    low_rows[...] = dn[...].astype(bf16)

    def grad_lay(r):
        index = t
        for bit in (1, 2):
            if r & bit:
                index = xor_index(index, bit)
        return tn(featb[:, pl.ds(pl.multiple_of(index * lay_t, lay_t), lay_t)], low_rows[...])

    for r in (3, 1):
        part3[r // 2] = grad_lay(r).astype(bf16)
        s3[2].go(0, r // 2)
    at_slot(LAYOUT)
    for r in (2, 0):
        s3[2].from_mate(r // 2)
        s3[2].merge(r // 2, pl.ds(0, lay_t), grad_lay(r))
        s3[2].go(1, r // 2)
    share_start(sh_in)

    ones = jnp.ones((8, win), bf16)
    short[...] = jnp.zeros_like(short)
    for n, at in ((0, 0), (2, cols_t)):
        total = nt(ones, qkvb[n])
        for r in range(4):
            short[r : r + 1, at : at + cols_t] = total[0:1, r * cols_t : (r + 1) * cols_t]

    acc[...] = jnp.zeros_like(acc)
    one, zero = bf16(1), bf16(0)
    hots = BUCKETS * ROWS
    @pl.loop(0, win // ROWS // 2)
    def _(i):
        total = None
        for u in range(2):
            at = pl.multiple_of(i * 2 * ROWS + u * ROWS, ROWS)
            x = rxb[pl.ds(at, ROWS), :].astype(f32).astype(bf16)
            y = ryb[pl.ds(at, ROWS), :].astype(f32).astype(bf16)
            for b in range(BUCKETS):
                hot[u, b * ROWS : (b + 1) * ROWS, :] = jnp.where(x == bf16(b), one, zero)
                hot[u, hots + b * ROWS : hots + (b + 1) * ROWS, :] = jnp.where(y == bf16(b), one, zero)
            left = jnp.concatenate(
                [arena[pl.ds(pl.multiple_of(h * win + at, ROWS), ROWS), 0:win] for h in range(heads)], axis=0
            )
            more = nt(left, hot[u])
            total = more if total is None else total + more
        acc[...] += total
        at_loop(TABLE, i, 16)

    row = lax.broadcasted_iota(jnp.int32, (ROWS, 2 * hots), 0)
    col = lax.broadcasted_iota(jnp.int32, (ROWS, 2 * hots), 1) % ROWS
    picked = jnp.concatenate(
        [
            jnp.sum(jnp.where(row == col, acc[h * ROWS : (h + 1) * ROWS, :], 0.0), axis=0, keepdims=True)
            for h in range(heads)
        ]
        + [jnp.zeros((16 - heads, 2 * hots), f32)],
        axis=0,
    )
    fold = (
        lax.broadcasted_iota(jnp.int32, (2 * hots, 128), 0) // ROWS
        == lax.broadcasted_iota(jnp.int32, (2 * hots, 128), 1)
    ).astype(f32)
    table = jnp.dot(picked, fold, preferred_element_type=f32, precision=lax.Precision.HIGHEST)
    for r in range(4):
        for a in range(HEADS_T):
            lane = 2 * cols_t + a * 2 * BUCKETS
            short[r : r + 1, lane : lane + 2 * BUCKETS] = table[
                r * HEADS_T + a : r * HEADS_T + a + 1, 0 : 2 * BUCKETS
            ]
    for r in range(4):
        small[0, own_row(12, r), :] = short[r : r + 1, :]

    small_move(0).start()
    at_slot(TAIL)
    for k in range(5, len(bits)):
        small_step(k)
    small_out[...] = small[len(bits)]
    for c in sh_block + [sh_in, sh_lay]:
        share_end(c)
    for g in s1 + s3:
        g.sent(0)
    for g in s2 + s1 + s3:
        for stage in range(1, 6):
            g.sent(stage)


def backward_window(n_dp, lay_rows, inv, gain, sums, dres, hid, pre, unit, nlow, low, feat, qkvt, ctxt, probs, rx, ry, w1, w2, wo, wqkv, block_own):
    win, model = dres.shape
    heads = 4 * HEADS_T
    cols_t = HEADS_T * HD
    lay_t = lay_rows // 4
    rest = 4 * cols_t + lay_t
    more = max(0, len(bits_of(n_dp)) - 3)
    levels = 5 + more
    f32, bf16 = jnp.float32, jnp.bfloat16
    shape = jax.ShapeDtypeStruct
    here = pl.BlockSpec(memory_space=pltpu.VMEM)
    away = pl.BlockSpec(memory_space=pl.ANY)
    outs = [
        (shape((4 * win, model), bf16), away),
        (shape((4 * win, model), bf16), away),
        (shape((model, model), bf16), away),
        (shape((model, model), bf16), away),
        (shape((rest, model), bf16), away),
        (shape((lay_rows, model), bf16), away),
        (shape((SMALL, model), f32), here),
    ]
    V = pltpu.VMEM
    S = pltpu.SemaphoreType.DMA
    return pl.pallas_call(
        functools.partial(backward_kernel, n_dp),
        in_specs=[here] * 3 + [away] * 17,
        out_specs=[spec for _, spec in outs],
        out_shape=[s for s, _ in outs],
        scratch_shapes=[
            V((8 * model, model), bf16), V((3 * model, model), bf16), V((2, win, model), f32), V((win, model), f32),
            V((win, model), f32), V((win, model), bf16), V((model, win), bf16), V((win, model), f32),
            V((win, model), bf16), V((3, model, win), bf16), V((model, win), bf16), V((model, win), bf16),
            V((win, model), bf16), V((win, lay_rows), bf16), V((model, model), bf16), V((win, win), jnp.int32),
            V((win, win), jnp.int32), V((2, 2 * BUCKETS * ROWS, win), bf16), V((heads * ROWS, 2 * BUCKETS * ROWS), f32),
            V((2, model, model), bf16), V((2, model, model), bf16), V((2, lay_t, model), bf16),
            V((2, model, model), bf16), V((2, model, model), bf16), V((2, rest, model), bf16),
            V((model, model), bf16), V((model, model), bf16), V((rest, model), bf16),
            V((model // 2, model), bf16), V((model // 2, model), bf16), V((rest // 2, model), bf16),
            V((3, model // 8, model), bf16), V((3, model // 8, model), bf16), V((3, rest // 8, model), bf16),
            V((model // 8, model), bf16), V((model // 8, model), bf16), V((rest // 8, model), bf16),
            V((2 * more + 1, model // 8, model), bf16), V((2 * more + 1, model // 8, model), bf16),
            V((2 * more + 1, rest // 8, model), bf16),
            V((rest, model), f32), V((levels + 1, SMALL, model), f32), V((levels, SMALL, model), f32), V((8, model), f32),
            S((29,)), S((9, 12 + max(1, more))), S((9, 12 + max(1, more))), S((9,)), S((6, 4)), S((6, 3)),
            S((levels,)), S((levels,)), S((2,)),
        ],
        compiler_params=pltpu.CompilerParams(
            vmem_limit_bytes=63 * 2**20, collective_id=1, has_side_effects=True
        ),
        name="backward_window",
    )(inv, gain, sums, dres, hid, pre, unit, nlow, low, feat, qkvt, ctxt, probs, rx, ry, w1, w2, wo, wqkv, block_own)


def finish_kernel(
    rates, small_ref, block_in, in_in, red1, red2, red3, lay_in,
    block_out, in_out, lay_out, qkv_out, qvb_out, table_out, wo_out, ob_out, g1_out, s1_out, w1_out, b1_out, w2_out, c2_out,
    g2_out, s2_out, in_low, low1, low2, low3, lay_low, in_wide, wide1, wide2, wide3, lay_wide, block_low, load_sem, store_sem,
):
    t = lax.axis_index("tensor")
    cols_t = HEADS_T * HD
    inverse = 1.0 / small_ref[6:7, 0:1]
    order = [
        (in_in, in_low, in_wide, in_out, None),
        (red2, low2, wide2, w2_out, 4),
        (red1, low1, wide1, w1_out, 3),
        (red3, low3, wide3, None, None),
        (lay_in, lay_low, lay_wide, lay_out, 6),
    ]
    loads = [pltpu.make_async_copy(src, low, load_sem.at[k]) for k, (src, low, _, _, _) in enumerate(order)]
    for c in loads:
        c.start()
    whole_in = pltpu.make_async_copy(block_in, block_low, load_sem.at[5])
    whole_in.start()
    whole_out = pltpu.make_async_copy(block_low, block_out, store_sem.at[9])

    def row(ref, index, rate):
        ref[...] = (small_ref[index : index + 1, :] * (inverse * rates[rate])).reshape(ref.shape)

    for ref, index, rate in ((ob_out, 0, 1), (g1_out, 1, 2), (s1_out, 2, 2), (c2_out, 3, 4), (g2_out, 4, 5), (s2_out, 5, 5)):
        row(ref, index, rate)
    b1_out[...] = (small_ref[pl.ds(8 + t, 1), :] * (inverse * rates[3])).reshape(b1_out.shape)
    own = small_ref[pl.ds(12 + t, 1), :]
    for k in range(2):
        qvb_out[k : k + 1, :] = own[:, k * cols_t : (k + 1) * cols_t] * (inverse * rates[0])
    for a in range(HEADS_T):
        at = 2 * cols_t + a * 2 * BUCKETS
        table_out[a : a + 1, :] = own[:, at : at + 2 * BUCKETS] * (inverse * rates[7])

    stores = []

    def store(k, src, dst):
        stores.append(pltpu.make_async_copy(src, dst, store_sem.at[k]))

    for k, (_, low, wide, out, rate) in enumerate(order):
        loads[k].wait()
        step = 128
        if out is not None:
            factor = inverse if rate is None else inverse * rates[rate]

            @pl.loop(0, low.shape[0] // step)
            def _(i, low=low, wide=wide, out=out, factor=factor, k=k):
                sl = pl.ds(pl.multiple_of(i * step, step), step)
                wide[sl, :] = low[sl, :].astype(jnp.float32) * factor
                pltpu.make_async_copy(wide.at[sl], out.at[sl], store_sem.at[k]).start()

            store(k, wide, out)
            if k == 0:
                whole_in.wait()
                whole_out.start()
            continue
        parts = ((2, 0, 0), (None, 1, 1), (0, 2, 0), (1, 3, 0))
        for j, (n, at, rate) in enumerate(parts):
            sl = pl.ds(at * cols_t, cols_t)
            wide[sl, :] = low[sl, :].astype(jnp.float32) * (inverse * rates[rate])
            store(5 + j, wide.at[sl], wo_out if n is None else qkv_out.at[n])
            stores[-1].start()
    whole_out.wait()
    for c in stores:
        c.wait()


def finish(rates, small, block_all, in_all, sum1, sum2, sum3, lay_all, cols_t):
    f32, bf16 = jnp.float32, jnp.bfloat16
    shape = jax.ShapeDtypeStruct
    here = pl.BlockSpec(memory_space=pltpu.VMEM)
    away = pl.BlockSpec(memory_space=pl.ANY)
    model = in_all.shape[1]
    vector = (shape((model,), f32), here)
    outs = [
        (shape(block_all.shape, bf16), away),
        (shape(in_all.shape, f32), away),
        (shape(lay_all.shape, f32), away),
        (shape((3, cols_t, model), f32), away),
        (shape((2, cols_t), f32), here),
        (shape((HEADS_T, 2 * BUCKETS), f32), here),
        (shape((cols_t, model), f32), away),
        vector, vector, vector,
        (shape(sum1.shape, f32), away),
        vector,
        (shape(sum2.shape, f32), away),
        vector, vector, vector,
    ]
    wide = [in_all, sum1, sum2, sum3, lay_all]
    return pl.pallas_call(
        finish_kernel,
        in_specs=[pl.BlockSpec(memory_space=pltpu.SMEM), here] + [away] * 6,
        out_specs=[spec for _, spec in outs],
        out_shape=[s for s, _ in outs],
        scratch_shapes=[pltpu.VMEM(v.shape, bf16) for v in wide]
        + [pltpu.VMEM(v.shape, f32) for v in wide]
        + [pltpu.VMEM(block_all.shape, bf16), pltpu.SemaphoreType.DMA((6,)), pltpu.SemaphoreType.DMA((10,))],
        compiler_params=pltpu.CompilerParams(vmem_limit_bytes=60 * 2**20),
        name="finish",
    )(rates, small, block_all, in_all, sum1, sum2, sum3, lay_all)


def local(
    n_dp, n_t,
    tokens_in, box_coords, rel_x, rel_y, mask_tokens, cotangent, layout_weight, qkv_weight, qv_bias,
    bias_table, out_weight, out_bias, ln1_gain, ln1_bias, ffn_in_weight, ffn_in_bias, ffn_out_weight,
    ffn_out_bias, ln2_gain, ln2_bias, group_rates,
):
    (
        probs, qkvt, context_t, layer_low, features, unit_one, inverse_one, normed_low, pre_all, hid_all,
        block_own, dresid_two, sums, wqkv, wo, w1, w2,
    ) = forward_window(
        [
            box_coords.T, mask_tokens.reshape(-1, 128), layout_weight, qv_bias, ffn_in_bias, bias_table.T,
            out_bias, ln1_gain, ln1_bias, ffn_out_bias, ln2_gain, ln2_bias,
        ],
        [
            tokens_in, cotangent, rel_x, rel_y, jnp.transpose(qkv_weight, (0, 2, 1)), out_weight, ffn_in_weight,
            ffn_out_weight,
        ],
    )
    block_all, in_all, sum1, sum2, sum3, lay_all, small = backward_window(
        n_dp, layout_weight.shape[0], inverse_one, ln1_gain, sums, dresid_two, hid_all, pre_all, unit_one, normed_low,
        layer_low, features, qkvt, context_t, probs, rel_x, rel_y, w1, w2, wo, wqkv, block_own,
    )
    out = list(finish(group_rates, small, block_all, in_all, sum1, sum2, sum3, lay_all, out_weight.shape[0]))
    out[3] = jnp.transpose(out[3], (0, 2, 1))
    out[5] = out[5].T
    return tuple(out)


def solution(mesh):
    placed = (
        P("dp", None), P("dp", None), P("dp", None, None), P("dp", None, None), P("dp"), P("dp", None),
        P(), P(None, None, "tensor"), P(None, "tensor"), P(None, "tensor"), P("tensor", None),
        P(), P(), P(), P(None, "tensor"), P("tensor"), P("tensor", None), P(), P(), P(), P(),
    )
    return jax.shard_map(
        functools.partial(local, mesh.shape["dp"], mesh.shape["tensor"]),
        mesh=mesh,
        in_specs=placed,
        out_specs=(
            P("dp", None), P("dp", None), P(), P(None, None, "tensor"), P(None, "tensor"),
            P(None, "tensor"), P("tensor", None), P(), P(), P(), P(None, "tensor"), P("tensor"),
            P("tensor", None), P(), P(), P(),
        ),
        check_vma=False,
    )
```

```python
import functools
import math

import jax
import jax.numpy as jnp
from jax import lax
from jax.experimental import pallas as pl
from jax.experimental.pallas import tpu as pltpu
from jax.sharding import PartitionSpec as P

HD = 64
LFREQ = 64
BUCKETS = 32
EPSILON = 1e-05
ROWS = 16
HEADS_T = 3
MESH = pl.DeviceIdType.MESH

F_FEAT, F_NEAR, F_HEAD, F_FAR, F_BOTH, F_OUT, F_CONTEXT, F_NORM, F_UP, F_THIRD, F_DONE = range(11)
AT_R, AT_Q, AT_K, AT_V, AT_O, U0, D0, U1, D1, U2, D2 = range(11)
WAYS = {
    AT_R: (1, 0),
    AT_Q: (2, 1),
    AT_K: (2, 1),
    AT_V: (2, 0),
    AT_O: (2, 1),
    U0: (4, 0),
    D0: (4, 0),
    U1: (4, 0),
    D1: (4, 0),
    U2: (2, 1),
    D2: (1, 0),
}
SEND_ORDER = (AT_Q, AT_K, AT_V, AT_O, AT_R, D1, D0, U0, U1, U2, D2)
FORWARD = {
    (F_NEAR, 0): ((AT_Q, 0),),
    (F_HEAD, 2): ((AT_K, 0), (AT_V, 0), (AT_Q, 1),),
    (F_HEAD, 4): ((AT_O, 0), (AT_K, 1), (AT_R, 0), (AT_V, 1),),
    (F_HEAD, 5): ((D1, 0),),
    (F_BOTH, 0): ((D0, 0),),
    (F_HEAD, 6): ((D1, 1),),
    (F_HEAD, 7): ((U0, 0),),
    (F_HEAD, 8): ((U1, 0), (D0, 1), (D1, 2),),
    (F_HEAD, 9): ((AT_O, 1),),
    (F_HEAD, 10): ((U0, 1),),
    (F_HEAD, 11): ((U1, 1),),
    (F_CONTEXT, 0): ((U2, 0), (D0, 2),),
    (F_NORM, 1): ((U0, 2),),
    (F_NORM, 3): ((U1, 2),),
    (F_UP, 2): ((D2, 0), (U2, 1),),
}

START, FFN, NORM, OUT, HEAD, SENT, MERGED, DLAYER, LAYOUT, TABLE, TAIL = range(11)
A0, A1, A2, B0, B1, B2, C0, C1, C2, C3, C4, C5, C6, BLOCK, BLOCK_ON, INPUT_ON, LAY, LAY_ON, SMALL_STEP = range(19)
X, Y, Z_NEAR, Z_FAR = range(4)
ORDERS = (
    ((Y, X, Z_NEAR, Z_FAR), (Z_FAR, Z_NEAR, Y)),
    ((Z_NEAR, Z_FAR, X, Y), (Z_FAR, Z_NEAR, Y)),
    ((X, Y, Z_NEAR, Z_FAR), (Z_FAR, Z_NEAR, Y)),
    ((X, Y, Z_NEAR, Z_FAR), (Z_FAR, Z_NEAR, Y)),
    ((X, Z_NEAR, Z_FAR, Y), (Z_FAR, Z_NEAR, Y)),
    ((Y, Z_NEAR, Z_FAR, X), (Z_FAR, Z_NEAR, Y)),
    ((Y, X, Z_NEAR, Z_FAR), (Z_FAR, Z_NEAR, Y)),
    ((Y, X, Z_NEAR, Z_FAR), (Z_FAR, Z_NEAR, Y)),
    ((Y, X, Z_NEAR, Z_FAR), (Z_FAR, Z_NEAR, Y)),
    ((X, Y, Z_NEAR, Z_FAR), (Z_FAR, Z_NEAR, Y)),
    ((Y, X, Z_NEAR, Z_FAR), (Y, Z_FAR, Z_NEAR)),
    ((X, Z_NEAR, Z_FAR, Y), (Z_FAR, Z_NEAR, Y)),
    ((X, Z_NEAR, Z_FAR, Y), (Z_FAR, Z_NEAR, Y)),
)
SCHEDULE = {
    (START, 0): ((BLOCK, 1), (BLOCK, 3),),
    (FFN, 11): ((A1, 0),),
    (NORM, 0): ((A2, 0), (BLOCK_ON, 3),),
    (OUT, 0): ((BLOCK_ON, 1),),
    (HEAD, 1): ((B2, 0),),
    (HEAD, 5): ((A1, 1), (B0, 0), (A2, 1),),
    (HEAD, 6): ((A0, 0), (B2, 1),),
    (HEAD, 9): ((A2, 2),),
    (HEAD, 10): ((B0, 1),),
    (SENT, 0): ((B1, 0), (B2, 2), (A2, 3),),
    (MERGED, 0): ((B0, 2), (B1, 1), (A0, 1),),
    (DLAYER, 0): ((B2, 3),),
    (DLAYER, 1): ((A1, 2), (A2, 4),),
    (DLAYER, 3): ((BLOCK, 2), (B0, 3),),
    (LAYOUT, 0): ((C3, 0),),
    (TABLE, 0): ((C0, 0), (C1, 0), (C5, 0), (A0, 2), (B1, 2), (A2, 5), (B2, 4),),
    (TABLE, 2): ((C4, 0),),
    (TABLE, 3): ((A1, 3),),
    (TABLE, 4): ((B0, 4),),
    (TABLE, 5): ((C2, 0), (C6, 0),),
    (TABLE, 6): ((B1, 3), (B2, 5),),
    (TABLE, 7): ((C3, 1), (A0, 3),),
    (TABLE, 8): ((A1, 4), (BLOCK_ON, 2),),
    (TABLE, 10): ((BLOCK, 0), (C5, 1),),
    (TABLE, 11): ((C6, 1), (B0, 5),),
    (TABLE, 15): ((A0, 4),),
    (TAIL, 0): (
        (A1, 5), (C3, 2), (A2, 6), (B1, 4), (B2, 6), (B0, 6), (C5, 2), (SMALL_STEP, 0), (C6, 2), (INPUT_ON, 0),
        (A0, 5), (C3, 3), (A1, 6), (C5, 3), (C0, 1), (C6, 3), (B1, 5), (C3, 4), (C1, 1), (C5, 4), (C0, 2), (C4, 1),
        (A0, 6), (C6, 4), (C3, 5), (C1, 2), (C2, 1), (C5, 5), (C0, 3), (B1, 6), (C4, 2), (C6, 5), (BLOCK_ON, 0),
        (C3, 6), (C1, 3), (C2, 2), (SMALL_STEP, 1), (C0, 4), (C5, 6), (C4, 3), (C1, 4), (C6, 6), (LAY, 0), (C2, 3),
        (SMALL_STEP, 2), (C0, 5), (C4, 4), (C1, 5), (C2, 4), (SMALL_STEP, 3), (C0, 6), (LAY_ON, 0), (C2, 5),
        (C4, 5), (C1, 6), (SMALL_STEP, 4), (C2, 6), (C4, 6),
    ),
}


def nt(a, b):
    return lax.dot_general(a, b, (((1,), (1,)), ((), ())), preferred_element_type=jnp.float32)


def nn(a, b):
    return jnp.dot(a, b, preferred_element_type=jnp.float32)


def xor_index(index, bit):
    return index + bit - 2 * bit * ((index // bit) % 2)


def signal_peers(peers):
    barrier = pltpu.get_barrier_semaphore()
    for peer in peers:
        pl.semaphore_signal(barrier, inc=1, device_id=peer, device_id_type=MESH)


def wait_peers(peers):
    pl.semaphore_wait(pltpu.get_barrier_semaphore(), len(peers))


def remote(src, dst, send, recv, peer):
    return pltpu.make_async_remote_copy(
        src_ref=src, dst_ref=dst, send_sem=send, recv_sem=recv, device_id=peer, device_id_type=MESH
    )


HERE, MATE, ACROSS, PASS, BESIDE, PASS_BESIDE, ALONG, PASS_ALONG, LAST_BESIDE, LAST_ALONG, PASS_LAST = range(11)


class Gather:
    def __init__(self, own, place, rows, kind, bit, sems, slot, peers):
        self.own, self.place, self.rows, self.kind, self.bit = own, place, rows, kind, bit
        self.send, self.recv, self.here = sems
        self.slot = slot
        self.mate, self.across, self.near, self.sides = peers

    def part(self, flip_zero, flip_one):
        if self.kind == 1:
            return pl.ds(0, self.rows)
        if self.kind == 2:
            side = self.sides[self.bit]
            side = 1 - side if flip_zero else side
            return pl.ds(pl.multiple_of(side * (self.rows // 2), 16), self.rows // 2)
        zero = 1 - self.sides[0] if flip_zero else self.sides[0]
        one = 1 - self.sides[1] if flip_one else self.sides[1]
        return pl.ds(pl.multiple_of((zero + 2 * one) * (self.rows // 4), 16), self.rows // 4)

    def halved(self, part, second):
        h = part.size // 2
        return pl.ds(pl.multiple_of(part.start + (h if second else 0), 16), h)

    def copy(self, name):
        s = self.slot
        whole = pl.ds(0, self.rows)
        mine = self.part(False, False)
        if name == HERE:
            return pltpu.make_async_copy(self.own(whole), self.place(0, whole), self.here.at[s])

        def pass_on(rows, k):
            return self.place(2, rows), self.place(3, rows), self.mate, k

        def relay(rows, to, k):
            return self.place(2, rows), self.place(2, rows), self.near[to], k

        src, dst, peer, k = {
            MATE: lambda: (self.own(whole), self.place(1, whole), self.mate, 0),
            ACROSS: lambda: (self.own(mine), self.place(2, mine), self.across, 1),
            PASS: lambda: pass_on(mine, 2),
            BESIDE: lambda: relay(mine, self.bit, 3),
            PASS_BESIDE: lambda: pass_on(self.part(True, False), 4),
            ALONG: lambda: relay(mine, 1, 5),
            PASS_ALONG: lambda: pass_on(self.part(False, True), 6),
            LAST_BESIDE: lambda: relay(self.halved(self.part(False, True), False), 0, 7),
            LAST_ALONG: lambda: relay(self.halved(self.part(True, False), True), 1, 8),
            PASS_LAST: lambda: pass_on(self.part(True, True), 9),
        }[name]()
        return remote(src, dst, self.send.at[s, k], self.recv.at[s, k], peer)

    def names(self, stage):
        return {
            1: (((PASS,), (ACROSS,)),),
            2: (((BESIDE, PASS), (ACROSS,)), ((PASS_BESIDE,), (BESIDE,))),
            4: (
                ((BESIDE, ALONG, PASS), (ACROSS,)),
                ((LAST_BESIDE, LAST_ALONG, PASS_BESIDE, PASS_ALONG), (BESIDE, ALONG)),
                ((PASS_LAST,), (LAST_BESIDE, LAST_ALONG)),
            ),
        }[self.kind][stage]

    def stages(self):
        return {1: 1, 2: 2, 4: 3}[self.kind]

    def start(self):
        self.copy(ACROSS).start()
        self.copy(MATE).start()
        self.copy(HERE).start()

    def forward(self, stage):
        starts, waits = self.names(stage)
        for name in waits:
            self.copy(name).wait_recv()
        for name in starts:
            self.copy(name).start()

    def arrive_near(self):
        self.copy(HERE).wait()
        self.copy(MATE).wait_recv()

    def arrive_far(self):
        for stage in range(self.stages()):
            for name in self.names(stage)[0]:
                if name in (PASS, PASS_BESIDE, PASS_ALONG, PASS_LAST):
                    self.copy(name).wait_recv()

    def finish(self):
        for name in (MATE, ACROSS) + sum((self.names(stage)[0] for stage in range(self.stages())), ()):
            self.copy(name).wait_send()


def waves(column, frequency, quarter):
    angle = column * frequency
    turns = jnp.floor(angle * (2.0 / math.pi) + 0.5)
    rest = ((angle - turns * 1.5703125) - turns * 4.837512969970703125e-4) - turns * 7.549789948768648e-8
    quadrant = turns.astype(jnp.int32) + quarter
    z = rest * rest
    sine = ((-1.9515295891e-4 * z + 8.3321608736e-3) * z - 1.6666654611e-1) * z * rest + rest
    cosine = ((2.443315711809948e-5 * z - 1.388731625493765e-3) * z + 4.166664568298827e-2) * z * z - 0.5 * z + 1.0
    value = jnp.where(quadrant % 2 == 1, cosine, sine)
    return jnp.where((quadrant // 2) % 2 == 1, -value, value)


def gelu(v):
    return 0.5 * v * (1.0 + jnp.tanh(math.sqrt(2.0 / math.pi) * (v + 0.044715 * (v * v * v))))


def row_of(ref):
    return ref[...].reshape(1, ref.shape[0])


def column_of(row):
    return jnp.broadcast_to(row, (8, 128)).T[:, 0:1]


def forward_kernel(
    box_ref, mask_ref, qvb_ref, b1_ref, table_ref, ob_ref, g1_ref, s1_ref, c2_ref, g2_ref, s2_ref,
    tok_in, cot_in, rx_in, ry_in, lay_in, qkv_own, wo_own, w1_own, w2_own,
    probs_out, qkvt_out, ctxt_out, low_out, feat_out, unit_out, inv_out, nlow_out, pre_out, hid_out,
    block_out, dres_out, sums_out, wqkv_out, wo_out, w1_out, w2_out,
    low, feat, unit_rows, nlow, block_rows, dres_rows, lay, tokb, cotb, rxb, ryb, vec, rows_own, wqkv, wo, w1, w2, rows, cols, tabs, layer_in, qkvt, pbuf, ctxt, ctx, normed, pre,
    hid, acc, send, recv, here, out_sem, p_sem, in_sem,
):
    t, d = lax.axis_index("tensor"), lax.axis_index("dp")
    mate, across = {"tensor": xor_index(t, 1)}, {"tensor": xor_index(t, 2)}
    near = [{"dp": xor_index(d, 1)}, {"dp": xor_index(d, 2)}]
    peers = (mate, across, near, (d % 2, (d // 2) % 2))
    win, model = tokb.shape
    heads = 4 * HEADS_T
    cols_t = HEADS_T * HD
    hid_t = w1_own.shape[1]
    sems = (send, recv, here)
    f32, bf16 = jnp.float32, jnp.bfloat16
    block = 128

    everyone = [mate, across] + near
    signal_peers(everyone)
    own_rows = pl.ds(pl.multiple_of(t * win, win), win)
    loads = [
        pltpu.make_async_copy(src, dst, in_sem.at[k])
        for k, (src, dst) in enumerate(
            [(tok_in.at[own_rows], tokb), (rx_in.at[t], rxb), (ry_in.at[t], ryb), (cot_in.at[own_rows], cotb), (lay_in, lay)]
        )
    ]
    for c in loads:
        c.start()
    for k, ref in enumerate((ob_ref, g1_ref, s1_ref, c2_ref, g2_ref, s2_ref)):
        vec[k : k + 1, :] = row_of(ref)
    rows_own[...] = jnp.zeros_like(rows_own)
    rows_own[0:1, :] = row_of(b1_ref)
    rows_own[1 : 1 + HEADS_T, 0 : 2 * BUCKETS] = table_ref[...].astype(f32)
    rows_own[4:6, 0:cols_t] = qvb_ref[...]

    def piece_rows(r, s, count):
        return pl.ds(pl.multiple_of(r * count + s.start, 16), s.size)

    gathers = {}

    def chunk(name, own, place, count):
        gathers[name] = Gather(own, place, count, *WAYS[name], sems, name, peers)

    chunk(AT_R, lambda s: rows_own.at[s], lambda r, s: rows.at[r, s], 8)
    for n, name in enumerate((AT_Q, AT_K, AT_V)):
        chunk(
            name,
            lambda s, n=n: qkv_own.at[n, s],
            lambda r, s, n=n: wqkv.at[n, piece_rows(r, s, cols_t)],
            cols_t,
        )
    chunk(AT_O, lambda s: wo_own.at[s], lambda r, s: wo.at[piece_rows(r, s, cols_t)], cols_t)
    third = hid_t // 3
    for k in range(3):
        units = pl.ds(k * third, third)
        chunk(
            U0 + 2 * k, lambda s, units=units: w1_own.at[s, units], lambda r, s, units=units: w1.at[r, s, units], model
        )

        def moved(s, k=k):
            return pl.ds(pl.multiple_of(s.start + k * third, 16), s.size)

        chunk(
            D0 + 2 * k, lambda s, moved=moved: w2_own.at[moved(s)], lambda r, s, moved=moved: w2.at[r, moved(s)], third
        )

    def at_slot(phase, index=0):
        for name, stage in FORWARD.get((phase, index), ()):
            gathers[name].forward(stage)

    def at_loop(phase, index, count, first=0, step=1):
        for k in range(count):
            if (phase, first + step * k) in FORWARD:
                @pl.when(index == k)
                def _(k=k):
                    at_slot(phase, first + step * k)

    def near_pieces(names):
        for name in names:
            gathers[name].arrive_near()

    def far_pieces(names):
        for name in names:
            gathers[name].arrive_far()

    lane = lax.broadcasted_iota(jnp.int32, (1, 128), 1)
    quarter = jnp.where(lane >= LFREQ, 1, 0)
    frequency = jnp.exp((lane % LFREQ).astype(f32) * (-math.log(1000.0) / LFREQ))
    loads[0].wait()
    loads[4].wait()

    def layer_rows(i):
        sl = pl.ds(pl.multiple_of(i * block, block), block)
        box = box_ref[:, pl.ds(pl.multiple_of(t * win + i * block, block), block)].astype(f32)
        for m in range(4):
            feat[sl, 2 * LFREQ * m : 2 * LFREQ * (m + 1)] = waves(
                column_of(box[m : m + 1, :]), frequency, quarter
            ).astype(bf16)
        value = tokb[sl, :].astype(f32) + nn(feat[sl, :], lay[...])
        layer_in[sl, :] = value
        low[sl, :] = value.astype(bf16)
        at_loop(F_FEAT, i, 4)

    wait_peers(everyone)
    for name in SEND_ORDER:
        gathers[name].start()
    pl.loop(0, win // block)(layer_rows)

    def bias_columns(pieces):
        for r in pieces:
            turned = rows[r, :, 0:256].T
            for n, row in ((0, 4), (2, 5)):
                cols[n, pl.ds(r * cols_t, cols_t), :] = turned[0:cols_t, row : row + 1]
            tabs[HEADS_T * r : HEADS_T * (r + 1), :] = rows[r, 1 : 1 + HEADS_T, 0:128]

    def project(pieces):
        for n in range(3):
            for r in pieces:
                sl = pl.ds(r * cols_t, cols_t)
                value = nt(wqkv[n, sl, :], low[...])
                if n != 1:
                    value = value + cols[n, sl, :]
                qkvt[n, sl, :] = value.astype(bf16)

    near_pieces((AT_R, AT_Q, AT_K, AT_V))
    bias_columns((0, 1))
    project((0, 1))
    at_slot(F_NEAR)
    for c in loads[1:3]:
        c.wait()

    def table_row(h):
        return (tabs[pl.ds(h, 1), :] * 2048.0 + 32768.5).astype(jnp.int32) - 32768

    def p_copy(i, slot):
        return pltpu.make_async_copy(pbuf.at[slot], probs_out.at[pl.ds(2 * i, 2)], p_sem.at[slot])

    def two_heads(i):
        slot = i % 2
        sl = pl.ds(pl.multiple_of(i * 2 * HD, 2 * HD), 2 * HD)
        q = (qkvt[0, sl, :].astype(f32).T * HD ** (-0.5)).astype(bf16)
        tab = jnp.broadcast_to((table_row(2 * i) << 16) + table_row(2 * i + 1), (win, 128))
        bias = ([], [])
        for c in range(win // 128):
            at = slice(128 * c, 128 * c + 128)
            word = jnp.take_along_axis(tab, rxb[:, at], axis=1) + jnp.take_along_axis(
                tab, ryb[:, at] + BUCKETS, axis=1
            )
            second = word << 16
            bias[0].append((word - (second >> 16)).astype(f32) * 2.0**-27)
            bias[1].append(second.astype(f32) * 2.0**-27)

        @pl.when(i >= 2)
        def _():
            p_copy(i - 2, slot).wait()

        for u in range(2):
            rows_u = pl.ds(pl.multiple_of(i * 2 * HD + u * HD, HD), HD)
            s = nn(q[:, u * HD : (u + 1) * HD], qkvt[1, rows_u, :]) + jnp.concatenate(bias[u], axis=1)
            m = jnp.max(s, axis=1, keepdims=True)
            e = jnp.exp(s - m)
            p = e * (1.0 / jnp.sum(e, axis=1, keepdims=True))
            pbuf[slot, u] = p
            ctxt[rows_u, :] = nt(qkvt[2, rows_u, :], p.astype(bf16)).astype(bf16)
            at_loop(F_HEAD, i, heads // 2, u, 2)
        p_copy(i, slot).start()

    pl.loop(0, heads // 4)(two_heads)
    at_slot(F_FAR)
    far_pieces((AT_R, AT_Q, AT_K, AT_V))
    bias_columns((2, 3))
    project((2, 3))
    at_slot(F_BOTH)
    pl.loop(heads // 4, heads // 2)(two_heads)

    last = heads // 2
    outs = [
        (qkvt, qkvt_out), (ctxt, ctxt_out), (wqkv, wqkv_out), (low, low_out), (feat, feat_out),
    ]
    done = []

    def leave(src, dst):
        c = pltpu.make_async_copy(src, dst, out_sem.at[len(done)])
        c.start()
        done.append(c)

    for src, dst in outs:
        leave(src, dst)
    at_slot(F_OUT)
    near_pieces((AT_O,))
    far_pieces((AT_O,))
    leave(wo, wo_out)
    ctx[...] = ctxt[...].astype(f32).T.astype(bf16)
    at_slot(F_CONTEXT)

    @pl.loop(0, win // block)
    def _(i):
        sl = pl.ds(pl.multiple_of(i * block, block), block)
        value = layer_in[sl, :] + nn(ctx[sl, :], wo[...]) + vec[0:1, :]
        mean = jnp.mean(value, axis=1, keepdims=True)
        centered = value - mean
        inverse = lax.rsqrt(jnp.mean(centered * centered, axis=1, keepdims=True) + EPSILON)
        unit = centered * inverse
        unit_rows[sl, :] = unit
        inv_out[sl, :] = inverse
        value = unit * vec[1:2, :] + vec[2:3, :]
        normed[sl, :] = value
        nlow[sl, :] = value.astype(bf16)
        at_loop(F_NORM, i, 4)

    leave(unit_rows, unit_out)
    leave(nlow, nlow_out)
    near_pieces(range(U0, D2 + 1))
    for src, dst in ((w1, w1_out), (w2, w2_out)):
        leave(src.at[pl.ds(0, 2)], dst.at[pl.ds(0, 2)])
    for r in range(2):
        @pl.loop(0, win // 256)
        def _(i, r=r):
            sl = pl.ds(pl.multiple_of(i * 256, 256), 256)
            value = nn(nlow[sl, :], w1[r]) + rows[r, 0:1, :]
            pre[r, sl, :] = value
            low_hid = gelu(value).astype(bf16)
            hid[r, sl, :] = low_hid
            more = nn(low_hid, w2[r])
            acc[sl, :] = more if r == 0 else acc[sl, :] + more
            at_loop(F_UP, i, 2, 2 * r)

        leave(pre.at[r], pre_out.at[r])
        leave(hid.at[r], hid_out.at[r])

    for k in range(3):
        at_slot(F_THIRD, k)
        far_pieces((U0 + 2 * k, D0 + 2 * k))
        units = pl.ds(k * third, third)

        @pl.loop(2, 4)
        def _(r, units=units):
            value = nn(nlow[...], w1[r, :, units]) + rows[r, 0:1, units]
            pre[r, :, units] = value
            low_hid = gelu(value).astype(bf16)
            hid[r, :, units] = low_hid
            acc[...] += nn(low_hid, w2[r, units, :])

        at_slot(F_DONE, k)

        for src, dst in ((pre, pre_out), (hid, hid_out)):
            leave(src.at[pl.ds(2, 2), :, units], dst.at[pl.ds(2, 2), :, units])
        leave(w1.at[pl.ds(2, 2), :, units], w1_out.at[pl.ds(2, 2), :, units])
        leave(w2.at[pl.ds(2, 2), units], w2_out.at[pl.ds(2, 2), units])

    loads[3].wait()

    sums_out[...] = jnp.zeros_like(sums_out)

    @pl.loop(0, win // block)
    def _(i):
        sl = pl.ds(pl.multiple_of(i * block, block), block)
        value = normed[sl, :] + acc[sl, :] + vec[3:4, :]
        mean = jnp.mean(value, axis=1, keepdims=True)
        centered = value - mean
        inverse = lax.rsqrt(jnp.mean(centered * centered, axis=1, keepdims=True) + EPSILON)
        unit = centered * inverse
        block_rows[sl, :] = (unit * vec[4:5, :] + vec[5:6, :]).astype(bf16)
        mask = column_of(mask_ref[pl.ds((win // block) * t + i, 1), :].astype(f32))
        selected = mask * cotb[sl, :].astype(f32)
        scaled = selected * vec[4:5, :]
        mean_one = jnp.mean(scaled, axis=1, keepdims=True)
        mean_two = jnp.mean(scaled * unit, axis=1, keepdims=True)
        dres = (scaled - mean_one - unit * mean_two) * inverse
        dres_rows[sl, :] = dres
        for src, dst, k in ((block_rows, block_out, 30), (dres_rows, dres_out, 31)):
            pltpu.make_async_copy(src.at[sl], dst.at[sl], out_sem.at[k]).start()
        sums_out[0:1, :] += jnp.sum(selected * unit, axis=0, keepdims=True)
        sums_out[1:2, :] += jnp.sum(selected, axis=0, keepdims=True)
        sums_out[2:3, :] += jnp.sum(dres, axis=0, keepdims=True)
        sums_out[3:4, :] += jnp.sum(mask, axis=0, keepdims=True)

    for i in (last - 2, last - 1):
        p_copy(i, i % 2).wait()
    for c in done:
        c.wait()
    for src, dst, k in ((block_rows, block_out, 30), (dres_rows, dres_out, 31)):
        pltpu.make_async_copy(src, dst, out_sem.at[k]).wait()
    for g in gathers.values():
        g.finish()


def forward_window(small, large):
    wo_own, w1_own = large[6:8]
    win, model = large[2].shape[1], large[0].shape[1]
    cols_t, hid_t = wo_own.shape[0], w1_own.shape[1]
    heads = 4 * HEADS_T
    f32, bf16 = jnp.float32, jnp.bfloat16
    shape = jax.ShapeDtypeStruct
    here = pl.BlockSpec(memory_space=pltpu.VMEM)
    away = pl.BlockSpec(memory_space=pl.ANY)
    outs = [
        (shape((heads, win, win), f32), away),
        (shape((3, model, win), bf16), away),
        (shape((model, win), bf16), away),
        (shape((win, model), bf16), away),
        (shape((win, 8 * LFREQ), bf16), away),
        (shape((win, model), f32), away),
        (shape((win, 1), f32), here),
        (shape((win, model), bf16), away),
        (shape((4, win, hid_t), f32), away),
        (shape((4, win, hid_t), bf16), away),
        (shape((win, model), bf16), away),
        (shape((win, model), f32), away),
        (shape((8, model), f32), here),
        (shape((3, model, model), bf16), away),
        (shape((model, model), bf16), away),
        (shape((4, model, hid_t), bf16), away),
        (shape((4, hid_t, model), bf16), away),
    ]
    return pl.pallas_call(
        forward_kernel,
        in_specs=[here] * len(small) + [away] * len(large),
        out_specs=[spec for _, spec in outs],
        out_shape=[s for s, _ in outs],
        scratch_shapes=[
            pltpu.VMEM((win, model), bf16),
            pltpu.VMEM((win, 8 * LFREQ), bf16),
            pltpu.VMEM((win, model), f32),
            pltpu.VMEM((win, model), bf16),
            pltpu.VMEM((win, model), bf16),
            pltpu.VMEM((win, model), f32),
            pltpu.VMEM((8 * LFREQ, model), bf16),
            pltpu.VMEM((win, model), bf16),
            pltpu.VMEM((win, model), bf16),
            pltpu.VMEM((win, win), jnp.int32),
            pltpu.VMEM((win, win), jnp.int32),
            pltpu.VMEM((8, model), f32),
            pltpu.VMEM((8, model), f32),
            pltpu.VMEM((3, model, model), bf16),
            pltpu.VMEM((model, model), bf16),
            pltpu.VMEM((4, model, hid_t), bf16),
            pltpu.VMEM((4, hid_t, model), bf16),
            pltpu.VMEM((4, 8, model), f32),
            pltpu.VMEM((3, model, 1), f32),
            pltpu.VMEM((heads, 128), f32),
            pltpu.VMEM((win, model), f32),
            pltpu.VMEM((3, model, win), bf16),
            pltpu.VMEM((2, 2, win, win), f32),
            pltpu.VMEM((model, win), bf16),
            pltpu.VMEM((win, model), bf16),
            pltpu.VMEM((win, model), f32),
            pltpu.VMEM((4, win, hid_t), f32),
            pltpu.VMEM((4, win, hid_t), bf16),
            pltpu.VMEM((win, model), f32),
            pltpu.SemaphoreType.DMA((11, 10)),
            pltpu.SemaphoreType.DMA((11, 10)),
            pltpu.SemaphoreType.DMA((11,)),
            pltpu.SemaphoreType.DMA((32,)),
            pltpu.SemaphoreType.DMA((2,)),
            pltpu.SemaphoreType.DMA((5,)),
        ],
        compiler_params=pltpu.CompilerParams(
            vmem_limit_bytes=60 * 2**20, collective_id=0, has_side_effects=True
        ),
        name="forward_window",
    )(*small, *large)


def bits_of(size):
    return [1 << b for b in range(size.bit_length() - 1)]


def tn(a, b):
    return lax.dot_general(a, b, (((0,), (0,)), ((), ())), preferred_element_type=jnp.float32)


UNIT = 128


class Reduce:
    def __init__(self, slot, order, part, core, landing, final, extra, result, acc, sems, peers):
        self.slot, self.order, self.part, self.core, self.landing = slot, order, part, core, landing
        self.final, self.extra, self.result, self.acc = final, extra, result, acc
        self.send, self.recv, self.here = sems
        self.mate, self.partners, self.further, self.sides = peers
        self.total = core.at[0] if acc is None else acc
        self.steps = order[0] + order[1]

    def move(self, k, src, dst, peer):
        return remote(src, dst, self.send.at[self.slot, k], self.recv.at[self.slot, k], peer)

    def region(self, fixed, other=None):
        index = [slice(None)]
        for axis in (Z_FAR, Z_NEAR, Y):
            if axis == other:
                index.append(pl.ds(1 - self.sides[axis], 1))
            elif axis in fixed:
                index.append(pl.ds(self.sides[axis], 1))
            else:
                index.append(slice(None))
        return tuple(index)

    def pieces(self, stage):
        return (0,) if X in self.order[0][:stage] else (0, 1)

    def moves(self, stage, piece=None):
        axis = self.steps[stage]
        peer = self.partners[axis]
        if stage >= len(self.order[0]):
            done = self.order[1][: stage - len(self.order[0])]
            rows = self.region([a for a in (Z_FAR, Z_NEAR, Y) if a not in done])
            src = self.result.at[rows] if done else self.final
            return [self.move(10 + len(done), src, self.result.at[rows], peer)]
        fixed = self.order[0][:stage]
        if axis == X:
            return [self.move(2 + 2 * stage, self.core.at[(1,) + self.region(fixed)], self.landing[stage].at[0], peer)] if piece != 0 else []
        return [
            self.move(2 + 2 * stage + p, self.core.at[(p,) + self.region(fixed, axis)], self.landing[stage].at[p], peer)
            for p in self.pieces(stage)
            if piece in (None, p)
        ]

    def to_mate(self, piece):
        return self.move(piece, self.part(piece), self.core.at[piece], self.mate)

    def own_copy(self):
        rows = self.region((Z_FAR, Z_NEAR, Y))
        return pltpu.make_async_copy(self.final, self.result.at[rows], self.here.at[self.slot])

    def more(self, k):
        return self.move(13 + k, self.final_of(k), self.extra.at[k], self.further[k])

    def final_of(self, k):
        return self.final if k == 0 else self.extra.at[len(self.further) + k]

    def merge(self, piece, unit, half, value):
        at = (unit, half)
        value = value.reshape(2, 2, 16, value.shape[-1]) + self.core[(piece,) + at].astype(jnp.float32)
        if piece == 0:
            self.total[at] = value.astype(self.total.dtype)
        else:
            self.core[(1,) + at] = value.astype(jnp.bfloat16)

    def take(self, stage):
        for m in self.moves(stage):
            m.wait_recv()
        count = len(self.order[0])
        if stage == count:
            self.own_copy().wait()
        if stage >= count:
            return
        axis = self.steps[stage]
        rows = self.region(self.order[0][: stage + 1])
        for p in (0,) if axis == X else self.pieces(stage):
            dst = self.total if p == 0 else self.core.at[p]
            value = dst[rows].astype(jnp.float32) + self.landing[stage][p].astype(jnp.float32)
            if stage + 1 == count:
                self.final[...] = value.astype(jnp.bfloat16)
            else:
                dst[rows] = value.astype(dst.dtype)
        if stage + 1 == count:
            for k in range(len(self.further)):
                self.more(k).start()
                self.more(k).wait()
                total = self.final_of(k)[...].astype(jnp.float32) + self.extra[k].astype(jnp.float32)
                self.final_of(k + 1)[...] = total.astype(jnp.bfloat16)
            if self.further:
                self.final[...] = self.final_of(len(self.further))[...]
            self.own_copy().start()

    def go(self, stage, piece=None):
        if stage < len(self.order[0]) and self.steps[stage] != X and self.acc is not None and piece != 1:
            rows = self.region(self.order[0][:stage], self.steps[stage])
            self.core[(0,) + rows] = self.acc[rows].astype(jnp.bfloat16)
        for m in self.moves(stage, piece):
            m.start()

    def next(self, stage):
        self.take(stage)
        if stage + 1 < len(self.steps):
            self.go(stage + 1)

    def sent(self):
        for stage in range(len(self.steps)):
            for m in self.moves(stage):
                m.wait_send()


def landing_shapes(units, order):
    shapes, pieces, dims = [], 2, {Z_FAR: 2, Z_NEAR: 2, Y: 2}
    for axis in order[0]:
        if axis == X:
            pieces = 1
        else:
            dims[axis] = 1
        shapes.append((pieces, units, dims[Z_FAR], dims[Z_NEAR], dims[Y], 16))
    return shapes


def xor_level(level, k):
    for bit in (1, 2):
        if k & bit:
            level = xor_index(level, bit)
    return level


def gelu_slope(v):
    k = math.sqrt(2.0 / math.pi)
    square = v * v
    t = jnp.tanh(k * v * (1.0 + 0.044715 * square))
    return 0.5 * (1.0 + t) + (0.5 * k) * v * (1.0 - t * t) * (1.0 + 3 * 0.044715 * square)


SMALL = 16


def backward_kernel(
    n_dp, inv_ref, gain_ref, sums_ref, dres_in, hid_in, pre_in, unit_in, nlow_in, low_in, feat_in, qkvt_in, ctxt_in,
    probs_in, rx_in, ry_in, w1_in, w2_in, wo_in, wqkv_in, block_in,
    block_all, in_all, red1, red2, red3, lay_all, small_out,
    arena, hidb, preb, dres, unit, nlow, nlow_t, dn, low_rows, qkvb, ctxtb, dctx, lowb, featb, wob, rxb, ryb, hot, acc,
    part1, part2, part3, core1, core2, core3, landings, finals, extras, acc3, small, small_in, short,
    load_sem, send, recv, here, share_send, share_recv, small_send, small_recv, p_sem,
):
    t, d = lax.axis_index("tensor"), lax.axis_index("dp")
    mate, across = {"tensor": xor_index(t, 1)}, {"tensor": xor_index(t, 2)}
    beside = {"dp": xor_index(d, 1)}
    along = [None] + [{"dp": d + 2 * (xor_level((d // 2) % 4, k) - (d // 2) % 4)} for k in range(1, 4)]
    further = [{"dp": xor_index(d, bit)} for bit in bits_of(n_dp) if bit >= 8]
    partners = {X: across, Y: beside, Z_NEAR: along[1], Z_FAR: along[2]}
    peers = (mate, partners, further, {Y: d % 2, Z_NEAR: (d // 2) % 2, Z_FAR: (d // 4) % 2})
    sems = (send, recv, here)
    f32, bf16 = jnp.float32, jnp.bfloat16
    win, model = dres.shape
    heads = 4 * HEADS_T
    cols_t = HEADS_T * HD
    hid_t = model
    block = 128

    everyone = [mate, across, beside] + along[1:] + further
    signal_peers(everyone)

    def load(k, src, dst):
        return pltpu.make_async_copy(src, dst, load_sem.at[k])

    def w_rows(r):
        return pl.ds(r * hid_t, hid_t)

    def h_rows(r):
        return pl.ds(r * win, win)

    order = (3, 1, 2, 0)
    ld_dres = load(0, dres_in, dres)
    ld_hid = {r: load(1 + r, hid_in.at[r], hidb.at[h_rows(r)]) for r in order}
    ld_w2 = {r: load(5 + r, w2_in.at[r], arena.at[w_rows(r)]) for r in order}
    ld_w1 = {r: load(9 + r, w1_in.at[r], arena.at[w_rows(4 + r)]) for r in order}
    ld_pre = {r: load(13 + r, pre_in.at[r], preb.at[i % 2]) for i, r in enumerate(order)}
    ld_rest = [
        load(17 + k, src, dst)
        for k, (src, dst) in enumerate(
            [
                (nlow_in, nlow), (unit_in, unit), (ctxt_in, ctxtb), (wo_in, wob), (qkvt_in, qkvb), (low_in, lowb),
                (feat_in, featb), (rx_in.at[t], rxb), (ry_in.at[t], ryb),
            ]
        )
    ]
    ld_wqkv = [load(26 + n, wqkv_in.at[n], hidb.at[pl.ds(n * model, model)]) for n in range(3)]
    ld_dres.start()
    for r in order:
        ld_hid[r].start()
    for r in order[:2]:
        ld_pre[r].start()
    for r in order:
        ld_w2[r].start()
    ld_rest[0].start()
    for r in order:
        ld_w1[r].start()
    for c in ld_rest[1:]:
        c.start()

    def chunks(first, units, parts, core, result, acc=None):
        out, at = [], 0
        for k, (count, part) in enumerate(zip(units, parts)):
            rows = pl.ds(at, count)
            slot = first + k
            out.append(
                Reduce(
                    slot, ORDERS[slot], part, core.at[:, rows], landings[slot], finals[slot], extras[slot],
                    result.at[rows], None if acc is None else acc.at[rows], sems, peers,
                )
            )
            at += count
        return out

    third = hid_t // 3

    def pairs(ref):
        return [lambda p, k=k: ref.at[p, pl.ds(2 * k, 2)] for k in range(3)]

    s2 = chunks(0, [2] * 3, pairs(part2), core2, red2)
    s1 = chunks(3, [2] * 3, pairs(part1), core1, red1)
    s3 = chunks(
        6, [1] * 7,
        [lambda p, k=k: part2.at[p, pl.ds(k, 1)] for k in range(6)] + [lambda p: part3.at[p]],
        core3, red3, acc3,
    )
    lay_t = featb.shape[1] // 4

    def share(k, src, whole, rows, part=0, parts=1):
        def at(index):
            return whole.at[pl.ds(pl.multiple_of((index * parts + part) * rows, rows), rows)]

        def moved(j, from_ref, index, peer):
            return remote(from_ref, at(index), share_send.at[k, j], share_recv.at[k, j], peer)

        far = xor_index(t, 2)
        return {
            "here": pltpu.make_async_copy(src, at(t), share_send.at[k, 3]),
            "across": moved(0, src, t, across),
            "mate": moved(1, src, t, mate),
            "pass": moved(2, at(far), far, mate),
        }

    def share_start(c):
        for name in ("across", "mate", "here"):
            c[name].start()

    def share_pass(c):
        c["across"].wait_recv()
        c["pass"].start()

    def share_end(c):
        c["here"].wait()
        c["mate"].wait_recv()
        c["pass"].wait_recv()
        for name in ("across", "mate", "pass"):
            c[name].wait_send()

    quarter_win = win // 4
    sh_block = [
        share(k, block_in.at[pl.ds(k * quarter_win, quarter_win)], block_all, quarter_win, k, 4) for k in range(4)
    ]
    sh_in = share(4, low_rows, in_all, win)
    sh_lay = share(5, red3.at[pl.ds(6, 1)], lay_all, 1)
    bits = [mate, across, beside, along[1], along[2]] + further

    def small_move(k):
        return remote(small.at[k], small_in.at[k], small_send.at[k], small_recv.at[k], bits[k])

    def small_step(k):
        small_move(k).wait()
        small[k + 1] = small[k] + small_in[k]
        if k + 1 < len(bits):
            small_move(k + 1).start()

    named = dict(zip(range(A0, C6 + 1), s2 + s1 + s3))

    def run(what, stage):
        if what in named:
            named[what].next(stage)
        elif what == BLOCK:
            share_start(sh_block[stage])
        elif what == BLOCK_ON:
            share_pass(sh_block[stage])
        elif what == INPUT_ON:
            share_pass(sh_in)
        elif what == LAY:
            share_start(sh_lay)
        elif what == LAY_ON:
            share_pass(sh_lay)
        elif what == SMALL_STEP:
            small_step(stage)

    def at_slot(phase, index=0):
        for what, stage in SCHEDULE.get((phase, index), ()):
            run(what, stage)

    def at_loop(phase, index, count, first=0):
        for k in range(count):
            if (phase, first + k) in SCHEDULE:
                @pl.when(index == k)
                def _(k=k):
                    at_slot(phase, first + k)


    small[0] = jnp.zeros_like(small[0])
    small[0, 3:4, :] = sums_ref[2:3, :]
    small[0, 4:6, :] = sums_ref[0:2, :]
    small[0, 6:7, :] = sums_ref[3:4, :]

    def own_row(base, r):
        index = t
        for bit in (1, 2):
            if r & bit:
                index = xor_index(index, bit)
        return pl.ds(base + index, 1)

    ld_dres.wait()

    @pl.loop(0, win // block)
    def _(i):
        sl = pl.ds(pl.multiple_of(i * block, block), block)
        low_rows[sl, :] = dres[sl, :].astype(bf16)

    def grad_w2(r, c):
        sl = pl.ds(pl.multiple_of(c * third, third), third)
        return tn(hidb[h_rows(r), sl], low_rows[...])

    def grad_w1(r, c):
        sl = pl.ds(pl.multiple_of(c * third, third), third)
        return nn(nlow_t[sl, :], hidb[h_rows(r), :])

    def blocks(value):
        return value.reshape(value.shape[0] // UNIT, 2, 2, 2, 16, value.shape[1])

    def for_mate(group, grad, r, part):
        @pl.loop(0, 3)
        def _(c):
            part[r // 2, pl.ds(2 * c, 2)] = blocks(grad(r, c).astype(bf16))

        for g in group:
            g.to_mate(r // 2).start()

    def merge_all(g, piece, value):
        half = UNIT // 2
        for k in range(value.shape[0] // half):
            g.merge(piece, k // 2, k % 2, value[k * half : (k + 1) * half])

    def for_own(group, grad, r):
        for c, g in enumerate(group):
            g.to_mate(r // 2).wait_recv()
            merge_all(g, r // 2, grad(r, c))
            g.go(0, r // 2)

    for r in order[:2]:
        ld_hid[r].wait()
        if r == order[0]:
            for_mate((), grad_w2, r, part2)
            wait_peers(everyone)
            at_slot(START)
            for g in s2:
                g.to_mate(r // 2).start()
        else:
            for_mate(s2, grad_w2, r, part2)

    ld_rest[0].wait()
    nlow_t[...] = nlow[...].astype(f32).T.astype(bf16)
    for j, r in enumerate(order):
        ld_pre[r].wait()
        ld_w2[r].wait()
        ld_w1[r].wait()

        @pl.loop(0, 2)
        def _(i, j=j, r=r):
            count = win // 2
            sl = pl.ds(pl.multiple_of(i * count, count), count)
            hs = pl.ds(pl.multiple_of(r * win + i * count, count), count)
            dhid = nt(low_rows[sl, :], arena[w_rows(r), :])
            dpre = (dhid * gelu_slope(preb[j % 2, sl, :])).astype(bf16)
            hidb[hs, :] = dpre
            row = own_row(8, r)
            small[0, row, :] += jnp.sum(dpre.astype(f32), axis=0, keepdims=True)
            more = nt(dpre, arena[w_rows(4 + r), :])
            dn[sl, :] = more if j == 0 else dn[sl, :] + more
            at_loop(FFN, i, 2, 3 * j)

        if j + 2 < 4:
            ld_pre[order[j + 2]].start()
        if j < 2:
            for_mate(s1, grad_w1, r, part1)
        else:
            for_own(s1, grad_w1, r)
        if j == 0:
            for q in order[2:]:
                ld_hid[q].wait()
                for_own(s2, grad_w2, q)
        at_slot(FFN, 3 * j + 2)

    for c in ld_wqkv:
        c.start()

    def p_load(h, slot):
        return pltpu.make_async_copy(probs_in.at[h], preb.at[slot, :, pl.ds(0, win)], p_sem.at[slot])

    for h in range(2):
        p_load(h, h).start()
    for g in s2:
        for p in range(2):
            g.to_mate(p).wait_send()

    ld_rest[1].wait()

    @pl.loop(0, win // block)
    def _(i):
        sl = pl.ds(pl.multiple_of(i * block, block), block)
        up = dres[sl, :] + dn[sl, :]
        units = unit[sl, :]
        scaled = up * row_of(gain_ref)
        mean_one = jnp.mean(scaled, axis=1, keepdims=True)
        mean_two = jnp.mean(scaled * units, axis=1, keepdims=True)
        value = (scaled - mean_one - units * mean_two) * inv_ref[sl, :]
        dn[sl, :] = value
        low_rows[sl, :] = value.astype(bf16)
        small[0, 0:1, :] += jnp.sum(value, axis=0, keepdims=True)
        small[0, 1:2, :] += jnp.sum(up * units, axis=0, keepdims=True)
        small[0, 2:3, :] += jnp.sum(up, axis=0, keepdims=True)

    at_slot(NORM)
    for c in ld_rest[2:]:
        c.wait()

    @pl.loop(0, 4)
    def _(r):
        sl = pl.ds(pl.multiple_of(r * cols_t, cols_t), cols_t)
        dctx[sl, :] = nt(wob[sl, :], low_rows[...]).astype(bf16)

    at_slot(OUT)

    @pl.loop(0, heads)
    def _(h):
        slot = h % 2
        sl = pl.ds(pl.multiple_of(h * HD, HD), HD)
        dc_t = dctx[sl, :]
        dc = dc_t.astype(f32).T.astype(bf16)
        p_load(h, slot).wait()
        p = preb[slot, :, 0:win]
        dp = nn(dc, qkvb[2, sl, :])
        row_dot = jnp.sum(p * dp, axis=1, keepdims=True)
        ds = (p * (dp - row_dot)).astype(bf16)
        qkvb[2, sl, :] = nn(dc_t, p.astype(bf16)).astype(bf16)
        dq = nt(qkvb[1, sl, :], ds) * HD ** (-0.5)
        dk = nn(qkvb[0, sl, :], ds) * HD ** (-0.5)
        qkvb[0, sl, :] = dq.astype(bf16)
        qkvb[1, sl, :] = dk.astype(bf16)
        arena[pl.ds(pl.multiple_of(h * win, win), win), 0:win] = ds

        @pl.when(h + 2 < heads)
        def _():
            p_load(h + 2, slot).start()

        at_loop(HEAD, h, heads)

    for c in ld_wqkv:
        c.wait()
    def rows_of(r):
        return pl.ds(r * cols_t, cols_t)

    def grad_out(r):
        return nn(ctxtb[rows_of(r), :], low_rows[...])

    def grad_proj(n, r):
        return nn(qkvb[n, rows_of(r), :], lowb[...])

    halves = (lambda r: grad_proj(2, r), grad_out, lambda r: grad_proj(0, r), lambda r: grad_proj(1, r))
    sixth = UNIT // 2
    each = cols_t // sixth
    for r in (3, 1):
        for k, grad in enumerate(halves):
            value = grad(r).astype(bf16)
            for j in range(each):
                at = k * each + j
                part2[r // 2, at // 2, at % 2] = value[j * sixth : (j + 1) * sixth].reshape(2, 2, 16, model)
            if k % 2 == 1:
                for g in s3[:6][3 * (k // 2) : 3 * (k // 2) + 3]:
                    g.to_mate(r // 2).start()
    at_slot(SENT)
    for r in (2, 0):
        for k, grad in enumerate(halves):
            value = grad(r)
            for j in range(each):
                at = k * each + j
                g = s3[at // 2]
                if at % 2 == 0:
                    g.to_mate(r // 2).wait_recv()
                g.merge(r // 2, 0, at % 2, value[j * sixth : (j + 1) * sixth])
                if at % 2 == 1:
                    g.go(0, r // 2)
    at_slot(MERGED)

    @pl.loop(0, win // block)
    def _(i):
        sl = pl.ds(pl.multiple_of(i * block, block), block)
        value = dn[sl, :]
        for n in range(3):
            value = value + tn(qkvb[n, :, sl], hidb[pl.ds(n * model, model), :])
        dn[sl, :] = value
        at_loop(DLAYER, i, 4)

    low_rows[...] = dn[...].astype(bf16)

    def grad_lay(r):
        index = t
        for bit in (1, 2):
            if r & bit:
                index = xor_index(index, bit)
        return tn(featb[:, pl.ds(pl.multiple_of(index * lay_t, lay_t), lay_t)], low_rows[...])

    for r in (3, 1):
        part3[r // 2] = blocks(grad_lay(r).astype(bf16))
        s3[6].to_mate(r // 2).start()
    at_slot(LAYOUT)
    for_own(s3[6:], lambda r, c: grad_lay(r), 2)
    for_own(s3[6:], lambda r, c: grad_lay(r), 0)
    share_start(sh_in)

    ones = jnp.ones((8, win), bf16)
    short[...] = jnp.zeros_like(short)
    for n, at in ((0, 0), (2, cols_t)):
        total = nt(ones, qkvb[n])
        for r in range(4):
            short[r : r + 1, at : at + cols_t] = total[0:1, r * cols_t : (r + 1) * cols_t]

    acc[...] = jnp.zeros_like(acc)
    one, zero = bf16(1), bf16(0)
    hots = BUCKETS * ROWS
    @pl.loop(0, win // ROWS // 2)
    def _(i):
        total = None
        for u in range(2):
            at = pl.multiple_of(i * 2 * ROWS + u * ROWS, ROWS)
            x = rxb[pl.ds(at, ROWS), :].astype(f32).astype(bf16)
            y = ryb[pl.ds(at, ROWS), :].astype(f32).astype(bf16)
            for b in range(BUCKETS):
                hot[u, b * ROWS : (b + 1) * ROWS, :] = jnp.where(x == bf16(b), one, zero)
                hot[u, hots + b * ROWS : hots + (b + 1) * ROWS, :] = jnp.where(y == bf16(b), one, zero)
            left = jnp.concatenate(
                [arena[pl.ds(pl.multiple_of(h * win + at, ROWS), ROWS), 0:win] for h in range(heads)], axis=0
            )
            more = nt(left, hot[u])
            total = more if total is None else total + more
        acc[...] += total
        at_loop(TABLE, i, 16)

    row = lax.broadcasted_iota(jnp.int32, (ROWS, 2 * hots), 0)
    col = lax.broadcasted_iota(jnp.int32, (ROWS, 2 * hots), 1) % ROWS
    picked = jnp.concatenate(
        [
            jnp.sum(jnp.where(row == col, acc[h * ROWS : (h + 1) * ROWS, :], 0.0), axis=0, keepdims=True)
            for h in range(heads)
        ]
        + [jnp.zeros((16 - heads, 2 * hots), f32)],
        axis=0,
    )
    fold = (
        lax.broadcasted_iota(jnp.int32, (2 * hots, 128), 0) // ROWS
        == lax.broadcasted_iota(jnp.int32, (2 * hots, 128), 1)
    ).astype(f32)
    table = jnp.dot(picked, fold, preferred_element_type=f32, precision=lax.Precision.HIGHEST)
    for r in range(4):
        for a in range(HEADS_T):
            lane = 2 * cols_t + a * 2 * BUCKETS
            short[r : r + 1, lane : lane + 2 * BUCKETS] = table[
                r * HEADS_T + a : r * HEADS_T + a + 1, 0 : 2 * BUCKETS
            ]
    for r in range(4):
        small[0, own_row(12, r), :] = short[r : r + 1, :]

    small_move(0).start()
    at_slot(TAIL)
    for k in range(5, len(bits)):
        small_step(k)
    small_out[...] = small[len(bits)]
    for c in sh_block + [sh_in, sh_lay]:
        share_end(c)
    for g in s1 + s3:
        for p in range(2):
            g.to_mate(p).wait_send()
    for g in s2 + s1 + s3:
        g.sent()


def backward_window(n_dp, lay_rows, inv, gain, sums, dres, hid, pre, unit, nlow, low, feat, qkvt, ctxt, probs, rx, ry, w1, w2, wo, wqkv, block_own):
    win, model = dres.shape
    heads = 4 * HEADS_T
    cols_t = HEADS_T * HD
    lay_t = lay_rows // 4
    units = model // UNIT
    rest = (4 * cols_t + lay_t) // UNIT
    block = (2, 2, 2, 16, model)
    more = max(0, len(bits_of(n_dp)) - 3)
    levels = 5 + more
    sizes = [2] * 6 + [1] * 7
    f32, bf16 = jnp.float32, jnp.bfloat16
    shape = jax.ShapeDtypeStruct
    here = pl.BlockSpec(memory_space=pltpu.VMEM)
    away = pl.BlockSpec(memory_space=pl.ANY)
    outs = [
        (shape((4 * win, model), bf16), away),
        (shape((4 * win, model), bf16), away),
        (shape((units,) + block, bf16), away),
        (shape((units,) + block, bf16), away),
        (shape((rest,) + block, bf16), away),
        (shape((4,) + block, bf16), away),
        (shape((SMALL, model), f32), here),
    ]
    V = pltpu.VMEM
    S = pltpu.SemaphoreType.DMA
    return pl.pallas_call(
        functools.partial(backward_kernel, n_dp),
        in_specs=[here] * 3 + [away] * 17,
        out_specs=[spec for _, spec in outs],
        out_shape=[s for s, _ in outs],
        scratch_shapes=[
            V((8 * model, model), bf16), V((3 * model, model), bf16), V((2, win, model), f32), V((win, model), f32),
            V((win, model), f32), V((win, model), bf16), V((model, win), bf16), V((win, model), f32),
            V((win, model), bf16), V((3, model, win), bf16), V((model, win), bf16), V((model, win), bf16),
            V((win, model), bf16), V((win, lay_rows), bf16), V((model, model), bf16), V((win, win), jnp.int32),
            V((win, win), jnp.int32), V((2, 2 * BUCKETS * ROWS, win), bf16), V((heads * ROWS, 2 * BUCKETS * ROWS), f32),
            V((2, units) + block, bf16), V((2, units) + block, bf16), V((2, 1) + block, bf16),
            V((2, units) + block, bf16), V((2, units) + block, bf16), V((2, rest) + block, bf16),
            [[V(s + (model,), bf16) for s in landing_shapes(n, o)] for n, o in zip(sizes, ORDERS)],
            [V((n, 1, 1, 1, 16, model), bf16) for n in sizes],
            [V((2 * more + 1, n, 1, 1, 1, 16, model), bf16) for n in sizes], V((rest,) + block, f32),
            V((levels + 1, SMALL, model), f32), V((levels, SMALL, model), f32), V((8, model), f32),
            S((29,)), S((len(sizes), 13 + more)), S((len(sizes), 13 + more)), S((len(sizes),)), S((6, 4)), S((6, 3)),
            S((levels,)), S((levels,)), S((2,)),
        ],
        compiler_params=pltpu.CompilerParams(
            vmem_limit_bytes=63 * 2**20, collective_id=1, has_side_effects=True
        ),
        name="backward_window",
    )(inv, gain, sums, dres, hid, pre, unit, nlow, low, feat, qkvt, ctxt, probs, rx, ry, w1, w2, wo, wqkv, block_own)


def finish_kernel(
    rates, small_ref, block_in, in_in, red1, red2, red3, lay_in,
    block_out, in_out, lay_out, qkv_out, qvb_out, table_out, wo_out, ob_out, g1_out, s1_out, w1_out, b1_out, w2_out, c2_out,
    g2_out, s2_out, in_low, low1, low2, low3, lay_low, in_wide, wide1, wide2, wide3, lay_wide, block_low, load_sem, store_sem,
):
    t = lax.axis_index("tensor")
    cols_t = HEADS_T * HD
    inverse = 1.0 / small_ref[6:7, 0:1]
    order = [
        (in_in, in_low, in_wide, in_out, None),
        (red2, low2, wide2, w2_out, 4),
        (red1, low1, wide1, w1_out, 3),
        (red3, low3, wide3, None, None),
        (lay_in, lay_low, lay_wide, lay_out, 6),
    ]
    loads = [pltpu.make_async_copy(src, low, load_sem.at[k]) for k, (src, low, _, _, _) in enumerate(order)]
    for c in loads:
        c.start()
    whole_in = pltpu.make_async_copy(block_in, block_low, load_sem.at[5])
    whole_in.start()
    whole_out = pltpu.make_async_copy(block_low, block_out, store_sem.at[9])

    def row(ref, index, rate):
        ref[...] = (small_ref[index : index + 1, :] * (inverse * rates[rate])).reshape(ref.shape)

    for ref, index, rate in ((ob_out, 0, 1), (g1_out, 1, 2), (s1_out, 2, 2), (c2_out, 3, 4), (g2_out, 4, 5), (s2_out, 5, 5)):
        row(ref, index, rate)
    b1_out[...] = (small_ref[pl.ds(8 + t, 1), :] * (inverse * rates[3])).reshape(b1_out.shape)
    own = small_ref[pl.ds(12 + t, 1), :]
    for k in range(2):
        qvb_out[k : k + 1, :] = own[:, k * cols_t : (k + 1) * cols_t] * (inverse * rates[0])
    for a in range(HEADS_T):
        at = 2 * cols_t + a * 2 * BUCKETS
        table_out[a : a + 1, :] = own[:, at : at + 2 * BUCKETS] * (inverse * rates[7])

    stores = []

    def store(k, src, dst):
        stores.append(pltpu.make_async_copy(src, dst, store_sem.at[k]))

    for k, (_, low, wide, out, rate) in enumerate(order):
        loads[k].wait()
        step = 128
        if out is not None:
            factor = inverse if rate is None else inverse * rates[rate]

            @pl.loop(0, low.shape[0] // step)
            def _(i, low=low, wide=wide, out=out, factor=factor, k=k):
                sl = pl.ds(pl.multiple_of(i * step, step), step)
                wide[sl, :] = low[sl, :].astype(jnp.float32) * factor
                pltpu.make_async_copy(wide.at[sl], out.at[sl], store_sem.at[k]).start()

            store(k, wide, out)
            if k == 0:
                whole_in.wait()
                whole_out.start()
            continue
        parts = ((2, 0, 0), (None, 1, 1), (0, 2, 0), (1, 3, 0))
        for j, (n, at, rate) in enumerate(parts):
            sl = pl.ds(at * cols_t, cols_t)
            wide[sl, :] = low[sl, :].astype(jnp.float32) * (inverse * rates[rate])
            store(5 + j, wide.at[sl], wo_out if n is None else qkv_out.at[n])
            stores[-1].start()
    whole_out.wait()
    for c in stores:
        c.wait()


def finish(rates, small, block_all, in_all, sum1, sum2, sum3, lay_all, cols_t):
    f32, bf16 = jnp.float32, jnp.bfloat16
    shape = jax.ShapeDtypeStruct
    here = pl.BlockSpec(memory_space=pltpu.VMEM)
    away = pl.BlockSpec(memory_space=pl.ANY)
    model = in_all.shape[1]
    vector = (shape((model,), f32), here)
    outs = [
        (shape(block_all.shape, bf16), away),
        (shape(in_all.shape, f32), away),
        (shape(lay_all.shape, f32), away),
        (shape((3, cols_t, model), f32), away),
        (shape((2, cols_t), f32), here),
        (shape((HEADS_T, 2 * BUCKETS), f32), here),
        (shape((cols_t, model), f32), away),
        vector, vector, vector,
        (shape(sum1.shape, f32), away),
        vector,
        (shape(sum2.shape, f32), away),
        vector, vector, vector,
    ]
    wide = [in_all, sum1, sum2, sum3, lay_all]
    return pl.pallas_call(
        finish_kernel,
        in_specs=[pl.BlockSpec(memory_space=pltpu.SMEM), here] + [away] * 6,
        out_specs=[spec for _, spec in outs],
        out_shape=[s for s, _ in outs],
        scratch_shapes=[pltpu.VMEM(v.shape, bf16) for v in wide]
        + [pltpu.VMEM(v.shape, f32) for v in wide]
        + [pltpu.VMEM(block_all.shape, bf16), pltpu.SemaphoreType.DMA((6,)), pltpu.SemaphoreType.DMA((10,))],
        compiler_params=pltpu.CompilerParams(vmem_limit_bytes=60 * 2**20),
        name="finish",
    )(rates, small, block_all, in_all, sum1, sum2, sum3, lay_all)


def local(
    n_dp, n_t,
    tokens_in, box_coords, rel_x, rel_y, mask_tokens, cotangent, layout_weight, qkv_weight, qv_bias,
    bias_table, out_weight, out_bias, ln1_gain, ln1_bias, ffn_in_weight, ffn_in_bias, ffn_out_weight,
    ffn_out_bias, ln2_gain, ln2_bias, group_rates,
):
    (
        probs, qkvt, context_t, layer_low, features, unit_one, inverse_one, normed_low, pre_all, hid_all,
        block_own, dresid_two, sums, wqkv, wo, w1, w2,
    ) = forward_window(
        [
            box_coords.T, mask_tokens.reshape(-1, 128), qv_bias, ffn_in_bias, bias_table.T,
            out_bias, ln1_gain, ln1_bias, ffn_out_bias, ln2_gain, ln2_bias,
        ],
        [
            tokens_in, cotangent, rel_x, rel_y, layout_weight, jnp.transpose(qkv_weight, (0, 2, 1)), out_weight,
            ffn_in_weight, ffn_out_weight,
        ],
    )
    block_all, in_all, sum1, sum2, sum3, lay_all, small = backward_window(
        n_dp, layout_weight.shape[0], inverse_one, ln1_gain, sums, dresid_two, hid_all, pre_all, unit_one, normed_low,
        layer_low, features, qkvt, context_t, probs, rel_x, rel_y, w1, w2, wo, wqkv, block_own,
    )
    sums = [v.reshape(-1, v.shape[-1]) for v in (sum1, sum2, sum3, lay_all)]
    out = list(finish(group_rates, small, block_all, in_all, *sums, out_weight.shape[0]))
    out[3] = jnp.transpose(out[3], (0, 2, 1))
    out[5] = out[5].T
    return tuple(out)


def solution(mesh):
    placed = (
        P("dp", None), P("dp", None), P("dp", None, None), P("dp", None, None), P("dp"), P("dp", None),
        P(), P(None, None, "tensor"), P(None, "tensor"), P(None, "tensor"), P("tensor", None),
        P(), P(), P(), P(None, "tensor"), P("tensor"), P("tensor", None), P(), P(), P(), P(),
    )
    return jax.shard_map(
        functools.partial(local, mesh.shape["dp"], mesh.shape["tensor"]),
        mesh=mesh,
        in_specs=placed,
        out_specs=(
            P("dp", None), P("dp", None), P(), P(None, None, "tensor"), P(None, "tensor"),
            P(None, "tensor"), P("tensor", None), P(), P(), P(), P(None, "tensor"), P("tensor"),
            P("tensor", None), P(), P(), P(),
        ),
        check_vma=False,
    )
```

```python
import functools
import math

import jax
import jax.numpy as jnp
from jax import lax
from jax.experimental import pallas as pl
from jax.experimental.pallas import tpu as pltpu
from jax.sharding import PartitionSpec as P

HD = 64
LFREQ = 64
BUCKETS = 32
EPSILON = 1e-05
ROWS = 16
HEADS_T = 3
MESH = pl.DeviceIdType.MESH

F_FEAT, F_NEAR, F_HEAD, F_FAR, F_BOTH, F_OUT, F_CONTEXT, F_NORM, F_UP, F_THIRD, F_DONE = range(11)
AT_R, AT_Q, AT_K, AT_V, AT_O, U0, D0, U1, D1, U2, D2 = range(11)
WAYS = {
    AT_R: (1, 0),
    AT_Q: (2, 0),
    AT_K: (2, 0),
    AT_V: (2, 1),
    AT_O: (2, 0),
    U0: (4, 0),
    D0: (4, 0),
    U1: (4, 0),
    D1: (2, 1),
    U2: (2, 0),
    D2: (1, 0),
}
SEND_ORDER = (AT_Q, AT_V, AT_K, D0, AT_R, U0, U1, AT_O, D1, U2, D2)
FORWARD = {
    (F_NEAR, 0): ((AT_Q, 0),),
    (F_HEAD, 1): ((AT_V, 0),),
    (F_HEAD, 2): ((AT_K, 0), (AT_Q, 1),),
    (F_HEAD, 3): ((D0, 0),),
    (F_HEAD, 4): ((AT_V, 1), (AT_R, 0), (U0, 0), (AT_K, 1),),
    (F_HEAD, 5): ((U1, 0), (D0, 1),),
    (F_HEAD, 6): ((AT_O, 0),),
    (F_HEAD, 7): ((U0, 1),),
    (F_HEAD, 9): ((U1, 1), (D0, 2), (D1, 0), (AT_O, 1),),
    (F_HEAD, 10): ((U0, 2),),
    (F_CONTEXT, 0): ((U2, 0),),
    (F_NORM, 1): ((U1, 2),),
    (F_NORM, 3): ((D1, 1),),
    (F_UP, 2): ((U2, 1), (D2, 0),),
}

START, FFN, NORM, OUT, HEAD, SENT, MERGED, DLAYER, LAYOUT, TABLE, TAIL = range(11)
A0, A1, A2, B0, B1, B2, C0, C1, C2, C3, C4, C5, C6, BLOCK, BLOCK_ON, INPUT_ON, LAY, LAY_ON, SMALL_STEP = range(19)
X, Y, Z_NEAR, Z_FAR = range(4)
ORDERS = (
    ((Z_NEAR, Z_FAR, X, Y), (Z_FAR, Z_NEAR, Y)),
    ((Y, X, Z_NEAR, Z_FAR), (Z_FAR, Z_NEAR, Y)),
    ((X, Y, Z_NEAR, Z_FAR), (Z_FAR, Z_NEAR, Y)),
    ((Y, X, Z_NEAR, Z_FAR), (Z_FAR, Z_NEAR, Y)),
    ((X, Y, Z_NEAR, Z_FAR), (Z_FAR, Z_NEAR, Y)),
    ((Z_NEAR, Z_FAR, X, Y), (Z_FAR, Z_NEAR, Y)),
    ((Y, X, Z_NEAR, Z_FAR), (Z_FAR, Z_NEAR, Y)),
    ((Y, X, Z_NEAR, Z_FAR), (Z_FAR, Z_NEAR, Y)),
    ((Y, X, Z_NEAR, Z_FAR), (Z_FAR, Z_NEAR, Y)),
    ((X, Y, Z_NEAR, Z_FAR), (Y, Z_FAR, Z_NEAR)),
    ((X, Z_NEAR, Z_FAR, Y), (Z_FAR, Z_NEAR, Y)),
    ((Y, X, Z_NEAR, Z_FAR), (Z_FAR, Z_NEAR, Y)),
    ((X, Y, Z_NEAR, Z_FAR), (Z_FAR, Z_NEAR, Y)),
)
SCHEDULE = {
    (START, 0): ((BLOCK, 2),),
    (FFN, 3): ((BLOCK_ON, 2),),
    (FFN, 10): ((A0, 0), (A2, 0),),
    (FFN, 11): ((A1, 0),),
    (HEAD, 2): ((A2, 1), (B1, 0),),
    (HEAD, 4): ((A0, 1), (B2, 0), (B0, 0), (A1, 1),),
    (HEAD, 5): ((BLOCK, 0),),
    (HEAD, 7): ((A0, 2),),
    (HEAD, 9): ((B1, 1),),
    (HEAD, 11): ((A0, 3), (B0, 1),),
    (SENT, 0): ((B1, 2), (B2, 1),),
    (MERGED, 0): ((A2, 2), (A1, 2), (A0, 4), (B0, 2), (B2, 2), (B1, 3), (BLOCK_ON, 0),),
    (LAYOUT, 0): ((C0, 0), (A2, 3),),
    (TABLE, 0): ((C1, 0), (C4, 0), (C2, 0), (C0, 1), (A0, 5), (B0, 3), (C3, 0), (B1, 4),),
    (TABLE, 3): ((C5, 0), (A2, 4),),
    (TABLE, 4): ((C4, 1), (B2, 3), (C6, 0), (C0, 2),),
    (TABLE, 5): ((BLOCK, 1), (BLOCK, 3), (B0, 4),),
    (TABLE, 7): ((B1, 5),),
    (TABLE, 8): ((A1, 3),),
    (TABLE, 12): ((A2, 5),),
    (TABLE, 13): ((C6, 1),),
    (TABLE, 14): ((C0, 3), (B2, 4),),
    (TABLE, 15): ((B0, 5), (A1, 4), (C3, 1), (C6, 2), (C0, 4), (B2, 5), (INPUT_ON, 0),),
    (TAIL, 0): (
        (C1, 1), (B1, 6), (A2, 6), (A0, 6), (C4, 2), (A1, 5), (C3, 2), (C2, 1), (SMALL_STEP, 0), (B0, 6), (C6, 3),
        (C0, 5), (C5, 1), (C1, 2), (C3, 3), (C2, 2), (B2, 6), (C6, 4), (C4, 3), (C5, 2), (BLOCK_ON, 1), (C1, 3),
        (C2, 3), (C6, 5), (C4, 4), (A1, 6), (C5, 3), (BLOCK_ON, 3), (C1, 4), (SMALL_STEP, 1), (C0, 6), (C3, 4),
        (C2, 4), (C4, 5), (C5, 4), (C6, 6), (LAY, 0), (C1, 5), (SMALL_STEP, 2), (C2, 5), (C3, 5), (C4, 6), (C5, 5),
        (SMALL_STEP, 3), (C1, 6), (LAY_ON, 0), (C3, 6), (C2, 6), (SMALL_STEP, 4), (C5, 6),
    ),
}


def nt(a, b):
    return lax.dot_general(a, b, (((1,), (1,)), ((), ())), preferred_element_type=jnp.float32)


def nn(a, b):
    return jnp.dot(a, b, preferred_element_type=jnp.float32)


def xor_index(index, bit):
    return index + bit - 2 * bit * ((index // bit) % 2)


def signal_peers(peers):
    barrier = pltpu.get_barrier_semaphore()
    for peer in peers:
        pl.semaphore_signal(barrier, inc=1, device_id=peer, device_id_type=MESH)


def wait_peers(peers):
    pl.semaphore_wait(pltpu.get_barrier_semaphore(), len(peers))


def remote(src, dst, send, recv, peer):
    return pltpu.make_async_remote_copy(
        src_ref=src, dst_ref=dst, send_sem=send, recv_sem=recv, device_id=peer, device_id_type=MESH
    )


HERE, MATE, ACROSS, PASS, BESIDE, PASS_BESIDE, ALONG, PASS_ALONG, LAST_BESIDE, LAST_ALONG, PASS_LAST = range(11)


class Gather:
    def __init__(self, own, place, rows, kind, bit, sems, slot, peers):
        self.own, self.place, self.rows, self.kind, self.bit = own, place, rows, kind, bit
        self.send, self.recv, self.here = sems
        self.slot = slot
        self.mate, self.across, self.near, self.sides = peers

    def part(self, flip_zero, flip_one):
        if self.kind == 1:
            return pl.ds(0, self.rows)
        if self.kind == 2:
            side = self.sides[self.bit]
            side = 1 - side if flip_zero else side
            return pl.ds(pl.multiple_of(side * (self.rows // 2), 16), self.rows // 2)
        zero = 1 - self.sides[0] if flip_zero else self.sides[0]
        one = 1 - self.sides[1] if flip_one else self.sides[1]
        return pl.ds(pl.multiple_of((zero + 2 * one) * (self.rows // 4), 16), self.rows // 4)

    def halved(self, part, second):
        h = part.size // 2
        return pl.ds(pl.multiple_of(part.start + (h if second else 0), 16), h)

    def copy(self, name):
        s = self.slot
        whole = pl.ds(0, self.rows)
        mine = self.part(False, False)
        if name == HERE:
            return pltpu.make_async_copy(self.own(whole), self.place(0, whole), self.here.at[s])

        def pass_on(rows, k):
            return self.place(2, rows), self.place(3, rows), self.mate, k

        def relay(rows, to, k):
            return self.place(2, rows), self.place(2, rows), self.near[to], k

        src, dst, peer, k = {
            MATE: lambda: (self.own(whole), self.place(1, whole), self.mate, 0),
            ACROSS: lambda: (self.own(mine), self.place(2, mine), self.across, 1),
            PASS: lambda: pass_on(mine, 2),
            BESIDE: lambda: relay(mine, self.bit, 3),
            PASS_BESIDE: lambda: pass_on(self.part(True, False), 4),
            ALONG: lambda: relay(mine, 1, 5),
            PASS_ALONG: lambda: pass_on(self.part(False, True), 6),
            LAST_BESIDE: lambda: relay(self.halved(self.part(False, True), False), 0, 7),
            LAST_ALONG: lambda: relay(self.halved(self.part(True, False), True), 1, 8),
            PASS_LAST: lambda: pass_on(self.part(True, True), 9),
        }[name]()
        return remote(src, dst, self.send.at[s, k], self.recv.at[s, k], peer)

    def names(self, stage):
        return {
            1: (((PASS,), (ACROSS,)),),
            2: (((BESIDE, PASS), (ACROSS,)), ((PASS_BESIDE,), (BESIDE,))),
            4: (
                ((BESIDE, ALONG, PASS), (ACROSS,)),
                ((LAST_BESIDE, LAST_ALONG, PASS_BESIDE, PASS_ALONG), (BESIDE, ALONG)),
                ((PASS_LAST,), (LAST_BESIDE, LAST_ALONG)),
            ),
        }[self.kind][stage]

    def stages(self):
        return {1: 1, 2: 2, 4: 3}[self.kind]

    def start(self):
        self.copy(ACROSS).start()
        self.copy(MATE).start()
        self.copy(HERE).start()

    def forward(self, stage):
        starts, waits = self.names(stage)
        for name in waits:
            self.copy(name).wait_recv()
        for name in starts:
            self.copy(name).start()

    def arrive_near(self):
        self.copy(HERE).wait()
        self.copy(MATE).wait_recv()

    def arrive_far(self):
        for stage in range(self.stages()):
            for name in self.names(stage)[0]:
                if name in (PASS, PASS_BESIDE, PASS_ALONG, PASS_LAST):
                    self.copy(name).wait_recv()

    def finish(self):
        for name in (MATE, ACROSS) + sum((self.names(stage)[0] for stage in range(self.stages())), ()):
            self.copy(name).wait_send()


def waves(column, frequency, quarter):
    angle = column * frequency
    turns = jnp.floor(angle * (2.0 / math.pi) + 0.5)
    rest = ((angle - turns * 1.5703125) - turns * 4.837512969970703125e-4) - turns * 7.549789948768648e-8
    quadrant = turns.astype(jnp.int32) + quarter
    z = rest * rest
    sine = ((-1.9515295891e-4 * z + 8.3321608736e-3) * z - 1.6666654611e-1) * z * rest + rest
    cosine = ((2.443315711809948e-5 * z - 1.388731625493765e-3) * z + 4.166664568298827e-2) * z * z - 0.5 * z + 1.0
    value = jnp.where(quadrant % 2 == 1, cosine, sine)
    return jnp.where((quadrant // 2) % 2 == 1, -value, value)


def gelu(v):
    return 0.5 * v * (1.0 + jnp.tanh(math.sqrt(2.0 / math.pi) * (v + 0.044715 * (v * v * v))))


def row_of(ref):
    return ref[...].reshape(1, ref.shape[0])


def column_of(row):
    return jnp.broadcast_to(row, (8, 128)).T[:, 0:1]


def forward_kernel(
    box_ref, mask_ref, qvb_ref, b1_ref, table_ref, ob_ref, g1_ref, s1_ref, c2_ref, g2_ref, s2_ref,
    tok_in, cot_in, rx_in, ry_in, lay_in, qkv_own, wo_own, w1_own, w2_own,
    probs_out, qkvt_out, ctxt_out, low_out, feat_out, unit_out, inv_out, nlow_out, pre_out, hid_out,
    block_out, dres_out, sums_out, wqkv_out, wo_out, w1_out, w2_out,
    low, feat, unit_rows, nlow, block_rows, dres_rows, lay, tokb, cotb, rxb, ryb, vec, rows_own, wqkv, wo, w1, w2, rows, cols, tabs, layer_in, qkvt, pbuf, ctxt, ctx, normed, pre,
    hid, acc, send, recv, here, out_sem, p_sem, in_sem,
):
    t, d = lax.axis_index("tensor"), lax.axis_index("dp")
    mate, across = {"tensor": xor_index(t, 1)}, {"tensor": xor_index(t, 2)}
    near = [{"dp": xor_index(d, 1)}, {"dp": xor_index(d, 2)}]
    peers = (mate, across, near, (d % 2, (d // 2) % 2))
    win, model = tokb.shape
    heads = 4 * HEADS_T
    cols_t = HEADS_T * HD
    hid_t = w1_own.shape[1]
    sems = (send, recv, here)
    f32, bf16 = jnp.float32, jnp.bfloat16
    block = 128

    everyone = [mate, across] + near
    signal_peers(everyone)
    own_rows = pl.ds(pl.multiple_of(t * win, win), win)
    loads = [
        pltpu.make_async_copy(src, dst, in_sem.at[k])
        for k, (src, dst) in enumerate(
            [(tok_in.at[own_rows], tokb), (rx_in.at[t], rxb), (ry_in.at[t], ryb), (cot_in.at[own_rows], cotb), (lay_in, lay)]
        )
    ]
    for c in loads:
        c.start()
    for k, ref in enumerate((ob_ref, g1_ref, s1_ref, c2_ref, g2_ref, s2_ref)):
        vec[k : k + 1, :] = row_of(ref)
    rows_own[...] = jnp.zeros_like(rows_own)
    rows_own[0:1, :] = row_of(b1_ref)
    rows_own[1 : 1 + HEADS_T, 0 : 2 * BUCKETS] = table_ref[...].astype(f32)
    rows_own[4:6, 0:cols_t] = qvb_ref[...]

    def piece_rows(r, s, count):
        return pl.ds(pl.multiple_of(r * count + s.start, 16), s.size)

    gathers = {}

    def chunk(name, own, place, count):
        gathers[name] = Gather(own, place, count, *WAYS[name], sems, name, peers)

    chunk(AT_R, lambda s: rows_own.at[s], lambda r, s: rows.at[r, s], 8)
    for n, name in enumerate((AT_Q, AT_K, AT_V)):
        chunk(
            name,
            lambda s, n=n: qkv_own.at[n, s],
            lambda r, s, n=n: wqkv.at[n, piece_rows(r, s, cols_t)],
            cols_t,
        )
    chunk(AT_O, lambda s: wo_own.at[s], lambda r, s: wo.at[piece_rows(r, s, cols_t)], cols_t)
    third = hid_t // 3
    for k in range(3):
        units = pl.ds(k * third, third)
        chunk(
            U0 + 2 * k, lambda s, units=units: w1_own.at[s, units], lambda r, s, units=units: w1.at[r, s, units], model
        )

        def moved(s, k=k):
            return pl.ds(pl.multiple_of(s.start + k * third, 16), s.size)

        chunk(
            D0 + 2 * k, lambda s, moved=moved: w2_own.at[moved(s)], lambda r, s, moved=moved: w2.at[r, moved(s)], third
        )

    def at_slot(phase, index=0):
        for name, stage in FORWARD.get((phase, index), ()):
            gathers[name].forward(stage)

    def at_loop(phase, index, count, first=0, step=1):
        for k in range(count):
            if (phase, first + step * k) in FORWARD:
                @pl.when(index == k)
                def _(k=k):
                    at_slot(phase, first + step * k)

    def near_pieces(names):
        for name in names:
            gathers[name].arrive_near()

    def far_pieces(names):
        for name in names:
            gathers[name].arrive_far()

    lane = lax.broadcasted_iota(jnp.int32, (1, 128), 1)
    quarter = jnp.where(lane >= LFREQ, 1, 0)
    frequency = jnp.exp((lane % LFREQ).astype(f32) * (-math.log(1000.0) / LFREQ))
    loads[0].wait()
    loads[4].wait()

    def layer_rows(i):
        sl = pl.ds(pl.multiple_of(i * block, block), block)
        box = box_ref[:, pl.ds(pl.multiple_of(t * win + i * block, block), block)].astype(f32)
        for m in range(4):
            feat[sl, 2 * LFREQ * m : 2 * LFREQ * (m + 1)] = waves(
                column_of(box[m : m + 1, :]), frequency, quarter
            ).astype(bf16)
        value = tokb[sl, :].astype(f32) + nn(feat[sl, :], lay[...])
        layer_in[sl, :] = value
        low[sl, :] = value.astype(bf16)
        at_loop(F_FEAT, i, 4)

    wait_peers(everyone)
    for name in SEND_ORDER:
        gathers[name].start()
    pl.loop(0, win // block)(layer_rows)

    def bias_columns(pieces):
        for r in pieces:
            turned = rows[r, :, 0:256].T
            for n, row in ((0, 4), (2, 5)):
                cols[n, pl.ds(r * cols_t, cols_t), :] = turned[0:cols_t, row : row + 1]
            tabs[HEADS_T * r : HEADS_T * (r + 1), :] = rows[r, 1 : 1 + HEADS_T, 0:128]

    def project(pieces):
        for n in range(3):
            for r in pieces:
                sl = pl.ds(r * cols_t, cols_t)
                value = nt(wqkv[n, sl, :], low[...])
                if n != 1:
                    value = value + cols[n, sl, :]
                qkvt[n, sl, :] = value.astype(bf16)

    near_pieces((AT_R, AT_Q, AT_K, AT_V))
    bias_columns((0, 1))
    project((0, 1))
    at_slot(F_NEAR)
    for c in loads[1:3]:
        c.wait()

    def table_row(h):
        return (tabs[pl.ds(h, 1), :] * 2048.0 + 32768.5).astype(jnp.int32) - 32768

    def p_copy(i, slot):
        return pltpu.make_async_copy(pbuf.at[slot], probs_out.at[pl.ds(2 * i, 2)], p_sem.at[slot])

    def two_heads(i):
        slot = i % 2
        sl = pl.ds(pl.multiple_of(i * 2 * HD, 2 * HD), 2 * HD)
        q = (qkvt[0, sl, :].astype(f32).T * HD ** (-0.5)).astype(bf16)
        tab = jnp.broadcast_to((table_row(2 * i) << 16) + table_row(2 * i + 1), (win, 128))
        bias = ([], [])
        for c in range(win // 128):
            at = slice(128 * c, 128 * c + 128)
            word = jnp.take_along_axis(tab, rxb[:, at], axis=1) + jnp.take_along_axis(
                tab, ryb[:, at] + BUCKETS, axis=1
            )
            second = word << 16
            bias[0].append((word - (second >> 16)).astype(f32) * 2.0**-27)
            bias[1].append(second.astype(f32) * 2.0**-27)

        @pl.when(i >= 2)
        def _():
            p_copy(i - 2, slot).wait()

        for u in range(2):
            rows_u = pl.ds(pl.multiple_of(i * 2 * HD + u * HD, HD), HD)
            s = nn(q[:, u * HD : (u + 1) * HD], qkvt[1, rows_u, :]) + jnp.concatenate(bias[u], axis=1)
            m = jnp.max(s, axis=1, keepdims=True)
            e = jnp.exp(s - m)
            p = e * (1.0 / jnp.sum(e, axis=1, keepdims=True))
            pbuf[slot, u] = p
            ctxt[rows_u, :] = nt(qkvt[2, rows_u, :], p.astype(bf16)).astype(bf16)
            at_loop(F_HEAD, i, heads // 2, u, 2)
        p_copy(i, slot).start()

    pl.loop(0, heads // 4)(two_heads)
    at_slot(F_FAR)
    far_pieces((AT_R, AT_Q, AT_K, AT_V))
    bias_columns((2, 3))
    project((2, 3))
    at_slot(F_BOTH)
    pl.loop(heads // 4, heads // 2)(two_heads)

    last = heads // 2
    outs = [
        (qkvt, qkvt_out), (ctxt, ctxt_out), (wqkv, wqkv_out), (low, low_out), (feat, feat_out),
    ]
    done = []

    def leave(src, dst):
        c = pltpu.make_async_copy(src, dst, out_sem.at[len(done)])
        c.start()
        done.append(c)

    for src, dst in outs:
        leave(src, dst)
    at_slot(F_OUT)
    near_pieces((AT_O,))
    far_pieces((AT_O,))
    leave(wo, wo_out)
    ctx[...] = ctxt[...].astype(f32).T.astype(bf16)
    at_slot(F_CONTEXT)

    @pl.loop(0, win // block)
    def _(i):
        sl = pl.ds(pl.multiple_of(i * block, block), block)
        value = layer_in[sl, :] + nn(ctx[sl, :], wo[...]) + vec[0:1, :]
        mean = jnp.mean(value, axis=1, keepdims=True)
        centered = value - mean
        inverse = lax.rsqrt(jnp.mean(centered * centered, axis=1, keepdims=True) + EPSILON)
        unit = centered * inverse
        unit_rows[sl, :] = unit
        inv_out[sl, :] = inverse
        value = unit * vec[1:2, :] + vec[2:3, :]
        normed[sl, :] = value
        nlow[sl, :] = value.astype(bf16)
        at_loop(F_NORM, i, 4)

    leave(unit_rows, unit_out)
    leave(nlow, nlow_out)
    near_pieces(range(U0, D2 + 1))
    for src, dst in ((w1, w1_out), (w2, w2_out)):
        leave(src.at[pl.ds(0, 2)], dst.at[pl.ds(0, 2)])
    for r in range(2):
        @pl.loop(0, win // 256)
        def _(i, r=r):
            sl = pl.ds(pl.multiple_of(i * 256, 256), 256)
            value = nn(nlow[sl, :], w1[r]) + rows[r, 0:1, :]
            pre[r, sl, :] = value
            low_hid = gelu(value).astype(bf16)
            hid[r, sl, :] = low_hid
            more = nn(low_hid, w2[r])
            acc[sl, :] = more if r == 0 else acc[sl, :] + more
            at_loop(F_UP, i, 2, 2 * r)

        leave(pre.at[r], pre_out.at[r])
        leave(hid.at[r], hid_out.at[r])

    for k in range(3):
        at_slot(F_THIRD, k)
        far_pieces((U0 + 2 * k, D0 + 2 * k))
        units = pl.ds(k * third, third)

        @pl.loop(2, 4)
        def _(r, units=units):
            value = nn(nlow[...], w1[r, :, units]) + rows[r, 0:1, units]
            pre[r, :, units] = value
            low_hid = gelu(value).astype(bf16)
            hid[r, :, units] = low_hid
            acc[...] += nn(low_hid, w2[r, units, :])

        at_slot(F_DONE, k)

        for src, dst in ((pre, pre_out), (hid, hid_out)):
            leave(src.at[pl.ds(2, 2), :, units], dst.at[pl.ds(2, 2), :, units])
        leave(w1.at[pl.ds(2, 2), :, units], w1_out.at[pl.ds(2, 2), :, units])
        leave(w2.at[pl.ds(2, 2), units], w2_out.at[pl.ds(2, 2), units])

    loads[3].wait()

    sums_out[...] = jnp.zeros_like(sums_out)

    @pl.loop(0, win // block)
    def _(i):
        sl = pl.ds(pl.multiple_of(i * block, block), block)
        value = normed[sl, :] + acc[sl, :] + vec[3:4, :]
        mean = jnp.mean(value, axis=1, keepdims=True)
        centered = value - mean
        inverse = lax.rsqrt(jnp.mean(centered * centered, axis=1, keepdims=True) + EPSILON)
        unit = centered * inverse
        block_rows[sl, :] = (unit * vec[4:5, :] + vec[5:6, :]).astype(bf16)
        mask = column_of(mask_ref[pl.ds((win // block) * t + i, 1), :].astype(f32))
        selected = mask * cotb[sl, :].astype(f32)
        scaled = selected * vec[4:5, :]
        mean_one = jnp.mean(scaled, axis=1, keepdims=True)
        mean_two = jnp.mean(scaled * unit, axis=1, keepdims=True)
        dres = (scaled - mean_one - unit * mean_two) * inverse
        dres_rows[sl, :] = dres
        for src, dst, k in ((block_rows, block_out, 30), (dres_rows, dres_out, 31)):
            pltpu.make_async_copy(src.at[sl], dst.at[sl], out_sem.at[k]).start()
        sums_out[0:1, :] += jnp.sum(selected * unit, axis=0, keepdims=True)
        sums_out[1:2, :] += jnp.sum(selected, axis=0, keepdims=True)
        sums_out[2:3, :] += jnp.sum(dres, axis=0, keepdims=True)
        sums_out[3:4, :] += jnp.sum(mask, axis=0, keepdims=True)

    for i in (last - 2, last - 1):
        p_copy(i, i % 2).wait()
    for c in done:
        c.wait()
    for src, dst, k in ((block_rows, block_out, 30), (dres_rows, dres_out, 31)):
        pltpu.make_async_copy(src, dst, out_sem.at[k]).wait()
    for g in gathers.values():
        g.finish()


def forward_window(small, large):
    wo_own, w1_own = large[6:8]
    win, model = large[2].shape[1], large[0].shape[1]
    cols_t, hid_t = wo_own.shape[0], w1_own.shape[1]
    heads = 4 * HEADS_T
    f32, bf16 = jnp.float32, jnp.bfloat16
    shape = jax.ShapeDtypeStruct
    here = pl.BlockSpec(memory_space=pltpu.VMEM)
    away = pl.BlockSpec(memory_space=pl.ANY)
    outs = [
        (shape((heads, win, win), f32), away),
        (shape((3, model, win), bf16), away),
        (shape((model, win), bf16), away),
        (shape((win, model), bf16), away),
        (shape((win, 8 * LFREQ), bf16), away),
        (shape((win, model), f32), away),
        (shape((win, 1), f32), here),
        (shape((win, model), bf16), away),
        (shape((4, win, hid_t), f32), away),
        (shape((4, win, hid_t), bf16), away),
        (shape((win, model), bf16), away),
        (shape((win, model), f32), away),
        (shape((8, model), f32), here),
        (shape((3, model, model), bf16), away),
        (shape((model, model), bf16), away),
        (shape((4, model, hid_t), bf16), away),
        (shape((4, hid_t, model), bf16), away),
    ]
    return pl.pallas_call(
        forward_kernel,
        in_specs=[here] * len(small) + [away] * len(large),
        out_specs=[spec for _, spec in outs],
        out_shape=[s for s, _ in outs],
        scratch_shapes=[
            pltpu.VMEM((win, model), bf16),
            pltpu.VMEM((win, 8 * LFREQ), bf16),
            pltpu.VMEM((win, model), f32),
            pltpu.VMEM((win, model), bf16),
            pltpu.VMEM((win, model), bf16),
            pltpu.VMEM((win, model), f32),
            pltpu.VMEM((8 * LFREQ, model), bf16),
            pltpu.VMEM((win, model), bf16),
            pltpu.VMEM((win, model), bf16),
            pltpu.VMEM((win, win), jnp.int32),
            pltpu.VMEM((win, win), jnp.int32),
            pltpu.VMEM((8, model), f32),
            pltpu.VMEM((8, model), f32),
            pltpu.VMEM((3, model, model), bf16),
            pltpu.VMEM((model, model), bf16),
            pltpu.VMEM((4, model, hid_t), bf16),
            pltpu.VMEM((4, hid_t, model), bf16),
            pltpu.VMEM((4, 8, model), f32),
            pltpu.VMEM((3, model, 1), f32),
            pltpu.VMEM((heads, 128), f32),
            pltpu.VMEM((win, model), f32),
            pltpu.VMEM((3, model, win), bf16),
            pltpu.VMEM((2, 2, win, win), f32),
            pltpu.VMEM((model, win), bf16),
            pltpu.VMEM((win, model), bf16),
            pltpu.VMEM((win, model), f32),
            pltpu.VMEM((4, win, hid_t), f32),
            pltpu.VMEM((4, win, hid_t), bf16),
            pltpu.VMEM((win, model), f32),
            pltpu.SemaphoreType.DMA((11, 10)),
            pltpu.SemaphoreType.DMA((11, 10)),
            pltpu.SemaphoreType.DMA((11,)),
            pltpu.SemaphoreType.DMA((32,)),
            pltpu.SemaphoreType.DMA((2,)),
            pltpu.SemaphoreType.DMA((5,)),
        ],
        compiler_params=pltpu.CompilerParams(
            vmem_limit_bytes=60 * 2**20, collective_id=0, has_side_effects=True
        ),
        name="forward_window",
    )(*small, *large)


def bits_of(size):
    return [1 << b for b in range(size.bit_length() - 1)]


def tn(a, b):
    return lax.dot_general(a, b, (((0,), (0,)), ((), ())), preferred_element_type=jnp.float32)


UNIT = 128


class Reduce:
    def __init__(self, slot, order, part, core, landing, final, extra, result, acc, sems, peers):
        self.slot, self.order, self.part, self.core, self.landing = slot, order, part, core, landing
        self.final, self.extra, self.result, self.acc = final, extra, result, acc
        self.send, self.recv, self.here = sems
        self.mate, self.partners, self.further, self.sides = peers
        self.total = core.at[0] if acc is None else acc
        self.steps = order[0] + order[1]

    def move(self, k, src, dst, peer):
        return remote(src, dst, self.send.at[self.slot, k], self.recv.at[self.slot, k], peer)

    def region(self, fixed, other=None):
        index = [slice(None)]
        for axis in (Z_FAR, Z_NEAR, Y):
            if axis == other:
                index.append(pl.ds(1 - self.sides[axis], 1))
            elif axis in fixed:
                index.append(pl.ds(self.sides[axis], 1))
            else:
                index.append(slice(None))
        return tuple(index)

    def pieces(self, stage):
        return (0,) if X in self.order[0][:stage] else (0, 1)

    def moves(self, stage, piece=None):
        axis = self.steps[stage]
        peer = self.partners[axis]
        if stage >= len(self.order[0]):
            done = self.order[1][: stage - len(self.order[0])]
            rows = self.region([a for a in (Z_FAR, Z_NEAR, Y) if a not in done])
            src = self.result.at[rows] if done else self.final
            return [self.move(10 + len(done), src, self.result.at[rows], peer)]
        fixed = self.order[0][:stage]
        if axis == X:
            return [self.move(2 + 2 * stage, self.core.at[(1,) + self.region(fixed)], self.landing[stage].at[0], peer)] if piece != 0 else []
        return [
            self.move(2 + 2 * stage + p, self.core.at[(p,) + self.region(fixed, axis)], self.landing[stage].at[p], peer)
            for p in self.pieces(stage)
            if piece in (None, p)
        ]

    def to_mate(self, piece):
        return self.move(piece, self.part(piece), self.core.at[piece], self.mate)

    def own_copy(self):
        rows = self.region((Z_FAR, Z_NEAR, Y))
        return pltpu.make_async_copy(self.final, self.result.at[rows], self.here.at[self.slot])

    def more(self, k):
        return self.move(13 + k, self.final_of(k), self.extra.at[k], self.further[k])

    def final_of(self, k):
        return self.final if k == 0 else self.extra.at[len(self.further) + k]

    def merge(self, piece, unit, half, value):
        at = (unit, half)
        value = value.reshape(2, 2, 16, value.shape[-1]) + self.core[(piece,) + at].astype(jnp.float32)
        if piece == 0:
            self.total[at] = value.astype(self.total.dtype)
        else:
            self.core[(1,) + at] = value.astype(jnp.bfloat16)

    def take(self, stage):
        for m in self.moves(stage):
            m.wait_recv()
        count = len(self.order[0])
        if stage == count:
            self.own_copy().wait()
        if stage >= count:
            return
        axis = self.steps[stage]
        rows = self.region(self.order[0][: stage + 1])
        for p in (0,) if axis == X else self.pieces(stage):
            dst = self.total if p == 0 else self.core.at[p]
            value = dst[rows].astype(jnp.float32) + self.landing[stage][p].astype(jnp.float32)
            if stage + 1 == count:
                self.final[...] = value.astype(jnp.bfloat16)
            else:
                dst[rows] = value.astype(dst.dtype)
        if stage + 1 == count:
            for k in range(len(self.further)):
                self.more(k).start()
                self.more(k).wait()
                total = self.final_of(k)[...].astype(jnp.float32) + self.extra[k].astype(jnp.float32)
                self.final_of(k + 1)[...] = total.astype(jnp.bfloat16)
            if self.further:
                self.final[...] = self.final_of(len(self.further))[...]
            self.own_copy().start()

    def go(self, stage, piece=None):
        if stage < len(self.order[0]) and self.steps[stage] != X and self.acc is not None and piece != 1:
            rows = self.region(self.order[0][:stage], self.steps[stage])
            self.core[(0,) + rows] = self.acc[rows].astype(jnp.bfloat16)
        for m in self.moves(stage, piece):
            m.start()

    def next(self, stage):
        self.take(stage)
        if stage + 1 < len(self.steps):
            self.go(stage + 1)

    def sent(self):
        for stage in range(len(self.steps)):
            for m in self.moves(stage):
                m.wait_send()


def landing_shapes(units, order):
    shapes, pieces, dims = [], 2, {Z_FAR: 2, Z_NEAR: 2, Y: 2}
    for axis in order[0]:
        if axis == X:
            pieces = 1
        else:
            dims[axis] = 1
        shapes.append((pieces, units, dims[Z_FAR], dims[Z_NEAR], dims[Y], 16))
    return shapes


def xor_level(level, k):
    for bit in (1, 2):
        if k & bit:
            level = xor_index(level, bit)
    return level


def gelu_slope(v):
    k = math.sqrt(2.0 / math.pi)
    square = v * v
    t = jnp.tanh(k * v * (1.0 + 0.044715 * square))
    return 0.5 * (1.0 + t) + (0.5 * k) * v * (1.0 - t * t) * (1.0 + 3 * 0.044715 * square)


SMALL = 16


def backward_kernel(
    n_dp, inv_ref, gain_ref, sums_ref, dres_in, hid_in, pre_in, unit_in, nlow_in, low_in, feat_in, qkvt_in, ctxt_in,
    probs_in, rx_in, ry_in, w1_in, w2_in, wo_in, wqkv_in, block_in,
    block_all, in_all, red1, red2, red3, lay_all, small_out,
    arena, hidb, preb, dres, unit, nlow, nlow_t, dn, low_rows, qkvb, ctxtb, dctx, lowb, featb, wob, rxb, ryb, hot, acc,
    part1, part2, part3, core1, core2, core3, landings, finals, extras, acc3, small, small_in, short,
    load_sem, send, recv, here, share_send, share_recv, small_send, small_recv, p_sem,
):
    t, d = lax.axis_index("tensor"), lax.axis_index("dp")
    mate, across = {"tensor": xor_index(t, 1)}, {"tensor": xor_index(t, 2)}
    beside = {"dp": xor_index(d, 1)}
    along = [None] + [{"dp": d + 2 * (xor_level((d // 2) % 4, k) - (d // 2) % 4)} for k in range(1, 4)]
    further = [{"dp": xor_index(d, bit)} for bit in bits_of(n_dp) if bit >= 8]
    partners = {X: across, Y: beside, Z_NEAR: along[1], Z_FAR: along[2]}
    peers = (mate, partners, further, {Y: d % 2, Z_NEAR: (d // 2) % 2, Z_FAR: (d // 4) % 2})
    sems = (send, recv, here)
    f32, bf16 = jnp.float32, jnp.bfloat16
    win, model = dres.shape
    heads = 4 * HEADS_T
    cols_t = HEADS_T * HD
    hid_t = model
    block = 128

    everyone = [mate, across, beside] + along[1:] + further
    signal_peers(everyone)

    def load(k, src, dst):
        return pltpu.make_async_copy(src, dst, load_sem.at[k])

    def w_rows(r):
        return pl.ds(r * hid_t, hid_t)

    def h_rows(r):
        return pl.ds(r * win, win)

    order = (3, 1, 2, 0)
    ld_dres = load(0, dres_in, dres)
    ld_hid = {r: load(1 + r, hid_in.at[r], hidb.at[h_rows(r)]) for r in order}
    ld_w2 = {r: load(5 + r, w2_in.at[r], arena.at[w_rows(r)]) for r in order}
    ld_w1 = {r: load(9 + r, w1_in.at[r], arena.at[w_rows(4 + r)]) for r in order}
    ld_pre = {r: load(13 + r, pre_in.at[r], preb.at[i % 2]) for i, r in enumerate(order)}
    ld_rest = [
        load(17 + k, src, dst)
        for k, (src, dst) in enumerate(
            [
                (nlow_in, nlow), (unit_in, unit), (ctxt_in, ctxtb), (wo_in, wob), (qkvt_in, qkvb), (low_in, lowb),
                (feat_in, featb), (rx_in.at[t], rxb), (ry_in.at[t], ryb),
            ]
        )
    ]
    ld_wqkv = [load(26 + n, wqkv_in.at[n], hidb.at[pl.ds(n * model, model)]) for n in range(3)]
    ld_dres.start()
    for r in order:
        ld_hid[r].start()
    for r in order[:2]:
        ld_pre[r].start()
    for r in order:
        ld_w2[r].start()
    ld_rest[0].start()
    for r in order:
        ld_w1[r].start()
    for c in ld_rest[1:]:
        c.start()

    def chunks(first, units, parts, core, result, acc=None):
        out, at = [], 0
        for k, (count, part) in enumerate(zip(units, parts)):
            rows = pl.ds(at, count)
            slot = first + k
            out.append(
                Reduce(
                    slot, ORDERS[slot], part, core.at[:, rows], landings[slot], finals[slot], extras[slot],
                    result.at[rows], None if acc is None else acc.at[rows], sems, peers,
                )
            )
            at += count
        return out

    third = hid_t // 3

    def pairs(ref):
        return [lambda p, k=k: ref.at[p, pl.ds(2 * k, 2)] for k in range(3)]

    s2 = chunks(0, [2] * 3, pairs(part2), core2, red2)
    s1 = chunks(3, [2] * 3, pairs(part1), core1, red1)
    s3 = chunks(
        6, [1] * 7,
        [lambda p, k=k: part2.at[p, pl.ds(k, 1)] for k in range(6)] + [lambda p: part3.at[p]],
        core3, red3, acc3,
    )
    lay_t = featb.shape[1] // 4

    def share(k, src, whole, rows, part=0, parts=1):
        def at(index):
            return whole.at[pl.ds(pl.multiple_of((index * parts + part) * rows, rows), rows)]

        def moved(j, from_ref, index, peer):
            return remote(from_ref, at(index), share_send.at[k, j], share_recv.at[k, j], peer)

        far = xor_index(t, 2)
        return {
            "here": pltpu.make_async_copy(src, at(t), share_send.at[k, 3]),
            "across": moved(0, src, t, across),
            "mate": moved(1, src, t, mate),
            "pass": moved(2, at(far), far, mate),
        }

    def share_start(c):
        for name in ("across", "mate", "here"):
            c[name].start()

    def share_pass(c):
        c["across"].wait_recv()
        c["pass"].start()

    def share_end(c):
        c["here"].wait()
        c["mate"].wait_recv()
        c["pass"].wait_recv()
        for name in ("across", "mate", "pass"):
            c[name].wait_send()

    quarter_win = win // 4
    sh_block = [
        share(k, block_in.at[pl.ds(k * quarter_win, quarter_win)], block_all, quarter_win, k, 4) for k in range(4)
    ]
    sh_in = share(4, low_rows, in_all, win)
    sh_lay = share(5, red3.at[pl.ds(6, 1)], lay_all, 1)
    bits = [mate, across, beside, along[1], along[2]] + further

    def small_move(k):
        return remote(small.at[k], small_in.at[k], small_send.at[k], small_recv.at[k], bits[k])

    def small_step(k):
        small_move(k).wait()
        small[k + 1] = small[k] + small_in[k]
        if k + 1 < len(bits):
            small_move(k + 1).start()

    named = dict(zip(range(A0, C6 + 1), s2 + s1 + s3))

    def run(what, stage):
        if what in named:
            named[what].next(stage)
        elif what == BLOCK:
            share_start(sh_block[stage])
        elif what == BLOCK_ON:
            share_pass(sh_block[stage])
        elif what == INPUT_ON:
            share_pass(sh_in)
        elif what == LAY:
            share_start(sh_lay)
        elif what == LAY_ON:
            share_pass(sh_lay)
        elif what == SMALL_STEP:
            small_step(stage)

    def at_slot(phase, index=0):
        for what, stage in SCHEDULE.get((phase, index), ()):
            run(what, stage)

    def at_loop(phase, index, count, first=0):
        for k in range(count):
            if (phase, first + k) in SCHEDULE:
                @pl.when(index == k)
                def _(k=k):
                    at_slot(phase, first + k)


    small[0] = jnp.zeros_like(small[0])
    small[0, 3:4, :] = sums_ref[2:3, :]
    small[0, 4:6, :] = sums_ref[0:2, :]
    small[0, 6:7, :] = sums_ref[3:4, :]

    def own_row(base, r):
        index = t
        for bit in (1, 2):
            if r & bit:
                index = xor_index(index, bit)
        return pl.ds(base + index, 1)

    ld_dres.wait()

    @pl.loop(0, win // block)
    def _(i):
        sl = pl.ds(pl.multiple_of(i * block, block), block)
        low_rows[sl, :] = dres[sl, :].astype(bf16)

    def grad_w2(r, c):
        sl = pl.ds(pl.multiple_of(c * third, third), third)
        return tn(hidb[h_rows(r), sl], low_rows[...])

    def grad_w1(r, c):
        sl = pl.ds(pl.multiple_of(c * third, third), third)
        return nn(nlow_t[sl, :], hidb[h_rows(r), :])

    def blocks(value):
        return value.reshape(value.shape[0] // UNIT, 2, 2, 2, 16, value.shape[1])

    def for_mate(group, grad, r, part):
        @pl.loop(0, 3)
        def _(c):
            part[r // 2, pl.ds(2 * c, 2)] = blocks(grad(r, c).astype(bf16))

        for g in group:
            g.to_mate(r // 2).start()

    def merge_all(g, piece, value):
        half = UNIT // 2
        for k in range(value.shape[0] // half):
            g.merge(piece, k // 2, k % 2, value[k * half : (k + 1) * half])

    def for_own(group, grad, r):
        for c, g in enumerate(group):
            g.to_mate(r // 2).wait_recv()
            merge_all(g, r // 2, grad(r, c))
            g.go(0, r // 2)

    for r in order[:2]:
        ld_hid[r].wait()
        if r == order[0]:
            for_mate((), grad_w2, r, part2)
            wait_peers(everyone)
            at_slot(START)
            for g in s2:
                g.to_mate(r // 2).start()
        else:
            for_mate(s2, grad_w2, r, part2)

    ld_rest[0].wait()
    nlow_t[...] = nlow[...].astype(f32).T.astype(bf16)
    for j, r in enumerate(order):
        ld_pre[r].wait()
        ld_w2[r].wait()
        ld_w1[r].wait()

        @pl.loop(0, 2)
        def _(i, j=j, r=r):
            count = win // 2
            sl = pl.ds(pl.multiple_of(i * count, count), count)
            hs = pl.ds(pl.multiple_of(r * win + i * count, count), count)
            dhid = nt(low_rows[sl, :], arena[w_rows(r), :])
            dpre = (dhid * gelu_slope(preb[j % 2, sl, :])).astype(bf16)
            hidb[hs, :] = dpre
            row = own_row(8, r)
            small[0, row, :] += jnp.sum(dpre.astype(f32), axis=0, keepdims=True)
            more = nt(dpre, arena[w_rows(4 + r), :])
            dn[sl, :] = more if j == 0 else dn[sl, :] + more
            at_loop(FFN, i, 2, 3 * j)

        if j + 2 < 4:
            ld_pre[order[j + 2]].start()
        if j < 2:
            for_mate(s1, grad_w1, r, part1)
        else:
            for_own(s1, grad_w1, r)
        if j == 0:
            for q in order[2:]:
                ld_hid[q].wait()
                for_own(s2, grad_w2, q)
        at_slot(FFN, 3 * j + 2)

    for c in ld_wqkv:
        c.start()

    def p_load(h, slot):
        return pltpu.make_async_copy(probs_in.at[h], preb.at[slot, :, pl.ds(0, win)], p_sem.at[slot])

    for h in range(2):
        p_load(h, h).start()
    for g in s2:
        for p in range(2):
            g.to_mate(p).wait_send()

    ld_rest[1].wait()

    @pl.loop(0, win // block)
    def _(i):
        sl = pl.ds(pl.multiple_of(i * block, block), block)
        up = dres[sl, :] + dn[sl, :]
        units = unit[sl, :]
        scaled = up * row_of(gain_ref)
        mean_one = jnp.mean(scaled, axis=1, keepdims=True)
        mean_two = jnp.mean(scaled * units, axis=1, keepdims=True)
        value = (scaled - mean_one - units * mean_two) * inv_ref[sl, :]
        dn[sl, :] = value
        low_rows[sl, :] = value.astype(bf16)
        small[0, 0:1, :] += jnp.sum(value, axis=0, keepdims=True)
        small[0, 1:2, :] += jnp.sum(up * units, axis=0, keepdims=True)
        small[0, 2:3, :] += jnp.sum(up, axis=0, keepdims=True)

    at_slot(NORM)
    for c in ld_rest[2:]:
        c.wait()

    @pl.loop(0, 4)
    def _(r):
        sl = pl.ds(pl.multiple_of(r * cols_t, cols_t), cols_t)
        dctx[sl, :] = nt(wob[sl, :], low_rows[...]).astype(bf16)

    at_slot(OUT)

    @pl.loop(0, heads)
    def _(h):
        slot = h % 2
        sl = pl.ds(pl.multiple_of(h * HD, HD), HD)
        dc_t = dctx[sl, :]
        dc = dc_t.astype(f32).T.astype(bf16)
        p_load(h, slot).wait()
        p = preb[slot, :, 0:win]
        dp = nn(dc, qkvb[2, sl, :])
        row_dot = jnp.sum(p * dp, axis=1, keepdims=True)
        ds = (p * (dp - row_dot)).astype(bf16)
        qkvb[2, sl, :] = nn(dc_t, p.astype(bf16)).astype(bf16)
        dq = nt(qkvb[1, sl, :], ds) * HD ** (-0.5)
        dk = nn(qkvb[0, sl, :], ds) * HD ** (-0.5)
        qkvb[0, sl, :] = dq.astype(bf16)
        qkvb[1, sl, :] = dk.astype(bf16)
        arena[pl.ds(pl.multiple_of(h * win, win), win), 0:win] = ds

        @pl.when(h + 2 < heads)
        def _():
            p_load(h + 2, slot).start()

        at_loop(HEAD, h, heads)

    for c in ld_wqkv:
        c.wait()
    def rows_of(r):
        return pl.ds(r * cols_t, cols_t)

    def grad_out(r):
        return nn(ctxtb[rows_of(r), :], low_rows[...])

    def grad_proj(n, r):
        return nn(qkvb[n, rows_of(r), :], lowb[...])

    halves = (lambda r: grad_proj(2, r), grad_out, lambda r: grad_proj(0, r), lambda r: grad_proj(1, r))
    sixth = UNIT // 2
    each = cols_t // sixth
    for r in (3, 1):
        for k, grad in enumerate(halves):
            value = grad(r).astype(bf16)
            for j in range(each):
                at = k * each + j
                part2[r // 2, at // 2, at % 2] = value[j * sixth : (j + 1) * sixth].reshape(2, 2, 16, model)
            if k % 2 == 1:
                for g in s3[:6][3 * (k // 2) : 3 * (k // 2) + 3]:
                    g.to_mate(r // 2).start()
    at_slot(SENT)
    for r in (2, 0):
        for k, grad in enumerate(halves):
            value = grad(r)
            for j in range(each):
                at = k * each + j
                g = s3[at // 2]
                if at % 2 == 0:
                    g.to_mate(r // 2).wait_recv()
                g.merge(r // 2, 0, at % 2, value[j * sixth : (j + 1) * sixth])
                if at % 2 == 1:
                    g.go(0, r // 2)
    at_slot(MERGED)

    @pl.loop(0, win // block)
    def _(i):
        sl = pl.ds(pl.multiple_of(i * block, block), block)
        value = dn[sl, :]
        for n in range(3):
            value = value + tn(qkvb[n, :, sl], hidb[pl.ds(n * model, model), :])
        dn[sl, :] = value
        at_loop(DLAYER, i, 4)

    low_rows[...] = dn[...].astype(bf16)

    def grad_lay(r):
        index = t
        for bit in (1, 2):
            if r & bit:
                index = xor_index(index, bit)
        return tn(featb[:, pl.ds(pl.multiple_of(index * lay_t, lay_t), lay_t)], low_rows[...])

    for r in (3, 1):
        part3[r // 2] = blocks(grad_lay(r).astype(bf16))
        s3[6].to_mate(r // 2).start()
    at_slot(LAYOUT)
    for_own(s3[6:], lambda r, c: grad_lay(r), 2)
    for_own(s3[6:], lambda r, c: grad_lay(r), 0)
    share_start(sh_in)

    ones = jnp.ones((8, win), bf16)
    short[...] = jnp.zeros_like(short)
    for n, at in ((0, 0), (2, cols_t)):
        total = nt(ones, qkvb[n])
        for r in range(4):
            short[r : r + 1, at : at + cols_t] = total[0:1, r * cols_t : (r + 1) * cols_t]

    acc[...] = jnp.zeros_like(acc)
    one, zero = bf16(1), bf16(0)
    hots = BUCKETS * ROWS
    @pl.loop(0, win // ROWS // 2)
    def _(i):
        total = None
        for u in range(2):
            at = pl.multiple_of(i * 2 * ROWS + u * ROWS, ROWS)
            x = rxb[pl.ds(at, ROWS), :].astype(f32).astype(bf16)
            y = ryb[pl.ds(at, ROWS), :].astype(f32).astype(bf16)
            for b in range(BUCKETS):
                hot[u, b * ROWS : (b + 1) * ROWS, :] = jnp.where(x == bf16(b), one, zero)
                hot[u, hots + b * ROWS : hots + (b + 1) * ROWS, :] = jnp.where(y == bf16(b), one, zero)
            left = jnp.concatenate(
                [arena[pl.ds(pl.multiple_of(h * win + at, ROWS), ROWS), 0:win] for h in range(heads)], axis=0
            )
            more = nt(left, hot[u])
            total = more if total is None else total + more
        acc[...] += total
        at_loop(TABLE, i, 16)

    row = lax.broadcasted_iota(jnp.int32, (ROWS, 2 * hots), 0)
    col = lax.broadcasted_iota(jnp.int32, (ROWS, 2 * hots), 1) % ROWS
    picked = jnp.concatenate(
        [
            jnp.sum(jnp.where(row == col, acc[h * ROWS : (h + 1) * ROWS, :], 0.0), axis=0, keepdims=True)
            for h in range(heads)
        ]
        + [jnp.zeros((16 - heads, 2 * hots), f32)],
        axis=0,
    )
    fold = (
        lax.broadcasted_iota(jnp.int32, (2 * hots, 128), 0) // ROWS
        == lax.broadcasted_iota(jnp.int32, (2 * hots, 128), 1)
    ).astype(f32)
    table = jnp.dot(picked, fold, preferred_element_type=f32, precision=lax.Precision.HIGHEST)
    for r in range(4):
        for a in range(HEADS_T):
            lane = 2 * cols_t + a * 2 * BUCKETS
            short[r : r + 1, lane : lane + 2 * BUCKETS] = table[
                r * HEADS_T + a : r * HEADS_T + a + 1, 0 : 2 * BUCKETS
            ]
    for r in range(4):
        small[0, own_row(12, r), :] = short[r : r + 1, :]

    small_move(0).start()
    at_slot(TAIL)
    for k in range(5, len(bits)):
        small_step(k)
    small_out[...] = small[len(bits)]
    for c in sh_block + [sh_in, sh_lay]:
        share_end(c)
    for g in s1 + s3:
        for p in range(2):
            g.to_mate(p).wait_send()
    for g in s2 + s1 + s3:
        g.sent()


def backward_window(n_dp, lay_rows, inv, gain, sums, dres, hid, pre, unit, nlow, low, feat, qkvt, ctxt, probs, rx, ry, w1, w2, wo, wqkv, block_own):
    win, model = dres.shape
    heads = 4 * HEADS_T
    cols_t = HEADS_T * HD
    lay_t = lay_rows // 4
    units = model // UNIT
    rest = (4 * cols_t + lay_t) // UNIT
    block = (2, 2, 2, 16, model)
    more = max(0, len(bits_of(n_dp)) - 3)
    levels = 5 + more
    sizes = [2] * 6 + [1] * 7
    f32, bf16 = jnp.float32, jnp.bfloat16
    shape = jax.ShapeDtypeStruct
    here = pl.BlockSpec(memory_space=pltpu.VMEM)
    away = pl.BlockSpec(memory_space=pl.ANY)
    outs = [
        (shape((4 * win, model), bf16), away),
        (shape((4 * win, model), bf16), away),
        (shape((units,) + block, bf16), away),
        (shape((units,) + block, bf16), away),
        (shape((rest,) + block, bf16), away),
        (shape((4,) + block, bf16), away),
        (shape((SMALL, model), f32), here),
    ]
    V = pltpu.VMEM
    S = pltpu.SemaphoreType.DMA
    return pl.pallas_call(
        functools.partial(backward_kernel, n_dp),
        in_specs=[here] * 3 + [away] * 17,
        out_specs=[spec for _, spec in outs],
        out_shape=[s for s, _ in outs],
        scratch_shapes=[
            V((8 * model, model), bf16), V((3 * model, model), bf16), V((2, win, model), f32), V((win, model), f32),
            V((win, model), f32), V((win, model), bf16), V((model, win), bf16), V((win, model), f32),
            V((win, model), bf16), V((3, model, win), bf16), V((model, win), bf16), V((model, win), bf16),
            V((win, model), bf16), V((win, lay_rows), bf16), V((model, model), bf16), V((win, win), jnp.int32),
            V((win, win), jnp.int32), V((2, 2 * BUCKETS * ROWS, win), bf16), V((heads * ROWS, 2 * BUCKETS * ROWS), f32),
            V((2, units) + block, bf16), V((2, units) + block, bf16), V((2, 1) + block, bf16),
            V((2, units) + block, bf16), V((2, units) + block, bf16), V((2, rest) + block, bf16),
            [[V(s + (model,), bf16) for s in landing_shapes(n, o)] for n, o in zip(sizes, ORDERS)],
            [V((n, 1, 1, 1, 16, model), bf16) for n in sizes],
            [V((2 * more + 1, n, 1, 1, 1, 16, model), bf16) for n in sizes], V((rest,) + block, f32),
            V((levels + 1, SMALL, model), f32), V((levels, SMALL, model), f32), V((8, model), f32),
            S((29,)), S((len(sizes), 13 + more)), S((len(sizes), 13 + more)), S((len(sizes),)), S((6, 4)), S((6, 3)),
            S((levels,)), S((levels,)), S((2,)),
        ],
        compiler_params=pltpu.CompilerParams(
            vmem_limit_bytes=63 * 2**20, collective_id=1, has_side_effects=True
        ),
        name="backward_window",
    )(inv, gain, sums, dres, hid, pre, unit, nlow, low, feat, qkvt, ctxt, probs, rx, ry, w1, w2, wo, wqkv, block_own)


def finish_kernel(
    rates, small_ref, in_in, red1, red2, red3, lay_in,
    in_out, lay_out, qkv_out, qvb_out, table_out, wo_out, ob_out, g1_out, s1_out, w1_out, b1_out, w2_out, c2_out,
    g2_out, s2_out, in_low, low1, low2, low3, lay_low, in_wide, wide1, wide2, wide3, lay_wide, load_sem, store_sem,
):
    t = lax.axis_index("tensor")
    cols_t = HEADS_T * HD
    inverse = 1.0 / small_ref[6:7, 0:1]
    jobs = []

    def job(src, low, wide, out, rate):
        jobs.append((src, low, wide, out, rate))

    def split(src, low, wide, out, rate, step):
        for at in range(0, low.shape[0], step):
            sl = pl.ds(at, step)
            job(src.at[sl], low.at[sl], None if wide is None else wide.at[sl], out.at[sl], rate)

    split(in_in, in_low, in_wide, in_out, None, 256)
    split(red2, low2, wide2, w2_out, 4, 256)
    split(red1, low1, wide1, w1_out, 3, 256)
    for n, at, rate in ((2, 0, 0), (None, 1, 1), (0, 2, 0), (1, 3, 0)):
        sl = pl.ds(at * cols_t, cols_t)
        job(red3.at[sl], low3.at[sl], wide3.at[sl], wo_out if n is None else qkv_out.at[n], rate)
    split(lay_in, lay_low, lay_wide, lay_out, 6, 256)
    loads = [pltpu.make_async_copy(src, low, load_sem.at[k]) for k, (src, low, _, _, _) in enumerate(jobs)]
    ahead = len(loads)
    for c in loads[:ahead]:
        c.start()

    def row(ref, index, rate):
        ref[...] = (small_ref[index : index + 1, :] * (inverse * rates[rate])).reshape(ref.shape)

    for ref, index, rate in ((ob_out, 0, 1), (g1_out, 1, 2), (s1_out, 2, 2), (c2_out, 3, 4), (g2_out, 4, 5), (s2_out, 5, 5)):
        row(ref, index, rate)
    b1_out[...] = (small_ref[pl.ds(8 + t, 1), :] * (inverse * rates[3])).reshape(b1_out.shape)
    own = small_ref[pl.ds(12 + t, 1), :]
    for k in range(2):
        qvb_out[k : k + 1, :] = own[:, k * cols_t : (k + 1) * cols_t] * (inverse * rates[0])
    for a in range(HEADS_T):
        at = 2 * cols_t + a * 2 * BUCKETS
        table_out[a : a + 1, :] = own[:, at : at + 2 * BUCKETS] * (inverse * rates[7])

    stores = []
    for k, (_, low, wide, out, rate) in enumerate(jobs):
        loads[k].wait()
        if k + ahead < len(jobs):
            loads[k + ahead].start()
        if wide is None:
            stores.append(pltpu.make_async_copy(low, out, store_sem.at[k]))
        else:
            factor = inverse if rate is None else inverse * rates[rate]
            wide[...] = low[...].astype(jnp.float32) * factor
            stores.append(pltpu.make_async_copy(wide, out, store_sem.at[k]))
        stores[-1].start()
    for c in stores:
        c.wait()


def finish(rates, small, block_all, in_all, sum1, sum2, sum3, lay_all, cols_t):
    f32, bf16 = jnp.float32, jnp.bfloat16
    shape = jax.ShapeDtypeStruct
    here = pl.BlockSpec(memory_space=pltpu.VMEM)
    away = pl.BlockSpec(memory_space=pl.ANY)
    model = in_all.shape[1]
    vector = (shape((model,), f32), here)
    outs = [
        (shape(in_all.shape, f32), away),
        (shape(lay_all.shape, f32), away),
        (shape((3, cols_t, model), f32), away),
        (shape((2, cols_t), f32), here),
        (shape((HEADS_T, 2 * BUCKETS), f32), here),
        (shape((cols_t, model), f32), away),
        vector, vector, vector,
        (shape(sum1.shape, f32), away),
        vector,
        (shape(sum2.shape, f32), away),
        vector, vector, vector,
    ]
    wide = [in_all, sum1, sum2, sum3, lay_all]
    return pl.pallas_call(
        finish_kernel,
        in_specs=[pl.BlockSpec(memory_space=pltpu.SMEM), here] + [away] * 5,
        out_specs=[spec for _, spec in outs],
        out_shape=[s for s, _ in outs],
        scratch_shapes=[pltpu.VMEM(v.shape, bf16) for v in wide]
        + [pltpu.VMEM(v.shape, f32) for v in wide]
        + [pltpu.SemaphoreType.DMA((32,)), pltpu.SemaphoreType.DMA((32,))],
        compiler_params=pltpu.CompilerParams(vmem_limit_bytes=60 * 2**20),
        name="finish",
    )(rates, small, in_all, sum1, sum2, sum3, lay_all)


def local(
    n_dp, n_t,
    tokens_in, box_coords, rel_x, rel_y, mask_tokens, cotangent, layout_weight, qkv_weight, qv_bias,
    bias_table, out_weight, out_bias, ln1_gain, ln1_bias, ffn_in_weight, ffn_in_bias, ffn_out_weight,
    ffn_out_bias, ln2_gain, ln2_bias, group_rates,
):
    (
        probs, qkvt, context_t, layer_low, features, unit_one, inverse_one, normed_low, pre_all, hid_all,
        block_own, dresid_two, sums, wqkv, wo, w1, w2,
    ) = forward_window(
        [
            box_coords.T, mask_tokens.reshape(-1, 128), qv_bias, ffn_in_bias, bias_table.T,
            out_bias, ln1_gain, ln1_bias, ffn_out_bias, ln2_gain, ln2_bias,
        ],
        [
            tokens_in, cotangent, rel_x, rel_y, layout_weight, jnp.transpose(qkv_weight, (0, 2, 1)), out_weight,
            ffn_in_weight, ffn_out_weight,
        ],
    )
    block_all, in_all, sum1, sum2, sum3, lay_all, small = backward_window(
        n_dp, layout_weight.shape[0], inverse_one, ln1_gain, sums, dresid_two, hid_all, pre_all, unit_one, normed_low,
        layer_low, features, qkvt, context_t, probs, rel_x, rel_y, w1, w2, wo, wqkv, block_own,
    )
    sums = [v.reshape(-1, v.shape[-1]) for v in (sum1, sum2, sum3, lay_all)]
    out = [block_all] + list(finish(group_rates, small, block_all, in_all, *sums, out_weight.shape[0]))
    out[3] = jnp.transpose(out[3], (0, 2, 1))
    out[5] = out[5].T
    return tuple(out)


def solution(mesh):
    placed = (
        P("dp", None), P("dp", None), P("dp", None, None), P("dp", None, None), P("dp"), P("dp", None),
        P(), P(None, None, "tensor"), P(None, "tensor"), P(None, "tensor"), P("tensor", None),
        P(), P(), P(), P(None, "tensor"), P("tensor"), P("tensor", None), P(), P(), P(), P(),
    )
    return jax.shard_map(
        functools.partial(local, mesh.shape["dp"], mesh.shape["tensor"]),
        mesh=mesh,
        in_specs=placed,
        out_specs=(
            P("dp", None), P("dp", None), P(), P(None, None, "tensor"), P(None, "tensor"),
            P(None, "tensor"), P("tensor", None), P(), P(), P(), P(None, "tensor"), P("tensor"),
            P("tensor", None), P(), P(), P(),
        ),
        check_vma=False,
    )
```

```python
import functools
import math

import jax
import jax.numpy as jnp
from jax import lax
from jax.experimental import pallas as pl
from jax.experimental.pallas import tpu as pltpu
from jax.sharding import PartitionSpec as P

HD = 64
LFREQ = 64
BUCKETS = 32
EPSILON = 1e-05
ROWS = 16
HEADS_T = 3
MESH = pl.DeviceIdType.MESH

F_FEAT, F_NEAR, F_HEAD, F_FAR, F_BOTH, F_OUT, F_CONTEXT, F_NORM, F_UP, F_THIRD, F_DONE = range(11)
AT_R, AT_Q, AT_K, AT_V, AT_O, U0, D0, U1, D1, U2, D2 = range(11)
WAYS = {
    AT_R: (1, 0),
    AT_Q: (2, 0),
    AT_K: (2, 0),
    AT_V: (2, 1),
    AT_O: (2, 0),
    U0: (4, 0),
    D0: (4, 0),
    U1: (4, 0),
    D1: (2, 1),
    U2: (2, 0),
    D2: (1, 0),
}
SEND_ORDER = (AT_Q, AT_V, AT_K, D0, AT_R, U0, U1, AT_O, D1, U2, D2)
FORWARD = {
    (F_NEAR, 0): ((AT_Q, 0),),
    (F_HEAD, 1): ((AT_V, 0),),
    (F_HEAD, 2): ((AT_K, 0), (AT_Q, 1),),
    (F_HEAD, 3): ((D0, 0),),
    (F_HEAD, 4): ((AT_V, 1), (AT_R, 0), (U0, 0), (AT_K, 1),),
    (F_HEAD, 5): ((U1, 0), (D0, 1),),
    (F_HEAD, 6): ((AT_O, 0),),
    (F_HEAD, 7): ((U0, 1),),
    (F_HEAD, 9): ((U1, 1), (D0, 2), (D1, 0), (AT_O, 1),),
    (F_HEAD, 10): ((U0, 2),),
    (F_CONTEXT, 0): ((U2, 0),),
    (F_NORM, 1): ((U1, 2),),
    (F_NORM, 3): ((D1, 1),),
    (F_UP, 2): ((U2, 1), (D2, 0),),
}

START, FFN, NORM, OUT, HEAD, SENT, MERGED, DLAYER, LAYOUT, TABLE, TAIL = range(11)
A0, A1, A2, B0, B1, B2, C0, C1, C2, C3, C4, C5, C6, BLOCK, BLOCK_ON, INPUT_ON, LAY, LAY_ON, SMALL_STEP = range(19)
X, Y, Z_NEAR, Z_FAR = range(4)
ORDERS = (
    ((Z_NEAR, Z_FAR, X, Y), (Z_FAR, Z_NEAR, Y)),
    ((Y, X, Z_NEAR, Z_FAR), (Z_FAR, Z_NEAR, Y)),
    ((X, Y, Z_NEAR, Z_FAR), (Z_FAR, Z_NEAR, Y)),
    ((Y, X, Z_NEAR, Z_FAR), (Z_FAR, Z_NEAR, Y)),
    ((X, Y, Z_NEAR, Z_FAR), (Z_FAR, Z_NEAR, Y)),
    ((Z_NEAR, Z_FAR, X, Y), (Z_FAR, Z_NEAR, Y)),
    ((Y, X, Z_NEAR, Z_FAR), (Z_FAR, Z_NEAR, Y)),
    ((Y, X, Z_NEAR, Z_FAR), (Z_FAR, Z_NEAR, Y)),
    ((Y, X, Z_NEAR, Z_FAR), (Z_FAR, Z_NEAR, Y)),
    ((X, Y, Z_NEAR, Z_FAR), (Y, Z_FAR, Z_NEAR)),
    ((X, Z_NEAR, Z_FAR, Y), (Z_FAR, Z_NEAR, Y)),
    ((Y, X, Z_NEAR, Z_FAR), (Z_FAR, Z_NEAR, Y)),
    ((X, Y, Z_NEAR, Z_FAR), (Z_FAR, Z_NEAR, Y)),
)
SCHEDULE = {
    (START, 0): ((BLOCK, 2),),
    (FFN, 3): ((BLOCK_ON, 2),),
    (FFN, 10): ((A0, 0), (A2, 0),),
    (FFN, 11): ((A1, 0),),
    (HEAD, 2): ((A2, 1), (B1, 0),),
    (HEAD, 4): ((A0, 1), (B2, 0), (B0, 0), (A1, 1),),
    (HEAD, 5): ((BLOCK, 0),),
    (HEAD, 7): ((A0, 2),),
    (HEAD, 9): ((B1, 1),),
    (HEAD, 11): ((A0, 3), (B0, 1),),
    (SENT, 0): ((B1, 2), (B2, 1),),
    (MERGED, 0): ((A2, 2), (A1, 2), (A0, 4), (B0, 2), (B2, 2), (B1, 3), (BLOCK_ON, 0),),
    (LAYOUT, 0): ((C0, 0), (A2, 3),),
    (TABLE, 0): ((C1, 0), (C4, 0), (C2, 0), (C0, 1), (A0, 5), (B0, 3), (C3, 0), (B1, 4),),
    (TABLE, 3): ((C5, 0), (A2, 4),),
    (TABLE, 4): ((C4, 1), (B2, 3), (C6, 0), (C0, 2),),
    (TABLE, 5): ((BLOCK, 1), (BLOCK, 3), (B0, 4),),
    (TABLE, 7): ((B1, 5),),
    (TABLE, 8): ((A1, 3),),
    (TABLE, 12): ((A2, 5),),
    (TABLE, 13): ((C6, 1),),
    (TABLE, 14): ((C0, 3), (B2, 4),),
    (TABLE, 15): ((B0, 5), (A1, 4), (C3, 1), (C6, 2), (C0, 4), (B2, 5), (INPUT_ON, 0),),
    (TAIL, 0): (
        (C1, 1), (B1, 6), (A2, 6), (A0, 6), (C4, 2), (A1, 5), (C3, 2), (C2, 1), (SMALL_STEP, 0), (B0, 6), (C6, 3),
        (C0, 5), (C5, 1), (C1, 2), (C3, 3), (C2, 2), (B2, 6), (C6, 4), (C4, 3), (C5, 2), (BLOCK_ON, 1), (C1, 3),
        (C2, 3), (C6, 5), (C4, 4), (A1, 6), (C5, 3), (BLOCK_ON, 3), (C1, 4), (SMALL_STEP, 1), (C0, 6), (C3, 4),
        (C2, 4), (C4, 5), (C5, 4), (C6, 6), (LAY, 0), (C1, 5), (SMALL_STEP, 2), (C2, 5), (C3, 5), (C4, 6), (C5, 5),
        (SMALL_STEP, 3), (C1, 6), (LAY_ON, 0), (C3, 6), (C2, 6), (SMALL_STEP, 4), (C5, 6),
    ),
}


def nt(a, b):
    return lax.dot_general(a, b, (((1,), (1,)), ((), ())), preferred_element_type=jnp.float32)


def nn(a, b):
    return jnp.dot(a, b, preferred_element_type=jnp.float32)


def xor_index(index, bit):
    return index + bit - 2 * bit * ((index // bit) % 2)


def signal_peers(peers):
    barrier = pltpu.get_barrier_semaphore()
    for peer in peers:
        pl.semaphore_signal(barrier, inc=1, device_id=peer, device_id_type=MESH)


def wait_peers(peers):
    pl.semaphore_wait(pltpu.get_barrier_semaphore(), len(peers))


def remote(src, dst, send, recv, peer):
    return pltpu.make_async_remote_copy(
        src_ref=src, dst_ref=dst, send_sem=send, recv_sem=recv, device_id=peer, device_id_type=MESH
    )


HERE, MATE, ACROSS, PASS, BESIDE, PASS_BESIDE, ALONG, PASS_ALONG, LAST_BESIDE, LAST_ALONG, PASS_LAST = range(11)


class Gather:
    def __init__(self, own, place, rows, kind, bit, sems, slot, peers):
        self.own, self.place, self.rows, self.kind, self.bit = own, place, rows, kind, bit
        self.send, self.recv, self.here = sems
        self.slot = slot
        self.mate, self.across, self.near, self.sides = peers

    def part(self, flip_zero, flip_one):
        if self.kind == 1:
            return pl.ds(0, self.rows)
        if self.kind == 2:
            side = self.sides[self.bit]
            side = 1 - side if flip_zero else side
            return pl.ds(pl.multiple_of(side * (self.rows // 2), 16), self.rows // 2)
        zero = 1 - self.sides[0] if flip_zero else self.sides[0]
        one = 1 - self.sides[1] if flip_one else self.sides[1]
        return pl.ds(pl.multiple_of((zero + 2 * one) * (self.rows // 4), 16), self.rows // 4)

    def halved(self, part, second):
        h = part.size // 2
        return pl.ds(pl.multiple_of(part.start + (h if second else 0), 16), h)

    def copy(self, name):
        s = self.slot
        whole = pl.ds(0, self.rows)
        mine = self.part(False, False)
        if name == HERE:
            return pltpu.make_async_copy(self.own(whole), self.place(0, whole), self.here.at[s])

        def pass_on(rows, k):
            return self.place(2, rows), self.place(3, rows), self.mate, k

        def relay(rows, to, k):
            return self.place(2, rows), self.place(2, rows), self.near[to], k

        src, dst, peer, k = {
            MATE: lambda: (self.own(whole), self.place(1, whole), self.mate, 0),
            ACROSS: lambda: (self.own(mine), self.place(2, mine), self.across, 1),
            PASS: lambda: pass_on(mine, 2),
            BESIDE: lambda: relay(mine, self.bit, 3),
            PASS_BESIDE: lambda: pass_on(self.part(True, False), 4),
            ALONG: lambda: relay(mine, 1, 5),
            PASS_ALONG: lambda: pass_on(self.part(False, True), 6),
            LAST_BESIDE: lambda: relay(self.halved(self.part(False, True), False), 0, 7),
            LAST_ALONG: lambda: relay(self.halved(self.part(True, False), True), 1, 8),
            PASS_LAST: lambda: pass_on(self.part(True, True), 9),
        }[name]()
        return remote(src, dst, self.send.at[s, k], self.recv.at[s, k], peer)

    def names(self, stage):
        return {
            1: (((PASS,), (ACROSS,)),),
            2: (((BESIDE, PASS), (ACROSS,)), ((PASS_BESIDE,), (BESIDE,))),
            4: (
                ((BESIDE, ALONG, PASS), (ACROSS,)),
                ((LAST_BESIDE, LAST_ALONG, PASS_BESIDE, PASS_ALONG), (BESIDE, ALONG)),
                ((PASS_LAST,), (LAST_BESIDE, LAST_ALONG)),
            ),
        }[self.kind][stage]

    def stages(self):
        return {1: 1, 2: 2, 4: 3}[self.kind]

    def start(self):
        self.copy(ACROSS).start()
        self.copy(MATE).start()
        self.copy(HERE).start()

    def forward(self, stage):
        starts, waits = self.names(stage)
        for name in waits:
            self.copy(name).wait_recv()
        for name in starts:
            self.copy(name).start()

    def arrive_near(self):
        self.copy(HERE).wait()
        self.copy(MATE).wait_recv()

    def arrive_far(self):
        for stage in range(self.stages()):
            for name in self.names(stage)[0]:
                if name in (PASS, PASS_BESIDE, PASS_ALONG, PASS_LAST):
                    self.copy(name).wait_recv()

    def finish(self):
        for name in (MATE, ACROSS) + sum((self.names(stage)[0] for stage in range(self.stages())), ()):
            self.copy(name).wait_send()


def waves(column, frequency, quarter):
    angle = column * frequency
    turns = jnp.floor(angle * (2.0 / math.pi) + 0.5)
    rest = ((angle - turns * 1.5703125) - turns * 4.837512969970703125e-4) - turns * 7.549789948768648e-8
    quadrant = turns.astype(jnp.int32) + quarter
    z = rest * rest
    sine = ((-1.9515295891e-4 * z + 8.3321608736e-3) * z - 1.6666654611e-1) * z * rest + rest
    cosine = ((2.443315711809948e-5 * z - 1.388731625493765e-3) * z + 4.166664568298827e-2) * z * z - 0.5 * z + 1.0
    value = jnp.where(quadrant % 2 == 1, cosine, sine)
    return jnp.where((quadrant // 2) % 2 == 1, -value, value)


def gelu(v):
    return 0.5 * v * (1.0 + jnp.tanh(math.sqrt(2.0 / math.pi) * (v + 0.044715 * (v * v * v))))


def row_of(ref):
    return ref[...].reshape(1, ref.shape[0])


def column_of(row):
    return jnp.broadcast_to(row, (8, 128)).T[:, 0:1]


def forward_kernel(
    box_ref, mask_ref, qvb_ref, b1_ref, table_ref, ob_ref, g1_ref, s1_ref, c2_ref, g2_ref, s2_ref,
    tok_in, cot_in, rx_in, ry_in, lay_in, qkv_own, wo_own, w1_own, w2_own,
    probs_out, qkvt_out, ctxt_out, low_out, feat_out, unit_out, inv_out, nlow_out, pre_out, hid_out,
    block_out, dres_out, sums_out, wqkv_out, wo_out, w1_out, w2_out,
    low, feat, unit_rows, nlow, block_rows, dres_rows, lay, tokb, cotb, rxb, ryb, vec, rows_own, wqkv, wo, w1, w2, rows, cols, tabs, layer_in, qkvt, pbuf, ctxt, ctx, normed, pre,
    hid, acc, send, recv, here, out_sem, p_sem, in_sem,
):
    t, d = lax.axis_index("tensor"), lax.axis_index("dp")
    mate, across = {"tensor": xor_index(t, 1)}, {"tensor": xor_index(t, 2)}
    near = [{"dp": xor_index(d, 1)}, {"dp": xor_index(d, 2)}]
    peers = (mate, across, near, (d % 2, (d // 2) % 2))
    win, model = tokb.shape
    heads = 4 * HEADS_T
    cols_t = HEADS_T * HD
    hid_t = w1_own.shape[1]
    sems = (send, recv, here)
    f32, bf16 = jnp.float32, jnp.bfloat16
    block = 128

    everyone = [mate, across] + near
    signal_peers(everyone)
    own_rows = pl.ds(pl.multiple_of(t * win, win), win)
    loads = [
        pltpu.make_async_copy(src, dst, in_sem.at[k])
        for k, (src, dst) in enumerate(
            [(tok_in.at[own_rows], tokb), (rx_in.at[t], rxb), (ry_in.at[t], ryb), (cot_in.at[own_rows], cotb), (lay_in, lay)]
        )
    ]
    for c in loads:
        c.start()
    for k, ref in enumerate((ob_ref, g1_ref, s1_ref, c2_ref, g2_ref, s2_ref)):
        vec[k : k + 1, :] = row_of(ref)
    rows_own[...] = jnp.zeros_like(rows_own)
    rows_own[0:1, :] = row_of(b1_ref)
    rows_own[1 : 1 + HEADS_T, 0 : 2 * BUCKETS] = table_ref[...].astype(f32)
    rows_own[4:6, 0:cols_t] = qvb_ref[...]

    def piece_rows(r, s, count):
        return pl.ds(pl.multiple_of(r * count + s.start, 16), s.size)

    gathers = {}

    def chunk(name, own, place, count):
        gathers[name] = Gather(own, place, count, *WAYS[name], sems, name, peers)

    chunk(AT_R, lambda s: rows_own.at[s], lambda r, s: rows.at[r, s], 8)
    for n, name in enumerate((AT_Q, AT_K, AT_V)):
        chunk(
            name,
            lambda s, n=n: qkv_own.at[n, s],
            lambda r, s, n=n: wqkv.at[n, piece_rows(r, s, cols_t)],
            cols_t,
        )
    chunk(AT_O, lambda s: wo_own.at[s], lambda r, s: wo.at[piece_rows(r, s, cols_t)], cols_t)
    third = hid_t // 3
    for k in range(3):
        units = pl.ds(k * third, third)
        chunk(
            U0 + 2 * k, lambda s, units=units: w1_own.at[s, units], lambda r, s, units=units: w1.at[r, s, units], model
        )

        def moved(s, k=k):
            return pl.ds(pl.multiple_of(s.start + k * third, 16), s.size)

        chunk(
            D0 + 2 * k, lambda s, moved=moved: w2_own.at[moved(s)], lambda r, s, moved=moved: w2.at[r, moved(s)], third
        )

    def at_slot(phase, index=0):
        for name, stage in FORWARD.get((phase, index), ()):
            gathers[name].forward(stage)

    def at_loop(phase, index, count, first=0, step=1):
        for k in range(count):
            if (phase, first + step * k) in FORWARD:
                @pl.when(index == k)
                def _(k=k):
                    at_slot(phase, first + step * k)

    def near_pieces(names):
        for name in names:
            gathers[name].arrive_near()

    def far_pieces(names):
        for name in names:
            gathers[name].arrive_far()

    lane = lax.broadcasted_iota(jnp.int32, (1, 128), 1)
    quarter = jnp.where(lane >= LFREQ, 1, 0)
    frequency = jnp.exp((lane % LFREQ).astype(f32) * (-math.log(1000.0) / LFREQ))
    loads[0].wait()
    loads[4].wait()

    def layer_rows(i):
        sl = pl.ds(pl.multiple_of(i * block, block), block)
        box = box_ref[:, pl.ds(pl.multiple_of(t * win + i * block, block), block)].astype(f32)
        for m in range(4):
            feat[sl, 2 * LFREQ * m : 2 * LFREQ * (m + 1)] = waves(
                column_of(box[m : m + 1, :]), frequency, quarter
            ).astype(bf16)
        value = tokb[sl, :].astype(f32) + nn(feat[sl, :], lay[...])
        layer_in[sl, :] = value
        low[sl, :] = value.astype(bf16)
        at_loop(F_FEAT, i, 4)

    wait_peers(everyone)
    for name in SEND_ORDER:
        gathers[name].start()
    pl.loop(0, win // block)(layer_rows)

    def bias_columns(pieces):
        for r in pieces:
            turned = rows[r, :, 0:256].T
            for n, row in ((0, 4), (2, 5)):
                cols[n, pl.ds(r * cols_t, cols_t), :] = turned[0:cols_t, row : row + 1]
            tabs[HEADS_T * r : HEADS_T * (r + 1), :] = rows[r, 1 : 1 + HEADS_T, 0:128]

    def project(pieces):
        for n in range(3):
            sl = pl.ds(pieces[0] * cols_t, len(pieces) * cols_t)
            if True:
                value = nt(wqkv[n, sl, :], low[...])
                if n != 1:
                    value = value + cols[n, sl, :]
                qkvt[n, sl, :] = value.astype(bf16)

    near_pieces((AT_R, AT_Q, AT_K, AT_V))
    bias_columns((0, 1))
    project((0, 1))
    at_slot(F_NEAR)
    for c in loads[1:3]:
        c.wait()

    def table_row(h):
        return (tabs[pl.ds(h, 1), :] * 2048.0 + 32768.5).astype(jnp.int32) - 32768

    def p_copy(i, slot):
        return pltpu.make_async_copy(pbuf.at[slot], probs_out.at[pl.ds(2 * i, 2)], p_sem.at[slot])

    def two_heads(i):
        slot = i % 2
        sl = pl.ds(pl.multiple_of(i * 2 * HD, 2 * HD), 2 * HD)
        q = (qkvt[0, sl, :].astype(f32).T * HD ** (-0.5)).astype(bf16)
        tab = jnp.broadcast_to((table_row(2 * i) << 16) + table_row(2 * i + 1), (win, 128))
        bias = ([], [])
        for c in range(win // 128):
            at = slice(128 * c, 128 * c + 128)
            word = jnp.take_along_axis(tab, rxb[:, at], axis=1) + jnp.take_along_axis(
                tab, ryb[:, at] + BUCKETS, axis=1
            )
            second = word << 16
            bias[0].append((word - (second >> 16)).astype(f32) * 2.0**-27)
            bias[1].append(second.astype(f32) * 2.0**-27)

        @pl.when(i >= 2)
        def _():
            p_copy(i - 2, slot).wait()

        for u in range(2):
            rows_u = pl.ds(pl.multiple_of(i * 2 * HD + u * HD, HD), HD)
            s = nn(q[:, u * HD : (u + 1) * HD], qkvt[1, rows_u, :]) + jnp.concatenate(bias[u], axis=1)
            m = jnp.max(s, axis=1, keepdims=True)
            e = jnp.exp(s - m)
            p = e * (1.0 / jnp.sum(e, axis=1, keepdims=True))
            pbuf[slot, u] = p
            ctxt[rows_u, :] = nt(qkvt[2, rows_u, :], p.astype(bf16)).astype(bf16)
            at_loop(F_HEAD, i, heads // 2, u, 2)
        p_copy(i, slot).start()

    pl.loop(0, heads // 4)(two_heads)
    at_slot(F_FAR)
    far_pieces((AT_R, AT_Q, AT_K, AT_V))
    bias_columns((2, 3))
    project((2, 3))
    at_slot(F_BOTH)
    pl.loop(heads // 4, heads // 2)(two_heads)

    last = heads // 2
    outs = [
        (qkvt, qkvt_out), (ctxt, ctxt_out), (wqkv, wqkv_out), (low, low_out), (feat, feat_out),
    ]
    done = []

    def leave(src, dst):
        c = pltpu.make_async_copy(src, dst, out_sem.at[len(done)])
        c.start()
        done.append(c)

    for src, dst in outs:
        leave(src, dst)
    at_slot(F_OUT)
    near_pieces((AT_O,))
    far_pieces((AT_O,))
    leave(wo, wo_out)
    ctx[...] = ctxt[...].astype(f32).T.astype(bf16)
    at_slot(F_CONTEXT)

    @pl.loop(0, win // block)
    def _(i):
        sl = pl.ds(pl.multiple_of(i * block, block), block)
        value = layer_in[sl, :] + nn(ctx[sl, :], wo[...]) + vec[0:1, :]
        mean = jnp.mean(value, axis=1, keepdims=True)
        centered = value - mean
        inverse = lax.rsqrt(jnp.mean(centered * centered, axis=1, keepdims=True) + EPSILON)
        unit = centered * inverse
        unit_rows[sl, :] = unit
        inv_out[sl, :] = inverse
        value = unit * vec[1:2, :] + vec[2:3, :]
        normed[sl, :] = value
        nlow[sl, :] = value.astype(bf16)
        at_loop(F_NORM, i, 4)

    leave(unit_rows, unit_out)
    leave(nlow, nlow_out)
    near_pieces(range(U0, D2 + 1))
    for src, dst in ((w1, w1_out), (w2, w2_out)):
        leave(src.at[pl.ds(0, 2)], dst.at[pl.ds(0, 2)])
    for r in range(2):
        value = nn(nlow[...], w1[r]) + rows[r, 0:1, :]
        pre[r] = value
        low_hid = gelu(value).astype(bf16)
        hid[r] = low_hid
        more = nn(low_hid, w2[r])
        acc[...] = more if r == 0 else acc[...] + more
        for i in range(2):
            at_slot(F_UP, 2 * r + i)

        leave(pre.at[r], pre_out.at[r])
        leave(hid.at[r], hid_out.at[r])

    for k in range(3):
        at_slot(F_THIRD, k)
        far_pieces((U0 + 2 * k, D0 + 2 * k))
        units = pl.ds(k * third, third)

        for r in range(2, 4):
            value = nn(nlow[...], w1[r, :, units]) + rows[r, 0:1, units]
            pre[r, :, units] = value
            low_hid = gelu(value).astype(bf16)
            hid[r, :, units] = low_hid
            acc[...] += nn(low_hid, w2[r, units, :])

        at_slot(F_DONE, k)

        for src, dst in ((pre, pre_out), (hid, hid_out)):
            leave(src.at[pl.ds(2, 2), :, units], dst.at[pl.ds(2, 2), :, units])
        leave(w1.at[pl.ds(2, 2), :, units], w1_out.at[pl.ds(2, 2), :, units])
        leave(w2.at[pl.ds(2, 2), units], w2_out.at[pl.ds(2, 2), units])

    loads[3].wait()

    sums_out[...] = jnp.zeros_like(sums_out)

    @pl.loop(0, win // block)
    def _(i):
        sl = pl.ds(pl.multiple_of(i * block, block), block)
        value = normed[sl, :] + acc[sl, :] + vec[3:4, :]
        mean = jnp.mean(value, axis=1, keepdims=True)
        centered = value - mean
        inverse = lax.rsqrt(jnp.mean(centered * centered, axis=1, keepdims=True) + EPSILON)
        unit = centered * inverse
        block_rows[sl, :] = (unit * vec[4:5, :] + vec[5:6, :]).astype(bf16)
        mask = column_of(mask_ref[pl.ds((win // block) * t + i, 1), :].astype(f32))
        selected = mask * cotb[sl, :].astype(f32)
        scaled = selected * vec[4:5, :]
        mean_one = jnp.mean(scaled, axis=1, keepdims=True)
        mean_two = jnp.mean(scaled * unit, axis=1, keepdims=True)
        dres = (scaled - mean_one - unit * mean_two) * inverse
        dres_rows[sl, :] = dres
        for src, dst, k in ((block_rows, block_out, 30), (dres_rows, dres_out, 31)):
            pltpu.make_async_copy(src.at[sl], dst.at[sl], out_sem.at[k]).start()
        sums_out[0:1, :] += jnp.sum(selected * unit, axis=0, keepdims=True)
        sums_out[1:2, :] += jnp.sum(selected, axis=0, keepdims=True)
        sums_out[2:3, :] += jnp.sum(dres, axis=0, keepdims=True)
        sums_out[3:4, :] += jnp.sum(mask, axis=0, keepdims=True)

    for i in (last - 2, last - 1):
        p_copy(i, i % 2).wait()
    for c in done:
        c.wait()
    for src, dst, k in ((block_rows, block_out, 30), (dres_rows, dres_out, 31)):
        pltpu.make_async_copy(src, dst, out_sem.at[k]).wait()
    for g in gathers.values():
        g.finish()


def forward_window(small, large):
    wo_own, w1_own = large[6:8]
    win, model = large[2].shape[1], large[0].shape[1]
    cols_t, hid_t = wo_own.shape[0], w1_own.shape[1]
    heads = 4 * HEADS_T
    f32, bf16 = jnp.float32, jnp.bfloat16
    shape = jax.ShapeDtypeStruct
    here = pl.BlockSpec(memory_space=pltpu.VMEM)
    away = pl.BlockSpec(memory_space=pl.ANY)
    outs = [
        (shape((heads, win, win), f32), away),
        (shape((3, model, win), bf16), away),
        (shape((model, win), bf16), away),
        (shape((win, model), bf16), away),
        (shape((win, 8 * LFREQ), bf16), away),
        (shape((win, model), f32), away),
        (shape((win, 1), f32), here),
        (shape((win, model), bf16), away),
        (shape((4, win, hid_t), f32), away),
        (shape((4, win, hid_t), bf16), away),
        (shape((win, model), bf16), away),
        (shape((win, model), f32), away),
        (shape((8, model), f32), here),
        (shape((3, model, model), bf16), away),
        (shape((model, model), bf16), away),
        (shape((4, model, hid_t), bf16), away),
        (shape((4, hid_t, model), bf16), away),
    ]
    return pl.pallas_call(
        forward_kernel,
        in_specs=[here] * len(small) + [away] * len(large),
        out_specs=[spec for _, spec in outs],
        out_shape=[s for s, _ in outs],
        scratch_shapes=[
            pltpu.VMEM((win, model), bf16),
            pltpu.VMEM((win, 8 * LFREQ), bf16),
            pltpu.VMEM((win, model), f32),
            pltpu.VMEM((win, model), bf16),
            pltpu.VMEM((win, model), bf16),
            pltpu.VMEM((win, model), f32),
            pltpu.VMEM((8 * LFREQ, model), bf16),
            pltpu.VMEM((win, model), bf16),
            pltpu.VMEM((win, model), bf16),
            pltpu.VMEM((win, win), jnp.int32),
            pltpu.VMEM((win, win), jnp.int32),
            pltpu.VMEM((8, model), f32),
            pltpu.VMEM((8, model), f32),
            pltpu.VMEM((3, model, model), bf16),
            pltpu.VMEM((model, model), bf16),
            pltpu.VMEM((4, model, hid_t), bf16),
            pltpu.VMEM((4, hid_t, model), bf16),
            pltpu.VMEM((4, 8, model), f32),
            pltpu.VMEM((3, model, 1), f32),
            pltpu.VMEM((heads, 128), f32),
            pltpu.VMEM((win, model), f32),
            pltpu.VMEM((3, model, win), bf16),
            pltpu.VMEM((2, 2, win, win), f32),
            pltpu.VMEM((model, win), bf16),
            pltpu.VMEM((win, model), bf16),
            pltpu.VMEM((win, model), f32),
            pltpu.VMEM((4, win, hid_t), f32),
            pltpu.VMEM((4, win, hid_t), bf16),
            pltpu.VMEM((win, model), f32),
            pltpu.SemaphoreType.DMA((11, 10)),
            pltpu.SemaphoreType.DMA((11, 10)),
            pltpu.SemaphoreType.DMA((11,)),
            pltpu.SemaphoreType.DMA((32,)),
            pltpu.SemaphoreType.DMA((2,)),
            pltpu.SemaphoreType.DMA((5,)),
        ],
        compiler_params=pltpu.CompilerParams(
            vmem_limit_bytes=60 * 2**20, collective_id=0, has_side_effects=True
        ),
        name="forward_window",
    )(*small, *large)


def bits_of(size):
    return [1 << b for b in range(size.bit_length() - 1)]


def tn(a, b):
    return lax.dot_general(a, b, (((0,), (0,)), ((), ())), preferred_element_type=jnp.float32)


UNIT = 128


class Reduce:
    def __init__(self, slot, order, part, core, landing, final, extra, result, acc, sems, peers):
        self.slot, self.order, self.part, self.core, self.landing = slot, order, part, core, landing
        self.final, self.extra, self.result, self.acc = final, extra, result, acc
        self.send, self.recv, self.here = sems
        self.mate, self.partners, self.further, self.sides = peers
        self.total = core.at[0] if acc is None else acc
        self.steps = order[0] + order[1]

    def move(self, k, src, dst, peer):
        return remote(src, dst, self.send.at[self.slot, k], self.recv.at[self.slot, k], peer)

    def region(self, fixed, other=None):
        index = [slice(None)]
        for axis in (Z_FAR, Z_NEAR, Y):
            if axis == other:
                index.append(pl.ds(1 - self.sides[axis], 1))
            elif axis in fixed:
                index.append(pl.ds(self.sides[axis], 1))
            else:
                index.append(slice(None))
        return tuple(index)

    def pieces(self, stage):
        return (0,) if X in self.order[0][:stage] else (0, 1)

    def moves(self, stage, piece=None):
        axis = self.steps[stage]
        peer = self.partners[axis]
        if stage >= len(self.order[0]):
            done = self.order[1][: stage - len(self.order[0])]
            rows = self.region([a for a in (Z_FAR, Z_NEAR, Y) if a not in done])
            src = self.result.at[rows] if done else self.final
            return [self.move(10 + len(done), src, self.result.at[rows], peer)]
        fixed = self.order[0][:stage]
        if axis == X:
            return [self.move(2 + 2 * stage, self.core.at[(1,) + self.region(fixed)], self.landing[stage].at[0], peer)] if piece != 0 else []
        return [
            self.move(2 + 2 * stage + p, self.core.at[(p,) + self.region(fixed, axis)], self.landing[stage].at[p], peer)
            for p in self.pieces(stage)
            if piece in (None, p)
        ]

    def to_mate(self, piece):
        return self.move(piece, self.part(piece), self.core.at[piece], self.mate)

    def own_copy(self):
        rows = self.region((Z_FAR, Z_NEAR, Y))
        return pltpu.make_async_copy(self.final, self.result.at[rows], self.here.at[self.slot])

    def more(self, k):
        return self.move(13 + k, self.final_of(k), self.extra.at[k], self.further[k])

    def final_of(self, k):
        return self.final if k == 0 else self.extra.at[len(self.further) + k]

    def merge(self, piece, unit, half, value):
        at = (unit, half)
        value = value.reshape(2, 2, 16, value.shape[-1]) + self.core[(piece,) + at].astype(jnp.float32)
        if piece == 0:
            self.total[at] = value.astype(self.total.dtype)
        else:
            self.core[(1,) + at] = value.astype(jnp.bfloat16)

    def take(self, stage):
        for m in self.moves(stage):
            m.wait_recv()
        count = len(self.order[0])
        if stage == count:
            self.own_copy().wait()
        if stage >= count:
            return
        axis = self.steps[stage]
        rows = self.region(self.order[0][: stage + 1])
        for p in (0,) if axis == X else self.pieces(stage):
            dst = self.total if p == 0 else self.core.at[p]
            value = dst[rows].astype(jnp.float32) + self.landing[stage][p].astype(jnp.float32)
            if stage + 1 == count:
                self.final[...] = value.astype(jnp.bfloat16)
            else:
                dst[rows] = value.astype(dst.dtype)
        if stage + 1 == count:
            for k in range(len(self.further)):
                self.more(k).start()
                self.more(k).wait()
                total = self.final_of(k)[...].astype(jnp.float32) + self.extra[k].astype(jnp.float32)
                self.final_of(k + 1)[...] = total.astype(jnp.bfloat16)
            if self.further:
                self.final[...] = self.final_of(len(self.further))[...]
            self.own_copy().start()

    def go(self, stage, piece=None):
        if stage < len(self.order[0]) and self.steps[stage] != X and self.acc is not None and piece != 1:
            rows = self.region(self.order[0][:stage], self.steps[stage])
            self.core[(0,) + rows] = self.acc[rows].astype(jnp.bfloat16)
        for m in self.moves(stage, piece):
            m.start()

    def next(self, stage):
        self.take(stage)
        if stage + 1 < len(self.steps):
            self.go(stage + 1)

    def sent(self):
        for stage in range(len(self.steps)):
            for m in self.moves(stage):
                m.wait_send()


def landing_shapes(units, order):
    shapes, pieces, dims = [], 2, {Z_FAR: 2, Z_NEAR: 2, Y: 2}
    for axis in order[0]:
        if axis == X:
            pieces = 1
        else:
            dims[axis] = 1
        shapes.append((pieces, units, dims[Z_FAR], dims[Z_NEAR], dims[Y], 16))
    return shapes


def xor_level(level, k):
    for bit in (1, 2):
        if k & bit:
            level = xor_index(level, bit)
    return level


def gelu_slope(v):
    k = math.sqrt(2.0 / math.pi)
    square = v * v
    t = jnp.tanh(k * v * (1.0 + 0.044715 * square))
    return 0.5 * (1.0 + t) + (0.5 * k) * v * (1.0 - t * t) * (1.0 + 3 * 0.044715 * square)


SMALL = 16


def backward_kernel(
    n_dp, inv_ref, gain_ref, sums_ref, dres_in, hid_in, pre_in, unit_in, nlow_in, low_in, feat_in, qkvt_in, ctxt_in,
    probs_in, rx_in, ry_in, w1_in, w2_in, wo_in, wqkv_in, block_in,
    block_all, in_all, red1, red2, red3, lay_all, small_out,
    arena, hidb, preb, dres, unit, nlow, nlow_t, dn, low_rows, qkvb, ctxtb, dctx, lowb, featb, wob, rxb, ryb, hot, acc,
    part1, part2, part3, core1, core2, core3, landings, finals, extras, acc3, small, small_in, short,
    load_sem, send, recv, here, share_send, share_recv, small_send, small_recv, p_sem,
):
    t, d = lax.axis_index("tensor"), lax.axis_index("dp")
    mate, across = {"tensor": xor_index(t, 1)}, {"tensor": xor_index(t, 2)}
    beside = {"dp": xor_index(d, 1)}
    along = [None] + [{"dp": d + 2 * (xor_level((d // 2) % 4, k) - (d // 2) % 4)} for k in range(1, 4)]
    further = [{"dp": xor_index(d, bit)} for bit in bits_of(n_dp) if bit >= 8]
    partners = {X: across, Y: beside, Z_NEAR: along[1], Z_FAR: along[2]}
    peers = (mate, partners, further, {Y: d % 2, Z_NEAR: (d // 2) % 2, Z_FAR: (d // 4) % 2})
    sems = (send, recv, here)
    f32, bf16 = jnp.float32, jnp.bfloat16
    win, model = dres.shape
    heads = 4 * HEADS_T
    cols_t = HEADS_T * HD
    hid_t = model
    block = 128

    everyone = [mate, across, beside] + along[1:] + further
    signal_peers(everyone)

    def load(k, src, dst):
        return pltpu.make_async_copy(src, dst, load_sem.at[k])

    def w_rows(r):
        return pl.ds(r * hid_t, hid_t)

    def h_rows(r):
        return pl.ds(r * win, win)

    order = (3, 1, 2, 0)
    ld_dres = load(0, dres_in, dres)
    ld_hid = {r: load(1 + r, hid_in.at[r], hidb.at[h_rows(r)]) for r in order}
    ld_w2 = {r: load(5 + r, w2_in.at[r], arena.at[w_rows(r)]) for r in order}
    ld_w1 = {r: load(9 + r, w1_in.at[r], arena.at[w_rows(4 + r)]) for r in order}
    ld_pre = {r: load(13 + r, pre_in.at[r], preb.at[i % 2]) for i, r in enumerate(order)}
    ld_rest = [
        load(17 + k, src, dst)
        for k, (src, dst) in enumerate(
            [
                (nlow_in, nlow), (unit_in, unit), (ctxt_in, ctxtb), (wo_in, wob), (qkvt_in, qkvb), (low_in, lowb),
                (feat_in, featb), (rx_in.at[t], rxb), (ry_in.at[t], ryb),
            ]
        )
    ]
    ld_wqkv = [load(26 + n, wqkv_in.at[n], hidb.at[pl.ds(n * model, model)]) for n in range(3)]
    ld_dres.start()
    for r in order:
        ld_hid[r].start()
    for r in order[:2]:
        ld_pre[r].start()
    for r in order:
        ld_w2[r].start()
    ld_rest[0].start()
    for r in order:
        ld_w1[r].start()
    for c in ld_rest[1:]:
        c.start()

    def chunks(first, units, parts, core, result, acc=None):
        out, at = [], 0
        for k, (count, part) in enumerate(zip(units, parts)):
            rows = pl.ds(at, count)
            slot = first + k
            out.append(
                Reduce(
                    slot, ORDERS[slot], part, core.at[:, rows], landings[slot], finals[slot], extras[slot],
                    result.at[rows], None if acc is None else acc.at[rows], sems, peers,
                )
            )
            at += count
        return out

    third = hid_t // 3

    def pairs(ref):
        return [lambda p, k=k: ref.at[p, pl.ds(2 * k, 2)] for k in range(3)]

    s2 = chunks(0, [2] * 3, pairs(part2), core2, red2)
    s1 = chunks(3, [2] * 3, pairs(part1), core1, red1)
    s3 = chunks(
        6, [1] * 7,
        [lambda p, k=k: part2.at[p, pl.ds(k, 1)] for k in range(6)] + [lambda p: part3.at[p]],
        core3, red3, acc3,
    )
    lay_t = featb.shape[1] // 4

    def share(k, src, whole, rows, part=0, parts=1):
        def at(index):
            return whole.at[pl.ds(pl.multiple_of((index * parts + part) * rows, rows), rows)]

        def moved(j, from_ref, index, peer):
            return remote(from_ref, at(index), share_send.at[k, j], share_recv.at[k, j], peer)

        far = xor_index(t, 2)
        return {
            "here": pltpu.make_async_copy(src, at(t), share_send.at[k, 3]),
            "across": moved(0, src, t, across),
            "mate": moved(1, src, t, mate),
            "pass": moved(2, at(far), far, mate),
        }

    def share_start(c):
        for name in ("across", "mate", "here"):
            c[name].start()

    def share_pass(c):
        c["across"].wait_recv()
        c["pass"].start()

    def share_end(c):
        c["here"].wait()
        c["mate"].wait_recv()
        c["pass"].wait_recv()
        for name in ("across", "mate", "pass"):
            c[name].wait_send()

    quarter_win = win // 4
    sh_block = [
        share(k, block_in.at[pl.ds(k * quarter_win, quarter_win)], block_all, quarter_win, k, 4) for k in range(4)
    ]
    sh_in = share(4, low_rows, in_all, win)
    sh_lay = share(5, red3.at[pl.ds(6, 1)], lay_all, 1)
    bits = [mate, across, beside, along[1], along[2]] + further

    def small_move(k):
        return remote(small.at[k], small_in.at[k], small_send.at[k], small_recv.at[k], bits[k])

    def small_step(k):
        small_move(k).wait()
        small[k + 1] = small[k] + small_in[k]
        if k + 1 < len(bits):
            small_move(k + 1).start()

    named = dict(zip(range(A0, C6 + 1), s2 + s1 + s3))

    def run(what, stage):
        if what in named:
            named[what].next(stage)
        elif what == BLOCK:
            share_start(sh_block[stage])
        elif what == BLOCK_ON:
            share_pass(sh_block[stage])
        elif what == INPUT_ON:
            share_pass(sh_in)
        elif what == LAY:
            share_start(sh_lay)
        elif what == LAY_ON:
            share_pass(sh_lay)
        elif what == SMALL_STEP:
            small_step(stage)

    def at_slot(phase, index=0):
        for what, stage in SCHEDULE.get((phase, index), ()):
            run(what, stage)

    def at_loop(phase, index, count, first=0):
        for k in range(count):
            if (phase, first + k) in SCHEDULE:
                @pl.when(index == k)
                def _(k=k):
                    at_slot(phase, first + k)


    small[0] = jnp.zeros_like(small[0])
    small[0, 3:4, :] = sums_ref[2:3, :]
    small[0, 4:6, :] = sums_ref[0:2, :]
    small[0, 6:7, :] = sums_ref[3:4, :]

    def own_row(base, r):
        index = t
        for bit in (1, 2):
            if r & bit:
                index = xor_index(index, bit)
        return pl.ds(base + index, 1)

    ld_dres.wait()

    @pl.loop(0, win // block)
    def _(i):
        sl = pl.ds(pl.multiple_of(i * block, block), block)
        low_rows[sl, :] = dres[sl, :].astype(bf16)

    def grad_w2(r, c):
        sl = pl.ds(pl.multiple_of(c * third, third), third)
        return tn(hidb[h_rows(r), sl], low_rows[...])

    def grad_w1(r, c):
        sl = pl.ds(pl.multiple_of(c * third, third), third)
        return nn(nlow_t[sl, :], hidb[h_rows(r), :])

    def blocks(value):
        return value.reshape(value.shape[0] // UNIT, 2, 2, 2, 16, value.shape[1])

    def for_mate(group, grad, r, part):
        @pl.loop(0, 3)
        def _(c):
            part[r // 2, pl.ds(2 * c, 2)] = blocks(grad(r, c).astype(bf16))

        for g in group:
            g.to_mate(r // 2).start()

    def merge_all(g, piece, value):
        half = UNIT // 2
        for k in range(value.shape[0] // half):
            g.merge(piece, k // 2, k % 2, value[k * half : (k + 1) * half])

    def for_own(group, grad, r):
        for c, g in enumerate(group):
            g.to_mate(r // 2).wait_recv()
            merge_all(g, r // 2, grad(r, c))
            g.go(0, r // 2)

    for r in order[:2]:
        ld_hid[r].wait()
        if r == order[0]:
            for_mate((), grad_w2, r, part2)
            wait_peers(everyone)
            at_slot(START)
            for g in s2:
                g.to_mate(r // 2).start()
        else:
            for_mate(s2, grad_w2, r, part2)

    ld_rest[0].wait()
    nlow_t[...] = nlow[...].astype(f32).T.astype(bf16)
    for j, r in enumerate(order):
        ld_pre[r].wait()
        ld_w2[r].wait()
        ld_w1[r].wait()

        @pl.loop(0, 2)
        def _(i, j=j, r=r):
            count = win // 2
            sl = pl.ds(pl.multiple_of(i * count, count), count)
            hs = pl.ds(pl.multiple_of(r * win + i * count, count), count)
            dhid = nt(low_rows[sl, :], arena[w_rows(r), :])
            dpre = (dhid * gelu_slope(preb[j % 2, sl, :])).astype(bf16)
            hidb[hs, :] = dpre
            row = own_row(8, r)
            small[0, row, :] += jnp.sum(dpre.astype(f32), axis=0, keepdims=True)
            more = nt(dpre, arena[w_rows(4 + r), :])
            dn[sl, :] = more if j == 0 else dn[sl, :] + more
            at_loop(FFN, i, 2, 3 * j)

        if j + 2 < 4:
            ld_pre[order[j + 2]].start()
        if j < 2:
            for_mate(s1, grad_w1, r, part1)
        else:
            for_own(s1, grad_w1, r)
        if j == 0:
            for q in order[2:]:
                ld_hid[q].wait()
                for_own(s2, grad_w2, q)
        at_slot(FFN, 3 * j + 2)

    for c in ld_wqkv:
        c.start()

    def p_load(h, slot):
        return pltpu.make_async_copy(probs_in.at[h], preb.at[slot, :, pl.ds(0, win)], p_sem.at[slot])

    for h in range(2):
        p_load(h, h).start()
    for g in s2:
        for p in range(2):
            g.to_mate(p).wait_send()

    ld_rest[1].wait()

    @pl.loop(0, win // block)
    def _(i):
        sl = pl.ds(pl.multiple_of(i * block, block), block)
        up = dres[sl, :] + dn[sl, :]
        units = unit[sl, :]
        scaled = up * row_of(gain_ref)
        mean_one = jnp.mean(scaled, axis=1, keepdims=True)
        mean_two = jnp.mean(scaled * units, axis=1, keepdims=True)
        value = (scaled - mean_one - units * mean_two) * inv_ref[sl, :]
        dn[sl, :] = value
        low_rows[sl, :] = value.astype(bf16)
        small[0, 0:1, :] += jnp.sum(value, axis=0, keepdims=True)
        small[0, 1:2, :] += jnp.sum(up * units, axis=0, keepdims=True)
        small[0, 2:3, :] += jnp.sum(up, axis=0, keepdims=True)

    at_slot(NORM)
    for c in ld_rest[2:]:
        c.wait()

    @pl.loop(0, 4)
    def _(r):
        sl = pl.ds(pl.multiple_of(r * cols_t, cols_t), cols_t)
        dctx[sl, :] = nt(wob[sl, :], low_rows[...]).astype(bf16)

    at_slot(OUT)

    @pl.loop(0, heads)
    def _(h):
        slot = h % 2
        sl = pl.ds(pl.multiple_of(h * HD, HD), HD)
        dc_t = dctx[sl, :]
        dc = dc_t.astype(f32).T.astype(bf16)
        p_load(h, slot).wait()
        p = preb[slot, :, 0:win]
        dp = nn(dc, qkvb[2, sl, :])
        row_dot = jnp.sum(p * dp, axis=1, keepdims=True)
        ds = (p * (dp - row_dot)).astype(bf16)
        qkvb[2, sl, :] = nn(dc_t, p.astype(bf16)).astype(bf16)
        dq = nt(qkvb[1, sl, :], ds) * HD ** (-0.5)
        dk = nn(qkvb[0, sl, :], ds) * HD ** (-0.5)
        qkvb[0, sl, :] = dq.astype(bf16)
        qkvb[1, sl, :] = dk.astype(bf16)
        arena[pl.ds(pl.multiple_of(h * win, win), win), 0:win] = ds

        @pl.when(h + 2 < heads)
        def _():
            p_load(h + 2, slot).start()

        at_loop(HEAD, h, heads)

    for c in ld_wqkv:
        c.wait()
    def rows_of(r):
        return pl.ds(r * cols_t, cols_t)

    def grad_out(r):
        return nn(ctxtb[rows_of(r), :], low_rows[...])

    def grad_proj(n, r):
        return nn(qkvb[n, rows_of(r), :], lowb[...])

    halves = (lambda r: grad_proj(2, r), grad_out, lambda r: grad_proj(0, r), lambda r: grad_proj(1, r))
    sixth = UNIT // 2
    each = cols_t // sixth
    for r in (3, 1):
        for k, grad in enumerate(halves):
            value = grad(r).astype(bf16)
            for j in range(each):
                at = k * each + j
                part2[r // 2, at // 2, at % 2] = value[j * sixth : (j + 1) * sixth].reshape(2, 2, 16, model)
            if k % 2 == 1:
                for g in s3[:6][3 * (k // 2) : 3 * (k // 2) + 3]:
                    g.to_mate(r // 2).start()
    at_slot(SENT)
    for r in (2, 0):
        for k, grad in enumerate(halves):
            value = grad(r)
            for j in range(each):
                at = k * each + j
                g = s3[at // 2]
                if at % 2 == 0:
                    g.to_mate(r // 2).wait_recv()
                g.merge(r // 2, 0, at % 2, value[j * sixth : (j + 1) * sixth])
                if at % 2 == 1:
                    g.go(0, r // 2)
    at_slot(MERGED)

    @pl.loop(0, win // block)
    def _(i):
        sl = pl.ds(pl.multiple_of(i * block, block), block)
        value = dn[sl, :]
        for n in range(3):
            value = value + tn(qkvb[n, :, sl], hidb[pl.ds(n * model, model), :])
        dn[sl, :] = value
        at_loop(DLAYER, i, 4)

    low_rows[...] = dn[...].astype(bf16)

    def grad_lay(r):
        index = t
        for bit in (1, 2):
            if r & bit:
                index = xor_index(index, bit)
        return tn(featb[:, pl.ds(pl.multiple_of(index * lay_t, lay_t), lay_t)], low_rows[...])

    for r in (3, 1):
        part3[r // 2] = blocks(grad_lay(r).astype(bf16))
        s3[6].to_mate(r // 2).start()
    at_slot(LAYOUT)
    for_own(s3[6:], lambda r, c: grad_lay(r), 2)
    for_own(s3[6:], lambda r, c: grad_lay(r), 0)
    share_start(sh_in)

    ones = jnp.ones((8, win), bf16)
    short[...] = jnp.zeros_like(short)
    for n, at in ((0, 0), (2, cols_t)):
        total = nt(ones, qkvb[n])
        for r in range(4):
            short[r : r + 1, at : at + cols_t] = total[0:1, r * cols_t : (r + 1) * cols_t]

    acc[...] = jnp.zeros_like(acc)
    one, zero = bf16(1), bf16(0)
    hots = BUCKETS * ROWS
    @pl.loop(0, win // ROWS // 2)
    def _(i):
        total = None
        for u in range(2):
            at = pl.multiple_of(i * 2 * ROWS + u * ROWS, ROWS)
            x = rxb[pl.ds(at, ROWS), :].astype(f32).astype(bf16)
            y = ryb[pl.ds(at, ROWS), :].astype(f32).astype(bf16)
            for b in range(BUCKETS):
                hot[u, b * ROWS : (b + 1) * ROWS, :] = jnp.where(x == bf16(b), one, zero)
                hot[u, hots + b * ROWS : hots + (b + 1) * ROWS, :] = jnp.where(y == bf16(b), one, zero)
            left = jnp.concatenate(
                [arena[pl.ds(pl.multiple_of(h * win + at, ROWS), ROWS), 0:win] for h in range(heads)], axis=0
            )
            more = nt(left, hot[u])
            total = more if total is None else total + more
        acc[...] += total
        at_loop(TABLE, i, 16)

    row = lax.broadcasted_iota(jnp.int32, (ROWS, 2 * hots), 0)
    col = lax.broadcasted_iota(jnp.int32, (ROWS, 2 * hots), 1) % ROWS
    picked = jnp.concatenate(
        [
            jnp.sum(jnp.where(row == col, acc[h * ROWS : (h + 1) * ROWS, :], 0.0), axis=0, keepdims=True)
            for h in range(heads)
        ]
        + [jnp.zeros((16 - heads, 2 * hots), f32)],
        axis=0,
    )
    fold = (
        lax.broadcasted_iota(jnp.int32, (2 * hots, 128), 0) // ROWS
        == lax.broadcasted_iota(jnp.int32, (2 * hots, 128), 1)
    ).astype(f32)
    table = jnp.dot(picked, fold, preferred_element_type=f32, precision=lax.Precision.HIGHEST)
    for r in range(4):
        for a in range(HEADS_T):
            lane = 2 * cols_t + a * 2 * BUCKETS
            short[r : r + 1, lane : lane + 2 * BUCKETS] = table[
                r * HEADS_T + a : r * HEADS_T + a + 1, 0 : 2 * BUCKETS
            ]
    for r in range(4):
        small[0, own_row(12, r), :] = short[r : r + 1, :]

    small_move(0).start()
    at_slot(TAIL)
    for k in range(5, len(bits)):
        small_step(k)
    small_out[...] = small[len(bits)]
    for c in sh_block + [sh_in, sh_lay]:
        share_end(c)
    for g in s1 + s3:
        for p in range(2):
            g.to_mate(p).wait_send()
    for g in s2 + s1 + s3:
        g.sent()


def backward_window(n_dp, lay_rows, inv, gain, sums, dres, hid, pre, unit, nlow, low, feat, qkvt, ctxt, probs, rx, ry, w1, w2, wo, wqkv, block_own):
    win, model = dres.shape
    heads = 4 * HEADS_T
    cols_t = HEADS_T * HD
    lay_t = lay_rows // 4
    units = model // UNIT
    rest = (4 * cols_t + lay_t) // UNIT
    block = (2, 2, 2, 16, model)
    more = max(0, len(bits_of(n_dp)) - 3)
    levels = 5 + more
    sizes = [2] * 6 + [1] * 7
    f32, bf16 = jnp.float32, jnp.bfloat16
    shape = jax.ShapeDtypeStruct
    here = pl.BlockSpec(memory_space=pltpu.VMEM)
    away = pl.BlockSpec(memory_space=pl.ANY)
    outs = [
        (shape((4 * win, model), bf16), away),
        (shape((4 * win, model), bf16), away),
        (shape((units,) + block, bf16), away),
        (shape((units,) + block, bf16), away),
        (shape((rest,) + block, bf16), away),
        (shape((4,) + block, bf16), away),
        (shape((SMALL, model), f32), here),
    ]
    V = pltpu.VMEM
    S = pltpu.SemaphoreType.DMA
    return pl.pallas_call(
        functools.partial(backward_kernel, n_dp),
        in_specs=[here] * 3 + [away] * 17,
        out_specs=[spec for _, spec in outs],
        out_shape=[s for s, _ in outs],
        scratch_shapes=[
            V((8 * model, model), bf16), V((3 * model, model), bf16), V((2, win, model), f32), V((win, model), f32),
            V((win, model), f32), V((win, model), bf16), V((model, win), bf16), V((win, model), f32),
            V((win, model), bf16), V((3, model, win), bf16), V((model, win), bf16), V((model, win), bf16),
            V((win, model), bf16), V((win, lay_rows), bf16), V((model, model), bf16), V((win, win), jnp.int32),
            V((win, win), jnp.int32), V((2, 2 * BUCKETS * ROWS, win), bf16), V((heads * ROWS, 2 * BUCKETS * ROWS), f32),
            V((2, units) + block, bf16), V((2, units) + block, bf16), V((2, 1) + block, bf16),
            V((2, units) + block, bf16), V((2, units) + block, bf16), V((2, rest) + block, bf16),
            [[V(s + (model,), bf16) for s in landing_shapes(n, o)] for n, o in zip(sizes, ORDERS)],
            [V((n, 1, 1, 1, 16, model), bf16) for n in sizes],
            [V((2 * more + 1, n, 1, 1, 1, 16, model), bf16) for n in sizes], V((rest,) + block, f32),
            V((levels + 1, SMALL, model), f32), V((levels, SMALL, model), f32), V((8, model), f32),
            S((29,)), S((len(sizes), 13 + more)), S((len(sizes), 13 + more)), S((len(sizes),)), S((6, 4)), S((6, 3)),
            S((levels,)), S((levels,)), S((2,)),
        ],
        compiler_params=pltpu.CompilerParams(
            vmem_limit_bytes=63 * 2**20, collective_id=1, has_side_effects=True
        ),
        name="backward_window",
    )(inv, gain, sums, dres, hid, pre, unit, nlow, low, feat, qkvt, ctxt, probs, rx, ry, w1, w2, wo, wqkv, block_own)


def finish_kernel(
    rates, small_ref, in_in, red1, red2, red3, lay_in,
    in_out, lay_out, qkv_out, qvb_out, table_out, wo_out, ob_out, g1_out, s1_out, w1_out, b1_out, w2_out, c2_out,
    g2_out, s2_out, in_low, low1, low2, low3, lay_low, in_wide, wide1, wide2, wide3, lay_wide, load_sem, store_sem,
):
    t = lax.axis_index("tensor")
    cols_t = HEADS_T * HD
    inverse = 1.0 / small_ref[6:7, 0:1]
    jobs = []

    def job(src, low, wide, out, rate):
        jobs.append((src, low, wide, out, rate))

    def split(src, low, wide, out, rate, step):
        for at in range(0, low.shape[0], step):
            sl = pl.ds(at, step)
            job(src.at[sl], low.at[sl], None if wide is None else wide.at[sl], out.at[sl], rate)

    split(in_in, in_low, in_wide, in_out, None, 256)
    split(red2, low2, wide2, w2_out, 4, 256)
    split(red1, low1, wide1, w1_out, 3, 256)
    for n, at, rate in ((2, 0, 0), (None, 1, 1), (0, 2, 0), (1, 3, 0)):
        sl = pl.ds(at * cols_t, cols_t)
        job(red3.at[sl], low3.at[sl], wide3.at[sl], wo_out if n is None else qkv_out.at[n], rate)
    split(lay_in, lay_low, lay_wide, lay_out, 6, 256)
    loads = [pltpu.make_async_copy(src, low, load_sem.at[k]) for k, (src, low, _, _, _) in enumerate(jobs)]
    ahead = len(loads)
    for c in loads[:ahead]:
        c.start()

    def row(ref, index, rate):
        ref[...] = (small_ref[index : index + 1, :] * (inverse * rates[rate])).reshape(ref.shape)

    for ref, index, rate in ((ob_out, 0, 1), (g1_out, 1, 2), (s1_out, 2, 2), (c2_out, 3, 4), (g2_out, 4, 5), (s2_out, 5, 5)):
        row(ref, index, rate)
    b1_out[...] = (small_ref[pl.ds(8 + t, 1), :] * (inverse * rates[3])).reshape(b1_out.shape)
    own = small_ref[pl.ds(12 + t, 1), :]
    for k in range(2):
        qvb_out[k : k + 1, :] = own[:, k * cols_t : (k + 1) * cols_t] * (inverse * rates[0])
    for a in range(HEADS_T):
        at = 2 * cols_t + a * 2 * BUCKETS
        table_out[a : a + 1, :] = own[:, at : at + 2 * BUCKETS] * (inverse * rates[7])

    stores = []
    for k, (_, low, wide, out, rate) in enumerate(jobs):
        loads[k].wait()
        if k + ahead < len(jobs):
            loads[k + ahead].start()
        if wide is None:
            stores.append(pltpu.make_async_copy(low, out, store_sem.at[k]))
        else:
            factor = inverse if rate is None else inverse * rates[rate]
            wide[...] = low[...].astype(jnp.float32) * factor
            stores.append(pltpu.make_async_copy(wide, out, store_sem.at[k]))
        stores[-1].start()
    for c in stores:
        c.wait()


def finish(rates, small, block_all, in_all, sum1, sum2, sum3, lay_all, cols_t):
    f32, bf16 = jnp.float32, jnp.bfloat16
    shape = jax.ShapeDtypeStruct
    here = pl.BlockSpec(memory_space=pltpu.VMEM)
    away = pl.BlockSpec(memory_space=pl.ANY)
    model = in_all.shape[1]
    vector = (shape((model,), f32), here)
    outs = [
        (shape(in_all.shape, f32), away),
        (shape(lay_all.shape, f32), away),
        (shape((3, cols_t, model), f32), away),
        (shape((2, cols_t), f32), here),
        (shape((HEADS_T, 2 * BUCKETS), f32), here),
        (shape((cols_t, model), f32), away),
        vector, vector, vector,
        (shape(sum1.shape, f32), away),
        vector,
        (shape(sum2.shape, f32), away),
        vector, vector, vector,
    ]
    wide = [in_all, sum1, sum2, sum3, lay_all]
    return pl.pallas_call(
        finish_kernel,
        in_specs=[pl.BlockSpec(memory_space=pltpu.SMEM), here] + [away] * 5,
        out_specs=[spec for _, spec in outs],
        out_shape=[s for s, _ in outs],
        scratch_shapes=[pltpu.VMEM(v.shape, bf16) for v in wide]
        + [pltpu.VMEM(v.shape, f32) for v in wide]
        + [pltpu.SemaphoreType.DMA((32,)), pltpu.SemaphoreType.DMA((32,))],
        compiler_params=pltpu.CompilerParams(vmem_limit_bytes=60 * 2**20),
        name="finish",
    )(rates, small, in_all, sum1, sum2, sum3, lay_all)


def local(
    n_dp, n_t,
    tokens_in, box_coords, rel_x, rel_y, mask_tokens, cotangent, layout_weight, qkv_weight, qv_bias,
    bias_table, out_weight, out_bias, ln1_gain, ln1_bias, ffn_in_weight, ffn_in_bias, ffn_out_weight,
    ffn_out_bias, ln2_gain, ln2_bias, group_rates,
):
    (
        probs, qkvt, context_t, layer_low, features, unit_one, inverse_one, normed_low, pre_all, hid_all,
        block_own, dresid_two, sums, wqkv, wo, w1, w2,
    ) = forward_window(
        [
            box_coords.T, mask_tokens.reshape(-1, 128), qv_bias, ffn_in_bias, bias_table.T,
            out_bias, ln1_gain, ln1_bias, ffn_out_bias, ln2_gain, ln2_bias,
        ],
        [
            tokens_in, cotangent, rel_x, rel_y, layout_weight, jnp.transpose(qkv_weight, (0, 2, 1)), out_weight,
            ffn_in_weight, ffn_out_weight,
        ],
    )
    block_all, in_all, sum1, sum2, sum3, lay_all, small = backward_window(
        n_dp, layout_weight.shape[0], inverse_one, ln1_gain, sums, dresid_two, hid_all, pre_all, unit_one, normed_low,
        layer_low, features, qkvt, context_t, probs, rel_x, rel_y, w1, w2, wo, wqkv, block_own,
    )
    sums = [v.reshape(-1, v.shape[-1]) for v in (sum1, sum2, sum3, lay_all)]
    out = [block_all] + list(finish(group_rates, small, block_all, in_all, *sums, out_weight.shape[0]))
    out[3] = jnp.transpose(out[3], (0, 2, 1))
    out[5] = out[5].T
    return tuple(out)


def solution(mesh):
    placed = (
        P("dp", None), P("dp", None), P("dp", None, None), P("dp", None, None), P("dp"), P("dp", None),
        P(), P(None, None, "tensor"), P(None, "tensor"), P(None, "tensor"), P("tensor", None),
        P(), P(), P(), P(None, "tensor"), P("tensor"), P("tensor", None), P(), P(), P(), P(),
    )
    return jax.shard_map(
        functools.partial(local, mesh.shape["dp"], mesh.shape["tensor"]),
        mesh=mesh,
        in_specs=placed,
        out_specs=(
            P("dp", None), P("dp", None), P(), P(None, None, "tensor"), P(None, "tensor"),
            P(None, "tensor"), P("tensor", None), P(), P(), P(), P(None, "tensor"), P("tensor"),
            P("tensor", None), P(), P(), P(),
        ),
        check_vma=False,
    )
```

```python
import functools
import math

import jax
import jax.numpy as jnp
from jax import lax
from jax.experimental import pallas as pl
from jax.experimental.pallas import tpu as pltpu
from jax.sharding import PartitionSpec as P

HD = 64
LFREQ = 64
BUCKETS = 32
EPSILON = 1e-05
ROWS = 16
HEADS_T = 3
MESH = pl.DeviceIdType.MESH

F_FEAT, F_NEAR, F_HEAD, F_FAR, F_BOTH, F_OUT, F_CONTEXT, F_NORM, F_UP, F_THIRD, F_DONE = range(11)
AT_R, AT_Q, AT_K, AT_V, AT_O, U0, D0, U1, D1, U2, D2 = range(11)
WAYS = {
    AT_R: (1, 0),
    AT_Q: (2, 1),
    AT_K: (2, 1),
    AT_V: (2, 0),
    AT_O: (2, 1),
    U0: (4, 0),
    D0: (4, 0),
    U1: (4, 0),
    D1: (4, 0),
    U2: (4, 0),
    D2: (1, 0),
}
SEND_ORDER = (AT_K, AT_V, AT_Q, U1, AT_R, D0, U0, AT_O, D1, U2, D2)
FORWARD = {
    (F_NEAR, 0): ((AT_K, 0),),
    (F_HEAD, 1): ((AT_V, 0),),
    (F_HEAD, 2): ((AT_Q, 0),),
    (F_HEAD, 3): ((AT_K, 1), (U1, 0),),
    (F_HEAD, 4): ((AT_V, 1), (AT_R, 0), (AT_Q, 1), (D0, 0),),
    (F_HEAD, 5): ((U0, 0), (U1, 1),),
    (F_HEAD, 6): ((AT_O, 0),),
    (F_HEAD, 7): ((D0, 1), (U0, 1), (D1, 0), (U1, 2),),
    (F_HEAD, 8): ((U2, 0),),
    (F_HEAD, 9): ((AT_O, 1),),
    (F_HEAD, 10): ((D0, 2), (U0, 2),),
    (F_CONTEXT, 0): ((D1, 1),),
    (F_NORM, 1): ((U2, 1),),
    (F_NORM, 2): ((D2, 0),),
    (F_NORM, 3): ((D1, 2),),
    (F_UP, 0): ((U2, 2),),
}

START, FFN, NORM, OUT, HEAD, SENT, MERGED, DLAYER, LAYOUT, TABLE, TAIL = range(11)
A0, A1, A2, B0, B1, B2, C0, C1, C2, C3, C4, C5, C6, BLOCK, BLOCK_ON, INPUT_ON, LAY, LAY_ON, SMALL_STEP = range(19)
X, Y, Z_NEAR, Z_FAR = range(4)
ORDERS = (
    ((Z_NEAR, Z_FAR, X, Y), (Z_FAR, Z_NEAR, Y)),
    ((Y, X, Z_NEAR, Z_FAR), (Z_FAR, Z_NEAR, Y)),
    ((X, Y, Z_NEAR, Z_FAR), (Z_FAR, Z_NEAR, Y)),
    ((Y, X, Z_NEAR, Z_FAR), (Z_FAR, Z_NEAR, Y)),
    ((X, Y, Z_NEAR, Z_FAR), (Z_FAR, Z_NEAR, Y)),
    ((Z_NEAR, Z_FAR, X, Y), (Z_FAR, Z_NEAR, Y)),
    ((Y, X, Z_NEAR, Z_FAR), (Z_FAR, Z_NEAR, Y)),
    ((Y, X, Z_NEAR, Z_FAR), (Z_FAR, Z_NEAR, Y)),
    ((Y, X, Z_NEAR, Z_FAR), (Z_FAR, Z_NEAR, Y)),
    ((X, Y, Z_NEAR, Z_FAR), (Y, Z_FAR, Z_NEAR)),
    ((X, Z_NEAR, Z_FAR, Y), (Z_FAR, Z_NEAR, Y)),
    ((Y, X, Z_NEAR, Z_FAR), (Z_FAR, Z_NEAR, Y)),
    ((X, Y, Z_NEAR, Z_FAR), (Z_FAR, Z_NEAR, Y)),
)
SCHEDULE = {
    (START, 0): ((BLOCK, 2),),
    (FFN, 3): ((BLOCK_ON, 2),),
    (FFN, 10): ((A0, 0), (A2, 0),),
    (FFN, 11): ((A1, 0),),
    (HEAD, 2): ((A2, 1), (B1, 0),),
    (HEAD, 4): ((A0, 1), (B2, 0), (B0, 0), (A1, 1),),
    (HEAD, 5): ((BLOCK, 0),),
    (HEAD, 7): ((A0, 2),),
    (HEAD, 9): ((B1, 1),),
    (HEAD, 11): ((A0, 3), (B0, 1),),
    (SENT, 0): ((B1, 2), (B2, 1),),
    (MERGED, 0): ((A2, 2), (A1, 2), (A0, 4), (B0, 2), (B2, 2), (B1, 3), (BLOCK_ON, 0),),
    (LAYOUT, 0): ((C0, 0), (A2, 3),),
    (TABLE, 0): ((C1, 0), (C4, 0), (C2, 0), (C0, 1), (A0, 5), (B0, 3), (C3, 0), (B1, 4),),
    (TABLE, 3): ((C5, 0), (A2, 4),),
    (TABLE, 4): ((C4, 1), (B2, 3), (C6, 0), (C0, 2),),
    (TABLE, 5): ((BLOCK, 1), (BLOCK, 3), (B0, 4),),
    (TABLE, 7): ((B1, 5),),
    (TABLE, 8): ((A1, 3),),
    (TABLE, 12): ((A2, 5),),
    (TABLE, 13): ((C6, 1),),
    (TABLE, 14): ((C0, 3), (B2, 4),),
    (TABLE, 15): ((B0, 5), (A1, 4), (C3, 1), (C6, 2), (C0, 4), (B2, 5), (INPUT_ON, 0),),
    (TAIL, 0): (
        (C1, 1), (B1, 6), (A2, 6), (A0, 6), (C4, 2), (A1, 5), (C3, 2), (C2, 1), (SMALL_STEP, 0), (B0, 6), (C6, 3),
        (C0, 5), (C5, 1), (C1, 2), (C3, 3), (C2, 2), (B2, 6), (C6, 4), (C4, 3), (C5, 2), (BLOCK_ON, 1), (C1, 3),
        (C2, 3), (C6, 5), (C4, 4), (A1, 6), (C5, 3), (BLOCK_ON, 3), (C1, 4), (SMALL_STEP, 1), (C0, 6), (C3, 4),
        (C2, 4), (C4, 5), (C5, 4), (C6, 6), (LAY, 0), (C1, 5), (SMALL_STEP, 2), (C2, 5), (C3, 5), (C4, 6), (C5, 5),
        (SMALL_STEP, 3), (C1, 6), (LAY_ON, 0), (C3, 6), (C2, 6), (SMALL_STEP, 4), (C5, 6),
    ),
}


def nt(a, b):
    return lax.dot_general(a, b, (((1,), (1,)), ((), ())), preferred_element_type=jnp.float32)


def nn(a, b):
    return jnp.dot(a, b, preferred_element_type=jnp.float32)


def xor_index(index, bit):
    return index + bit - 2 * bit * ((index // bit) % 2)


def signal_peers(peers):
    barrier = pltpu.get_barrier_semaphore()
    for peer in peers:
        pl.semaphore_signal(barrier, inc=1, device_id=peer, device_id_type=MESH)


def wait_peers(peers):
    pl.semaphore_wait(pltpu.get_barrier_semaphore(), len(peers))


def remote(src, dst, send, recv, peer):
    return pltpu.make_async_remote_copy(
        src_ref=src, dst_ref=dst, send_sem=send, recv_sem=recv, device_id=peer, device_id_type=MESH
    )


HERE, MATE, ACROSS, PASS, BESIDE, PASS_BESIDE, ALONG, PASS_ALONG, LAST_BESIDE, LAST_ALONG, PASS_LAST = range(11)


class Gather:
    def __init__(self, own, place, rows, kind, bit, sems, slot, peers):
        self.own, self.place, self.rows, self.kind, self.bit = own, place, rows, kind, bit
        self.send, self.recv, self.here = sems
        self.slot = slot
        self.mate, self.across, self.near, self.sides = peers

    def part(self, flip_zero, flip_one):
        if self.kind == 1:
            return pl.ds(0, self.rows)
        if self.kind == 2:
            side = self.sides[self.bit]
            side = 1 - side if flip_zero else side
            return pl.ds(pl.multiple_of(side * (self.rows // 2), 16), self.rows // 2)
        zero = 1 - self.sides[0] if flip_zero else self.sides[0]
        one = 1 - self.sides[1] if flip_one else self.sides[1]
        return pl.ds(pl.multiple_of((zero + 2 * one) * (self.rows // 4), 16), self.rows // 4)

    def halved(self, part, second):
        h = part.size // 2
        return pl.ds(pl.multiple_of(part.start + (h if second else 0), 16), h)

    def copy(self, name):
        s = self.slot
        whole = pl.ds(0, self.rows)
        mine = self.part(False, False)
        if name == HERE:
            return pltpu.make_async_copy(self.own(whole), self.place(0, whole), self.here.at[s])

        def pass_on(rows, k):
            return self.place(2, rows), self.place(3, rows), self.mate, k

        def relay(rows, to, k):
            return self.place(2, rows), self.place(2, rows), self.near[to], k

        src, dst, peer, k = {
            MATE: lambda: (self.own(whole), self.place(1, whole), self.mate, 0),
            ACROSS: lambda: (self.own(mine), self.place(2, mine), self.across, 1),
            PASS: lambda: pass_on(mine, 2),
            BESIDE: lambda: relay(mine, self.bit, 3),
            PASS_BESIDE: lambda: pass_on(self.part(True, False), 4),
            ALONG: lambda: relay(mine, 1, 5),
            PASS_ALONG: lambda: pass_on(self.part(False, True), 6),
            LAST_BESIDE: lambda: relay(self.halved(self.part(False, True), False), 0, 7),
            LAST_ALONG: lambda: relay(self.halved(self.part(True, False), True), 1, 8),
            PASS_LAST: lambda: pass_on(self.part(True, True), 9),
        }[name]()
        return remote(src, dst, self.send.at[s, k], self.recv.at[s, k], peer)

    def names(self, stage):
        return {
            1: (((PASS,), (ACROSS,)),),
            2: (((BESIDE, PASS), (ACROSS,)), ((PASS_BESIDE,), (BESIDE,))),
            4: (
                ((BESIDE, ALONG, PASS), (ACROSS,)),
                ((LAST_BESIDE, LAST_ALONG, PASS_BESIDE, PASS_ALONG), (BESIDE, ALONG)),
                ((PASS_LAST,), (LAST_BESIDE, LAST_ALONG)),
            ),
        }[self.kind][stage]

    def stages(self):
        return {1: 1, 2: 2, 4: 3}[self.kind]

    def start(self):
        self.copy(ACROSS).start()
        self.copy(MATE).start()
        self.copy(HERE).start()

    def forward(self, stage):
        starts, waits = self.names(stage)
        for name in waits:
            self.copy(name).wait_recv()
        for name in starts:
            self.copy(name).start()

    def arrive_near(self):
        self.copy(HERE).wait()
        self.copy(MATE).wait_recv()

    def arrive_far(self):
        for stage in range(self.stages()):
            for name in self.names(stage)[0]:
                if name in (PASS, PASS_BESIDE, PASS_ALONG, PASS_LAST):
                    self.copy(name).wait_recv()

    def finish(self):
        for name in (MATE, ACROSS) + sum((self.names(stage)[0] for stage in range(self.stages())), ()):
            self.copy(name).wait_send()


def waves(column, frequency, quarter):
    angle = column * frequency
    turns = jnp.floor(angle * (2.0 / math.pi) + 0.5)
    rest = ((angle - turns * 1.5703125) - turns * 4.837512969970703125e-4) - turns * 7.549789948768648e-8
    quadrant = turns.astype(jnp.int32) + quarter
    z = rest * rest
    sine = ((-1.9515295891e-4 * z + 8.3321608736e-3) * z - 1.6666654611e-1) * z * rest + rest
    cosine = ((2.443315711809948e-5 * z - 1.388731625493765e-3) * z + 4.166664568298827e-2) * z * z - 0.5 * z + 1.0
    value = jnp.where(quadrant % 2 == 1, cosine, sine)
    return jnp.where((quadrant // 2) % 2 == 1, -value, value)


def gelu(v):
    return 0.5 * v * (1.0 + jnp.tanh(math.sqrt(2.0 / math.pi) * (v + 0.044715 * (v * v * v))))


def row_of(ref):
    return ref[...].reshape(1, ref.shape[0])


def column_of(row):
    return jnp.broadcast_to(row, (8, 128)).T[:, 0:1]


def forward_kernel(
    box_ref, mask_ref, qvb_ref, b1_ref, table_ref, ob_ref, g1_ref, s1_ref, c2_ref, g2_ref, s2_ref,
    tok_in, cot_in, rx_in, ry_in, lay_in, qkv_own, wo_own, w1_own, w2_own,
    probs_out, qkvt_out, ctxt_out, low_out, feat_out, unit_out, inv_out, nlow_out, pre_out, hid_out,
    block_out, dres_out, sums_out, wqkv_out, wo_out, w1_out, w2_out,
    low, feat, unit_rows, nlow, block_rows, dres_rows, lay, tokb, cotb, rxb, ryb, vec, rows_own, wqkv, wo, w1, w2, rows, cols, tabs, layer_in, qkvt, pbuf, ctxt, ctx, normed, pre,
    hid, acc, send, recv, here, out_sem, p_sem, in_sem,
):
    t, d = lax.axis_index("tensor"), lax.axis_index("dp")
    mate, across = {"tensor": xor_index(t, 1)}, {"tensor": xor_index(t, 2)}
    near = [{"dp": xor_index(d, 1)}, {"dp": xor_index(d, 2)}]
    peers = (mate, across, near, (d % 2, (d // 2) % 2))
    win, model = tokb.shape
    heads = 4 * HEADS_T
    cols_t = HEADS_T * HD
    hid_t = w1_own.shape[1]
    sems = (send, recv, here)
    f32, bf16 = jnp.float32, jnp.bfloat16
    block = 128

    everyone = [mate, across] + near
    signal_peers(everyone)
    own_rows = pl.ds(pl.multiple_of(t * win, win), win)
    loads = [
        pltpu.make_async_copy(src, dst, in_sem.at[k])
        for k, (src, dst) in enumerate(
            [(tok_in.at[own_rows], tokb), (rx_in.at[t], rxb), (ry_in.at[t], ryb), (cot_in.at[own_rows], cotb), (lay_in, lay)]
        )
    ]
    for c in loads:
        c.start()
    for k, ref in enumerate((ob_ref, g1_ref, s1_ref, c2_ref, g2_ref, s2_ref)):
        vec[k : k + 1, :] = row_of(ref)
    rows_own[...] = jnp.zeros_like(rows_own)
    rows_own[0:1, :] = row_of(b1_ref)
    rows_own[1 : 1 + HEADS_T, 0 : 2 * BUCKETS] = table_ref[...].astype(f32)
    rows_own[4:6, 0:cols_t] = qvb_ref[...]

    def piece_rows(r, s, count):
        return pl.ds(pl.multiple_of(r * count + s.start, 16), s.size)

    gathers = {}

    def chunk(name, own, place, count):
        gathers[name] = Gather(own, place, count, *WAYS[name], sems, name, peers)

    chunk(AT_R, lambda s: rows_own.at[s], lambda r, s: rows.at[r, s], 8)
    for n, name in enumerate((AT_Q, AT_K, AT_V)):
        chunk(
            name,
            lambda s, n=n: qkv_own.at[n, s],
            lambda r, s, n=n: wqkv.at[n, piece_rows(r, s, cols_t)],
            cols_t,
        )
    chunk(AT_O, lambda s: wo_own.at[s], lambda r, s: wo.at[piece_rows(r, s, cols_t)], cols_t)
    third = hid_t // 3
    for k in range(3):
        units = pl.ds(k * third, third)
        chunk(
            U0 + 2 * k, lambda s, units=units: w1_own.at[s, units], lambda r, s, units=units: w1.at[r, s, units], model
        )

        def moved(s, k=k):
            return pl.ds(pl.multiple_of(s.start + k * third, 16), s.size)

        chunk(
            D0 + 2 * k, lambda s, moved=moved: w2_own.at[moved(s)], lambda r, s, moved=moved: w2.at[r, moved(s)], third
        )

    def at_slot(phase, index=0):
        for name, stage in FORWARD.get((phase, index), ()):
            gathers[name].forward(stage)

    def at_loop(phase, index, count, first=0, step=1):
        for k in range(count):
            if (phase, first + step * k) in FORWARD:
                @pl.when(index == k)
                def _(k=k):
                    at_slot(phase, first + step * k)

    def near_pieces(names):
        for name in names:
            gathers[name].arrive_near()

    def far_pieces(names):
        for name in names:
            gathers[name].arrive_far()

    lane = lax.broadcasted_iota(jnp.int32, (1, 128), 1)
    quarter = jnp.where(lane >= LFREQ, 1, 0)
    frequency = jnp.exp((lane % LFREQ).astype(f32) * (-math.log(1000.0) / LFREQ))
    loads[0].wait()
    loads[4].wait()

    def layer_rows(i):
        sl = pl.ds(pl.multiple_of(i * block, block), block)
        box = box_ref[:, pl.ds(pl.multiple_of(t * win + i * block, block), block)].astype(f32)
        for m in range(4):
            feat[sl, 2 * LFREQ * m : 2 * LFREQ * (m + 1)] = waves(
                column_of(box[m : m + 1, :]), frequency, quarter
            ).astype(bf16)
        value = tokb[sl, :].astype(f32) + nn(feat[sl, :], lay[...])
        layer_in[sl, :] = value
        low[sl, :] = value.astype(bf16)
        at_loop(F_FEAT, i, 4)

    wait_peers(everyone)
    for name in SEND_ORDER:
        gathers[name].start()
    pl.loop(0, win // block)(layer_rows)

    def bias_columns(pieces):
        for r in pieces:
            turned = rows[r, :, 0:256].T
            for n, row in ((0, 4), (2, 5)):
                cols[n, pl.ds(r * cols_t, cols_t), :] = turned[0:cols_t, row : row + 1]
            tabs[HEADS_T * r : HEADS_T * (r + 1), :] = rows[r, 1 : 1 + HEADS_T, 0:128]

    def project(pieces):
        for n in range(3):
            sl = pl.ds(pieces[0] * cols_t, len(pieces) * cols_t)
            if True:
                value = nt(wqkv[n, sl, :], low[...])
                if n != 1:
                    value = value + cols[n, sl, :]
                qkvt[n, sl, :] = value.astype(bf16)

    near_pieces((AT_R, AT_Q, AT_K, AT_V))
    bias_columns((0, 1))
    project((0, 1))
    at_slot(F_NEAR)
    for c in loads[1:3]:
        c.wait()

    def table_row(h):
        return (tabs[pl.ds(h, 1), :] * 2048.0 + 32768.5).astype(jnp.int32) - 32768

    def p_copy(i, slot):
        return pltpu.make_async_copy(pbuf.at[slot], probs_out.at[pl.ds(2 * i, 2)], p_sem.at[slot])

    def two_heads(i):
        slot = i % 2
        sl = pl.ds(pl.multiple_of(i * 2 * HD, 2 * HD), 2 * HD)
        q = (qkvt[0, sl, :].astype(f32).T * HD ** (-0.5)).astype(bf16)
        tab = jnp.broadcast_to((table_row(2 * i) << 16) + table_row(2 * i + 1), (win, 128))
        bias = ([], [])
        for c in range(win // 128):
            at = slice(128 * c, 128 * c + 128)
            word = jnp.take_along_axis(tab, rxb[:, at], axis=1) + jnp.take_along_axis(
                tab, ryb[:, at] + BUCKETS, axis=1
            )
            second = word << 16
            bias[0].append((word - (second >> 16)).astype(f32) * 2.0**-27)
            bias[1].append(second.astype(f32) * 2.0**-27)

        @pl.when(i >= 2)
        def _():
            p_copy(i - 2, slot).wait()

        for u in range(2):
            rows_u = pl.ds(pl.multiple_of(i * 2 * HD + u * HD, HD), HD)
            s = nn(q[:, u * HD : (u + 1) * HD], qkvt[1, rows_u, :]) + jnp.concatenate(bias[u], axis=1)
            m = jnp.max(s, axis=1, keepdims=True)
            e = jnp.exp(s - m)
            p = e * (1.0 / jnp.sum(e, axis=1, keepdims=True))
            pbuf[slot, u] = p
            ctxt[rows_u, :] = nt(qkvt[2, rows_u, :], p.astype(bf16)).astype(bf16)
            at_loop(F_HEAD, i, heads // 2, u, 2)
        p_copy(i, slot).start()

    pl.loop(0, heads // 4)(two_heads)
    at_slot(F_FAR)
    far_pieces((AT_R, AT_Q, AT_K, AT_V))
    bias_columns((2, 3))
    project((2, 3))
    at_slot(F_BOTH)
    pl.loop(heads // 4, heads // 2)(two_heads)

    last = heads // 2
    outs = [
        (qkvt, qkvt_out), (ctxt, ctxt_out), (wqkv, wqkv_out), (low, low_out), (feat, feat_out),
    ]
    done = []

    def leave(src, dst):
        c = pltpu.make_async_copy(src, dst, out_sem.at[len(done)])
        c.start()
        done.append(c)

    for src, dst in outs:
        leave(src, dst)
    at_slot(F_OUT)
    near_pieces((AT_O,))
    far_pieces((AT_O,))
    leave(wo, wo_out)
    ctx[...] = ctxt[...].astype(f32).T.astype(bf16)
    at_slot(F_CONTEXT)

    @pl.loop(0, win // block)
    def _(i):
        sl = pl.ds(pl.multiple_of(i * block, block), block)
        value = layer_in[sl, :] + nn(ctx[sl, :], wo[...]) + vec[0:1, :]
        mean = jnp.mean(value, axis=1, keepdims=True)
        centered = value - mean
        inverse = lax.rsqrt(jnp.mean(centered * centered, axis=1, keepdims=True) + EPSILON)
        unit = centered * inverse
        unit_rows[sl, :] = unit
        inv_out[sl, :] = inverse
        value = unit * vec[1:2, :] + vec[2:3, :]
        normed[sl, :] = value
        nlow[sl, :] = value.astype(bf16)
        at_loop(F_NORM, i, 4)

    leave(unit_rows, unit_out)
    leave(nlow, nlow_out)
    near_pieces(range(U0, D2 + 1))
    for src, dst in ((w1, w1_out), (w2, w2_out)):
        leave(src.at[pl.ds(0, 2)], dst.at[pl.ds(0, 2)])
    for r in range(2):
        value = nn(nlow[...], w1[r]) + rows[r, 0:1, :]
        pre[r] = value
        low_hid = gelu(value).astype(bf16)
        hid[r] = low_hid
        more = nn(low_hid, w2[r])
        acc[...] = more if r == 0 else acc[...] + more
        for i in range(2):
            at_slot(F_UP, 2 * r + i)

        leave(pre.at[r], pre_out.at[r])
        leave(hid.at[r], hid_out.at[r])

    for k in range(3):
        at_slot(F_THIRD, k)
        far_pieces((U0 + 2 * k, D0 + 2 * k))
        units = pl.ds(k * third, third)

        for r in range(2, 4):
            value = nn(nlow[...], w1[r, :, units]) + rows[r, 0:1, units]
            pre[r, :, units] = value
            low_hid = gelu(value).astype(bf16)
            hid[r, :, units] = low_hid
            acc[...] += nn(low_hid, w2[r, units, :])

        at_slot(F_DONE, k)

        for src, dst in ((pre, pre_out), (hid, hid_out)):
            leave(src.at[pl.ds(2, 2), :, units], dst.at[pl.ds(2, 2), :, units])
        leave(w1.at[pl.ds(2, 2), :, units], w1_out.at[pl.ds(2, 2), :, units])
        leave(w2.at[pl.ds(2, 2), units], w2_out.at[pl.ds(2, 2), units])

    loads[3].wait()

    sums_out[...] = jnp.zeros_like(sums_out)

    @pl.loop(0, win // block)
    def _(i):
        sl = pl.ds(pl.multiple_of(i * block, block), block)
        value = normed[sl, :] + acc[sl, :] + vec[3:4, :]
        mean = jnp.mean(value, axis=1, keepdims=True)
        centered = value - mean
        inverse = lax.rsqrt(jnp.mean(centered * centered, axis=1, keepdims=True) + EPSILON)
        unit = centered * inverse
        block_rows[sl, :] = (unit * vec[4:5, :] + vec[5:6, :]).astype(bf16)
        mask = column_of(mask_ref[pl.ds((win // block) * t + i, 1), :].astype(f32))
        selected = mask * cotb[sl, :].astype(f32)
        scaled = selected * vec[4:5, :]
        mean_one = jnp.mean(scaled, axis=1, keepdims=True)
        mean_two = jnp.mean(scaled * unit, axis=1, keepdims=True)
        dres = (scaled - mean_one - unit * mean_two) * inverse
        dres_rows[sl, :] = dres
        for src, dst, k in ((block_rows, block_out, 30), (dres_rows, dres_out, 31)):
            pltpu.make_async_copy(src.at[sl], dst.at[sl], out_sem.at[k]).start()
        sums_out[0:1, :] += jnp.sum(selected * unit, axis=0, keepdims=True)
        sums_out[1:2, :] += jnp.sum(selected, axis=0, keepdims=True)
        sums_out[2:3, :] += jnp.sum(dres, axis=0, keepdims=True)
        sums_out[3:4, :] += jnp.sum(mask, axis=0, keepdims=True)

    for i in (last - 2, last - 1):
        p_copy(i, i % 2).wait()
    for c in done:
        c.wait()
    for src, dst, k in ((block_rows, block_out, 30), (dres_rows, dres_out, 31)):
        pltpu.make_async_copy(src, dst, out_sem.at[k]).wait()
    for g in gathers.values():
        g.finish()


def forward_window(small, large):
    wo_own, w1_own = large[6:8]
    win, model = large[2].shape[1], large[0].shape[1]
    cols_t, hid_t = wo_own.shape[0], w1_own.shape[1]
    heads = 4 * HEADS_T
    f32, bf16 = jnp.float32, jnp.bfloat16
    shape = jax.ShapeDtypeStruct
    here = pl.BlockSpec(memory_space=pltpu.VMEM)
    away = pl.BlockSpec(memory_space=pl.ANY)
    outs = [
        (shape((heads, win, win), f32), away),
        (shape((3, model, win), bf16), away),
        (shape((model, win), bf16), away),
        (shape((win, model), bf16), away),
        (shape((win, 8 * LFREQ), bf16), away),
        (shape((win, model), f32), away),
        (shape((win, 1), f32), here),
        (shape((win, model), bf16), away),
        (shape((4, win, hid_t), f32), away),
        (shape((4, win, hid_t), bf16), away),
        (shape((win, model), bf16), away),
        (shape((win, model), f32), away),
        (shape((8, model), f32), here),
        (shape((3, model, model), bf16), away),
        (shape((model, model), bf16), away),
        (shape((4, model, hid_t), bf16), away),
        (shape((4, hid_t, model), bf16), away),
    ]
    return pl.pallas_call(
        forward_kernel,
        in_specs=[here] * len(small) + [away] * len(large),
        out_specs=[spec for _, spec in outs],
        out_shape=[s for s, _ in outs],
        scratch_shapes=[
            pltpu.VMEM((win, model), bf16),
            pltpu.VMEM((win, 8 * LFREQ), bf16),
            pltpu.VMEM((win, model), f32),
            pltpu.VMEM((win, model), bf16),
            pltpu.VMEM((win, model), bf16),
            pltpu.VMEM((win, model), f32),
            pltpu.VMEM((8 * LFREQ, model), bf16),
            pltpu.VMEM((win, model), bf16),
            pltpu.VMEM((win, model), bf16),
            pltpu.VMEM((win, win), jnp.int32),
            pltpu.VMEM((win, win), jnp.int32),
            pltpu.VMEM((8, model), f32),
            pltpu.VMEM((8, model), f32),
            pltpu.VMEM((3, model, model), bf16),
            pltpu.VMEM((model, model), bf16),
            pltpu.VMEM((4, model, hid_t), bf16),
            pltpu.VMEM((4, hid_t, model), bf16),
            pltpu.VMEM((4, 8, model), f32),
            pltpu.VMEM((3, model, 1), f32),
            pltpu.VMEM((heads, 128), f32),
            pltpu.VMEM((win, model), f32),
            pltpu.VMEM((3, model, win), bf16),
            pltpu.VMEM((2, 2, win, win), f32),
            pltpu.VMEM((model, win), bf16),
            pltpu.VMEM((win, model), bf16),
            pltpu.VMEM((win, model), f32),
            pltpu.VMEM((4, win, hid_t), f32),
            pltpu.VMEM((4, win, hid_t), bf16),
            pltpu.VMEM((win, model), f32),
            pltpu.SemaphoreType.DMA((11, 10)),
            pltpu.SemaphoreType.DMA((11, 10)),
            pltpu.SemaphoreType.DMA((11,)),
            pltpu.SemaphoreType.DMA((32,)),
            pltpu.SemaphoreType.DMA((2,)),
            pltpu.SemaphoreType.DMA((5,)),
        ],
        compiler_params=pltpu.CompilerParams(
            vmem_limit_bytes=60 * 2**20, collective_id=0, has_side_effects=True
        ),
        name="forward_window",
    )(*small, *large)


def bits_of(size):
    return [1 << b for b in range(size.bit_length() - 1)]


def tn(a, b):
    return lax.dot_general(a, b, (((0,), (0,)), ((), ())), preferred_element_type=jnp.float32)


UNIT = 128


class Reduce:
    def __init__(self, slot, order, part, core, landing, final, extra, result, acc, sems, peers):
        self.slot, self.order, self.part, self.core, self.landing = slot, order, part, core, landing
        self.final, self.extra, self.result, self.acc = final, extra, result, acc
        self.send, self.recv, self.here = sems
        self.mate, self.partners, self.further, self.sides = peers
        self.total = core.at[0] if acc is None else acc
        self.steps = order[0] + order[1]

    def move(self, k, src, dst, peer):
        return remote(src, dst, self.send.at[self.slot, k], self.recv.at[self.slot, k], peer)

    def region(self, fixed, other=None):
        index = [slice(None)]
        for axis in (Z_FAR, Z_NEAR, Y):
            if axis == other:
                index.append(pl.ds(1 - self.sides[axis], 1))
            elif axis in fixed:
                index.append(pl.ds(self.sides[axis], 1))
            else:
                index.append(slice(None))
        return tuple(index)

    def pieces(self, stage):
        return (0,) if X in self.order[0][:stage] else (0, 1)

    def moves(self, stage, piece=None):
        axis = self.steps[stage]
        peer = self.partners[axis]
        if stage >= len(self.order[0]):
            done = self.order[1][: stage - len(self.order[0])]
            rows = self.region([a for a in (Z_FAR, Z_NEAR, Y) if a not in done])
            src = self.result.at[rows] if done else self.final
            return [self.move(10 + len(done), src, self.result.at[rows], peer)]
        fixed = self.order[0][:stage]
        if axis == X:
            return [self.move(2 + 2 * stage, self.core.at[(1,) + self.region(fixed)], self.landing[stage].at[0], peer)] if piece != 0 else []
        return [
            self.move(2 + 2 * stage + p, self.core.at[(p,) + self.region(fixed, axis)], self.landing[stage].at[p], peer)
            for p in self.pieces(stage)
            if piece in (None, p)
        ]

    def to_mate(self, piece):
        return self.move(piece, self.part(piece), self.core.at[piece], self.mate)

    def own_copy(self):
        rows = self.region((Z_FAR, Z_NEAR, Y))
        return pltpu.make_async_copy(self.final, self.result.at[rows], self.here.at[self.slot])

    def more(self, k):
        return self.move(13 + k, self.final_of(k), self.extra.at[k], self.further[k])

    def final_of(self, k):
        return self.final if k == 0 else self.extra.at[len(self.further) + k]

    def merge(self, piece, unit, half, value):
        at = (unit, half)
        value = value.reshape(2, 2, 16, value.shape[-1]) + self.core[(piece,) + at].astype(jnp.float32)
        if piece == 0:
            self.total[at] = value.astype(self.total.dtype)
        else:
            self.core[(1,) + at] = value.astype(jnp.bfloat16)

    def take(self, stage):
        for m in self.moves(stage):
            m.wait_recv()
        count = len(self.order[0])
        if stage == count:
            self.own_copy().wait()
        if stage >= count:
            return
        axis = self.steps[stage]
        rows = self.region(self.order[0][: stage + 1])
        for p in (0,) if axis == X else self.pieces(stage):
            dst = self.total if p == 0 else self.core.at[p]
            value = dst[rows].astype(jnp.float32) + self.landing[stage][p].astype(jnp.float32)
            if stage + 1 == count:
                self.final[...] = value.astype(jnp.bfloat16)
            else:
                dst[rows] = value.astype(dst.dtype)
        if stage + 1 == count:
            for k in range(len(self.further)):
                self.more(k).start()
                self.more(k).wait()
                total = self.final_of(k)[...].astype(jnp.float32) + self.extra[k].astype(jnp.float32)
                self.final_of(k + 1)[...] = total.astype(jnp.bfloat16)
            if self.further:
                self.final[...] = self.final_of(len(self.further))[...]
            self.own_copy().start()

    def go(self, stage, piece=None):
        if stage < len(self.order[0]) and self.steps[stage] != X and self.acc is not None and piece != 1:
            rows = self.region(self.order[0][:stage], self.steps[stage])
            self.core[(0,) + rows] = self.acc[rows].astype(jnp.bfloat16)
        for m in self.moves(stage, piece):
            m.start()

    def next(self, stage):
        self.take(stage)
        if stage + 1 < len(self.steps):
            self.go(stage + 1)

    def sent(self):
        for stage in range(len(self.steps)):
            for m in self.moves(stage):
                m.wait_send()


def landing_shapes(units, order):
    shapes, pieces, dims = [], 2, {Z_FAR: 2, Z_NEAR: 2, Y: 2}
    for axis in order[0]:
        if axis == X:
            pieces = 1
        else:
            dims[axis] = 1
        shapes.append((pieces, units, dims[Z_FAR], dims[Z_NEAR], dims[Y], 16))
    return shapes


def xor_level(level, k):
    for bit in (1, 2):
        if k & bit:
            level = xor_index(level, bit)
    return level


def gelu_slope(v):
    k = math.sqrt(2.0 / math.pi)
    square = v * v
    t = jnp.tanh(k * v * (1.0 + 0.044715 * square))
    return 0.5 * (1.0 + t) + (0.5 * k) * v * (1.0 - t * t) * (1.0 + 3 * 0.044715 * square)


SMALL = 16


def backward_kernel(
    n_dp, inv_ref, gain_ref, sums_ref, dres_in, hid_in, pre_in, unit_in, nlow_in, low_in, feat_in, qkvt_in, ctxt_in,
    probs_in, rx_in, ry_in, w1_in, w2_in, wo_in, wqkv_in, block_in,
    block_all, in_all, red1, red2, red3, lay_all, small_out,
    arena, hidb, preb, dres, unit, nlow, nlow_t, dn, low_rows, qkvb, ctxtb, dctx, lowb, featb, wob, rxb, ryb, hot, acc,
    part1, part2, part3, core1, core2, core3, landings, finals, extras, acc3, small, small_in, short,
    load_sem, send, recv, here, share_send, share_recv, small_send, small_recv, p_sem,
):
    t, d = lax.axis_index("tensor"), lax.axis_index("dp")
    mate, across = {"tensor": xor_index(t, 1)}, {"tensor": xor_index(t, 2)}
    beside = {"dp": xor_index(d, 1)}
    along = [None] + [{"dp": d + 2 * (xor_level((d // 2) % 4, k) - (d // 2) % 4)} for k in range(1, 4)]
    further = [{"dp": xor_index(d, bit)} for bit in bits_of(n_dp) if bit >= 8]
    partners = {X: across, Y: beside, Z_NEAR: along[1], Z_FAR: along[2]}
    peers = (mate, partners, further, {Y: d % 2, Z_NEAR: (d // 2) % 2, Z_FAR: (d // 4) % 2})
    sems = (send, recv, here)
    f32, bf16 = jnp.float32, jnp.bfloat16
    win, model = dres.shape
    heads = 4 * HEADS_T
    cols_t = HEADS_T * HD
    hid_t = model
    block = 128

    everyone = [mate, across, beside] + along[1:] + further
    signal_peers(everyone)

    def load(k, src, dst):
        return pltpu.make_async_copy(src, dst, load_sem.at[k])

    def w_rows(r):
        return pl.ds(r * hid_t, hid_t)

    def h_rows(r):
        return pl.ds(r * win, win)

    order = (3, 1, 2, 0)
    ld_dres = load(0, dres_in, dres)
    ld_hid = {r: load(1 + r, hid_in.at[r], hidb.at[h_rows(r)]) for r in order}
    ld_w2 = {r: load(5 + r, w2_in.at[r], arena.at[w_rows(r)]) for r in order}
    ld_w1 = {r: load(9 + r, w1_in.at[r], arena.at[w_rows(4 + r)]) for r in order}
    ld_pre = {r: load(13 + r, pre_in.at[r], preb.at[i % 2]) for i, r in enumerate(order)}
    ld_rest = [
        load(17 + k, src, dst)
        for k, (src, dst) in enumerate(
            [
                (nlow_in, nlow), (unit_in, unit), (ctxt_in, ctxtb), (wo_in, wob), (qkvt_in, qkvb), (low_in, lowb),
                (feat_in, featb), (rx_in.at[t], rxb), (ry_in.at[t], ryb),
            ]
        )
    ]
    ld_wqkv = [load(26 + n, wqkv_in.at[n], hidb.at[pl.ds(n * model, model)]) for n in range(3)]
    ld_dres.start()
    for r in order:
        ld_hid[r].start()
    for r in order[:2]:
        ld_pre[r].start()
    for r in order:
        ld_w2[r].start()
    ld_rest[0].start()
    for r in order:
        ld_w1[r].start()
    for c in ld_rest[1:]:
        c.start()

    def chunks(first, units, parts, core, result, acc=None):
        out, at = [], 0
        for k, (count, part) in enumerate(zip(units, parts)):
            rows = pl.ds(at, count)
            slot = first + k
            out.append(
                Reduce(
                    slot, ORDERS[slot], part, core.at[:, rows], landings[slot], finals[slot], extras[slot],
                    result.at[rows], None if acc is None else acc.at[rows], sems, peers,
                )
            )
            at += count
        return out

    third = hid_t // 3

    def pairs(ref):
        return [lambda p, k=k: ref.at[p, pl.ds(2 * k, 2)] for k in range(3)]

    s2 = chunks(0, [2] * 3, pairs(part2), core2, red2)
    s1 = chunks(3, [2] * 3, pairs(part1), core1, red1)
    s3 = chunks(
        6, [1] * 7,
        [lambda p, k=k: part2.at[p, pl.ds(k, 1)] for k in range(6)] + [lambda p: part3.at[p]],
        core3, red3, acc3,
    )
    lay_t = featb.shape[1] // 4

    def share(k, src, whole, rows, part=0, parts=1):
        def at(index):
            return whole.at[pl.ds(pl.multiple_of((index * parts + part) * rows, rows), rows)]

        def moved(j, from_ref, index, peer):
            return remote(from_ref, at(index), share_send.at[k, j], share_recv.at[k, j], peer)

        far = xor_index(t, 2)
        return {
            "here": pltpu.make_async_copy(src, at(t), share_send.at[k, 3]),
            "across": moved(0, src, t, across),
            "mate": moved(1, src, t, mate),
            "pass": moved(2, at(far), far, mate),
        }

    def share_start(c):
        for name in ("across", "mate", "here"):
            c[name].start()

    def share_pass(c):
        c["across"].wait_recv()
        c["pass"].start()

    def share_end(c):
        c["here"].wait()
        c["mate"].wait_recv()
        c["pass"].wait_recv()
        for name in ("across", "mate", "pass"):
            c[name].wait_send()

    quarter_win = win // 4
    sh_block = [
        share(k, block_in.at[pl.ds(k * quarter_win, quarter_win)], block_all, quarter_win, k, 4) for k in range(4)
    ]
    sh_in = share(4, low_rows, in_all, win)
    sh_lay = share(5, red3.at[pl.ds(6, 1)], lay_all, 1)
    bits = [mate, across, beside, along[1], along[2]] + further

    def small_move(k):
        return remote(small.at[k], small_in.at[k], small_send.at[k], small_recv.at[k], bits[k])

    def small_step(k):
        small_move(k).wait()
        small[k + 1] = small[k] + small_in[k]
        if k + 1 < len(bits):
            small_move(k + 1).start()

    named = dict(zip(range(A0, C6 + 1), s2 + s1 + s3))

    def run(what, stage):
        if what in named:
            named[what].next(stage)
        elif what == BLOCK:
            share_start(sh_block[stage])
        elif what == BLOCK_ON:
            share_pass(sh_block[stage])
        elif what == INPUT_ON:
            share_pass(sh_in)
        elif what == LAY:
            share_start(sh_lay)
        elif what == LAY_ON:
            share_pass(sh_lay)
        elif what == SMALL_STEP:
            small_step(stage)

    def at_slot(phase, index=0):
        for what, stage in SCHEDULE.get((phase, index), ()):
            run(what, stage)

    def at_loop(phase, index, count, first=0):
        for k in range(count):
            if (phase, first + k) in SCHEDULE:
                @pl.when(index == k)
                def _(k=k):
                    at_slot(phase, first + k)


    small[0] = jnp.zeros_like(small[0])
    small[0, 3:4, :] = sums_ref[2:3, :]
    small[0, 4:6, :] = sums_ref[0:2, :]
    small[0, 6:7, :] = sums_ref[3:4, :]

    def own_row(base, r):
        index = t
        for bit in (1, 2):
            if r & bit:
                index = xor_index(index, bit)
        return pl.ds(base + index, 1)

    ld_dres.wait()

    @pl.loop(0, win // block)
    def _(i):
        sl = pl.ds(pl.multiple_of(i * block, block), block)
        low_rows[sl, :] = dres[sl, :].astype(bf16)

    def grad_w2(r, c):
        sl = pl.ds(pl.multiple_of(c * third, third), third)
        return tn(hidb[h_rows(r), sl], low_rows[...])

    def grad_w1(r, c):
        sl = pl.ds(pl.multiple_of(c * third, third), third)
        return nn(nlow_t[sl, :], hidb[h_rows(r), :])

    def blocks(value):
        return value.reshape(value.shape[0] // UNIT, 2, 2, 2, 16, value.shape[1])

    def for_mate(group, grad, r, part):
        @pl.loop(0, 3)
        def _(c):
            part[r // 2, pl.ds(2 * c, 2)] = blocks(grad(r, c).astype(bf16))

        for g in group:
            g.to_mate(r // 2).start()

    def merge_all(g, piece, value):
        half = UNIT // 2
        for k in range(value.shape[0] // half):
            g.merge(piece, k // 2, k % 2, value[k * half : (k + 1) * half])

    def for_own(group, grad, r):
        for c, g in enumerate(group):
            g.to_mate(r // 2).wait_recv()
            merge_all(g, r // 2, grad(r, c))
            g.go(0, r // 2)

    for r in order[:2]:
        ld_hid[r].wait()
        if r == order[0]:
            for_mate((), grad_w2, r, part2)
            wait_peers(everyone)
            at_slot(START)
            for g in s2:
                g.to_mate(r // 2).start()
        else:
            for_mate(s2, grad_w2, r, part2)

    ld_rest[0].wait()
    nlow_t[...] = nlow[...].astype(f32).T.astype(bf16)
    for j, r in enumerate(order):
        ld_pre[r].wait()
        ld_w2[r].wait()
        ld_w1[r].wait()

        @pl.loop(0, 2)
        def _(i, j=j, r=r):
            count = win // 2
            sl = pl.ds(pl.multiple_of(i * count, count), count)
            hs = pl.ds(pl.multiple_of(r * win + i * count, count), count)
            dhid = nt(low_rows[sl, :], arena[w_rows(r), :])
            dpre = (dhid * gelu_slope(preb[j % 2, sl, :])).astype(bf16)
            hidb[hs, :] = dpre
            row = own_row(8, r)
            small[0, row, :] += jnp.sum(dpre.astype(f32), axis=0, keepdims=True)
            more = nt(dpre, arena[w_rows(4 + r), :])
            dn[sl, :] = more if j == 0 else dn[sl, :] + more
            at_loop(FFN, i, 2, 3 * j)

        if j + 2 < 4:
            ld_pre[order[j + 2]].start()
        if j < 2:
            for_mate(s1, grad_w1, r, part1)
        else:
            for_own(s1, grad_w1, r)
        if j == 0:
            for q in order[2:]:
                ld_hid[q].wait()
                for_own(s2, grad_w2, q)
        at_slot(FFN, 3 * j + 2)

    for c in ld_wqkv:
        c.start()

    def p_load(h, slot):
        return pltpu.make_async_copy(probs_in.at[h], preb.at[slot, :, pl.ds(0, win)], p_sem.at[slot])

    for h in range(2):
        p_load(h, h).start()
    for g in s2:
        for p in range(2):
            g.to_mate(p).wait_send()

    ld_rest[1].wait()

    @pl.loop(0, win // block)
    def _(i):
        sl = pl.ds(pl.multiple_of(i * block, block), block)
        up = dres[sl, :] + dn[sl, :]
        units = unit[sl, :]
        scaled = up * row_of(gain_ref)
        mean_one = jnp.mean(scaled, axis=1, keepdims=True)
        mean_two = jnp.mean(scaled * units, axis=1, keepdims=True)
        value = (scaled - mean_one - units * mean_two) * inv_ref[sl, :]
        dn[sl, :] = value
        low_rows[sl, :] = value.astype(bf16)
        small[0, 0:1, :] += jnp.sum(value, axis=0, keepdims=True)
        small[0, 1:2, :] += jnp.sum(up * units, axis=0, keepdims=True)
        small[0, 2:3, :] += jnp.sum(up, axis=0, keepdims=True)

    at_slot(NORM)
    for c in ld_rest[2:]:
        c.wait()

    @pl.loop(0, 4)
    def _(r):
        sl = pl.ds(pl.multiple_of(r * cols_t, cols_t), cols_t)
        dctx[sl, :] = nt(wob[sl, :], low_rows[...]).astype(bf16)

    at_slot(OUT)

    @pl.loop(0, heads)
    def _(h):
        slot = h % 2
        sl = pl.ds(pl.multiple_of(h * HD, HD), HD)
        dc_t = dctx[sl, :]
        dc = dc_t.astype(f32).T.astype(bf16)
        p_load(h, slot).wait()
        p = preb[slot, :, 0:win]
        dp = nn(dc, qkvb[2, sl, :])
        row_dot = jnp.sum(p * dp, axis=1, keepdims=True)
        ds = (p * (dp - row_dot)).astype(bf16)
        qkvb[2, sl, :] = nn(dc_t, p.astype(bf16)).astype(bf16)
        dq = nt(qkvb[1, sl, :], ds) * HD ** (-0.5)
        dk = nn(qkvb[0, sl, :], ds) * HD ** (-0.5)
        qkvb[0, sl, :] = dq.astype(bf16)
        qkvb[1, sl, :] = dk.astype(bf16)
        arena[pl.ds(pl.multiple_of(h * win, win), win), 0:win] = ds

        @pl.when(h + 2 < heads)
        def _():
            p_load(h + 2, slot).start()

        at_loop(HEAD, h, heads)

    for c in ld_wqkv:
        c.wait()
    def rows_of(r):
        return pl.ds(r * cols_t, cols_t)

    def grad_out(r):
        return nn(ctxtb[rows_of(r), :], low_rows[...])

    def grad_proj(n, r):
        return nn(qkvb[n, rows_of(r), :], lowb[...])

    halves = (lambda r: grad_proj(2, r), grad_out, lambda r: grad_proj(0, r), lambda r: grad_proj(1, r))
    sixth = UNIT // 2
    each = cols_t // sixth
    for r in (3, 1):
        for k, grad in enumerate(halves):
            value = grad(r).astype(bf16)
            for j in range(each):
                at = k * each + j
                part2[r // 2, at // 2, at % 2] = value[j * sixth : (j + 1) * sixth].reshape(2, 2, 16, model)
            if k % 2 == 1:
                for g in s3[:6][3 * (k // 2) : 3 * (k // 2) + 3]:
                    g.to_mate(r // 2).start()
    at_slot(SENT)
    for r in (2, 0):
        for k, grad in enumerate(halves):
            value = grad(r)
            for j in range(each):
                at = k * each + j
                g = s3[at // 2]
                if at % 2 == 0:
                    g.to_mate(r // 2).wait_recv()
                g.merge(r // 2, 0, at % 2, value[j * sixth : (j + 1) * sixth])
                if at % 2 == 1:
                    g.go(0, r // 2)
    at_slot(MERGED)

    @pl.loop(0, win // block)
    def _(i):
        sl = pl.ds(pl.multiple_of(i * block, block), block)
        value = dn[sl, :]
        for n in range(3):
            value = value + tn(qkvb[n, :, sl], hidb[pl.ds(n * model, model), :])
        dn[sl, :] = value
        at_loop(DLAYER, i, 4)

    low_rows[...] = dn[...].astype(bf16)

    def grad_lay(r):
        index = t
        for bit in (1, 2):
            if r & bit:
                index = xor_index(index, bit)
        return tn(featb[:, pl.ds(pl.multiple_of(index * lay_t, lay_t), lay_t)], low_rows[...])

    for r in (3, 1):
        part3[r // 2] = blocks(grad_lay(r).astype(bf16))
        s3[6].to_mate(r // 2).start()
    at_slot(LAYOUT)
    for_own(s3[6:], lambda r, c: grad_lay(r), 2)
    for_own(s3[6:], lambda r, c: grad_lay(r), 0)
    share_start(sh_in)

    ones = jnp.ones((8, win), bf16)
    short[...] = jnp.zeros_like(short)
    for n, at in ((0, 0), (2, cols_t)):
        total = nt(ones, qkvb[n])
        for r in range(4):
            short[r : r + 1, at : at + cols_t] = total[0:1, r * cols_t : (r + 1) * cols_t]

    acc[...] = jnp.zeros_like(acc)
    one, zero = bf16(1), bf16(0)
    hots = BUCKETS * ROWS
    @pl.loop(0, win // ROWS // 2)
    def _(i):
        total = None
        for u in range(2):
            at = pl.multiple_of(i * 2 * ROWS + u * ROWS, ROWS)
            x = rxb[pl.ds(at, ROWS), :].astype(f32).astype(bf16)
            y = ryb[pl.ds(at, ROWS), :].astype(f32).astype(bf16)
            for b in range(BUCKETS):
                hot[u, b * ROWS : (b + 1) * ROWS, :] = jnp.where(x == bf16(b), one, zero)
                hot[u, hots + b * ROWS : hots + (b + 1) * ROWS, :] = jnp.where(y == bf16(b), one, zero)
            left = jnp.concatenate(
                [arena[pl.ds(pl.multiple_of(h * win + at, ROWS), ROWS), 0:win] for h in range(heads)], axis=0
            )
            more = nt(left, hot[u])
            total = more if total is None else total + more
        acc[...] += total
        at_loop(TABLE, i, 16)

    row = lax.broadcasted_iota(jnp.int32, (ROWS, 2 * hots), 0)
    col = lax.broadcasted_iota(jnp.int32, (ROWS, 2 * hots), 1) % ROWS
    picked = jnp.concatenate(
        [
            jnp.sum(jnp.where(row == col, acc[h * ROWS : (h + 1) * ROWS, :], 0.0), axis=0, keepdims=True)
            for h in range(heads)
        ]
        + [jnp.zeros((16 - heads, 2 * hots), f32)],
        axis=0,
    )
    fold = (
        lax.broadcasted_iota(jnp.int32, (2 * hots, 128), 0) // ROWS
        == lax.broadcasted_iota(jnp.int32, (2 * hots, 128), 1)
    ).astype(f32)
    table = jnp.dot(picked, fold, preferred_element_type=f32, precision=lax.Precision.HIGHEST)
    for r in range(4):
        for a in range(HEADS_T):
            lane = 2 * cols_t + a * 2 * BUCKETS
            short[r : r + 1, lane : lane + 2 * BUCKETS] = table[
                r * HEADS_T + a : r * HEADS_T + a + 1, 0 : 2 * BUCKETS
            ]
    for r in range(4):
        small[0, own_row(12, r), :] = short[r : r + 1, :]

    small_move(0).start()
    at_slot(TAIL)
    for k in range(5, len(bits)):
        small_step(k)
    small_out[...] = small[len(bits)]
    for c in sh_block + [sh_in, sh_lay]:
        share_end(c)
    for g in s1 + s3:
        for p in range(2):
            g.to_mate(p).wait_send()
    for g in s2 + s1 + s3:
        g.sent()


def backward_window(n_dp, lay_rows, inv, gain, sums, dres, hid, pre, unit, nlow, low, feat, qkvt, ctxt, probs, rx, ry, w1, w2, wo, wqkv, block_own):
    win, model = dres.shape
    heads = 4 * HEADS_T
    cols_t = HEADS_T * HD
    lay_t = lay_rows // 4
    units = model // UNIT
    rest = (4 * cols_t + lay_t) // UNIT
    block = (2, 2, 2, 16, model)
    more = max(0, len(bits_of(n_dp)) - 3)
    levels = 5 + more
    sizes = [2] * 6 + [1] * 7
    f32, bf16 = jnp.float32, jnp.bfloat16
    shape = jax.ShapeDtypeStruct
    here = pl.BlockSpec(memory_space=pltpu.VMEM)
    away = pl.BlockSpec(memory_space=pl.ANY)
    outs = [
        (shape((4 * win, model), bf16), away),
        (shape((4 * win, model), bf16), away),
        (shape((units,) + block, bf16), away),
        (shape((units,) + block, bf16), away),
        (shape((rest,) + block, bf16), away),
        (shape((4,) + block, bf16), away),
        (shape((SMALL, model), f32), here),
    ]
    V = pltpu.VMEM
    S = pltpu.SemaphoreType.DMA
    return pl.pallas_call(
        functools.partial(backward_kernel, n_dp),
        in_specs=[here] * 3 + [away] * 17,
        out_specs=[spec for _, spec in outs],
        out_shape=[s for s, _ in outs],
        scratch_shapes=[
            V((8 * model, model), bf16), V((3 * model, model), bf16), V((2, win, model), f32), V((win, model), f32),
            V((win, model), f32), V((win, model), bf16), V((model, win), bf16), V((win, model), f32),
            V((win, model), bf16), V((3, model, win), bf16), V((model, win), bf16), V((model, win), bf16),
            V((win, model), bf16), V((win, lay_rows), bf16), V((model, model), bf16), V((win, win), jnp.int32),
            V((win, win), jnp.int32), V((2, 2 * BUCKETS * ROWS, win), bf16), V((heads * ROWS, 2 * BUCKETS * ROWS), f32),
            V((2, units) + block, bf16), V((2, units) + block, bf16), V((2, 1) + block, bf16),
            V((2, units) + block, bf16), V((2, units) + block, bf16), V((2, rest) + block, bf16),
            [[V(s + (model,), bf16) for s in landing_shapes(n, o)] for n, o in zip(sizes, ORDERS)],
            [V((n, 1, 1, 1, 16, model), bf16) for n in sizes],
            [V((2 * more + 1, n, 1, 1, 1, 16, model), bf16) for n in sizes], V((rest,) + block, f32),
            V((levels + 1, SMALL, model), f32), V((levels, SMALL, model), f32), V((8, model), f32),
            S((29,)), S((len(sizes), 13 + more)), S((len(sizes), 13 + more)), S((len(sizes),)), S((6, 4)), S((6, 3)),
            S((levels,)), S((levels,)), S((2,)),
        ],
        compiler_params=pltpu.CompilerParams(
            vmem_limit_bytes=63 * 2**20, collective_id=1, has_side_effects=True
        ),
        name="backward_window",
    )(inv, gain, sums, dres, hid, pre, unit, nlow, low, feat, qkvt, ctxt, probs, rx, ry, w1, w2, wo, wqkv, block_own)


def finish_kernel(
    rates, small_ref, in_in, red1, red2, red3, lay_in,
    in_out, lay_out, qkv_out, qvb_out, table_out, wo_out, ob_out, g1_out, s1_out, w1_out, b1_out, w2_out, c2_out,
    g2_out, s2_out, in_low, low1, low2, low3, lay_low, in_wide, wide1, wide2, wide3, lay_wide, load_sem, store_sem,
):
    t = lax.axis_index("tensor")
    cols_t = HEADS_T * HD
    inverse = 1.0 / small_ref[6:7, 0:1]
    jobs = []

    def job(src, low, wide, out, rate):
        jobs.append((src, low, wide, out, rate))

    def split(src, low, wide, out, rate, step):
        for at in range(0, low.shape[0], step):
            sl = pl.ds(at, step)
            job(src.at[sl], low.at[sl], None if wide is None else wide.at[sl], out.at[sl], rate)

    split(in_in, in_low, in_wide, in_out, None, 256)
    split(red2, low2, wide2, w2_out, 4, 256)
    split(red1, low1, wide1, w1_out, 3, 256)
    for n, at, rate in ((2, 0, 0), (None, 1, 1), (0, 2, 0), (1, 3, 0)):
        sl = pl.ds(at * cols_t, cols_t)
        job(red3.at[sl], low3.at[sl], wide3.at[sl], wo_out if n is None else qkv_out.at[n], rate)
    split(lay_in, lay_low, lay_wide, lay_out, 6, 256)
    loads = [pltpu.make_async_copy(src, low, load_sem.at[k]) for k, (src, low, _, _, _) in enumerate(jobs)]
    ahead = len(loads)
    for c in loads[:ahead]:
        c.start()

    def row(ref, index, rate):
        ref[...] = (small_ref[index : index + 1, :] * (inverse * rates[rate])).reshape(ref.shape)

    for ref, index, rate in ((ob_out, 0, 1), (g1_out, 1, 2), (s1_out, 2, 2), (c2_out, 3, 4), (g2_out, 4, 5), (s2_out, 5, 5)):
        row(ref, index, rate)
    b1_out[...] = (small_ref[pl.ds(8 + t, 1), :] * (inverse * rates[3])).reshape(b1_out.shape)
    own = small_ref[pl.ds(12 + t, 1), :]
    for k in range(2):
        qvb_out[k : k + 1, :] = own[:, k * cols_t : (k + 1) * cols_t] * (inverse * rates[0])
    for a in range(HEADS_T):
        at = 2 * cols_t + a * 2 * BUCKETS
        table_out[a : a + 1, :] = own[:, at : at + 2 * BUCKETS] * (inverse * rates[7])

    stores = []
    for k, (_, low, wide, out, rate) in enumerate(jobs):
        loads[k].wait()
        if k + ahead < len(jobs):
            loads[k + ahead].start()
        if wide is None:
            stores.append(pltpu.make_async_copy(low, out, store_sem.at[k]))
        else:
            factor = inverse if rate is None else inverse * rates[rate]
            wide[...] = low[...].astype(jnp.float32) * factor
            stores.append(pltpu.make_async_copy(wide, out, store_sem.at[k]))
        stores[-1].start()
    for c in stores:
        c.wait()


def finish(rates, small, block_all, in_all, sum1, sum2, sum3, lay_all, cols_t):
    f32, bf16 = jnp.float32, jnp.bfloat16
    shape = jax.ShapeDtypeStruct
    here = pl.BlockSpec(memory_space=pltpu.VMEM)
    away = pl.BlockSpec(memory_space=pl.ANY)
    model = in_all.shape[1]
    vector = (shape((model,), f32), here)
    outs = [
        (shape(in_all.shape, f32), away),
        (shape(lay_all.shape, f32), away),
        (shape((3, cols_t, model), f32), away),
        (shape((2, cols_t), f32), here),
        (shape((HEADS_T, 2 * BUCKETS), f32), here),
        (shape((cols_t, model), f32), away),
        vector, vector, vector,
        (shape(sum1.shape, f32), away),
        vector,
        (shape(sum2.shape, f32), away),
        vector, vector, vector,
    ]
    wide = [in_all, sum1, sum2, sum3, lay_all]
    return pl.pallas_call(
        finish_kernel,
        in_specs=[pl.BlockSpec(memory_space=pltpu.SMEM), here] + [away] * 5,
        out_specs=[spec for _, spec in outs],
        out_shape=[s for s, _ in outs],
        scratch_shapes=[pltpu.VMEM(v.shape, bf16) for v in wide]
        + [pltpu.VMEM(v.shape, f32) for v in wide]
        + [pltpu.SemaphoreType.DMA((32,)), pltpu.SemaphoreType.DMA((32,))],
        compiler_params=pltpu.CompilerParams(vmem_limit_bytes=60 * 2**20),
        name="finish",
    )(rates, small, in_all, sum1, sum2, sum3, lay_all)


def local(
    n_dp, n_t,
    tokens_in, box_coords, rel_x, rel_y, mask_tokens, cotangent, layout_weight, qkv_weight, qv_bias,
    bias_table, out_weight, out_bias, ln1_gain, ln1_bias, ffn_in_weight, ffn_in_bias, ffn_out_weight,
    ffn_out_bias, ln2_gain, ln2_bias, group_rates,
):
    (
        probs, qkvt, context_t, layer_low, features, unit_one, inverse_one, normed_low, pre_all, hid_all,
        block_own, dresid_two, sums, wqkv, wo, w1, w2,
    ) = forward_window(
        [
            box_coords.T, mask_tokens.reshape(-1, 128), qv_bias, ffn_in_bias, bias_table.T,
            out_bias, ln1_gain, ln1_bias, ffn_out_bias, ln2_gain, ln2_bias,
        ],
        [
            tokens_in, cotangent, rel_x, rel_y, layout_weight, jnp.transpose(qkv_weight, (0, 2, 1)), out_weight,
            ffn_in_weight, ffn_out_weight,
        ],
    )
    block_all, in_all, sum1, sum2, sum3, lay_all, small = backward_window(
        n_dp, layout_weight.shape[0], inverse_one, ln1_gain, sums, dresid_two, hid_all, pre_all, unit_one, normed_low,
        layer_low, features, qkvt, context_t, probs, rel_x, rel_y, w1, w2, wo, wqkv, block_own,
    )
    sums = [v.reshape(-1, v.shape[-1]) for v in (sum1, sum2, sum3, lay_all)]
    out = [block_all] + list(finish(group_rates, small, block_all, in_all, *sums, out_weight.shape[0]))
    out[3] = jnp.transpose(out[3], (0, 2, 1))
    out[5] = out[5].T
    return tuple(out)


def solution(mesh):
    placed = (
        P("dp", None), P("dp", None), P("dp", None, None), P("dp", None, None), P("dp"), P("dp", None),
        P(), P(None, None, "tensor"), P(None, "tensor"), P(None, "tensor"), P("tensor", None),
        P(), P(), P(), P(None, "tensor"), P("tensor"), P("tensor", None), P(), P(), P(), P(),
    )
    return jax.shard_map(
        functools.partial(local, mesh.shape["dp"], mesh.shape["tensor"]),
        mesh=mesh,
        in_specs=placed,
        out_specs=(
            P("dp", None), P("dp", None), P(), P(None, None, "tensor"), P(None, "tensor"),
            P(None, "tensor"), P("tensor", None), P(), P(), P(), P(None, "tensor"), P("tensor"),
            P("tensor", None), P(), P(), P(),
        ),
        check_vma=False,
    )
```
